32 devices in a mesh: batch: 4 (over z), lat: 8 (over y, x, core).
Axes of the slice: x: 2, y: 2, z: 4, core: 2. Of those that a mesh axis runs over, the one named last changes fastest.
Arguments:
- tokens: bfloat16 [12, 96, 180, 768], P('batch', 'lat'), may hold values from -6 to 6
- cotangent: bfloat16 [12, 96, 180, 768], P('batch', 'lat'), may hold values from -6 to 6
- sample_weight: int32 [12], P('batch'), may hold values from 1 to 4
- row_count: int32 [8], replicated, may hold values from 11 to 12, as said below
- band_count: int32 [8], replicated, may hold values from 1 to 13, as said below
- norm1_gain: float32 [768], replicated, may hold values from 0.25 to 1.75
- norm1_bias: float32 [768], replicated, may hold values from -1.5 to 1.5
- spec_w1: bfloat16 [2, 8, 96, 96], replicated, may hold values from -0.4375 to 0.4375
- spec_b1: float32 [2, 8, 96], replicated, may hold values from -1.5 to 1.5
- spec_w2: bfloat16 [2, 8, 96, 96], replicated, may hold values from -0.4375 to 0.4375
- spec_b2: float32 [2, 8, 96], replicated, may hold values from -1.5 to 1.5
- norm2_gain: float32 [768], replicated, may hold values from 0.25 to 1.75
- norm2_bias: float32 [768], replicated, may hold values from -1.5 to 1.5
- fc1_weight: bfloat16 [768, 3072], replicated, may hold values from -0.21875 to 0.21875
- fc1_bias: float32 [3072], replicated, may hold values from -1.5 to 1.5
- fc2_weight: bfloat16 [3072, 768], replicated, may hold values from -0.109375 to 0.109375
- fc2_bias: float32 [768], replicated, may hold values from -1.5 to 1.5
Outputs:
- mixed: bfloat16 [12, 96, 180, 768], P('batch', 'lat')
- spectrum_out: bfloat16 [12, 104, 2, 91, 768], P('batch', 'lat')
- tokens_grad: float32 [12, 96, 180, 768], P('batch', 'lat')
- norm1_gain_grad: float32 [768], replicated
- norm1_bias_grad: float32 [768], replicated
- spec_w1_grad: float32 [2, 8, 96, 96], replicated
- spec_b1_grad: float32 [2, 8, 96], replicated
- spec_w2_grad: float32 [2, 8, 96, 96], replicated
- spec_b2_grad: float32 [2, 8, 96], replicated
- norm2_gain_grad: float32 [768], replicated
- norm2_bias_grad: float32 [768], replicated
- fc1_weight_grad: float32 [768, 3072], replicated
- fc1_bias_grad: float32 [3072], replicated
- fc2_weight_grad: float32 [3072, 768], replicated
- fc2_bias_grad: float32 [768], replicated
- zero_fraction: float32 [], replicated
The draws below stay inside these ranges and needn't reach their ends.
Inputs may be any that keep to these rules, and one draw needn't show every extreme that they name: Index i of lat holds row_count[i] consecutive latitude rows, in order of i and of rows, in the first slots of its block; the counts sum to 90 and the largest is 12. Index i of lat owns band_count[i] consecutive latitude wavenumbers, in order from 0; the counts sum to 90 and the largest is 13.
All inputs are finite; a program needn't handle non-finite values.
Results may differ from the reference program's by a relative error of at most 0.012.
The reference program's roundings to bfloat16 on the way count: a program that leaves them out, or rounds other values in their place, can miss the bound.
Values may be sent and summed in bfloat16 or wider, within the bound.
A program may use at most 640 MiB of HBM per device.

```python
import math
import jax
import jax.numpy as jnp
from jax import lax

D = 768
FF = 3072
BLOCKS = 8
BS = 96
H = 90
W = 180
KW = 91
SAMPLES = 12
RMAX = 12
MB = 13
N_LAT = 8


def draw_row_count(key, part):
    key = jax.random.fold_in(key, 11)
    ranking = jnp.argsort(jax.random.permutation(key, N_LAT)).astype(jnp.int32)
    shortfall = N_LAT * RMAX - H
    return (RMAX - (ranking < shortfall).astype(jnp.int32)).astype(jnp.int32)


def draw_band_count(key, part):
    key = jax.random.fold_in(key, 23)
    first_key, second_key = jax.random.split(key)
    ranking = jnp.argsort(jax.random.permutation(first_key, N_LAT)).astype(jnp.int32)
    limit_raised = max(1, N_LAT // 8)
    raised = 1 + jax.random.randint(second_key, (), 0, limit_raised)
    shortfall = N_LAT * RMAX - H + raised
    others = N_LAT - raised
    position = ranking - raised
    cuts = shortfall // others + (position < shortfall % others).astype(jnp.int32)
    return jnp.where(ranking < raised, RMAX + 1, RMAX - cuts).astype(jnp.int32)


def touch_ends(values, rng, smallest, top_value):
    longest = values.shape.index(max(values.shape))
    spots = []
    for shift in (0, 1):
        where = [jax.random.randint(jax.random.fold_in(rng, axis), (), 0, length) for axis, length in enumerate(values.shape)]
        where[longest] = (where[longest] + shift) % values.shape[longest]
        spots.append(tuple(where))
    return values.at[spots[0]].set(smallest).at[spots[1]].set(top_value)


def steps_of(own_key, extent, cuts, smallest, top_value):
    loudness = 1.0
    for dim, blocks in cuts:
        draws = jax.random.uniform(jax.random.fold_in(jax.random.fold_in(own_key, 6), dim), (blocks,), jnp.float32, smallest / len(cuts), top_value / len(cuts))
        loudness = loudness * jnp.repeat(jnp.exp(draws), extent[dim] // blocks).reshape((-1,) + (1,) * (len(extent) - 1 - dim))
    return loudness


def scatter_about(stream_key, shape, scale, bound, cuts=(), held_as=jnp.bfloat16):
    drawn = jax.random.normal(stream_key, shape, jnp.float32) * scale
    if len(cuts) > 0:
        drawn = steps_of(stream_key, shape, cuts, -0.22, 0.18) * drawn
    return jnp.clip(drawn, min=-bound, max=bound).astype(held_as)


def setup_inputs(seed: int = 0) -> dict:
    seeds = jax.random.split(jax.random.key(seed), 18)
    return {
        "tokens": scatter_about(seeds[0], (SAMPLES, N_LAT * RMAX, W, D), 1.0, 6.0, ((0, 4), (1, 8))),
        "cotangent": scatter_about(seeds[1], (SAMPLES, N_LAT * RMAX, W, D), 1.0, 6.0, ((0, 4), (1, 8))),
        "sample_weight": touch_ends(jax.random.randint(seeds[2], (SAMPLES,), 1, 5), jax.random.fold_in(seeds[2], 1), 1, 4).astype(jnp.int32),
        "row_count": draw_row_count(jax.random.fold_in(seeds[17], 71), 0),
        "band_count": draw_band_count(jax.random.fold_in(seeds[17], 71), 0),
        "norm1_gain": jnp.clip(1.0 + 0.15 * jax.random.normal(seeds[5], (D,), jnp.float32), 0.25, 1.75),
        "norm1_bias": scatter_about(seeds[6], (D,), 0.3, 1.5, (), jnp.float32),
        "spec_w1": scatter_about(seeds[7], (2, BLOCKS, BS, BS), (2 * BS) ** -0.5, 0.4375),
        "spec_b1": scatter_about(seeds[8], (2, BLOCKS, BS), 0.3, 1.5, (), jnp.float32),
        "spec_w2": scatter_about(seeds[9], (2, BLOCKS, BS, BS), (2 * BS) ** -0.5, 0.4375),
        "spec_b2": scatter_about(seeds[10], (2, BLOCKS, BS), 0.3, 1.5, (), jnp.float32),
        "norm2_gain": jnp.clip(1.0 + 0.15 * jax.random.normal(seeds[11], (D,), jnp.float32), 0.25, 1.75),
        "norm2_bias": scatter_about(seeds[12], (D,), 0.3, 1.5, (), jnp.float32),
        "fc1_weight": scatter_about(seeds[13], (D, FF), D ** -0.5, 0.21875),
        "fc1_bias": scatter_about(seeds[14], (FF,), 0.3, 1.5, (), jnp.float32),
        "fc2_weight": scatter_about(seeds[15], (FF, D), FF ** -0.5, 0.109375),
        "fc2_bias": scatter_about(seeds[16], (D,), 0.3, 1.5, (), jnp.float32),
    }


NORM_EPS = 1e-06
SHRINK_LAMBDA = 0.01
SHRINK_SOFTNESS = 0.1
TOP_PRECISION = lax.Precision.HIGHEST

@jax.custom_vjp
def low(v):
    return lax.optimization_barrier(v.astype(jnp.bfloat16)).astype(jnp.float32)

@jax.custom_vjp
def low_back(v):
    return v

def low_keep(v):
    return (low(v), None)

def low_pass(kept, grad):
    return (grad,)

def back_keep(v):
    return (v, None)

def back_low(kept, grad):
    return (low(grad),)
low.defvjp(low_keep, low_pass)
low_back.defvjp(back_keep, back_low)

def smooth_shrink(values):
    upper = jnp.maximum(values - SHRINK_LAMBDA, 0.0)
    lower = jnp.maximum(-values - SHRINK_LAMBDA, 0.0)
    return upper * upper / (upper + SHRINK_SOFTNESS) - lower * lower / (lower + SHRINK_SOFTNESS)

def lon_tables(grid_width):
    mode_count = grid_width // 2 + 1
    mode_index = jnp.arange(mode_count, dtype=jnp.int32)
    turn_count = mode_index[:, None] * jnp.arange(grid_width, dtype=jnp.int32)[None, :] % grid_width
    angles = turn_count.astype(jnp.float32) * (2.0 * math.pi / grid_width)
    cosine = jnp.cos(angles)
    sines = jnp.sin(angles)
    factor = jnp.where((mode_index == 0) | (2 * mode_index == grid_width), 1.0, 2.0)[:, None]
    root_width = math.sqrt(grid_width)
    forward = jnp.concatenate([cosine, -sines], 0).T / root_width
    inverse = jnp.concatenate([factor * cosine, -factor * sines], 0) / root_width
    return (forward, inverse)

def lat_tables(wavenumbers, wave_valid, lat_rows, row_valid, period):
    turn_count = wavenumbers[:, None] * lat_rows[None, :] % period
    angles = turn_count.astype(jnp.float32) * (2.0 * math.pi / period)
    weights = (wave_valid[:, None] & row_valid[None, :]).astype(jnp.float32) / math.sqrt(period)
    cosine = jnp.cos(angles) * weights
    sines = jnp.sin(angles) * weights
    forward = jnp.stack([jnp.stack([cosine, sines], -1), jnp.stack([-sines, cosine], -1)], 1)
    inverse = jnp.stack([jnp.stack([cosine.T, -sines.T], -1), jnp.stack([sines.T, cosine.T], -1)], 1)
    return (forward, inverse)

def complex_matrix(weight):
    top_row = jnp.stack([weight[0], weight[1]], 2)
    bottom_row = jnp.stack([-weight[1], weight[0]], 2)
    return jnp.stack([top_row, bottom_row], 0)

def layer_norm(values, norm_gain, norm_bias):
    average = lax.optimization_barrier(jnp.mean(values, -1, keepdims=True))
    centred = values - average
    inv_std = lax.rsqrt(lax.optimization_barrier(jnp.mean(centred * centred, -1, keepdims=True)) + NORM_EPS)
    return centred * inv_std * norm_gain + norm_bias

def afno_layer(params, grid_in):
    gain_one, bias_one, weight_one, offset_one, weight_two, offset_two, gain_two, bias_two, up_weight, up_bias, down_weight, down_bias = params
    lon_forward, lon_inverse = lon_tables(W)
    all_true = jnp.ones((H,), dtype=bool)
    positions = jnp.arange(H, dtype=jnp.int32)
    lat_forward, lat_inverse = lat_tables(positions, all_true, positions, all_true, H)
    normed_one = layer_norm(grid_in, gain_one, bias_one)
    lon_spec = jnp.einsum('hwd,wk->hkd', normed_one, lon_forward, precision=TOP_PRECISION)
    lon_spec = low_back(low(lon_spec)).reshape(H, 2, KW, D)
    spectrum = jnp.einsum('pori,rikd->pokd', lat_forward, lon_spec, precision=TOP_PRECISION)
    spectrum = low_back(low(spectrum)).reshape(H, 2, KW, BLOCKS, BS)
    first_pre = jnp.einsum('mckbi,cbiqo->mqkbo', spectrum, complex_matrix(weight_one), precision=TOP_PRECISION) + offset_one[None, :, None, :, :]
    first_pre = low_back(first_pre)
    hidden = low(jax.nn.gelu(first_pre, approximate=False))
    second_pre = jnp.einsum('mckbi,cbiqo->mqkbo', hidden, complex_matrix(weight_two), precision=TOP_PRECISION) + offset_two[None, :, None, :, :]
    shrunk = smooth_shrink(second_pre)
    shrunk = low_back(low(shrunk)).reshape(H, 2, KW, D)
    zero_count = jnp.sum(jnp.where(jnp.abs(second_pre) <= SHRINK_LAMBDA, 1.0, 0.0))
    returned = jnp.einsum('ropi,pikd->rokd', lat_inverse, shrunk, precision=TOP_PRECISION)
    returned = low_back(low(returned)).reshape(H, 2 * KW, D)
    filtered = jnp.einsum('hkd,kw->hwd', returned, lon_inverse, precision=TOP_PRECISION)
    summed = grid_in + filtered + normed_one
    normed_two = low(layer_norm(summed, gain_two, bias_two)).reshape(H * W, D)
    up_pre = jnp.dot(normed_two, up_weight, precision=TOP_PRECISION, preferred_element_type=jnp.float32) + up_bias
    up_pre = low_back(up_pre)
    activated = low(jax.nn.gelu(up_pre, approximate=False))
    down_out = jnp.dot(activated, down_weight, precision=TOP_PRECISION, preferred_element_type=jnp.float32) + down_bias
    down_out = low_back(down_out)
    return (summed + down_out.reshape(H, W, D), (shrunk, zero_count))

def reference(tokens, cotangent, sample_weight, row_count, band_count, norm1_gain, norm1_bias, spec_w1, spec_b1, spec_w2, spec_b2, norm2_gain, norm2_bias, fc1_weight, fc1_bias, fc2_weight, fc2_bias):
    params = tuple((argument.astype(jnp.float32) for argument in (norm1_gain, norm1_bias, spec_w1, spec_b1, spec_w2, spec_b2, norm2_gain, norm2_bias, fc1_weight, fc1_bias, fc2_weight, fc2_bias)))
    row_end = jnp.cumsum(row_count).astype(jnp.int32)
    row_start = (row_end - row_count).astype(jnp.int32)
    grid_rows = jnp.arange(H, dtype=jnp.int32)
    owner_lane = lax.optimization_barrier(jnp.sum((row_end[None, :] <= grid_rows[:, None]).astype(jnp.int32), 1)).astype(jnp.int32)
    grid_slot = (owner_lane * RMAX + grid_rows - row_start[owner_lane]).astype(jnp.int32)
    row_steps = jnp.arange(RMAX, dtype=jnp.int32)
    slot_rows = jnp.clip((row_start[:, None] + row_steps[None, :]).reshape(-1), 0, H - 1).astype(jnp.int32)
    slot_valid = (row_steps[None, :] < row_count[:, None]).reshape(-1)
    band_end = jnp.cumsum(band_count).astype(jnp.int32)
    band_start = (band_end - band_count).astype(jnp.int32)
    band_steps = jnp.arange(MB, dtype=jnp.int32)
    band_modes = jnp.clip((band_start[:, None] + band_steps[None, :]).reshape(-1), 0, H - 1).astype(jnp.int32)
    band_valid = (band_steps[None, :] < band_count[:, None]).reshape(-1)

    def one_sample(carry, inputs):
        sample_tokens, sample_cot, weight_int = inputs
        grid_in = sample_tokens.astype(jnp.float32)[grid_slot]
        weight_scale = weight_int.astype(jnp.float32) * 0.5
        grid_cot = sample_cot.astype(jnp.float32)[grid_slot] * weight_scale
        mixed_grid, pullback, aux_values = jax.vjp(afno_layer, params, grid_in, has_aux=True)
        shrunk, zero_count = aux_values
        param_grads, grid_grad = pullback(grid_cot)
        totals = jax.tree.map(jnp.add, carry[0], param_grads)
        mixed_slab = jnp.where(slot_valid[:, None, None], mixed_grid[slot_rows], 0.0).astype(jnp.bfloat16)
        grad_slab = jnp.where(slot_valid[:, None, None], grid_grad[slot_rows], 0.0)
        band_out = jnp.where(band_valid[:, None, None, None], shrunk[band_modes], 0.0).astype(jnp.bfloat16)
        return ((totals, carry[1] + zero_count), (mixed_slab, band_out, grad_slab))
    start_carry = (tuple((jnp.zeros_like(argument) for argument in params)), jnp.zeros((), jnp.float32))
    final_carry, stacked = lax.scan(one_sample, start_carry, (tokens, cotangent, sample_weight))
    totals, zero_total = final_carry
    mixed, spectrum_out, tokens_grad = stacked
    zero_fraction = zero_total / (SAMPLES * H * KW * 2 * D)
    return (mixed, spectrum_out, tokens_grad, totals[0], totals[1], totals[2], totals[3], totals[4], totals[5], totals[6], totals[7], totals[8], totals[9], totals[10], totals[11], zero_fraction)
```

```python
import functools
import math

import jax
import jax.numpy as jnp
import numpy as np
from jax import lax
from jax.experimental import pallas as pl
from jax.experimental.pallas import tpu as pltpu
from jax.sharding import PartitionSpec as P

H = 90
HP = 96

NORM_EPS = 1e-06
SHRINK_LAMBDA = 0.01
SHRINK_SOFTNESS = 0.1
INV_ROOT_TAU = 1.0 / math.sqrt(2.0 * math.pi)
BF = jnp.bfloat16
F32 = jnp.float32
VMEM_BYTES = 64 * 1024 * 1024


def dot(a, b):
    return jnp.dot(a, b, preferred_element_type=F32)


def dot_nt(a, b):
    return lax.dot_general(a, b, (((1,), (1,)), ((), ())), preferred_element_type=F32)


def dot_tn(a, b):
    return lax.dot_general(a, b, (((0,), (0,)), ((), ())), preferred_element_type=F32)


def dot_table(table_ref, x):
    return dot(table_ref[0], x) + dot(table_ref[1], x)


def two_parts(table):
    high = table.astype(BF)
    return high, (table - high.astype(table.dtype)).astype(BF)


def norm_parts(x):
    mean = jnp.mean(x, -1, keepdims=True)
    centred = x - mean
    rstd = lax.rsqrt(jnp.mean(centred * centred, -1, keepdims=True) + NORM_EPS)
    return centred * rstd, rstd


def norm_back(grad, unit, rstd, gain):
    e = grad * gain
    return rstd * (
        e - jnp.mean(e, -1, keepdims=True) - unit * jnp.mean(e * unit, -1, keepdims=True)
    )


def gauss_parts(v):
    d = 1.0 + jnp.abs(v) * (0.3275911 / math.sqrt(2.0))
    t = pl.reciprocal(d, approx=True)
    t = t * (2.0 - d * t)
    e = jnp.exp2(v * v * (-0.5 * math.log2(math.e)))
    poly = 1.061405429 * 0.5
    for c in (-1.453152027, 1.421413741, -0.284496736, 0.254829592):
        poly = poly * t + 0.5 * c
    tail = poly * t * e
    cdf = jnp.where(v >= 0.0, 1.0 - tail, tail)
    return cdf, v * e * INV_ROOT_TAU


def gelu_both(v):
    cdf, slope_part = gauss_parts(v)
    return v * cdf, cdf + slope_part


def shrink_both(u):
    a = jnp.maximum(jnp.abs(u) - SHRINK_LAMBDA, 0.0)
    d = a + SHRINK_SOFTNESS
    t = pl.reciprocal(d, approx=True)
    t = t * (2.0 - d * t)
    size = a * a * t
    value = jnp.where(u >= 0.0, size, -size)
    slope = a * (a + 2.0 * SHRINK_SOFTNESS) * (t * t)
    return value, slope


class Plan:
    def __init__(self, n, samples, rows, width, channels, bands):
        self.n, self.s, self.r, self.w, self.d, self.mb = n, samples, rows, width, channels, bands
        self.kw = width // 2 + 1
        self.kk = -(-self.kw // n)
        self.kp = self.kk + self.kk % 2
        self.q = self.kp // 2
        self.rp = -(-rows // 4) * 4
        self.t = 4 * self.rp
        self.pairs = n * self.q
        self.ki = n * self.kp * 2
        self.rb = max(b for b in (4, 3, 2, 1) if rows % b == 0)
        self.chunks = rows // self.rb
        self.flat = self.rb * width
        self.flatp = -(-self.flat // 256) * 256
        j = np.arange(n)[:, None]
        t = np.arange(self.kp)[None, :]
        self.k_index = (j * self.kk + t).astype(np.int64)
        self.k_valid = (t < self.kk) & (self.k_index < self.kw)
        k = np.where(self.k_valid, self.k_index, 0).reshape(-1)
        ok = self.k_valid.reshape(-1).astype(np.float64)
        angle = 2.0 * np.pi * ((k[:, None] * np.arange(width)[None, :]) % width) / width
        scale = ok[:, None] / math.sqrt(width)
        fwd = np.stack([np.cos(angle) * scale, -np.sin(angle) * scale], 1).reshape(self.ki, width)
        factor = np.where((k == 0) | (2 * k == width), 1.0, 2.0)[:, None, None]
        both = (fwd.reshape(-1, 2, width) * factor).reshape(self.ki, width)
        self.lon = np.stack(two_parts(fwd))
        self.lon_both = np.stack(two_parts(both))
        self.lon_t = np.stack(two_parts(np.ascontiguousarray(fwd.T)))
        self.lon_both_t = np.stack(two_parts(np.ascontiguousarray(both.T)))
        perm = np.zeros((16, self.rp, rows, 16))
        for a in range(16):
            for r in range(rows):
                perm[a, r, r, a] = 1.0
        self.perm = perm.reshape(16 * self.rp, rows * 16).astype(BF)
        self.perm_t = np.ascontiguousarray(self.perm.T)


def lat_matrix(plan, row_count):
    n, rp = plan.n, plan.rp
    start = jnp.cumsum(row_count) - row_count
    steps = jnp.arange(rp, dtype=jnp.int32)
    rows = start[:, None] + steps[None, :]
    valid = steps[None, :] < row_count[:, None]
    kh = jnp.arange(HP, dtype=jnp.int32)
    turns = kh[:, None, None] * rows[None] % H
    angle = turns.astype(F32) * (2.0 * math.pi / H)
    weight = jnp.where((kh < H)[:, None, None] & valid[None], 1.0 / math.sqrt(H), 0.0)
    cosine = jnp.cos(angle) * weight
    sine = jnp.sin(angle) * weight
    real = jnp.stack([cosine, sine], 2)
    imag = jnp.stack([-sine, cosine], 2)
    part = jnp.stack([real, imag], 0)
    eye = jnp.eye(2, dtype=F32)
    full = part[None, :, :, :, None] * eye[:, None, None, None, :, None, None]
    full = full.reshape(4 * HP, n * 4 * rp)
    high = lax.reduce_precision(full, 8, 7)
    return jnp.stack([high, full - high]).astype(BF)


def slot_matrix(plan, band_count):
    start = jnp.cumsum(band_count) - band_count
    steps = jnp.arange(plan.mb, dtype=jnp.int32)
    wave = start[:, None] + steps[None, :]
    valid = steps[None, :] < band_count[:, None]
    kh = jnp.arange(HP, dtype=jnp.int32)
    pick = ((wave[:, :, None] == kh) & valid[:, :, None]).astype(F32)
    eye = jnp.eye(4, dtype=F32)
    full = pick[:, None, :, None, :] * eye[None, :, None, :, None]
    return full.reshape(plan.n * 4 * plan.mb, 4 * HP).astype(BF)


def wide_weight(weight):
    blocks, size = weight.shape[1], weight.shape[2]
    half = blocks // 2
    w = weight.reshape(2, 2, half, size, size)
    eye = jnp.eye(half, dtype=weight.dtype)
    dense = w[:, :, :, :, None, :] * eye[None, None, :, None, :, None]
    dense = dense.reshape(2, 2, half * size, half * size)
    re, im = dense[0], dense[1]
    top = jnp.concatenate([re, im], 2)
    bottom = jnp.concatenate([-im, re], 2)
    return jnp.concatenate([top, bottom], 1)


def wide_bias(bias):
    return bias.reshape(2, 2, -1).transpose(1, 0, 2).reshape(2, 1, -1)


def narrow_bias(wide, blocks, size):
    return wide.reshape(2, 2, -1).transpose(1, 0, 2).reshape(2, blocks, size)


def narrow_grad(wide, blocks, size):
    half = blocks // 2
    g = wide.reshape(2, 2, half, size, 2, half, size)
    diag = jnp.stack([g[:, :, b, :, :, b, :] for b in range(half)], 1)
    real = diag[:, :, 0, :, 0] + diag[:, :, 1, :, 1]
    imag = diag[:, :, 0, :, 1] - diag[:, :, 1, :, 0]
    return jnp.stack([real, imag], 0).reshape(2, blocks, size, size)


def whole(shape):
    zeros = (0,) * len(shape)
    return pl.BlockSpec(shape, lambda *_: zeros)


def whole_once(shape):
    zeros = (0,) * len(shape)
    return pl.BlockSpec(shape, lambda *_: zeros, pipeline_mode=pl.Buffered(1))


SMEM = pl.BlockSpec(memory_space=pltpu.SMEM)
ANY = pl.BlockSpec(memory_space=pl.ANY)


def params():
    return pltpu.CompilerParams(
        dimension_semantics=("arbitrary",), vmem_limit_bytes=VMEM_BYTES
    )


def cost(flops, size):
    return pl.CostEstimate(flops=int(flops), bytes_accessed=int(size), transcendentals=0)


def interleave(plan, perm_ref, rows_ref, out_ref):
    def body(c, carry):
        at = pl.multiple_of(c * 16, 16)
        block = rows_ref[:, pl.ds(at, 16), :].reshape(plan.r * 16, plan.d)
        mixed = dot(perm_ref[...], block).astype(BF)
        out_ref[pl.ds(c * 4, 4)] = mixed.reshape(4, plan.t, plan.d)
        return carry

    lax.fori_loop(0, plan.ki // 16, body, 0)


def deinterleave(plan, perm_t_ref, in_ref, rows_ref):
    def body(c, carry):
        at = pl.multiple_of(c * 16, 16)
        block = in_ref[pl.ds(c * 4, 4)].reshape(4 * plan.t, plan.d)
        rows = dot(perm_t_ref[...], block).astype(BF)
        rows_ref[:, pl.ds(at, 16), :] = rows.reshape(plan.r, 16, plan.d)
        return carry

    lax.fori_loop(0, plan.ki // 16, body, 0)


def first_kernel(plan, tok_ref, gain_ref, bias_ref, lon_ref, perm_ref, out_ref, rows_ref):
    i = pl.program_id(0)
    for u in range(plan.rb):
        unit, _ = norm_parts(tok_ref[0, u].astype(F32))
        normed = (unit * gain_ref[...] + bias_ref[...]).astype(BF)
        rows_ref[i * plan.rb + u] = dot_table(lon_ref, normed).astype(BF)

    @pl.when(i == plan.chunks - 1)
    def _():
        interleave(plan, perm_ref, rows_ref, out_ref)


def row_block(plan, s):
    return pl.BlockSpec((1, plan.rb, plan.w, plan.d), lambda i: (s, i, 0, 0))


def own_block(plan):
    return pl.BlockSpec((plan.rb, plan.w, plan.d), lambda i: (i, 0, 0))


def first_call(plan, s, tokens, gain, bias):
    shape = (plan.pairs, plan.t, plan.d)
    return pl.pallas_call(
        functools.partial(first_kernel, plan),
        grid=(plan.chunks,),
        in_specs=[
            row_block(plan, s),
            whole((1, plan.d)),
            whole((1, plan.d)),
            whole((2, plan.ki, plan.w)),
            whole(plan.perm.shape),
        ],
        out_specs=whole(shape),
        out_shape=jax.ShapeDtypeStruct(shape, BF),
        scratch_shapes=[pltpu.VMEM((plan.r, plan.ki, plan.d), BF)],
        compiler_params=params(),
        cost_estimate=cost(9e9, 8e6),
        name="lon_forward",
    )(tokens, gain, bias, plan.lon, plan.perm)


def spectral_kernel(
    plan,
    valid_ref,
    in_ref,
    lat_ref,
    lat_t_ref,
    slot_ref,
    m1_ref,
    b1_ref,
    m2_ref,
    b2_ref,
    back_ref,
    band_ref,
    spec_ref,
    hid_ref,
    slope1_ref,
    slope2_ref,
    zero_ref,
    shr_ref,
):
    q = pl.program_id(0)
    half = plan.d // 2

    @pl.when(q == 0)
    def _():
        zero_ref[...] = jnp.zeros_like(zero_ref)

    x = in_ref[:, 0].reshape(plan.n * plan.t, plan.d)
    spec = dot_table(lat_ref, x).astype(BF)
    ok = (lax.broadcasted_iota(jnp.int32, (HP, 1), 0) < H).astype(F32)
    for g in range(2):
        lanes = slice(g * half, (g + 1) * half)
        for a in range(2):
            top = a * 2 * HP
            spec_ref[0, g, a * HP : (a + 1) * HP, :half] = spec[top : top + HP, lanes]
            spec_ref[0, g, a * HP : (a + 1) * HP, half:] = spec[top + HP : top + 2 * HP, lanes]
        u1 = dot(spec_ref[0, g], m1_ref[g]) + b1_ref[g]
        hidden, slope = gelu_both(u1)
        hid_ref[0, g] = hidden.astype(BF)
        slope1_ref[0, g] = slope.astype(BF)
        u2 = dot(hid_ref[0, g], m2_ref[g]) + b2_ref[g]
        small = (jnp.abs(u2) <= SHRINK_LAMBDA).astype(F32)
        for a in range(2):
            part = small[a * HP : (a + 1) * HP] * ok
            zero_ref[...] += jnp.sum(part, 0, keepdims=True) * valid_ref[q * 2 + a]
        value, slope = shrink_both(u2)
        slope2_ref[0, g] = slope.astype(BF)
        value = value.astype(BF)
        for a in range(2):
            top = a * 2 * HP
            shr_ref[top : top + HP, lanes] = value[a * HP : (a + 1) * HP, :half]
            shr_ref[top + HP : top + 2 * HP, lanes] = value[a * HP : (a + 1) * HP, half:]
    shrunk = shr_ref[...]
    back_ref[:, 0] = dot_table(lat_t_ref, shrunk).astype(BF).reshape(plan.n, plan.t, plan.d)
    band = dot(slot_ref[...], shrunk).astype(BF)
    rows = 4 * plan.mb
    for j in range(plan.n):
        band_ref[j, 0] = band[j * rows : (j + 1) * rows]


def pair_block(plan, rows):
    return pl.BlockSpec((plan.n, 1, rows, plan.d), lambda q: (0, q, 0, 0))


def spectral_call(plan, valid, received, lat, lat_t, slots, m1, b1, m2, b2):
    kept = (plan.q, 2, 2 * HP, plan.d)
    kept_spec = pl.BlockSpec((1, 2, 2 * HP, plan.d), lambda q: (q, 0, 0, 0))
    kept_shape = jax.ShapeDtypeStruct(kept, BF)
    rows = 4 * plan.mb
    return pl.pallas_call(
        functools.partial(spectral_kernel, plan),
        grid=(plan.q,),
        in_specs=[
            SMEM,
            pair_block(plan, plan.t),
            whole(lat.shape),
            whole(lat_t.shape),
            whole(slots.shape),
            whole(m1.shape),
            whole(b1.shape),
            whole(m2.shape),
            whole(b2.shape),
        ],
        out_specs=[
            pair_block(plan, plan.t),
            pair_block(plan, rows),
            kept_spec,
            kept_spec,
            kept_spec,
            kept_spec,
            whole((1, plan.d)),
        ],
        out_shape=[
            jax.ShapeDtypeStruct((plan.n, plan.q, plan.t, plan.d), BF),
            jax.ShapeDtypeStruct((plan.n, plan.q, rows, plan.d), BF),
            kept_shape,
            kept_shape,
            kept_shape,
            kept_shape,
            jax.ShapeDtypeStruct((1, plan.d), F32),
        ],
        scratch_shapes=[pltpu.VMEM((4 * HP, plan.d), BF)],
        compiler_params=params(),
        cost_estimate=cost(20e9, 25e6),
        name="spectral_forward",
    )(valid, received, lat, lat_t, slots, m1, b1, m2, b2)


def feed_kernel(
    plan,
    first,
    tiles,
    scale_ref,
    tok_ref,
    cot_ref,
    recv_ref,
    gain1_ref,
    bias1_ref,
    gain2_ref,
    bias2_ref,
    lon_t_ref,
    lon_ref,
    perm_ref,
    perm_t_ref,
    w1_ref,
    b1_ref,
    w2_ref,
    b2_ref,
    *rest,
):
    if first:
        in1_ref = in2_ref = None
    else:
        in1_ref, in2_ref = rest[:2]
        rest = rest[2:]
    (
        mixed_ref,
        send_ref,
        gx_ref,
        out1_ref,
        out2_ref,
        db1_ref,
        vec_ref,
        dw1,
        dw2,
        buf,
        rows_ref,
        x1_ref,
        xn,
        xn_t,
        gm,
        gm_t,
        act,
        gz,
        down,
        up,
        sem,
    ) = rest
    i = pl.program_id(0)
    last = plan.chunks - 1
    tile = act.shape[1]
    flat = plan.flat
    load = pltpu.make_async_copy(recv_ref, buf, sem.at[0])

    @pl.when(i == 0)
    def _():
        load.start()
        if first:
            dw1[...] = jnp.zeros_like(dw1)
            dw2[...] = jnp.zeros_like(dw2)
        else:
            pltpu.make_async_copy(in1_ref, dw1, sem.at[1]).start()
            pltpu.make_async_copy(in2_ref, dw2, sem.at[2]).start()
        db1_ref[...] = jnp.zeros_like(db1_ref)
        vec_ref[...] = jnp.zeros_like(vec_ref)
        if plan.flatp > flat:
            pad = jnp.zeros((plan.flatp - flat, tile), BF)
            act[flat:, :] = pad
            gz[flat:, :] = pad
            pad = jnp.zeros((plan.flatp - flat, plan.d), F32)
            down[flat:, :] = pad
            up[flat:, :] = pad
        load.wait()
        deinterleave(plan, perm_t_ref, buf, rows_ref)

    for u in range(plan.rb):
        span = slice(u * plan.w, (u + 1) * plan.w)
        x = tok_ref[0, u].astype(F32)
        unit, _ = norm_parts(x)
        filtered = dot_table(lon_t_ref, rows_ref[i * plan.rb + u])
        x1 = x + filtered + (unit * gain1_ref[...] + bias1_ref[...])
        x1_ref[u] = x1
        unit, _ = norm_parts(x1)
        down[span, :] = unit * gain2_ref[...] + bias2_ref[...]
        up[span, :] = cot_ref[0, u].astype(F32) * scale_ref[i * plan.rb + u]
    normed = down[...].astype(BF)
    xn[...] = normed[:flat]
    xn_t[...] = normed.T
    grads = up[...].astype(BF)
    gm[...] = grads[:flat]
    gm_t[...] = grads.T
    vec_ref[0:1] += jnp.sum(grads.astype(F32), 0, keepdims=True)
    down[...] = jnp.zeros_like(down)
    up[...] = jnp.zeros_like(up)

    if not first:

        @pl.when(i == 0)
        def _():
            pltpu.make_async_copy(in1_ref, dw1, sem.at[1]).wait()
            pltpu.make_async_copy(in2_ref, dw2, sem.at[2]).wait()

    def body(t, carry):
        at = pl.multiple_of(t * tile, tile)
        cols = pl.ds(at, tile)
        z = dot(xn[...], w1_ref[:, cols]) + b1_ref[:, cols]
        ga = dot_nt(gm[...], w2_ref[cols, :])
        hidden, slope = gelu_both(z)
        act[:flat, :] = hidden.astype(BF)
        grad = (ga * slope).astype(BF)
        gz[:flat, :] = grad
        db1_ref[:, cols] += jnp.sum(grad.astype(F32), 0, keepdims=True)
        down[:flat, :] += dot(act[:flat, :], w2_ref[cols, :])
        up[:flat, :] += dot_nt(gz[:flat, :], w1_ref[:, cols])
        dw1[:, cols] += dot(xn_t[...], gz[...])
        dw2[:, cols] += dot(gm_t[...], act[...])
        return carry

    lax.fori_loop(0, tiles, body, 0)

    @pl.when(i == last)
    def _():
        pltpu.make_async_copy(dw1, out1_ref, sem.at[1]).start()
        pltpu.make_async_copy(dw2, out2_ref, sem.at[2]).start()

    for u in range(plan.rb):
        span = slice(u * plan.w, (u + 1) * plan.w)
        x1 = x1_ref[u]
        scale = scale_ref[i * plan.rb + u]
        keep = jnp.where(scale > 0.0, 1.0, 0.0)
        mixed_ref[u] = ((x1 + down[span, :] + b2_ref[...]) * keep).astype(BF)
        unit, rstd = norm_parts(x1)
        grad = up[span, :]
        vec_ref[1:2] += jnp.sum(grad * unit, 0, keepdims=True)
        vec_ref[2:3] += jnp.sum(grad, 0, keepdims=True)
        gx = cot_ref[0, u].astype(F32) * scale + norm_back(grad, unit, rstd, gain2_ref[...])
        gx_ref[u] = gx.astype(gx_ref.dtype)
        rows_ref[i * plan.rb + u] = dot_table(lon_ref, gx.astype(BF)).astype(BF)

    if plan.flatp > flat:
        down[flat:, :] = jnp.zeros((plan.flatp - flat, plan.d), F32)
        up[flat:, :] = jnp.zeros((plan.flatp - flat, plan.d), F32)

    @pl.when(i == last)
    def _():
        interleave(plan, perm_ref, rows_ref, buf)
        store = pltpu.make_async_copy(buf, send_ref, sem.at[0])
        store.start()
        store.wait()
        pltpu.make_async_copy(dw1, out1_ref, sem.at[1]).wait()
        pltpu.make_async_copy(dw2, out2_ref, sem.at[2]).wait()


def feed_call(plan, s, scales, tokens, cotangent, received, vectors, w1, b1, w2, b2, sums):
    gain1, bias1, gain2, bias2 = vectors
    first = sums is None
    ff = w1.shape[1]
    tile = 512
    d, flat, flatp = plan.d, plan.flat, plan.flatp
    shape = (plan.pairs, plan.t, d)
    vec = whole((1, d))
    in_specs = [
        SMEM,
        row_block(plan, s),
        row_block(plan, s),
        ANY,
        vec,
        vec,
        vec,
        vec,
        whole((2, plan.w, plan.ki)),
        whole((2, plan.ki, plan.w)),
        whole(plan.perm.shape),
        whole(plan.perm_t.shape),
        whole_once((d, ff)),
        whole((1, ff)),
        whole_once((ff, d)),
        vec,
    ]
    operands = [
        scales,
        tokens,
        cotangent,
        received,
        gain1,
        bias1,
        gain2,
        bias2,
        plan.lon_both_t,
        plan.lon_both,
        plan.perm,
        plan.perm_t,
        w1,
        b1,
        w2,
        b2,
    ]
    aliases = {}
    if not first:
        aliases = {len(operands): 3, len(operands) + 1: 4}
        in_specs += [ANY, ANY]
        operands += list(sums)
    wide = jax.ShapeDtypeStruct((d, ff), F32)
    return pl.pallas_call(
        functools.partial(feed_kernel, plan, first, ff // tile),
        grid=(plan.chunks,),
        in_specs=in_specs,
        out_specs=[
            own_block(plan),
            ANY,
            own_block(plan),
            ANY,
            ANY,
            whole((1, ff)),
            whole((8, d)),
        ],
        out_shape=[
            jax.ShapeDtypeStruct((plan.r, plan.w, d), BF),
            jax.ShapeDtypeStruct(shape, BF),
            jax.ShapeDtypeStruct((plan.r, plan.w, d), BF),
            wide,
            wide,
            jax.ShapeDtypeStruct((1, ff), F32),
            jax.ShapeDtypeStruct((8, d), F32),
        ],
        scratch_shapes=[
            pltpu.VMEM((d, ff), F32),
            pltpu.VMEM((d, ff), F32),
            pltpu.VMEM(shape, BF),
            pltpu.VMEM((plan.r, plan.ki, d), BF),
            pltpu.VMEM((plan.rb, plan.w, d), F32),
            pltpu.VMEM((flat, d), BF),
            pltpu.VMEM((d, flatp), BF),
            pltpu.VMEM((flat, d), BF),
            pltpu.VMEM((d, flatp), BF),
            pltpu.VMEM((flatp, tile), BF),
            pltpu.VMEM((flatp, tile), BF),
            pltpu.VMEM((flatp, d), F32),
            pltpu.VMEM((flatp, d), F32),
            pltpu.SemaphoreType.DMA((3,)),
        ],
        input_output_aliases=aliases,
        compiler_params=params(),
        cost_estimate=cost(70e9, 60e6),
        name="feed_forward",
    )(*operands)


def spectral_back_kernel(
    plan,
    in_ref,
    spec_ref,
    hid_ref,
    slope1_ref,
    slope2_ref,
    lat_ref,
    lat_t_ref,
    m1t_ref,
    m2t_ref,
    out_ref,
    dm1_ref,
    dm2_ref,
    db1_ref,
    db2_ref,
    gs_ref,
    gu_ref,
):
    q = pl.program_id(0)
    half = plan.d // 2

    @pl.when(q == 0)
    def _():
        dm1_ref[...] = jnp.zeros_like(dm1_ref)
        dm2_ref[...] = jnp.zeros_like(dm2_ref)
        db1_ref[...] = jnp.zeros_like(db1_ref)
        db2_ref[...] = jnp.zeros_like(db2_ref)

    x = in_ref[:, 0].reshape(plan.n * plan.t, plan.d)
    grad = dot_table(lat_ref, x).astype(BF)
    for g in range(2):
        lanes = slice(g * half, (g + 1) * half)
        for a in range(2):
            top = a * 2 * HP
            gu_ref[a * HP : (a + 1) * HP, :half] = grad[top : top + HP, lanes]
            gu_ref[a * HP : (a + 1) * HP, half:] = grad[top + HP : top + 2 * HP, lanes]
        gu2 = gu_ref[...].astype(F32) * slope2_ref[0, g].astype(F32)
        db2_ref[g] += jnp.sum(gu2, 0, keepdims=True)
        gu2 = gu2.astype(BF)
        dm2_ref[g] += dot_tn(hid_ref[0, g], gu2)
        gu1 = (dot(gu2, m2t_ref[g]) * slope1_ref[0, g].astype(F32)).astype(BF)
        db1_ref[g] += jnp.sum(gu1.astype(F32), 0, keepdims=True)
        dm1_ref[g] += dot_tn(spec_ref[0, g], gu1)
        gs = dot(gu1, m1t_ref[g]).astype(BF)
        for a in range(2):
            top = a * 2 * HP
            gs_ref[top : top + HP, lanes] = gs[a * HP : (a + 1) * HP, :half]
            gs_ref[top + HP : top + 2 * HP, lanes] = gs[a * HP : (a + 1) * HP, half:]
    out_ref[:, 0] = dot_table(lat_t_ref, gs_ref[...]).astype(BF).reshape(plan.n, plan.t, plan.d)


def spectral_back_call(plan, received, kept, lat, lat_t, m1t, m2t):
    kept_spec = pl.BlockSpec((1, 2, 2 * HP, plan.d), lambda q: (q, 0, 0, 0))
    wide = (2, plan.d, plan.d)
    thin = (2, 1, plan.d)
    return pl.pallas_call(
        functools.partial(spectral_back_kernel, plan),
        grid=(plan.q,),
        in_specs=[pair_block(plan, plan.t)]
        + [kept_spec] * 4
        + [whole(lat.shape), whole(lat_t.shape), whole(wide), whole(wide)],
        out_specs=[
            pair_block(plan, plan.t),
            whole(wide),
            whole(wide),
            whole(thin),
            whole(thin),
        ],
        out_shape=[
            jax.ShapeDtypeStruct((plan.n, plan.q, plan.t, plan.d), BF),
            jax.ShapeDtypeStruct(wide, F32),
            jax.ShapeDtypeStruct(wide, F32),
            jax.ShapeDtypeStruct(thin, F32),
            jax.ShapeDtypeStruct(thin, F32),
        ],
        scratch_shapes=[
            pltpu.VMEM((4 * HP, plan.d), BF),
            pltpu.VMEM((2 * HP, plan.d), BF),
        ],
        compiler_params=params(),
        cost_estimate=cost(25e9, 30e6),
        name="spectral_backward",
    )(received, *kept, lat, lat_t, m1t, m2t)


def last_kernel(
    plan,
    scale_ref,
    tok_ref,
    gx_ref,
    in_ref,
    gain_ref,
    lon_t_ref,
    perm_t_ref,
    out_ref,
    vec_ref,
    rows_ref,
):
    i = pl.program_id(0)

    @pl.when(i == 0)
    def _():
        vec_ref[...] = jnp.zeros_like(vec_ref)
        deinterleave(plan, perm_t_ref, in_ref, rows_ref)

    for u in range(plan.rb):
        keep = jnp.where(scale_ref[i * plan.rb + u] > 0.0, 1.0, 0.0)
        unit, rstd = norm_parts(tok_ref[0, u].astype(F32))
        gx = gx_ref[u].astype(F32)
        grad = gx + dot_table(lon_t_ref, rows_ref[i * plan.rb + u])
        vec_ref[0:1] += jnp.sum(grad * unit, 0, keepdims=True) * keep
        vec_ref[1:2] += jnp.sum(grad, 0, keepdims=True) * keep
        out_ref[u] = (gx + norm_back(grad, unit, rstd, gain_ref[...])) * keep


def last_call(plan, s, scales, tokens, gx, received, gain):
    return pl.pallas_call(
        functools.partial(last_kernel, plan),
        grid=(plan.chunks,),
        in_specs=[
            SMEM,
            row_block(plan, s),
            own_block(plan),
            whole((plan.pairs, plan.t, plan.d)),
            whole((1, plan.d)),
            whole((2, plan.w, plan.ki)),
            whole(plan.perm_t.shape),
        ],
        out_specs=[own_block(plan), whole((8, plan.d))],
        out_shape=[
            jax.ShapeDtypeStruct((plan.r, plan.w, plan.d), F32),
            jax.ShapeDtypeStruct((8, plan.d), F32),
        ],
        scratch_shapes=[pltpu.VMEM((plan.r, plan.ki, plan.d), BF)],
        compiler_params=params(),
        cost_estimate=cost(5e9, 17e6),
        name="lon_backward",
    )(scales, tokens, gx, received, gain, plan.lon_t, plan.perm_t)


def exchange(x):
    return lax.all_to_all(x, "lat", split_axis=0, concat_axis=0, tiled=True)


def on_device(
    bands,
    tokens,
    cotangent,
    sample_weight,
    row_count,
    band_count,
    norm1_gain,
    norm1_bias,
    spec_w1,
    spec_b1,
    spec_w2,
    spec_b2,
    norm2_gain,
    norm2_bias,
    fc1_weight,
    fc1_bias,
    fc2_weight,
    fc2_bias,
):
    lane = lax.axis_index("lat")
    n = lax.axis_size("lat")
    samples, row_slots, width, channels = tokens.shape
    blocks, size = spec_w1.shape[1], spec_w1.shape[2]
    plan = Plan(n, samples, row_slots, width, channels, bands)
    lat = lat_matrix(plan, row_count)
    lat_t = lat.transpose(0, 2, 1)
    slots = slot_matrix(plan, band_count)
    m1, m2 = wide_weight(spec_w1), wide_weight(spec_w2)
    m1t, m2t = m1.transpose(0, 2, 1), m2.transpose(0, 2, 1)
    wb1, wb2 = wide_bias(spec_b1), wide_bias(spec_b2)
    row = lambda v: v.reshape(1, -1)
    vectors = (row(norm1_gain), row(norm1_bias), row(norm2_gain), row(norm2_bias))
    own_rows = jnp.sum(jnp.where(jnp.arange(n) == lane, row_count, 0))
    held = jnp.arange(row_slots) < own_rows
    scales = sample_weight.astype(F32)[:, None] * 0.5 * held[None, :].astype(F32)
    slot_step = jnp.arange(plan.kp)
    valid = ((slot_step < plan.kk) & (lane * plan.kk + slot_step < plan.kw)).astype(F32)
    grouped = (n, plan.q, plan.t, channels)
    listed = (plan.pairs, plan.t, channels)

    sent = [first_call(plan, s, tokens, vectors[0], vectors[1]) for s in range(samples)]
    spectra = [exchange(x.reshape(grouped)) for x in sent]
    forward = [
        spectral_call(plan, valid, x, lat, lat_t, slots, m1, wb1, m2, wb2) for x in spectra
    ]
    backs = [exchange(f[0]) for f in forward]
    band_parts = [exchange(f[1]) for f in forward]
    sums = None
    feeds = []
    for s in range(samples):
        feed = feed_call(
            plan,
            s,
            scales[s],
            tokens,
            cotangent,
            backs[s].reshape(listed),
            vectors,
            fc1_weight,
            row(fc1_bias),
            fc2_weight,
            row(fc2_bias),
            sums,
        )
        sums = (feed[3], feed[4])
        feeds.append(feed)
    returned = [exchange(f[1].reshape(grouped)) for f in feeds]
    backward = [
        spectral_back_call(plan, returned[s], forward[s][2:6], lat, lat_t, m1t, m2t)
        for s in range(samples)
    ]
    lon_grads = [exchange(b[0]) for b in backward]
    finals = [
        last_call(plan, s, scales[s], tokens, feeds[s][2], lon_grads[s].reshape(listed), vectors[0])
        for s in range(samples)
    ]

    mixed = jnp.stack([f[0] for f in feeds])
    tokens_grad = jnp.stack([f[0] for f in finals])
    spectrum = []
    for part in band_parts:
        part = part.reshape(n, plan.q, 2, 2, bands, channels)
        part = part.transpose(4, 3, 0, 1, 2, 5).reshape(bands, 2, n, plan.kp, channels)
        part = part[:, :, :, : plan.kk].reshape(bands, 2, n * plan.kk, channels)
        spectrum.append(part[:, :, : plan.kw])
    spectrum = jnp.stack(spectrum)

    total = lambda parts: functools.reduce(jnp.add, parts)
    feed_vec = total([f[6] for f in feeds])
    last_vec = total([f[1] for f in finals])
    small = (
        feed_vec[1],
        feed_vec[2],
        total([f[5] for f in feeds])[0],
        feed_vec[0],
        last_vec[0],
        last_vec[1],
        narrow_grad(total([b[1] for b in backward]), blocks, size),
        narrow_bias(total([b[3] for b in backward]), blocks, size),
        narrow_grad(total([b[2] for b in backward]), blocks, size),
        narrow_bias(total([b[4] for b in backward]), blocks, size),
        jnp.sum(total([f[6] for f in forward])),
    )
    large = lax.psum(sums, ("batch", "lat"))
    small = lax.psum(small, ("batch", "lat"))
    zero_fraction = small[10] / (lax.axis_size("batch") * samples * H * plan.kw * 2 * channels)
    return (
        mixed,
        spectrum,
        tokens_grad,
        small[4],
        small[5],
        small[6],
        small[7],
        small[8],
        small[9],
        small[0],
        small[1],
        large[0],
        small[2],
        large[1].T,
        small[3],
        zero_fraction,
    )


def solution(mesh):
    rows = P("batch", "lat", None, None)
    in_specs = (rows, rows, P("batch")) + (P(),) * 14
    out_specs = (rows, P("batch", "lat", None, None, None), rows) + (P(),) * 13
    lanes = mesh.shape["lat"]

    def run(tokens, cotangent, *rest):
        row_slots = tokens.shape[1] // lanes
        return jax.shard_map(
            functools.partial(on_device, row_slots + 1),
            mesh=mesh,
            in_specs=in_specs,
            out_specs=out_specs,
            check_vma=False,
        )(tokens, cotangent, *rest)

    return run
```

```python
import functools
import math

import jax
import jax.numpy as jnp
import numpy as np
from jax import lax
from jax.experimental import pallas as pl
from jax.experimental.pallas import tpu as pltpu
from jax.sharding import PartitionSpec as P

H = 90
HP = 96

NORM_EPS = 1e-06
SHRINK_LAMBDA = 0.01
SHRINK_SOFTNESS = 0.1
INV_ROOT_TAU = 1.0 / math.sqrt(2.0 * math.pi)
BF = jnp.bfloat16
F32 = jnp.float32
VMEM_BYTES = 64 * 1024 * 1024


def dot(a, b):
    return jnp.dot(a, b, preferred_element_type=F32)


def dot_nt(a, b):
    return lax.dot_general(a, b, (((1,), (1,)), ((), ())), preferred_element_type=F32)


def dot_tn(a, b):
    return lax.dot_general(a, b, (((0,), (0,)), ((), ())), preferred_element_type=F32)


def dot_table(table_ref, x):
    return dot(table_ref[0], x) + dot(table_ref[1], x)


def two_parts(table):
    high = table.astype(BF)
    return high, (table - high.astype(table.dtype)).astype(BF)


def norm_parts(x):
    mean = jnp.mean(x, -1, keepdims=True)
    centred = x - mean
    rstd = lax.rsqrt(jnp.mean(centred * centred, -1, keepdims=True) + NORM_EPS)
    return centred * rstd, rstd


def norm_back(grad, unit, rstd, gain):
    e = grad * gain
    return rstd * (
        e - jnp.mean(e, -1, keepdims=True) - unit * jnp.mean(e * unit, -1, keepdims=True)
    )


def gauss_parts(v):
    d = 1.0 + jnp.abs(v) * (0.3275911 / math.sqrt(2.0))
    t = pl.reciprocal(d, approx=True)
    e = jnp.exp2(v * v * (-0.5 * math.log2(math.e)))
    poly = 1.061405429 * 0.5
    for c in (-1.453152027, 1.421413741, -0.284496736, 0.254829592):
        poly = poly * t + 0.5 * c
    tail = poly * t * e
    cdf = jnp.where(v >= 0.0, 1.0 - tail, tail)
    return cdf, v * e * INV_ROOT_TAU


def gelu_both(v):
    cdf, slope_part = gauss_parts(v)
    return v * cdf, cdf + slope_part


def shrink_both(u):
    a = jnp.maximum(jnp.abs(u) - SHRINK_LAMBDA, 0.0)
    d = a + SHRINK_SOFTNESS
    t = pl.reciprocal(d, approx=True)
    t = t * (2.0 - d * t)
    size = a * a * t
    value = jnp.where(u >= 0.0, size, -size)
    slope = a * (a + 2.0 * SHRINK_SOFTNESS) * (t * t)
    return value, slope


class Plan:
    def __init__(self, n, samples, rows, width, channels, bands):
        self.n, self.s, self.r, self.w, self.d, self.mb = n, samples, rows, width, channels, bands
        self.kw = width // 2 + 1
        self.kk = -(-self.kw // n)
        self.kp = self.kk + self.kk % 2
        self.q = self.kp // 2
        self.rp = -(-rows // 4) * 4
        self.t = 4 * self.rp
        self.pairs = n * self.q
        self.ki = n * self.kp * 2
        self.rb = max(b for b in (4, 3, 2, 1) if rows % b == 0)
        self.chunks = rows // self.rb
        self.flat = self.rb * width
        self.flatp = max(-(-self.flat // 256) * 256, channels)
        j = np.arange(n)[:, None]
        t = np.arange(self.kp)[None, :]
        self.k_index = (j * self.kk + t).astype(np.int64)
        self.k_valid = (t < self.kk) & (self.k_index < self.kw)
        k = np.where(self.k_valid, self.k_index, 0).reshape(-1)
        ok = self.k_valid.reshape(-1).astype(np.float64)
        angle = 2.0 * np.pi * ((k[:, None] * np.arange(width)[None, :]) % width) / width
        scale = ok[:, None] / math.sqrt(width)
        fwd = np.stack([np.cos(angle) * scale, -np.sin(angle) * scale], 1).reshape(self.ki, width)
        factor = np.where((k == 0) | (2 * k == width), 1.0, 2.0)[:, None, None]
        both = (fwd.reshape(-1, 2, width) * factor).reshape(self.ki, width)
        self.lon = np.stack(two_parts(fwd))
        self.lon_both = np.stack(two_parts(both))
        self.lon_t = np.stack(two_parts(np.ascontiguousarray(fwd.T)))
        self.lon_both_t = np.stack(two_parts(np.ascontiguousarray(both.T)))
        perm = np.zeros((16, self.rp, rows, 16))
        for a in range(16):
            for r in range(rows):
                perm[a, r, r, a] = 1.0
        self.perm = perm.reshape(16 * self.rp, rows * 16).astype(BF)
        self.perm_t = np.ascontiguousarray(self.perm.T)


def lat_matrix(plan, row_count):
    n, rp = plan.n, plan.rp
    start = jnp.cumsum(row_count) - row_count
    steps = jnp.arange(rp, dtype=jnp.int32)
    rows = start[:, None] + steps[None, :]
    valid = steps[None, :] < row_count[:, None]
    kh = jnp.arange(HP, dtype=jnp.int32)
    turns = kh[:, None, None] * rows[None] % H
    angle = turns.astype(F32) * (2.0 * math.pi / H)
    weight = jnp.where((kh < H)[:, None, None] & valid[None], 1.0 / math.sqrt(H), 0.0)
    cosine = jnp.cos(angle) * weight
    sine = jnp.sin(angle) * weight
    real = jnp.stack([cosine, sine], 2)
    imag = jnp.stack([-sine, cosine], 2)
    part = jnp.stack([real, imag], 0)
    eye = jnp.eye(2, dtype=F32)
    full = part[None, :, :, :, None] * eye[:, None, None, None, :, None, None]
    full = full.reshape(4 * HP, n * 4 * rp)
    high = lax.reduce_precision(full, 8, 7)
    return jnp.stack([high, full - high]).astype(BF)


def slot_matrix(plan, band_count):
    start = jnp.cumsum(band_count) - band_count
    steps = jnp.arange(plan.mb, dtype=jnp.int32)
    wave = start[:, None] + steps[None, :]
    valid = steps[None, :] < band_count[:, None]
    kh = jnp.arange(HP, dtype=jnp.int32)
    pick = ((wave[:, :, None] == kh) & valid[:, :, None]).astype(F32)
    eye = jnp.eye(4, dtype=F32)
    full = pick[:, None, :, None, :] * eye[None, :, None, :, None]
    return full.reshape(plan.n * 4 * plan.mb, 4 * HP).astype(BF)


def wide_weight(weight):
    blocks, size = weight.shape[1], weight.shape[2]
    half = blocks // 2
    w = weight.reshape(2, 2, half, size, size)
    eye = jnp.eye(half, dtype=weight.dtype)
    dense = w[:, :, :, :, None, :] * eye[None, None, :, None, :, None]
    dense = dense.reshape(2, 2, half * size, half * size)
    re, im = dense[0], dense[1]
    top = jnp.concatenate([re, im], 2)
    bottom = jnp.concatenate([-im, re], 2)
    return jnp.concatenate([top, bottom], 1)


def wide_bias(bias):
    return bias.reshape(2, 2, -1).transpose(1, 0, 2).reshape(2, 1, -1)


def narrow_bias(wide, blocks, size):
    return wide.reshape(2, 2, -1).transpose(1, 0, 2).reshape(2, blocks, size)


def whole(shape):
    zeros = (0,) * len(shape)
    return pl.BlockSpec(shape, lambda *_: zeros)


def whole_once(shape):
    zeros = (0,) * len(shape)
    return pl.BlockSpec(shape, lambda *_: zeros, pipeline_mode=pl.Buffered(1))


SMEM = pl.BlockSpec(memory_space=pltpu.SMEM)
ANY = pl.BlockSpec(memory_space=pl.ANY)


def params(collective_id=None):
    if collective_id is None:
        return pltpu.CompilerParams(
            dimension_semantics=("arbitrary",), vmem_limit_bytes=VMEM_BYTES
        )
    return pltpu.CompilerParams(
        dimension_semantics=("arbitrary",),
        vmem_limit_bytes=VMEM_BYTES,
        collective_id=collective_id,
        has_side_effects=True,
    )


def ride_copy(n, me, src, dst, send, recv, e, step):
    peer = lax.rem(me + step, n)
    return pltpu.make_async_remote_copy(
        src_ref=src.at[peer],
        dst_ref=dst.at[me],
        send_sem=send.at[e, step],
        recv_sem=recv.at[e, step],
        device_id={"lat": peer},
        device_id_type=pl.DeviceIdType.MESH,
    )


def ride_arrival(n, me, src, dst, send, recv, e, step):
    peer = lax.rem(me + n - step, n)
    return pltpu.make_async_remote_copy(
        src_ref=src.at[peer],
        dst_ref=dst.at[peer],
        send_sem=send.at[e, step],
        recv_sem=recv.at[e, step],
        device_id={"lat": peer},
        device_id_type=pl.DeviceIdType.MESH,
    )


def ride_start(n, srcs, dsts, send, recv, own):
    me = lax.axis_index("lat")
    barrier = pltpu.get_barrier_semaphore()
    for step in range(1, n):
        pl.semaphore_signal(
            barrier,
            inc=1,
            device_id={"lat": lax.rem(me + step, n)},
            device_id_type=pl.DeviceIdType.MESH,
        )
    pl.semaphore_wait(barrier, n - 1)
    for e, (src, dst) in enumerate(zip(srcs, dsts)):
        for step in range(1, n):
            ride_copy(n, me, src, dst, send, recv, e, step).start()
        pltpu.make_async_copy(src.at[me], dst.at[me], own.at[e]).start()


def ride_wait(n, srcs, dsts, send, recv, own):
    me = lax.axis_index("lat")
    for e, (src, dst) in enumerate(zip(srcs, dsts)):
        pltpu.make_async_copy(src.at[me], dst.at[me], own.at[e]).wait()
        for step in range(1, n):
            ride_copy(n, me, src, dst, send, recv, e, step).wait_send()
            ride_arrival(n, me, src, dst, send, recv, e, step).wait_recv()


def cost(flops, size):
    return pl.CostEstimate(flops=int(flops), bytes_accessed=int(size), transcendentals=0)


def interleave(plan, perm_ref, rows_ref, out_ref):
    def body(c, carry):
        at = pl.multiple_of(c * 16, 16)
        block = rows_ref[:, pl.ds(at, 16), :].reshape(plan.r * 16, plan.d)
        mixed = dot(perm_ref[...], block).astype(BF)
        out_ref[pl.ds(c * 4, 4)] = mixed.reshape(4, plan.t, plan.d)
        return carry

    lax.fori_loop(0, plan.ki // 16, body, 0)


def deinterleave(plan, perm_t_ref, in_ref, rows_ref):
    def body(c, carry):
        at = pl.multiple_of(c * 16, 16)
        block = in_ref[pl.ds(c * 4, 4)].reshape(4 * plan.t, plan.d)
        rows = dot(perm_t_ref[...], block).astype(BF)
        rows_ref[:, pl.ds(at, 16), :] = rows.reshape(plan.r, 16, plan.d)
        return carry

    lax.fori_loop(0, plan.ki // 16, body, 0)


def interleave_out(plan, perm_ref, rows_ref, ring, sem, out_ref):
    def copy(c):
        return pltpu.make_async_copy(
            ring.at[lax.rem(c, 2)], out_ref.at[pl.ds(c * 4, 4)], sem.at[lax.rem(c, 2)]
        )

    def body(c, carry):
        @pl.when(c >= 2)
        def _():
            copy(c - 2).wait()

        at = pl.multiple_of(c * 16, 16)
        block = rows_ref[:, pl.ds(at, 16), :].reshape(plan.r * 16, plan.d)
        mixed = dot(perm_ref[...], block).astype(BF)
        ring[lax.rem(c, 2)] = mixed.reshape(4, plan.t, plan.d)
        copy(c).start()
        return carry

    lax.fori_loop(0, plan.ki // 16, body, 0)
    return [copy(plan.ki // 16 - 2), copy(plan.ki // 16 - 1)]


def ring_load(plan, in_ref, ring, sem, c):
    return pltpu.make_async_copy(
        in_ref.at[pl.ds(c * 4, 4)], ring.at[lax.rem(c, 2)], sem.at[lax.rem(c, 2)]
    )


def deinterleave_in(plan, perm_t_ref, in_ref, ring, sem, rows_ref):
    steps = plan.ki // 16

    def body(c, carry):
        ring_load(plan, in_ref, ring, sem, c).wait()
        at = pl.multiple_of(c * 16, 16)
        block = ring[lax.rem(c, 2)].reshape(4 * plan.t, plan.d)
        rows = dot(perm_t_ref[...], block).astype(BF)
        rows_ref[:, pl.ds(at, 16), :] = rows.reshape(plan.r, 16, plan.d)

        @pl.when(c + 2 < steps)
        def _():
            ring_load(plan, in_ref, ring, sem, c + 2).start()

        return carry

    lax.fori_loop(0, steps, body, 0)


def first_kernel(plan, tok_ref, gain_ref, bias_ref, lon_ref, perm_ref, out_ref, rows_ref):
    i = pl.program_id(0)
    for u in range(plan.rb):
        unit, _ = norm_parts(tok_ref[0, u].astype(F32))
        normed = (unit * gain_ref[...] + bias_ref[...]).astype(BF)
        rows_ref[i * plan.rb + u] = dot_table(lon_ref, normed).astype(BF)

    @pl.when(i == plan.chunks - 1)
    def _():
        interleave(plan, perm_ref, rows_ref, out_ref)


def row_block(plan, s):
    return pl.BlockSpec((1, plan.rb, plan.w, plan.d), lambda i: (s, i, 0, 0))


def own_block(plan):
    return pl.BlockSpec((plan.rb, plan.w, plan.d), lambda i: (i, 0, 0))


def first_call(plan, s, tokens, gain, bias):
    shape = (plan.pairs, plan.t, plan.d)
    return pl.pallas_call(
        functools.partial(first_kernel, plan),
        grid=(plan.chunks,),
        in_specs=[
            row_block(plan, s),
            whole((1, plan.d)),
            whole((1, plan.d)),
            whole((2, plan.ki, plan.w)),
            whole(plan.perm.shape),
        ],
        out_specs=whole(shape),
        out_shape=jax.ShapeDtypeStruct(shape, BF),
        scratch_shapes=[pltpu.VMEM((plan.r, plan.ki, plan.d), BF)],
        compiler_params=params(),
        cost_estimate=cost(9e9, 8e6),
        name="lon_forward",
    )(tokens, gain, bias, plan.lon, plan.perm)


def spectral_kernel(
    plan,
    valid_ref,
    in_ref,
    lat_ref,
    lat_t_ref,
    slot_ref,
    m1_ref,
    b1_ref,
    m2_ref,
    b2_ref,
    back_ref,
    band_ref,
    spec_ref,
    hid_ref,
    slope1_ref,
    slope2_ref,
    zero_ref,
    shr_ref,
):
    q = pl.program_id(0)
    half = plan.d // 2

    @pl.when(q == 0)
    def _():
        zero_ref[...] = jnp.zeros_like(zero_ref)

    x = in_ref[:, 0].reshape(plan.n * plan.t, plan.d)
    spec = dot_table(lat_ref, x).astype(BF)
    ok = (lax.broadcasted_iota(jnp.int32, (HP, 1), 0) < H).astype(F32)
    for g in range(2):
        lanes = slice(g * half, (g + 1) * half)
        for a in range(2):
            top = a * 2 * HP
            spec_ref[0, g, a * HP : (a + 1) * HP, :half] = spec[top : top + HP, lanes]
            spec_ref[0, g, a * HP : (a + 1) * HP, half:] = spec[top + HP : top + 2 * HP, lanes]
        u1 = dot(spec_ref[0, g], m1_ref[g]) + b1_ref[g]
        hidden, slope = gelu_both(u1)
        hid_ref[0, g] = hidden.astype(BF)
        slope1_ref[0, g] = slope.astype(BF)
        u2 = dot(hid_ref[0, g], m2_ref[g]) + b2_ref[g]
        small = (jnp.abs(u2) <= SHRINK_LAMBDA).astype(F32)
        for a in range(2):
            part = small[a * HP : (a + 1) * HP] * ok
            zero_ref[...] += jnp.sum(part, 0, keepdims=True) * valid_ref[q * 2 + a]
        value, slope = shrink_both(u2)
        slope2_ref[0, g] = slope.astype(BF)
        value = value.astype(BF)
        for a in range(2):
            top = a * 2 * HP
            shr_ref[top : top + HP, lanes] = value[a * HP : (a + 1) * HP, :half]
            shr_ref[top + HP : top + 2 * HP, lanes] = value[a * HP : (a + 1) * HP, half:]
    shrunk = shr_ref[...]
    back_ref[:, 0] = dot_table(lat_t_ref, shrunk).astype(BF).reshape(plan.n, plan.t, plan.d)
    band = dot(slot_ref[...], shrunk).astype(BF)
    rows = 4 * plan.mb
    for j in range(plan.n):
        band_ref[j, 0] = band[j * rows : (j + 1) * rows]


def pair_block(plan, rows):
    return pl.BlockSpec((plan.n, 1, rows, plan.d), lambda q: (0, q, 0, 0))


def spectral_call(plan, valid, received, lat, lat_t, slots, m1, b1, m2, b2):
    kept = (plan.q, 2, 2 * HP, plan.d)
    kept_spec = pl.BlockSpec((1, 2, 2 * HP, plan.d), lambda q: (q, 0, 0, 0))
    kept_shape = jax.ShapeDtypeStruct(kept, BF)
    rows = 4 * plan.mb
    return pl.pallas_call(
        functools.partial(spectral_kernel, plan),
        grid=(plan.q,),
        in_specs=[
            SMEM,
            pair_block(plan, plan.t),
            whole(lat.shape),
            whole(lat_t.shape),
            whole(slots.shape),
            whole(m1.shape),
            whole(b1.shape),
            whole(m2.shape),
            whole(b2.shape),
        ],
        out_specs=[
            pair_block(plan, plan.t),
            pair_block(plan, rows),
            kept_spec,
            kept_spec,
            kept_spec,
            kept_spec,
            whole((1, plan.d)),
        ],
        out_shape=[
            jax.ShapeDtypeStruct((plan.n, plan.q, plan.t, plan.d), BF),
            jax.ShapeDtypeStruct((plan.n, plan.q, rows, plan.d), BF),
            kept_shape,
            kept_shape,
            kept_shape,
            kept_shape,
            jax.ShapeDtypeStruct((1, plan.d), F32),
        ],
        scratch_shapes=[pltpu.VMEM((4 * HP, plan.d), BF)],
        compiler_params=params(),
        cost_estimate=cost(20e9, 25e6),
        name="spectral_forward",
    )(valid, received, lat, lat_t, slots, m1, b1, m2, b2)


def feed_kernel(
    plan,
    first,
    final,
    riders,
    tiles,
    scale_ref,
    tok_ref,
    cot_ref,
    recv_ref,
    gain1_ref,
    bias1_ref,
    gain2_ref,
    bias2_ref,
    lon_t_ref,
    lon_ref,
    perm_ref,
    perm_t_ref,
    w1_ref,
    b1_ref,
    w2_ref,
    b2_ref,
    *rest,
):
    srcs, rest = rest[:riders], rest[riders:]
    if first:
        in1_ref = in2_ref = None
    else:
        in1_ref, in2_ref = rest[:2]
        rest = rest[2:]
    mixed_ref, send_ref, gx_ref, out1_ref, out2_ref, db1_ref, vec_ref = rest[:7]
    dsts, rest = rest[7 : 7 + riders], rest[7 + riders :]
    (
        dw1,
        dw2,
        ring,
        rows_ref,
        x1_ref,
        xn,
        xn_t,
        gm,
        gm_t,
        act_a,
        gz_a,
        act_b,
        gz_b,
        down,
        up,
        sem,
        ring_sem,
        ride_send,
        ride_recv,
        ride_own,
    ) = rest
    i = pl.program_id(0)
    last = plan.chunks - 1
    tile = act_a.shape[1]
    flat = plan.flat
    ride = (plan.n, srcs, dsts, ride_send, ride_recv, ride_own)

    @pl.when(i == 0)
    def _():
        for c in range(2):
            ring_load(plan, recv_ref, ring, ring_sem, c).start()
        if not first:
            pltpu.make_async_copy(in1_ref, dw1, sem.at[1]).start()
            pltpu.make_async_copy(in2_ref, dw2, sem.at[2]).start()
        ride_start(*ride)
        if first:
            dw1[...] = jnp.zeros_like(dw1)
            dw2[...] = jnp.zeros_like(dw2)
        db1_ref[...] = jnp.zeros_like(db1_ref)
        vec_ref[...] = jnp.zeros_like(vec_ref)
        if plan.flatp > flat:
            pad = jnp.zeros((plan.flatp - flat, tile), BF)
            for ref in (act_a, gz_a, act_b, gz_b):
                ref[flat:, :] = pad
            pad = jnp.zeros((plan.flatp - flat, plan.d), F32)
            down[flat:, :] = pad
            up[flat:, :] = pad
        deinterleave_in(plan, perm_t_ref, recv_ref, ring, ring_sem, rows_ref)

    for u in range(plan.rb):
        span = slice(u * plan.w, (u + 1) * plan.w)
        x = tok_ref[0, u].astype(F32)
        unit, _ = norm_parts(x)
        filtered = dot_table(lon_t_ref, rows_ref[i * plan.rb + u])
        x1 = x + filtered + (unit * gain1_ref[...] + bias1_ref[...])
        x1_ref[u] = x1
        unit, _ = norm_parts(x1)
        down[span, :] = unit * gain2_ref[...] + bias2_ref[...]
        up[span, :] = cot_ref[0, u].astype(F32) * scale_ref[i * plan.rb + u]
    normed = down[...].astype(BF)
    xn[...] = normed[:flat]
    xn_t[...] = normed.T
    grads = up[...].astype(BF)
    gm[...] = grads[:flat]
    gm_t[...] = grads.T
    vec_ref[0:1] += jnp.sum(grads.astype(F32), 0, keepdims=True)
    down[...] = jnp.zeros_like(down)
    up[...] = jnp.zeros_like(up)

    if not first:

        @pl.when(i == 0)
        def _():
            pltpu.make_async_copy(in1_ref, dw1, sem.at[1]).wait()
            pltpu.make_async_copy(in2_ref, dw2, sem.at[2]).wait()

    def columns(t):
        return pl.ds(pl.multiple_of(t * tile, tile), tile)

    def enter(t, act, gz):
        cols = columns(t)
        z = dot(xn[...], w1_ref[:, cols]) + b1_ref[:, cols]
        ga = dot_nt(gm[...], w2_ref[cols, :])
        hidden, slope = gelu_both(z)
        grad = ga * slope
        act[:flat, :] = hidden.astype(BF)
        gz[:flat, :] = grad.astype(BF)
        db1_ref[:, cols] += jnp.sum(grad, 0, keepdims=True)

    def leave(t, act, gz):
        cols = columns(t)
        down[:flat, :] += dot(act[:flat, :], w2_ref[cols, :])
        up[:flat, :] += dot_nt(gz[:flat, :], w1_ref[:, cols])
        dw1[:, cols] += dot(xn_t[...], gz[...])
        dw2[:, cols] += dot(gm_t[...], act[...])

    enter(0, act_a, gz_a)

    def body(h, carry):
        t = 2 * h
        enter(t + 1, act_b, gz_b)
        leave(t, act_a, gz_a)
        enter(t + 2, act_a, gz_a)
        leave(t + 1, act_b, gz_b)
        return carry

    lax.fori_loop(0, tiles // 2 - 1, body, 0)
    enter(tiles - 1, act_b, gz_b)
    leave(tiles - 2, act_a, gz_a)
    leave(tiles - 1, act_b, gz_b)

    if not final:

        @pl.when(i == last)
        def _():
            pltpu.make_async_copy(dw1, out1_ref, sem.at[1]).start()
            pltpu.make_async_copy(dw2, out2_ref, sem.at[2]).start()

    for u in range(plan.rb):
        span = slice(u * plan.w, (u + 1) * plan.w)
        x1 = x1_ref[u]
        scale = scale_ref[i * plan.rb + u]
        keep = jnp.where(scale > 0.0, 1.0, 0.0)
        mixed_ref[u] = ((x1 + down[span, :] + b2_ref[...]) * keep).astype(BF)
        unit, rstd = norm_parts(x1)
        grad = up[span, :]
        vec_ref[1:2] += jnp.sum(grad * unit, 0, keepdims=True)
        vec_ref[2:3] += jnp.sum(grad, 0, keepdims=True)
        gx = cot_ref[0, u].astype(F32) * scale + norm_back(grad, unit, rstd, gain2_ref[...])
        gx_ref[u] = gx.astype(gx_ref.dtype)
        rows_ref[i * plan.rb + u] = dot_table(lon_ref, gx.astype(BF)).astype(BF)

    if plan.flatp > flat:
        down[flat:, :] = jnp.zeros((plan.flatp - flat, plan.d), F32)
        up[flat:, :] = jnp.zeros((plan.flatp - flat, plan.d), F32)

    @pl.when(i == last)
    def _():
        stores = interleave_out(plan, perm_ref, rows_ref, ring, ring_sem, send_ref)
        if final:
            pending = {}
            for t in range(tiles):
                cols = slice(t * tile, (t + 1) * tile)
                side = t % 2
                for copy in pending.pop(side, ()):
                    copy.wait()
                one, two = ((act_a, gz_a), (act_b, gz_b))[side]
                one[: plan.d, :] = dw1[:, cols].astype(BF)
                xn_part = (xn_t, gm_t)[side]
                xn_part[:tile, : plan.d] = dw2[:, cols].astype(BF).T
                copies = (
                    pltpu.make_async_copy(one.at[: plan.d], out1_ref.at[:, cols], sem.at[1 + side]),
                    pltpu.make_async_copy(
                        xn_part.at[:tile, : plan.d], out2_ref.at[cols], sem.at[3 + side]
                    ),
                )
                for copy in copies:
                    copy.start()
                pending[side] = copies
            for copies in pending.values():
                for copy in copies:
                    copy.wait()
        else:
            pltpu.make_async_copy(dw1, out1_ref, sem.at[1]).wait()
            pltpu.make_async_copy(dw2, out2_ref, sem.at[2]).wait()
        for store in stores:
            store.wait()
        ride_wait(*ride)


def feed_call(
    plan, s, scales, tokens, cotangent, received, vectors, w1, b1, w2, b2, sums, final, passengers
):
    gain1, bias1, gain2, bias2 = vectors
    first = sums is None
    ff = w1.shape[1]
    tile = 512
    d, flat = plan.d, plan.flat
    flatp = plan.flatp
    shape = (plan.pairs, plan.t, d)
    vec = whole((1, d))
    riders = len(passengers)
    in_specs = [
        SMEM,
        row_block(plan, s),
        row_block(plan, s),
        ANY,
        vec,
        vec,
        vec,
        vec,
        whole((2, plan.w, plan.ki)),
        whole((2, plan.ki, plan.w)),
        whole(plan.perm.shape),
        whole(plan.perm_t.shape),
        whole_once((d, ff)),
        whole((1, ff)),
        whole_once((ff, d)),
        vec,
    ] + [ANY] * riders
    operands = [
        scales,
        tokens,
        cotangent,
        received,
        gain1,
        bias1,
        gain2,
        bias2,
        plan.lon_both_t,
        plan.lon_both,
        plan.perm,
        plan.perm_t,
        w1,
        b1,
        w2,
        b2,
        *passengers,
    ]
    aliases = {}
    if not first:
        if not final:
            aliases = {len(operands): 3, len(operands) + 1: 4}
        in_specs += [ANY, ANY]
        operands += list(sums)
    if final:
        wides = [jax.ShapeDtypeStruct((d, ff), BF), jax.ShapeDtypeStruct((ff, d), BF)]
    else:
        wides = [jax.ShapeDtypeStruct((d, ff), F32)] * 2
    return pl.pallas_call(
        functools.partial(feed_kernel, plan, first, final, riders, ff // tile),
        grid=(plan.chunks,),
        in_specs=in_specs,
        out_specs=[
            own_block(plan),
            ANY,
            own_block(plan),
            ANY,
            ANY,
            whole((1, ff)),
            whole((8, d)),
        ]
        + [ANY] * riders,
        out_shape=[
            jax.ShapeDtypeStruct((plan.r, plan.w, d), BF),
            jax.ShapeDtypeStruct(shape, BF),
            jax.ShapeDtypeStruct((plan.r, plan.w, d), BF),
            *wides,
            jax.ShapeDtypeStruct((1, ff), F32),
            jax.ShapeDtypeStruct((8, d), F32),
        ]
        + [jax.ShapeDtypeStruct(p.shape, p.dtype) for p in passengers],
        scratch_shapes=[
            pltpu.VMEM((d, ff), F32),
            pltpu.VMEM((d, ff), F32),
            pltpu.VMEM((2, 4, plan.t, d), BF),
            pltpu.VMEM((plan.r, plan.ki, d), BF),
            pltpu.VMEM((plan.rb, plan.w, d), F32),
            pltpu.VMEM((flat, d), BF),
            pltpu.VMEM((d, flatp), BF),
            pltpu.VMEM((flat, d), BF),
            pltpu.VMEM((d, flatp), BF),
            pltpu.VMEM((flatp, tile), BF),
            pltpu.VMEM((flatp, tile), BF),
            pltpu.VMEM((flatp, tile), BF),
            pltpu.VMEM((flatp, tile), BF),
            pltpu.VMEM((flatp, d), F32),
            pltpu.VMEM((flatp, d), F32),
            pltpu.SemaphoreType.DMA((5,)),
            pltpu.SemaphoreType.DMA((2,)),
            pltpu.SemaphoreType.DMA((riders, plan.n)),
            pltpu.SemaphoreType.DMA((riders, plan.n)),
            pltpu.SemaphoreType.DMA((riders,)),
        ],
        input_output_aliases=aliases,
        compiler_params=params(s),
        cost_estimate=cost(70e9, 60e6),
        name="feed_forward",
    )(*operands)


def spectral_back_kernel(
    plan,
    in_ref,
    spec_ref,
    hid_ref,
    slope1_ref,
    slope2_ref,
    lat_ref,
    lat_t_ref,
    m1t_ref,
    m2t_ref,
    out_ref,
    dw1_ref,
    dw2_ref,
    db1_ref,
    db2_ref,
    dm1_ref,
    dm2_ref,
    gs_ref,
    gu_ref,
):
    q = pl.program_id(0)
    half = plan.d // 2

    @pl.when(q == 0)
    def _():
        dm1_ref[...] = jnp.zeros_like(dm1_ref)
        dm2_ref[...] = jnp.zeros_like(dm2_ref)
        db1_ref[...] = jnp.zeros_like(db1_ref)
        db2_ref[...] = jnp.zeros_like(db2_ref)

    x = in_ref[:, 0].reshape(plan.n * plan.t, plan.d)
    grad = dot_table(lat_ref, x).astype(BF)
    for g in range(2):
        lanes = slice(g * half, (g + 1) * half)
        for a in range(2):
            top = a * 2 * HP
            gu_ref[a * HP : (a + 1) * HP, :half] = grad[top : top + HP, lanes]
            gu_ref[a * HP : (a + 1) * HP, half:] = grad[top + HP : top + 2 * HP, lanes]
        gu2 = gu_ref[...].astype(F32) * slope2_ref[0, g].astype(F32)
        db2_ref[g] += jnp.sum(gu2, 0, keepdims=True)
        gu2 = gu2.astype(BF)
        dm2_ref[g] += dot_tn(hid_ref[0, g], gu2)
        gu1 = (dot(gu2, m2t_ref[g]) * slope1_ref[0, g].astype(F32)).astype(BF)
        db1_ref[g] += jnp.sum(gu1.astype(F32), 0, keepdims=True)
        dm1_ref[g] += dot_tn(spec_ref[0, g], gu1)
        gs = dot(gu1, m1t_ref[g]).astype(BF)
        for a in range(2):
            top = a * 2 * HP
            gs_ref[top : top + HP, lanes] = gs[a * HP : (a + 1) * HP, :half]
            gs_ref[top + HP : top + 2 * HP, lanes] = gs[a * HP : (a + 1) * HP, half:]
    out_ref[:, 0] = dot_table(lat_t_ref, gs_ref[...]).astype(BF).reshape(plan.n, plan.t, plan.d)

    @pl.when(q == plan.q - 1)
    def _():
        blocks, size = dw1_ref.shape[2:4]
        for wide, narrow in ((dm1_ref, dw1_ref), (dm2_ref, dw2_ref)):
            for g in range(2):
                for b in range(blocks):
                    re = slice(b * size, (b + 1) * size)
                    im = slice(half + b * size, half + (b + 1) * size)
                    narrow[0, g, b] = wide[g, re, re] + wide[g, im, im]
                    narrow[1, g, b] = wide[g, re, im] - wide[g, im, re]


def spectral_back_call(plan, blocks, size, received, kept, lat, lat_t, m1t, m2t):
    small = (2, 2, blocks // 2, size, size)
    kept_spec = pl.BlockSpec((1, 2, 2 * HP, plan.d), lambda q: (q, 0, 0, 0))
    wide = (2, plan.d, plan.d)
    thin = (2, 1, plan.d)
    return pl.pallas_call(
        functools.partial(spectral_back_kernel, plan),
        grid=(plan.q,),
        in_specs=[pair_block(plan, plan.t)]
        + [kept_spec] * 4
        + [whole(lat.shape), whole(lat_t.shape), whole(wide), whole(wide)],
        out_specs=[
            pair_block(plan, plan.t),
            whole(small),
            whole(small),
            whole(thin),
            whole(thin),
        ],
        out_shape=[
            jax.ShapeDtypeStruct((plan.n, plan.q, plan.t, plan.d), BF),
            jax.ShapeDtypeStruct(small, F32),
            jax.ShapeDtypeStruct(small, F32),
            jax.ShapeDtypeStruct(thin, F32),
            jax.ShapeDtypeStruct(thin, F32),
        ],
        scratch_shapes=[
            pltpu.VMEM(wide, F32),
            pltpu.VMEM(wide, F32),
            pltpu.VMEM((4 * HP, plan.d), BF),
            pltpu.VMEM((2 * HP, plan.d), BF),
        ],
        compiler_params=params(),
        cost_estimate=cost(25e9, 30e6),
        name="spectral_backward",
    )(received, *kept, lat, lat_t, m1t, m2t)


def last_kernel(
    plan,
    scale_ref,
    tok_ref,
    gx_ref,
    in_ref,
    gain_ref,
    lon_t_ref,
    perm_t_ref,
    *rest,
):
    out_ref, vec_ref, rows_ref = rest[-3:]
    i = pl.program_id(0)

    @pl.when(i == 0)
    def _():
        vec_ref[...] = jnp.zeros_like(vec_ref)
        deinterleave(plan, perm_t_ref, in_ref, rows_ref)

    for u in range(plan.rb):
        keep = jnp.where(scale_ref[i * plan.rb + u] > 0.0, 1.0, 0.0)
        unit, rstd = norm_parts(tok_ref[0, u].astype(F32))
        gx = gx_ref[u].astype(F32)
        grad = gx + dot_table(lon_t_ref, rows_ref[i * plan.rb + u])
        vec_ref[0:1] += jnp.sum(grad * unit, 0, keepdims=True) * keep
        vec_ref[1:2] += jnp.sum(grad, 0, keepdims=True) * keep
        out_ref[0, u] = (gx + norm_back(grad, unit, rstd, gain_ref[...])) * keep


def last_call(plan, s, scales, tokens, gx, received, gain, earlier):
    operands = [scales, tokens, gx, received, gain, plan.lon_t, plan.perm_t]
    in_specs = [
        SMEM,
        row_block(plan, s),
        own_block(plan),
        whole((plan.pairs, plan.t, plan.d)),
        whole((1, plan.d)),
        whole((2, plan.w, plan.ki)),
        whole(plan.perm_t.shape),
    ]
    aliases = {}
    if earlier is not None:
        aliases = {len(operands): 0}
        operands.append(earlier)
        in_specs.append(ANY)
    return pl.pallas_call(
        functools.partial(last_kernel, plan),
        grid=(plan.chunks,),
        in_specs=in_specs,
        out_specs=[row_block(plan, s), whole((8, plan.d))],
        out_shape=[
            jax.ShapeDtypeStruct((plan.s, plan.r, plan.w, plan.d), F32),
            jax.ShapeDtypeStruct((8, plan.d), F32),
        ],
        scratch_shapes=[pltpu.VMEM((plan.r, plan.ki, plan.d), BF)],
        input_output_aliases=aliases,
        compiler_params=params(),
        cost_estimate=cost(5e9, 17e6),
        name="lon_backward",
    )(*operands)


def band_kernel(plan, in_ref, *rest):
    out_ref, tall = rest[-2:]
    rows = 2 * plan.mb
    height = tall.shape[1] // rows
    for src in range(plan.n):
        for t in range(plan.kk):
            k = src * plan.kk + t
            if k >= plan.kw:
                continue
            at = (t % 2) * rows
            part = in_ref[src, t // 2].astype(F32)[at : at + rows]
            for g in range(plan.d // 128):
                tall[g, pl.ds(k, rows, stride=height), :] = part[:, g * 128 : (g + 1) * 128]
    for p in range(2):
        for m in range(plan.mb):
            top = (p * plan.mb + m) * height
            for g in range(plan.d // 128):
                out_ref[0, m, p, :, g * 128 : (g + 1) * 128] = tall[
                    g, top : top + plan.kw, :
                ].astype(BF)


def band_call(plan, s, received, earlier):
    height = -(-plan.kw // 8) * 8
    shape = (plan.s, plan.mb, 2, plan.kw, plan.d)
    operands = [received]
    in_specs = [whole(received.shape)]
    aliases = {}
    if earlier is not None:
        aliases = {1: 0}
        operands.append(earlier)
        in_specs.append(ANY)
    return pl.pallas_call(
        functools.partial(band_kernel, plan),
        grid=(1,),
        in_specs=in_specs,
        out_specs=pl.BlockSpec((1,) + shape[1:], lambda i: (s, 0, 0, 0, 0)),
        out_shape=jax.ShapeDtypeStruct(shape, BF),
        scratch_shapes=[pltpu.VMEM((plan.d // 128, 2 * plan.mb * height, 128), F32)],
        input_output_aliases=aliases,
        compiler_params=params(),
        cost_estimate=cost(1e9, 8e6),
        name="band_output",
    )(*operands)


def exchange(x):
    return lax.all_to_all(x, "lat", split_axis=0, concat_axis=0, tiled=True)


def on_device(
    bands,
    tokens,
    cotangent,
    sample_weight,
    row_count,
    band_count,
    norm1_gain,
    norm1_bias,
    spec_w1,
    spec_b1,
    spec_w2,
    spec_b2,
    norm2_gain,
    norm2_bias,
    fc1_weight,
    fc1_bias,
    fc2_weight,
    fc2_bias,
):
    lane = lax.axis_index("lat")
    n = lax.axis_size("lat")
    samples, row_slots, width, channels = tokens.shape
    blocks, size = spec_w1.shape[1], spec_w1.shape[2]
    plan = Plan(n, samples, row_slots, width, channels, bands)
    lat = lat_matrix(plan, row_count)
    lat_t = lat.transpose(0, 2, 1)
    slots = slot_matrix(plan, band_count)
    m1, m2 = wide_weight(spec_w1), wide_weight(spec_w2)
    m1t, m2t = m1.transpose(0, 2, 1), m2.transpose(0, 2, 1)
    wb1, wb2 = wide_bias(spec_b1), wide_bias(spec_b2)
    row = lambda v: v.reshape(1, -1)
    vectors = (row(norm1_gain), row(norm1_bias), row(norm2_gain), row(norm2_bias))
    own_rows = jnp.sum(jnp.where(jnp.arange(n) == lane, row_count, 0))
    held = jnp.arange(row_slots) < own_rows
    scales = sample_weight.astype(F32)[:, None] * 0.5 * held[None, :].astype(F32)
    slot_step = jnp.arange(plan.kp)
    valid = ((slot_step < plan.kk) & (lane * plan.kk + slot_step < plan.kw)).astype(F32)
    grouped = (n, plan.q, plan.t, channels)
    listed = (plan.pairs, plan.t, channels)

    sent = [first_call(plan, s, tokens, vectors[0], vectors[1]) for s in range(samples)]
    spectra = [exchange(x.reshape(grouped)) for x in sent]
    forward = [
        spectral_call(plan, valid, x, lat, lat_t, slots, m1, wb1, m2, wb2) for x in spectra
    ]

    def feed(s, back, sums, passengers):
        out = feed_call(
            plan,
            s,
            scales[s],
            tokens,
            cotangent,
            back.reshape(listed),
            vectors,
            fc1_weight,
            row(fc1_bias),
            fc2_weight,
            row(fc2_bias),
            sums,
            s == samples - 1,
            passengers,
        )
        feeds.append(out)
        return out[7:]

    def backward(s, grads):
        out = spectral_back_call(
            plan, blocks, size, grads, forward[s][2:6], lat, lat_t, m1t, m2t
        )
        spectral.append(out)
        return out[0]

    feeds, spectral, band_parts = [], [], []
    back = exchange(forward[0][0])
    grads, lon_grads = {}, {}
    for s in range(samples):
        sums = (feeds[-1][3], feeds[-1][4]) if s else None
        kinds, passengers = ["band"], [forward[s][1]]
        if s + 1 < samples:
            kinds.append("back")
            passengers.append(forward[s + 1][0])
        if s >= 1:
            kinds.append("grads")
            passengers.append(feeds[s - 1][1].reshape(grouped))
        if s >= 2:
            kinds.append("lon")
            passengers.append(backward(s - 2, grads[s - 2]))
        arrived = dict(zip(kinds, feed(s, back, sums, passengers)))
        band_parts.append(arrived["band"])
        back = arrived.get("back")
        if s >= 1:
            grads[s - 1] = arrived["grads"]
        if s >= 2:
            lon_grads[s - 2] = arrived["lon"]
    grads[samples - 1] = exchange(feeds[-1][1].reshape(grouped))
    for s in range(len(spectral), samples):
        lon_grads[s] = exchange(backward(s, grads[s]))

    tokens_grad, spectrum, finals = None, None, []
    for s in range(samples):
        tokens_grad, vec = last_call(
            plan,
            s,
            scales[s],
            tokens,
            feeds[s][2],
            lon_grads[s].reshape(listed),
            vectors[0],
            tokens_grad,
        )
        finals.append(vec)
        spectrum = band_call(plan, s, band_parts[s], spectrum)
    mixed = jnp.stack([f[0] for f in feeds])

    total = lambda parts: functools.reduce(jnp.add, parts)
    feed_vec = total([f[6] for f in feeds])
    last_vec = total(finals)
    block_grad = lambda i: total([b[i] for b in spectral]).reshape(2, blocks, size, size)
    small = (
        feed_vec[1],
        feed_vec[2],
        total([f[5] for f in feeds])[0],
        feed_vec[0],
        last_vec[0],
        last_vec[1],
        block_grad(1),
        narrow_bias(total([b[3] for b in spectral]), blocks, size),
        block_grad(2),
        narrow_bias(total([b[4] for b in spectral]), blocks, size),
        jnp.sum(total([f[6] for f in forward])),
    )
    large = lax.psum((feeds[-1][3], feeds[-1][4]), ("batch", "lat"))
    large = (large[0].astype(F32), large[1].astype(F32))
    small = lax.psum(small, ("batch", "lat"))
    zero_fraction = small[10] / (lax.axis_size("batch") * samples * H * plan.kw * 2 * channels)
    return (
        mixed,
        spectrum,
        tokens_grad,
        small[4],
        small[5],
        small[6],
        small[7],
        small[8],
        small[9],
        small[0],
        small[1],
        large[0],
        small[2],
        large[1],
        small[3],
        zero_fraction,
    )


def solution(mesh):
    rows = P("batch", "lat", None, None)
    in_specs = (rows, rows, P("batch")) + (P(),) * 14
    out_specs = (rows, P("batch", "lat", None, None, None), rows) + (P(),) * 13
    lanes = mesh.shape["lat"]

    def run(tokens, cotangent, *rest):
        row_slots = tokens.shape[1] // lanes
        return jax.shard_map(
            functools.partial(on_device, row_slots + 1),
            mesh=mesh,
            in_specs=in_specs,
            out_specs=out_specs,
            check_vma=False,
        )(tokens, cotangent, *rest)

    return run
```

```python
import functools
import itertools
import math

import jax
import jax.numpy as jnp
import numpy as np
from jax import lax
from jax.experimental import pallas as pl
from jax.experimental.pallas import tpu as pltpu
from jax.sharding import PartitionSpec as P

H = 90
HP = 96

NORM_EPS = 1e-06
SHRINK_LAMBDA = 0.01
SHRINK_SOFTNESS = 0.1
INV_ROOT_TAU = 1.0 / math.sqrt(2.0 * math.pi)
BF = jnp.bfloat16
F32 = jnp.float32
VMEM_BYTES = 64 * 1024 * 1024


def dot(a, b):
    return jnp.dot(a, b, preferred_element_type=F32)


def dot_nt(a, b):
    return lax.dot_general(a, b, (((1,), (1,)), ((), ())), preferred_element_type=F32)


def dot_tn(a, b):
    return lax.dot_general(a, b, (((0,), (0,)), ((), ())), preferred_element_type=F32)


def dot_table(table_ref, x):
    return dot(table_ref[0], x) + dot(table_ref[1], x)


def two_parts(table):
    high = table.astype(BF)
    return high, (table - high.astype(table.dtype)).astype(BF)


def norm_parts(x):
    mean = jnp.mean(x, -1, keepdims=True)
    centred = x - mean
    rstd = lax.rsqrt(jnp.mean(centred * centred, -1, keepdims=True) + NORM_EPS)
    return centred * rstd, rstd


def norm_back(grad, unit, rstd, gain):
    e = grad * gain
    return rstd * (
        e - jnp.mean(e, -1, keepdims=True) - unit * jnp.mean(e * unit, -1, keepdims=True)
    )


def gauss_parts(v):
    d = 1.0 + jnp.abs(v) * (0.3275911 / math.sqrt(2.0))
    t = pl.reciprocal(d, approx=True)
    e = jnp.exp2(v * v * (-0.5 * math.log2(math.e)))
    poly = 1.061405429 * 0.5
    for c in (-1.453152027, 1.421413741, -0.284496736, 0.254829592):
        poly = poly * t + 0.5 * c
    tail = poly * t * e
    cdf = jnp.where(v >= 0.0, 1.0 - tail, tail)
    return cdf, v * e * INV_ROOT_TAU


def gelu_both(v):
    cdf, slope_part = gauss_parts(v)
    return v * cdf, cdf + slope_part


def shrink_both(u):
    a = jnp.maximum(jnp.abs(u) - SHRINK_LAMBDA, 0.0)
    d = a + SHRINK_SOFTNESS
    t = pl.reciprocal(d, approx=True)
    t = t * (2.0 - d * t)
    size = a * a * t
    value = jnp.where(u >= 0.0, size, -size)
    slope = a * (a + 2.0 * SHRINK_SOFTNESS) * (t * t)
    return value, slope


class Plan:
    def __init__(self, n, samples, rows, width, channels, bands):
        self.n, self.s, self.r, self.w, self.d, self.mb = n, samples, rows, width, channels, bands
        self.kw = width // 2 + 1
        self.kk = -(-self.kw // n)
        self.kp = self.kk + self.kk % 2
        self.q = self.kp // 2
        self.rp = -(-rows // 4) * 4
        self.t = 4 * self.rp
        self.pairs = n * self.q
        self.ki = n * self.kp * 2
        self.rb = max(b for b in (4, 3, 2, 1) if rows % b == 0)
        self.chunks = rows // self.rb
        self.flat = self.rb * width
        self.flatp = max(-(-self.flat // 256) * 256, channels)
        j = np.arange(n)[:, None]
        t = np.arange(self.kp)[None, :]
        self.k_index = (j * self.kk + t).astype(np.int64)
        self.k_valid = (t < self.kk) & (self.k_index < self.kw)
        k = np.where(self.k_valid, self.k_index, 0).reshape(-1)
        ok = self.k_valid.reshape(-1).astype(np.float64)
        angle = 2.0 * np.pi * ((k[:, None] * np.arange(width)[None, :]) % width) / width
        scale = ok[:, None] / math.sqrt(width)
        fwd = np.stack([np.cos(angle) * scale, -np.sin(angle) * scale], 1).reshape(self.ki, width)
        factor = np.where((k == 0) | (2 * k == width), 1.0, 2.0)[:, None, None]
        both = (fwd.reshape(-1, 2, width) * factor).reshape(self.ki, width)
        self.lon = np.stack(two_parts(fwd))
        self.lon_both = np.stack(two_parts(both))
        self.lon_t = np.stack(two_parts(np.ascontiguousarray(fwd.T)))
        self.lon_both_t = np.stack(two_parts(np.ascontiguousarray(both.T)))
        perm = np.zeros((16, self.rp, rows, 16))
        for a in range(16):
            for r in range(rows):
                perm[a, r, r, a] = 1.0
        self.perm = perm.reshape(16 * self.rp, rows * 16).astype(BF)
        self.perm_t = np.ascontiguousarray(self.perm.T)


def lat_matrix(plan, row_count):
    n, rp = plan.n, plan.rp
    start = jnp.cumsum(row_count) - row_count
    steps = jnp.arange(rp, dtype=jnp.int32)
    rows = start[:, None] + steps[None, :]
    valid = steps[None, :] < row_count[:, None]
    kh = jnp.arange(HP, dtype=jnp.int32)
    turns = kh[:, None, None] * rows[None] % H
    angle = turns.astype(F32) * (2.0 * math.pi / H)
    weight = jnp.where((kh < H)[:, None, None] & valid[None], 1.0 / math.sqrt(H), 0.0)
    cosine = jnp.cos(angle) * weight
    sine = jnp.sin(angle) * weight
    real = jnp.stack([cosine, sine], 2)
    imag = jnp.stack([-sine, cosine], 2)
    part = jnp.stack([real, imag], 0)
    eye = jnp.eye(2, dtype=F32)
    full = part[None, :, :, :, None] * eye[:, None, None, None, :, None, None]
    full = full.reshape(4 * HP, n * 4 * rp)
    high = lax.reduce_precision(full, 8, 7)
    return jnp.stack([high, full - high]).astype(BF)


def slot_matrix(plan, band_count):
    start = jnp.cumsum(band_count) - band_count
    steps = jnp.arange(plan.mb, dtype=jnp.int32)
    wave = start[:, None] + steps[None, :]
    valid = steps[None, :] < band_count[:, None]
    kh = jnp.arange(HP, dtype=jnp.int32)
    pick = ((wave[:, :, None] == kh) & valid[:, :, None]).astype(F32)
    eye = jnp.eye(4, dtype=F32)
    full = pick[:, None, :, None, :] * eye[None, :, None, :, None]
    return full.reshape(plan.n * 4 * plan.mb, 4 * HP).astype(BF)


def wide_weight(weight):
    blocks, size = weight.shape[1], weight.shape[2]
    half = blocks // 2
    w = weight.reshape(2, 2, half, size, size)
    eye = jnp.eye(half, dtype=weight.dtype)
    dense = w[:, :, :, :, None, :] * eye[None, None, :, None, :, None]
    dense = dense.reshape(2, 2, half * size, half * size)
    re, im = dense[0], dense[1]
    top = jnp.concatenate([re, im], 2)
    bottom = jnp.concatenate([-im, re], 2)
    return jnp.concatenate([top, bottom], 1)


def wide_bias(bias):
    return bias.reshape(2, 2, -1).transpose(1, 0, 2).reshape(2, 1, -1)


def narrow_bias(wide, blocks, size):
    return wide.reshape(2, 2, -1).transpose(1, 0, 2).reshape(2, blocks, size)


def whole(shape):
    zeros = (0,) * len(shape)
    return pl.BlockSpec(shape, lambda *_: zeros)


def whole_once(shape):
    zeros = (0,) * len(shape)
    return pl.BlockSpec(shape, lambda *_: zeros, pipeline_mode=pl.Buffered(1))


SMEM = pl.BlockSpec(memory_space=pltpu.SMEM)
ANY = pl.BlockSpec(memory_space=pl.ANY)


def params(collective_id=None):
    if collective_id is None:
        return pltpu.CompilerParams(
            dimension_semantics=("arbitrary",), vmem_limit_bytes=VMEM_BYTES
        )
    return pltpu.CompilerParams(
        dimension_semantics=("arbitrary",),
        vmem_limit_bytes=VMEM_BYTES,
        collective_id=collective_id,
        has_side_effects=True,
    )


def ride_copy(n, me, src, dst, send, recv, e, step):
    peer = lax.rem(me + step, n)
    return pltpu.make_async_remote_copy(
        src_ref=src.at[peer],
        dst_ref=dst.at[me],
        send_sem=send.at[e, step],
        recv_sem=recv.at[e, step],
        device_id={"lat": peer},
        device_id_type=pl.DeviceIdType.MESH,
    )


def ride_arrival(n, me, src, dst, send, recv, e, step):
    peer = lax.rem(me + n - step, n)
    return pltpu.make_async_remote_copy(
        src_ref=src.at[peer],
        dst_ref=dst.at[peer],
        send_sem=send.at[e, step],
        recv_sem=recv.at[e, step],
        device_id={"lat": peer},
        device_id_type=pl.DeviceIdType.MESH,
    )


def ride_start(n, srcs, dsts, send, recv, own):
    me = lax.axis_index("lat")
    barrier = pltpu.get_barrier_semaphore()
    for step in range(1, n):
        pl.semaphore_signal(
            barrier,
            inc=1,
            device_id={"lat": lax.rem(me + step, n)},
            device_id_type=pl.DeviceIdType.MESH,
        )
    pl.semaphore_wait(barrier, n - 1)
    for e, (src, dst) in enumerate(zip(srcs, dsts)):
        for step in range(1, n):
            ride_copy(n, me, src, dst, send, recv, e, step).start()
        pltpu.make_async_copy(src.at[me], dst.at[me], own.at[e]).start()


def ride_wait(n, srcs, dsts, send, recv, own):
    me = lax.axis_index("lat")
    for e, (src, dst) in enumerate(zip(srcs, dsts)):
        pltpu.make_async_copy(src.at[me], dst.at[me], own.at[e]).wait()
        for step in range(1, n):
            ride_copy(n, me, src, dst, send, recv, e, step).wait_send()
            ride_arrival(n, me, src, dst, send, recv, e, step).wait_recv()


def cost(flops, size):
    return pl.CostEstimate(flops=int(flops), bytes_accessed=int(size), transcendentals=0)


def interleave(plan, perm_ref, rows_ref, out_ref):
    def body(c, carry):
        at = pl.multiple_of(c * 16, 16)
        block = rows_ref[:, pl.ds(at, 16), :].reshape(plan.r * 16, plan.d)
        mixed = dot(perm_ref[...], block).astype(BF)
        out_ref[pl.ds(c * 4, 4)] = mixed.reshape(4, plan.t, plan.d)
        return carry

    lax.fori_loop(0, plan.ki // 16, body, 0)


def deinterleave(plan, perm_t_ref, in_ref, rows_ref):
    def body(c, carry):
        at = pl.multiple_of(c * 16, 16)
        block = in_ref[pl.ds(c * 4, 4)].reshape(4 * plan.t, plan.d)
        rows = dot(perm_t_ref[...], block).astype(BF)
        rows_ref[:, pl.ds(at, 16), :] = rows.reshape(plan.r, 16, plan.d)
        return carry

    lax.fori_loop(0, plan.ki // 16, body, 0)


def interleave_out(plan, perm_ref, rows_ref, ring, sem, out_ref):
    def copy(c):
        return pltpu.make_async_copy(
            ring.at[lax.rem(c, 2)], out_ref.at[pl.ds(c * 4, 4)], sem.at[lax.rem(c, 2)]
        )

    def body(c, carry):
        @pl.when(c >= 2)
        def _():
            copy(c - 2).wait()

        at = pl.multiple_of(c * 16, 16)
        block = rows_ref[:, pl.ds(at, 16), :].reshape(plan.r * 16, plan.d)
        mixed = dot(perm_ref[...], block).astype(BF)
        ring[lax.rem(c, 2)] = mixed.reshape(4, plan.t, plan.d)
        copy(c).start()
        return carry

    lax.fori_loop(0, plan.ki // 16, body, 0)
    return [copy(plan.ki // 16 - 2), copy(plan.ki // 16 - 1)]


def ring_load(plan, in_ref, ring, sem, c):
    return pltpu.make_async_copy(
        in_ref.at[pl.ds(c * 4, 4)], ring.at[lax.rem(c, 2)], sem.at[lax.rem(c, 2)]
    )


def deinterleave_in(plan, perm_t_ref, in_ref, ring, sem, rows_ref):
    steps = plan.ki // 16

    def body(c, carry):
        ring_load(plan, in_ref, ring, sem, c).wait()
        at = pl.multiple_of(c * 16, 16)
        block = ring[lax.rem(c, 2)].reshape(4 * plan.t, plan.d)
        rows = dot(perm_t_ref[...], block).astype(BF)
        rows_ref[:, pl.ds(at, 16), :] = rows.reshape(plan.r, 16, plan.d)

        @pl.when(c + 2 < steps)
        def _():
            ring_load(plan, in_ref, ring, sem, c + 2).start()

        return carry

    lax.fori_loop(0, steps, body, 0)


class Riders:
    def __init__(self, plan, passengers):
        self.n = plan.n
        self.arrays = [a for a, _ in passengers]
        self.leads = [lead for _, lead in passengers]
        self.count = len(passengers)

    def shapes(self):
        return [
            jax.ShapeDtypeStruct(a.shape if lead is None else a.shape[1:], a.dtype)
            for a, lead in zip(self.arrays, self.leads)
        ]

    def specs(self):
        return [ANY] * self.count

    def scratch(self):
        if not self.count:
            return []
        dma = pltpu.SemaphoreType.DMA
        return [dma((self.count, self.n)), dma((self.count, self.n)), dma((self.count,))]

    def bind(self, srcs, dsts, sems):
        srcs = [r if lead is None else r.at[lead] for r, lead in zip(srcs, self.leads)]
        return (self.n, srcs, dsts) + tuple(sems)


def first_kernel(plan, riders, tok_ref, gain_ref, bias_ref, lon_ref, perm_ref, *rest):
    e = riders.count
    srcs, out_ref, dsts, rows_ref, sems = (
        rest[:e],
        rest[e],
        rest[e + 1 : 2 * e + 1],
        rest[2 * e + 1],
        rest[2 * e + 2 :],
    )
    i = pl.program_id(0)
    c = lax.rem(i, plan.chunks)
    if e:
        ride = riders.bind(srcs, dsts, sems)

        @pl.when(i == 0)
        def _():
            ride_start(*ride)

    for u in range(plan.rb):
        unit, _ = norm_parts(tok_ref[0, u].astype(F32))
        normed = (unit * gain_ref[...] + bias_ref[...]).astype(BF)
        rows_ref[c * plan.rb + u] = dot_table(lon_ref, normed).astype(BF)

    @pl.when(c == plan.chunks - 1)
    def _():
        interleave(plan, perm_ref, rows_ref, out_ref.at[0])

    if e:

        @pl.when(i == pl.num_programs(0) - 1)
        def _():
            ride_wait(*ride)


def row_block(plan, s):
    return pl.BlockSpec((1, plan.rb, plan.w, plan.d), lambda i: (s, i, 0, 0))


def own_block(plan):
    return pl.BlockSpec((plan.rb, plan.w, plan.d), lambda i: (i, 0, 0))


def first_call(plan, start, count, tokens, gain, bias, passengers=(), collective_id=None):
    shape = (plan.pairs, plan.t, plan.d)
    chunks = plan.chunks
    riders = Riders(plan, passengers)
    return pl.pallas_call(
        functools.partial(first_kernel, plan, riders),
        grid=(count * chunks,),
        in_specs=[
            pl.BlockSpec(
                (1, plan.rb, plan.w, plan.d),
                lambda i: (start + i // chunks, lax.rem(i, chunks), 0, 0),
            ),
            whole((1, plan.d)),
            whole((1, plan.d)),
            whole((2, plan.ki, plan.w)),
            whole(plan.perm.shape),
        ]
        + riders.specs(),
        out_specs=[pl.BlockSpec((1,) + shape, lambda i: (i // chunks, 0, 0, 0))] + riders.specs(),
        out_shape=[jax.ShapeDtypeStruct((count,) + shape, BF)] + riders.shapes(),
        scratch_shapes=[pltpu.VMEM((plan.r, plan.ki, plan.d), BF)] + riders.scratch(),
        compiler_params=params(collective_id),
        cost_estimate=cost(9e9 * count, 8e6 * count),
        name="lon_forward",
    )(tokens, gain, bias, plan.lon, plan.perm, *riders.arrays)


def spectral_kernel(
    plan,
    riders,
    valid_ref,
    in_ref,
    lat_ref,
    lat_t_ref,
    slot_ref,
    m1_ref,
    b1_ref,
    m2_ref,
    b2_ref,
    *rest,
):
    e = riders.count
    srcs, rest = rest[:e], rest[e:]
    back_ref, band_ref, spec_ref, hid_ref, slope1_ref, slope2_ref, zero_ref = rest[:7]
    dsts, shr_ref, sems = rest[7 : 7 + e], rest[7 + e], rest[8 + e :]
    q = pl.program_id(0)
    half = plan.d // 2
    if e:
        ride = riders.bind(srcs, dsts, sems)

        @pl.when(q == 0)
        def _():
            ride_start(*ride)

    @pl.when(q == 0)
    def _():
        zero_ref[...] = jnp.zeros_like(zero_ref)

    x = in_ref[:, 0].reshape(plan.n * plan.t, plan.d)
    spec = dot_table(lat_ref, x).astype(BF)
    ok = (lax.broadcasted_iota(jnp.int32, (HP, 1), 0) < H).astype(F32)
    for g in range(2):
        lanes = slice(g * half, (g + 1) * half)
        for a in range(2):
            top = a * 2 * HP
            spec_ref[0, g, a * HP : (a + 1) * HP, :half] = spec[top : top + HP, lanes]
            spec_ref[0, g, a * HP : (a + 1) * HP, half:] = spec[top + HP : top + 2 * HP, lanes]
        u1 = dot(spec_ref[0, g], m1_ref[g]) + b1_ref[g]
        hidden, slope = gelu_both(u1)
        hid_ref[0, g] = hidden.astype(BF)
        slope1_ref[0, g] = slope.astype(BF)
        u2 = dot(hid_ref[0, g], m2_ref[g]) + b2_ref[g]
        small = (jnp.abs(u2) <= SHRINK_LAMBDA).astype(F32)
        for a in range(2):
            part = small[a * HP : (a + 1) * HP] * ok
            zero_ref[...] += jnp.sum(part, 0, keepdims=True) * valid_ref[q * 2 + a]
        value, slope = shrink_both(u2)
        slope2_ref[0, g] = slope.astype(BF)
        value = value.astype(BF)
        for a in range(2):
            top = a * 2 * HP
            shr_ref[top : top + HP, lanes] = value[a * HP : (a + 1) * HP, :half]
            shr_ref[top + HP : top + 2 * HP, lanes] = value[a * HP : (a + 1) * HP, half:]
    shrunk = shr_ref[...]
    back_ref[:, 0] = dot_table(lat_t_ref, shrunk).astype(BF).reshape(plan.n, plan.t, plan.d)
    band = dot(slot_ref[...], shrunk).astype(BF)
    rows = 4 * plan.mb
    for j in range(plan.n):
        band_ref[j, 0] = band[j * rows : (j + 1) * rows]
    if e:

        @pl.when(q == plan.q - 1)
        def _():
            ride_wait(*ride)


def pair_block(plan, rows):
    return pl.BlockSpec((plan.n, 1, rows, plan.d), lambda q: (0, q, 0, 0))


def spectral_call(
    plan, valid, received, lat, lat_t, slots, m1, b1, m2, b2, passengers=(), collective_id=None
):
    riders = Riders(plan, passengers)
    kept = (plan.q, 2, 2 * HP, plan.d)
    kept_spec = pl.BlockSpec((1, 2, 2 * HP, plan.d), lambda q: (q, 0, 0, 0))
    kept_shape = jax.ShapeDtypeStruct(kept, BF)
    rows = 4 * plan.mb
    return pl.pallas_call(
        functools.partial(spectral_kernel, plan, riders),
        grid=(plan.q,),
        in_specs=[
            SMEM,
            pair_block(plan, plan.t),
            whole(lat.shape),
            whole(lat_t.shape),
            whole(slots.shape),
            whole(m1.shape),
            whole(b1.shape),
            whole(m2.shape),
            whole(b2.shape),
        ]
        + riders.specs(),
        out_specs=[
            pair_block(plan, plan.t),
            pair_block(plan, rows),
            kept_spec,
            kept_spec,
            kept_spec,
            kept_spec,
            whole((1, plan.d)),
        ]
        + riders.specs(),
        out_shape=[
            jax.ShapeDtypeStruct((plan.n, plan.q, plan.t, plan.d), BF),
            jax.ShapeDtypeStruct((plan.n, plan.q, rows, plan.d), BF),
            kept_shape,
            kept_shape,
            kept_shape,
            kept_shape,
            jax.ShapeDtypeStruct((1, plan.d), F32),
        ]
        + riders.shapes(),
        scratch_shapes=[pltpu.VMEM((4 * HP, plan.d), BF)] + riders.scratch(),
        compiler_params=params(collective_id),
        cost_estimate=cost(20e9, 25e6),
        name="spectral_forward",
    )(valid, received, lat, lat_t, slots, m1, b1, m2, b2, *riders.arrays)


def feed_kernel(
    plan,
    first,
    final,
    riders,
    tiles,
    scale_ref,
    tok_ref,
    cot_ref,
    recv_ref,
    gain1_ref,
    bias1_ref,
    gain2_ref,
    bias2_ref,
    lon_t_ref,
    lon_ref,
    perm_ref,
    perm_t_ref,
    w1_ref,
    b1_ref,
    w2_ref,
    b2_ref,
    *rest,
):
    e = riders.count
    srcs, rest = rest[:e], rest[e:]
    if first:
        in1_ref = in2_ref = None
    else:
        in1_ref, in2_ref = rest[:2]
        rest = rest[2:]
    mixed_ref, send_ref, gx_ref, out1_ref, out2_ref, db1_ref, vec_ref = rest[:7]
    dsts, rest = rest[7 : 7 + e], rest[7 + e :]
    (
        dw1,
        dw2,
        ring,
        rows_ref,
        x1_ref,
        xn,
        xn_t,
        gm,
        gm_t,
        act_a,
        gz_a,
        act_b,
        gz_b,
        down,
        up,
        sem,
        ring_sem,
        *ride_sems,
    ) = rest
    i = pl.program_id(0)
    last = plan.chunks - 1
    tile = act_a.shape[1]
    flat = plan.flat
    ride = riders.bind(srcs, dsts, ride_sems)

    @pl.when(i == 0)
    def _():
        for c in range(2):
            ring_load(plan, recv_ref, ring, ring_sem, c).start()
        if not first:
            pltpu.make_async_copy(in1_ref, dw1, sem.at[1]).start()
            pltpu.make_async_copy(in2_ref, dw2, sem.at[2]).start()
        ride_start(*ride)
        if first:
            dw1[...] = jnp.zeros_like(dw1)
            dw2[...] = jnp.zeros_like(dw2)
        db1_ref[...] = jnp.zeros_like(db1_ref)
        vec_ref[...] = jnp.zeros_like(vec_ref)
        if plan.flatp > flat:
            pad = jnp.zeros((plan.flatp - flat, tile), BF)
            for ref in (act_a, gz_a, act_b, gz_b):
                ref[flat:, :] = pad
            pad = jnp.zeros((plan.flatp - flat, plan.d), F32)
            down[flat:, :] = pad
            up[flat:, :] = pad
        deinterleave_in(plan, perm_t_ref, recv_ref, ring, ring_sem, rows_ref)

    for u in range(plan.rb):
        span = slice(u * plan.w, (u + 1) * plan.w)
        x = tok_ref[0, u].astype(F32)
        unit, _ = norm_parts(x)
        filtered = dot_table(lon_t_ref, rows_ref[i * plan.rb + u])
        x1 = x + filtered + (unit * gain1_ref[...] + bias1_ref[...])
        x1_ref[u] = x1
        unit, _ = norm_parts(x1)
        down[span, :] = unit * gain2_ref[...] + bias2_ref[...]
        up[span, :] = cot_ref[0, u].astype(F32) * scale_ref[i * plan.rb + u]
    normed = down[...].astype(BF)
    xn[...] = normed[:flat]
    xn_t[...] = normed.T
    grads = up[...].astype(BF)
    gm[...] = grads[:flat]
    gm_t[...] = grads.T
    vec_ref[0:1] += jnp.sum(grads.astype(F32), 0, keepdims=True)
    down[...] = jnp.zeros_like(down)
    up[...] = jnp.zeros_like(up)

    if not first:

        @pl.when(i == 0)
        def _():
            pltpu.make_async_copy(in1_ref, dw1, sem.at[1]).wait()
            pltpu.make_async_copy(in2_ref, dw2, sem.at[2]).wait()

    def columns(t):
        return pl.ds(pl.multiple_of(t * tile, tile), tile)

    def enter(t, act, gz):
        cols = columns(t)
        z = dot(xn[...], w1_ref[:, cols]) + b1_ref[:, cols]
        ga = dot_nt(gm[...], w2_ref[cols, :])
        hidden, slope = gelu_both(z)
        grad = ga * slope
        act[:flat, :] = hidden.astype(BF)
        gz[:flat, :] = grad.astype(BF)
        db1_ref[:, cols] += jnp.sum(grad, 0, keepdims=True)

    def leave(t, act, gz):
        cols = columns(t)
        down[:flat, :] += dot(act[:flat, :], w2_ref[cols, :])
        up[:flat, :] += dot_nt(gz[:flat, :], w1_ref[:, cols])
        dw1[:, cols] += dot(xn_t[...], gz[...])
        dw2[:, cols] += dot(gm_t[...], act[...])

    def body(t, carry):
        enter(t, act_a, gz_a)
        leave(t, act_a, gz_a)
        return carry

    lax.fori_loop(0, tiles, body, 0)

    if not final:

        @pl.when(i == last)
        def _():
            pltpu.make_async_copy(dw1, out1_ref, sem.at[1]).start()
            pltpu.make_async_copy(dw2, out2_ref, sem.at[2]).start()

    for u in range(plan.rb):
        span = slice(u * plan.w, (u + 1) * plan.w)
        x1 = x1_ref[u]
        scale = scale_ref[i * plan.rb + u]
        keep = jnp.where(scale > 0.0, 1.0, 0.0)
        mixed_ref[u] = ((x1 + down[span, :] + b2_ref[...]) * keep).astype(BF)
        unit, rstd = norm_parts(x1)
        grad = up[span, :]
        vec_ref[1:2] += jnp.sum(grad * unit, 0, keepdims=True)
        vec_ref[2:3] += jnp.sum(grad, 0, keepdims=True)
        gx = cot_ref[0, u].astype(F32) * scale + norm_back(grad, unit, rstd, gain2_ref[...])
        gx_ref[u] = gx.astype(gx_ref.dtype)
        rows_ref[i * plan.rb + u] = dot_table(lon_ref, gx.astype(BF)).astype(BF)

    if plan.flatp > flat:
        down[flat:, :] = jnp.zeros((plan.flatp - flat, plan.d), F32)
        up[flat:, :] = jnp.zeros((plan.flatp - flat, plan.d), F32)

    @pl.when(i == last)
    def _():
        stores = interleave_out(plan, perm_ref, rows_ref, ring, ring_sem, send_ref)
        if final:
            pending = {}
            for t in range(tiles):
                cols = slice(t * tile, (t + 1) * tile)
                side = t % 2
                for copy in pending.pop(side, ()):
                    copy.wait()
                one, two = ((act_a, gz_a), (act_b, gz_b))[side]
                one[: plan.d, :] = dw1[:, cols].astype(BF)
                xn_part = (xn_t, gm_t)[side]
                xn_part[:tile, : plan.d] = dw2[:, cols].astype(BF).T
                copies = (
                    pltpu.make_async_copy(one.at[: plan.d], out1_ref.at[:, cols], sem.at[1 + side]),
                    pltpu.make_async_copy(
                        xn_part.at[:tile, : plan.d], out2_ref.at[cols], sem.at[3 + side]
                    ),
                )
                for copy in copies:
                    copy.start()
                pending[side] = copies
            for copies in pending.values():
                for copy in copies:
                    copy.wait()
        else:
            pltpu.make_async_copy(dw1, out1_ref, sem.at[1]).wait()
            pltpu.make_async_copy(dw2, out2_ref, sem.at[2]).wait()
        for store in stores:
            store.wait()
        ride_wait(*ride)


def feed_call(
    plan, s, scales, tokens, cotangent, received, vectors, w1, b1, w2, b2, sums, final, passengers,
    collective_id
):
    gain1, bias1, gain2, bias2 = vectors
    first = sums is None
    ff = w1.shape[1]
    tile = 512
    d, flat = plan.d, plan.flat
    flatp = plan.flatp
    shape = (plan.pairs, plan.t, d)
    vec = whole((1, d))
    riders = Riders(plan, passengers)
    in_specs = [
        SMEM,
        row_block(plan, s),
        row_block(plan, s),
        ANY,
        vec,
        vec,
        vec,
        vec,
        whole((2, plan.w, plan.ki)),
        whole((2, plan.ki, plan.w)),
        whole(plan.perm.shape),
        whole(plan.perm_t.shape),
        whole_once((d, ff)),
        whole((1, ff)),
        whole_once((ff, d)),
        vec,
    ] + riders.specs()
    operands = [
        scales,
        tokens,
        cotangent,
        received,
        gain1,
        bias1,
        gain2,
        bias2,
        plan.lon_both_t,
        plan.lon_both,
        plan.perm,
        plan.perm_t,
        w1,
        b1,
        w2,
        b2,
        *riders.arrays,
    ]
    aliases = {}
    if not first:
        if not final:
            aliases = {len(operands): 3, len(operands) + 1: 4}
        in_specs += [ANY, ANY]
        operands += list(sums)
    if final:
        wides = [jax.ShapeDtypeStruct((d, ff), BF), jax.ShapeDtypeStruct((ff, d), BF)]
    else:
        wides = [jax.ShapeDtypeStruct((d, ff), F32)] * 2
    return pl.pallas_call(
        functools.partial(feed_kernel, plan, first, final, riders, ff // tile),
        grid=(plan.chunks,),
        in_specs=in_specs,
        out_specs=[
            own_block(plan),
            ANY,
            own_block(plan),
            ANY,
            ANY,
            whole((1, ff)),
            whole((8, d)),
        ]
        + riders.specs(),
        out_shape=[
            jax.ShapeDtypeStruct((plan.r, plan.w, d), BF),
            jax.ShapeDtypeStruct(shape, BF),
            jax.ShapeDtypeStruct((plan.r, plan.w, d), BF),
            *wides,
            jax.ShapeDtypeStruct((1, ff), F32),
            jax.ShapeDtypeStruct((8, d), F32),
        ]
        + riders.shapes(),
        scratch_shapes=[
            pltpu.VMEM((d, ff), F32),
            pltpu.VMEM((d, ff), F32),
            pltpu.VMEM((2, 4, plan.t, d), BF),
            pltpu.VMEM((plan.r, plan.ki, d), BF),
            pltpu.VMEM((plan.rb, plan.w, d), F32),
            pltpu.VMEM((flat, d), BF),
            pltpu.VMEM((d, flatp), BF),
            pltpu.VMEM((flat, d), BF),
            pltpu.VMEM((d, flatp), BF),
            pltpu.VMEM((flatp, tile), BF),
            pltpu.VMEM((flatp, tile), BF),
            pltpu.VMEM((flatp, tile), BF),
            pltpu.VMEM((flatp, tile), BF),
            pltpu.VMEM((flatp, d), F32),
            pltpu.VMEM((flatp, d), F32),
            pltpu.SemaphoreType.DMA((5,)),
            pltpu.SemaphoreType.DMA((2,)),
        ]
        + riders.scratch(),
        input_output_aliases=aliases,
        compiler_params=params(collective_id),
        cost_estimate=cost(70e9, 60e6),
        name="feed_forward",
    )(*operands)


def spectral_back_kernel(
    plan,
    in_ref,
    spec_ref,
    hid_ref,
    slope1_ref,
    slope2_ref,
    lat_ref,
    lat_t_ref,
    m1t_ref,
    m2t_ref,
    out_ref,
    dw1_ref,
    dw2_ref,
    db1_ref,
    db2_ref,
    dm1_ref,
    dm2_ref,
    gs_ref,
    gu_ref,
):
    q = pl.program_id(0)
    half = plan.d // 2

    @pl.when(q == 0)
    def _():
        dm1_ref[...] = jnp.zeros_like(dm1_ref)
        dm2_ref[...] = jnp.zeros_like(dm2_ref)
        db1_ref[...] = jnp.zeros_like(db1_ref)
        db2_ref[...] = jnp.zeros_like(db2_ref)

    x = in_ref[:, 0].reshape(plan.n * plan.t, plan.d)
    grad = dot_table(lat_ref, x).astype(BF)
    for g in range(2):
        lanes = slice(g * half, (g + 1) * half)
        for a in range(2):
            top = a * 2 * HP
            gu_ref[a * HP : (a + 1) * HP, :half] = grad[top : top + HP, lanes]
            gu_ref[a * HP : (a + 1) * HP, half:] = grad[top + HP : top + 2 * HP, lanes]
        gu2 = gu_ref[...].astype(F32) * slope2_ref[0, g].astype(F32)
        db2_ref[g] += jnp.sum(gu2, 0, keepdims=True)
        gu2 = gu2.astype(BF)
        dm2_ref[g] += dot_tn(hid_ref[0, g], gu2)
        gu1 = (dot(gu2, m2t_ref[g]) * slope1_ref[0, g].astype(F32)).astype(BF)
        db1_ref[g] += jnp.sum(gu1.astype(F32), 0, keepdims=True)
        dm1_ref[g] += dot_tn(spec_ref[0, g], gu1)
        gs = dot(gu1, m1t_ref[g]).astype(BF)
        for a in range(2):
            top = a * 2 * HP
            gs_ref[top : top + HP, lanes] = gs[a * HP : (a + 1) * HP, :half]
            gs_ref[top + HP : top + 2 * HP, lanes] = gs[a * HP : (a + 1) * HP, half:]
    out_ref[:, 0] = dot_table(lat_t_ref, gs_ref[...]).astype(BF).reshape(plan.n, plan.t, plan.d)

    @pl.when(q == plan.q - 1)
    def _():
        blocks, size = dw1_ref.shape[2:4]
        for wide, narrow in ((dm1_ref, dw1_ref), (dm2_ref, dw2_ref)):
            for g in range(2):
                for b in range(blocks):
                    re = slice(b * size, (b + 1) * size)
                    im = slice(half + b * size, half + (b + 1) * size)
                    narrow[0, g, b] = wide[g, re, re] + wide[g, im, im]
                    narrow[1, g, b] = wide[g, re, im] - wide[g, im, re]


def spectral_back_call(plan, blocks, size, received, kept, lat, lat_t, m1t, m2t):
    small = (2, 2, blocks // 2, size, size)
    kept_spec = pl.BlockSpec((1, 2, 2 * HP, plan.d), lambda q: (q, 0, 0, 0))
    wide = (2, plan.d, plan.d)
    thin = (2, 1, plan.d)
    return pl.pallas_call(
        functools.partial(spectral_back_kernel, plan),
        grid=(plan.q,),
        in_specs=[pair_block(plan, plan.t)]
        + [kept_spec] * 4
        + [whole(lat.shape), whole(lat_t.shape), whole(wide), whole(wide)],
        out_specs=[
            pair_block(plan, plan.t),
            whole(small),
            whole(small),
            whole(thin),
            whole(thin),
        ],
        out_shape=[
            jax.ShapeDtypeStruct((plan.n, plan.q, plan.t, plan.d), BF),
            jax.ShapeDtypeStruct(small, F32),
            jax.ShapeDtypeStruct(small, F32),
            jax.ShapeDtypeStruct(thin, F32),
            jax.ShapeDtypeStruct(thin, F32),
        ],
        scratch_shapes=[
            pltpu.VMEM(wide, F32),
            pltpu.VMEM(wide, F32),
            pltpu.VMEM((4 * HP, plan.d), BF),
            pltpu.VMEM((2 * HP, plan.d), BF),
        ],
        compiler_params=params(),
        cost_estimate=cost(1e9, 1e6),
        name="spectral_backward",
    )(received, *kept, lat, lat_t, m1t, m2t)


def last_kernel(
    plan,
    scale_ref,
    tok_ref,
    gx_ref,
    in_ref,
    gain_ref,
    lon_t_ref,
    perm_t_ref,
    *rest,
):
    out_ref, vec_ref, rows_ref = rest[-3:]
    i = pl.program_id(0)

    @pl.when(i == 0)
    def _():
        vec_ref[...] = jnp.zeros_like(vec_ref)
        deinterleave(plan, perm_t_ref, in_ref, rows_ref)

    for u in range(plan.rb):
        keep = jnp.where(scale_ref[i * plan.rb + u] > 0.0, 1.0, 0.0)
        unit, rstd = norm_parts(tok_ref[0, u].astype(F32))
        gx = gx_ref[u].astype(F32)
        grad = gx + dot_table(lon_t_ref, rows_ref[i * plan.rb + u])
        vec_ref[0:1] += jnp.sum(grad * unit, 0, keepdims=True) * keep
        vec_ref[1:2] += jnp.sum(grad, 0, keepdims=True) * keep
        out_ref[0, u] = (gx + norm_back(grad, unit, rstd, gain_ref[...])) * keep


def last_call(plan, s, scales, tokens, gx, received, gain, earlier):
    operands = [scales, tokens, gx, received, gain, plan.lon_t, plan.perm_t]
    in_specs = [
        SMEM,
        row_block(plan, s),
        own_block(plan),
        whole((plan.pairs, plan.t, plan.d)),
        whole((1, plan.d)),
        whole((2, plan.w, plan.ki)),
        whole(plan.perm_t.shape),
    ]
    aliases = {}
    if earlier is not None:
        aliases = {len(operands): 0}
        operands.append(earlier)
        in_specs.append(ANY)
    return pl.pallas_call(
        functools.partial(last_kernel, plan),
        grid=(plan.chunks,),
        in_specs=in_specs,
        out_specs=[row_block(plan, s), whole((2, plan.d))],
        out_shape=[
            jax.ShapeDtypeStruct((plan.s, plan.r, plan.w, plan.d), F32),
            jax.ShapeDtypeStruct((2, plan.d), F32),
        ],
        scratch_shapes=[pltpu.VMEM((plan.r, plan.ki, plan.d), BF)],
        input_output_aliases=aliases,
        compiler_params=params(),
        cost_estimate=cost(1e9, 1e6),
        name="lon_backward",
    )(*operands)


def band_kernel(plan, in_ref, *rest):
    out_ref, tall = rest[-2:]
    mb = plan.mb
    height = 2 * plan.kw
    for src in range(plan.n):
        for t in range(plan.kk):
            k = src * plan.kk + t
            if k >= plan.kw:
                continue
            both = in_ref[src, t // 2].astype(F32)
            for p in range(2):
                at = ((t % 2) * 2 + p) * mb
                part = both[at : at + mb]
                for g in range(plan.d // 128):
                    tall[g, pl.ds(2 * k + p, mb, stride=height), :] = part[
                        :, g * 128 : (g + 1) * 128
                    ]
    for m in range(mb):
        for g in range(plan.d // 128):
            piece = tall[g, m * height : (m + 1) * height, :].astype(BF)
            out_ref[0, m, :, :, g * 128 : (g + 1) * 128] = piece.reshape(plan.kw, 2, 128)


def band_call(plan, s, received, earlier):
    shape = (plan.s, plan.mb, plan.kw, 2, plan.d)
    operands = [received]
    in_specs = [whole(received.shape)]
    aliases = {}
    if earlier is not None:
        aliases = {1: 0}
        operands.append(earlier)
        in_specs.append(ANY)
    return pl.pallas_call(
        functools.partial(band_kernel, plan),
        grid=(1,),
        in_specs=in_specs,
        out_specs=pl.BlockSpec((1,) + shape[1:], lambda i: (s, 0, 0, 0, 0)),
        out_shape=jax.ShapeDtypeStruct(shape, BF),
        scratch_shapes=[pltpu.VMEM((plan.d // 128, 2 * plan.mb * plan.kw, 128), F32)],
        input_output_aliases=aliases,
        compiler_params=params(),
        cost_estimate=cost(1e8, 1e6),
        name="band_output",
    )(*operands)


def every_peer(total, step_of):
    def body(step, carry):
        step_of(step)
        return carry

    lax.fori_loop(1, total, body, 0)


def place(lanes, index):
    return {"batch": index // lanes, "lat": lax.rem(index, lanes)}


def greet_all(total, lanes, me):
    barrier = pltpu.get_barrier_semaphore()

    def greet(step):
        pl.semaphore_signal(
            barrier,
            inc=1,
            device_id=place(lanes, lax.rem(me + step, total)),
            device_id_type=pl.DeviceIdType.MESH,
        )

    every_peer(total, greet)
    pl.semaphore_wait(barrier, total - 1)


def block_sum_kernel(total, lanes, xs, *rest):
    ins, outs, helds, sems = rest[:xs], rest[xs : 2 * xs], rest[2 * xs : 3 * xs], rest[3 * xs :]
    me = lax.axis_index("batch") * lanes + lax.axis_index("lat")
    greet_all(total, lanes, me)

    def part(a, step, peer):
        return pltpu.make_async_remote_copy(
            src_ref=ins[a].at[peer],
            dst_ref=helds[a].at[step],
            send_sem=sems[4 * a].at[step],
            recv_sem=sems[4 * a + 1].at[step],
            device_id=place(lanes, peer),
            device_id_type=pl.DeviceIdType.MESH,
        )

    def result(a, step, peer, slot):
        return pltpu.make_async_remote_copy(
            src_ref=outs[a].at[me],
            dst_ref=outs[a].at[slot],
            send_sem=sems[4 * a + 2].at[step],
            recv_sem=sems[4 * a + 3].at[step],
            device_id=place(lanes, peer),
            device_id_type=pl.DeviceIdType.MESH,
        )

    ahead = lambda step: lax.rem(me + step, total)
    behind = lambda step: lax.rem(me + total - step, total)
    for a in range(xs):
        every_peer(total, lambda step: part(a, step, ahead(step)).start())
    for a in range(xs):
        helds[a][0] = ins[a][me]
        every_peer(total, lambda step: part(a, step, behind(step)).wait_recv())
        outs[a][me] = jnp.sum(helds[a][...].astype(F32), 0).astype(outs[a].dtype)
        every_peer(total, lambda step: result(a, step, ahead(step), me).start())
    for a in range(xs):
        every_peer(total, lambda step: part(a, step, ahead(step)).wait_send())
        every_peer(total, lambda step: result(a, step, behind(step), behind(step)).wait_recv())
        every_peer(total, lambda step: result(a, step, ahead(step), me).wait_send())


def block_sum(total, lanes, xs, collective_id):
    vmem = pl.BlockSpec(memory_space=pltpu.VMEM)
    sems = [pltpu.SemaphoreType.DMA((total,))] * (4 * len(xs))
    return pl.pallas_call(
        functools.partial(block_sum_kernel, total, lanes, len(xs)),
        in_specs=[vmem] * len(xs),
        out_specs=[vmem] * len(xs),
        out_shape=[jax.ShapeDtypeStruct(x.shape, x.dtype) for x in xs],
        scratch_shapes=[pltpu.VMEM(x.shape, x.dtype) for x in xs] + sems,
        compiler_params=pltpu.CompilerParams(
            collective_id=collective_id, has_side_effects=True, vmem_limit_bytes=VMEM_BYTES
        ),
        cost_estimate=cost(1e8, 1e6),
        name="block_sum",
    )(*xs)


def pack(total, parts, dtype, rows):
    flat = jnp.concatenate([x.reshape(-1).astype(dtype) for x in parts])
    unit = total * rows * 128
    padded = -(-flat.shape[0] // unit) * unit
    return jnp.pad(flat, (0, padded - flat.shape[0])).reshape(total, -1, 128)


def unpack(packed, parts):
    flat = packed.reshape(-1).astype(F32)
    out, at = [], 0
    for x in parts:
        out.append(flat[at : at + x.size].reshape(x.shape))
        at += x.size
    return out


def whole_sum_kernel(total, lanes, x_ref, out_ref, held, send, recv):
    me = lax.axis_index("batch") * lanes + lax.axis_index("lat")
    greet_all(total, lanes, me)

    def part(step, peer):
        return pltpu.make_async_remote_copy(
            src_ref=x_ref,
            dst_ref=held.at[step],
            send_sem=send.at[step],
            recv_sem=recv.at[step],
            device_id=place(lanes, peer),
            device_id_type=pl.DeviceIdType.MESH,
        )

    ahead = lambda step: lax.rem(me + step, total)
    every_peer(total, lambda step: part(step, ahead(step)).start())
    held[0] = x_ref[...]
    every_peer(total, lambda step: part(step, ahead(step)).wait_recv())
    out_ref[...] = jnp.sum(held[...], 0)
    every_peer(total, lambda step: part(step, ahead(step)).wait_send())


def whole_sum(total, lanes, x, collective_id):
    sems = [pltpu.SemaphoreType.DMA((total,))] * 2
    return pl.pallas_call(
        functools.partial(whole_sum_kernel, total, lanes),
        in_specs=[pl.BlockSpec(memory_space=pltpu.VMEM)],
        out_specs=pl.BlockSpec(memory_space=pltpu.VMEM),
        out_shape=jax.ShapeDtypeStruct(x.shape, x.dtype),
        scratch_shapes=[pltpu.VMEM((total,) + x.shape, x.dtype)] + sems,
        compiler_params=pltpu.CompilerParams(
            collective_id=collective_id, has_side_effects=True, vmem_limit_bytes=VMEM_BYTES
        ),
        cost_estimate=cost(1e8, 1e6),
        name="whole_sum",
    )(x)


def exchange(x):
    return lax.all_to_all(x, "lat", split_axis=0, concat_axis=0, tiled=True)


def on_device(
    bands,
    tokens,
    cotangent,
    sample_weight,
    row_count,
    band_count,
    norm1_gain,
    norm1_bias,
    spec_w1,
    spec_b1,
    spec_w2,
    spec_b2,
    norm2_gain,
    norm2_bias,
    fc1_weight,
    fc1_bias,
    fc2_weight,
    fc2_bias,
):
    lane = lax.axis_index("lat")
    n = lax.axis_size("lat")
    samples, row_slots, width, channels = tokens.shape
    blocks, size = spec_w1.shape[1], spec_w1.shape[2]
    plan = Plan(n, samples, row_slots, width, channels, bands)
    lat = lat_matrix(plan, row_count)
    lat_t = lat.transpose(0, 2, 1)
    slots = slot_matrix(plan, band_count)
    m1, m2 = wide_weight(spec_w1), wide_weight(spec_w2)
    m1t, m2t = m1.transpose(0, 2, 1), m2.transpose(0, 2, 1)
    wb1, wb2 = wide_bias(spec_b1), wide_bias(spec_b2)
    row = lambda v: v.reshape(1, -1)
    vectors = (row(norm1_gain), row(norm1_bias), row(norm2_gain), row(norm2_bias))
    own_rows = jnp.sum(jnp.where(jnp.arange(n) == lane, row_count, 0))
    held = jnp.arange(row_slots) < own_rows
    scales = sample_weight.astype(F32)[:, None] * 0.5 * held[None, :].astype(F32)
    slot_step = jnp.arange(plan.kp)
    valid = ((slot_step < plan.kk) & (lane * plan.kk + slot_step < plan.kw)).astype(F32)
    grouped = (n, plan.q, plan.t, channels)
    listed = (plan.pairs, plan.t, channels)

    ids = itertools.count()
    spread = (-1,) + grouped

    def spectral_forward(x, passengers=()):
        collective_id = next(ids) if passengers else None
        out = spectral_call(
            plan, valid, x, lat, lat_t, slots, m1, wb1, m2, wb2, passengers, collective_id
        )
        forward.append(out)
        return out[7:]

    def feed(s, back, sums, passengers):
        out = feed_call(
            plan,
            s,
            scales[s],
            tokens,
            cotangent,
            back.reshape(listed),
            vectors,
            fc1_weight,
            row(fc1_bias),
            fc2_weight,
            row(fc2_bias),
            sums,
            s == samples - 1,
            passengers,
            next(ids),
        )
        feeds.append(out)
        return out[7:]

    def backward(s, grads):
        out = spectral_back_call(
            plan, blocks, size, grads, forward[s][2:6], lat, lat_t, m1t, m2t
        )
        spectral.append(out)
        return out[0]

    forward, feeds, spectral, band_parts, grads = [], [], [], [], {}
    sent = first_call(plan, 0, 1, tokens, *vectors[:2])[0].reshape(spread)
    others, spectra = first_call(
        plan, 1, samples - 1, tokens, *vectors[:2], [(sent, 0)], next(ids)
    )
    others = others.reshape(spread)
    (spectra,) = spectral_forward(spectra, [(others, 0)])
    (back,) = spectral_forward(spectra, [(forward[0][0], None)])
    for s in range(samples):
        sums = (feeds[-1][3], feeds[-1][4]) if s else None
        kinds, passengers = [], []
        if s + 1 < samples:
            kinds.append("back")
            passengers.append((forward[s + 1][0], None))
        if s + 2 < samples:
            kinds.append("spectra")
            passengers.append((others, s + 1))
        if s >= 1:
            kinds.append("grads")
            passengers.append((feeds[s - 1][1].reshape(grouped), None))
        kinds.append("band")
        passengers.append((forward[s][1], None))
        arrived = dict(zip(kinds, feed(s, back, sums, passengers)))
        band_parts.append(arrived["band"])
        back = arrived.get("back")
        if s + 2 < samples:
            spectral_forward(arrived["spectra"])
        if s >= 1:
            grads[s - 1] = arrived["grads"]
    grads[samples - 1] = exchange(feeds[-1][1].reshape(grouped))
    grads[0] = lax.optimization_barrier((grads[0], feeds[-1][6]))[0]
    lon_grads = [exchange(backward(s, grads[s])) for s in range(samples)]

    tokens_grad, spectrum, finals = None, None, []
    for s in range(samples):
        tokens_grad, vec = last_call(
            plan,
            s,
            scales[s],
            tokens,
            feeds[s][2],
            lon_grads[s].reshape(listed),
            vectors[0],
            tokens_grad,
        )
        finals.append(vec)
        spectrum = band_call(plan, s, band_parts[s], spectrum)
    mixed = jnp.stack([f[0] for f in feeds])

    add = lambda parts: functools.reduce(jnp.add, parts)
    devices = lax.axis_size("batch") * n
    feed_vec = add([f[6] for f in feeds])
    block_grad = lambda i: add([b[i] for b in spectral]).reshape(2, blocks, size, size)
    large = lax.psum((feeds[-1][3], feeds[-1][4]), ("batch", "lat"))
    large = (large[0].astype(F32), large[1].astype(F32))
    zeros = jnp.sum(add([f[6] for f in forward]))
    small = [
        feed_vec[1],
        feed_vec[2],
        add([f[5] for f in feeds]),
        feed_vec[0],
        narrow_bias(add([b[3] for b in spectral]), blocks, size),
        narrow_bias(add([b[4] for b in spectral]), blocks, size),
        zeros.reshape(1),
    ]
    blocky = [block_grad(1), block_grad(2)]
    packed = [pack(devices, blocky, BF, 16), pack(devices, small, F32, 8)]
    packed = block_sum(devices, n, packed, next(ids))
    blocky = unpack(packed[0], blocky)
    small = unpack(packed[1], small)
    last_vec = whole_sum(devices, n, add(finals), next(ids))
    zero_fraction = small[6][0] / (lax.axis_size("batch") * samples * H * plan.kw * 2 * channels)
    return (
        mixed,
        spectrum.transpose(0, 1, 3, 2, 4),
        tokens_grad,
        last_vec[0],
        last_vec[1],
        blocky[0],
        small[4],
        blocky[1],
        small[5],
        small[0],
        small[1],
        large[0],
        small[2].reshape(-1),
        large[1],
        small[3],
        zero_fraction,
    )


def solution(mesh):
    rows = P("batch", "lat", None, None)
    in_specs = (rows, rows, P("batch")) + (P(),) * 14
    out_specs = (rows, P("batch", "lat", None, None, None), rows) + (P(),) * 13
    lanes = mesh.shape["lat"]

    def run(tokens, cotangent, *rest):
        row_slots = tokens.shape[1] // lanes
        return jax.shard_map(
            functools.partial(on_device, row_slots + 1),
            mesh=mesh,
            in_specs=in_specs,
            out_specs=out_specs,
            check_vma=False,
        )(tokens, cotangent, *rest)

    return run
```

```python
import functools
import itertools
import math

import jax
import jax.numpy as jnp
import numpy as np
from jax import lax
from jax.experimental import pallas as pl
from jax.experimental.pallas import tpu as pltpu
from jax.sharding import PartitionSpec as P

H = 90
HP = 96

NORM_EPS = 1e-06
SHRINK_LAMBDA = 0.01
SHRINK_SOFTNESS = 0.1
INV_ROOT_TAU = 1.0 / math.sqrt(2.0 * math.pi)
BF = jnp.bfloat16
F32 = jnp.float32
VMEM_BYTES = 64 * 1024 * 1024


def dot(a, b):
    return jnp.dot(a, b, preferred_element_type=F32)


def dot_nt(a, b):
    return lax.dot_general(a, b, (((1,), (1,)), ((), ())), preferred_element_type=F32)


def dot_tn(a, b):
    return lax.dot_general(a, b, (((0,), (0,)), ((), ())), preferred_element_type=F32)


def dot_table(table_ref, x):
    return dot(table_ref[0], x) + dot(table_ref[1], x)


def two_parts(table):
    high = table.astype(BF)
    return high, (table - high.astype(table.dtype)).astype(BF)


def norm_parts(x):
    mean = jnp.mean(x, -1, keepdims=True)
    centred = x - mean
    rstd = lax.rsqrt(jnp.mean(centred * centred, -1, keepdims=True) + NORM_EPS)
    return centred * rstd, rstd


def norm_back(grad, unit, rstd, gain):
    e = grad * gain
    return rstd * (
        e - jnp.mean(e, -1, keepdims=True) - unit * jnp.mean(e * unit, -1, keepdims=True)
    )


def gauss_parts(v):
    d = 1.0 + jnp.abs(v) * (0.3275911 / math.sqrt(2.0))
    t = pl.reciprocal(d, approx=True)
    e = jnp.exp2(v * v * (-0.5 * math.log2(math.e)))
    poly = 1.061405429 * 0.5
    for c in (-1.453152027, 1.421413741, -0.284496736, 0.254829592):
        poly = poly * t + 0.5 * c
    tail = poly * t * e
    cdf = jnp.where(v >= 0.0, 1.0 - tail, tail)
    return cdf, v * e * INV_ROOT_TAU


def gelu_both(v):
    cdf, slope_part = gauss_parts(v)
    return v * cdf, cdf + slope_part


def shrink_both(u):
    a = jnp.maximum(jnp.abs(u) - SHRINK_LAMBDA, 0.0)
    d = a + SHRINK_SOFTNESS
    t = pl.reciprocal(d, approx=True)
    t = t * (2.0 - d * t)
    size = a * a * t
    value = jnp.where(u >= 0.0, size, -size)
    slope = a * (a + 2.0 * SHRINK_SOFTNESS) * (t * t)
    return value, slope


class Plan:
    def __init__(self, n, samples, rows, width, channels, bands):
        self.n, self.s, self.r, self.w, self.d, self.mb = n, samples, rows, width, channels, bands
        self.kw = width // 2 + 1
        self.kk = -(-self.kw // n)
        self.kp = self.kk + self.kk % 2
        self.q = self.kp // 2
        self.rp = -(-rows // 4) * 4
        self.t = 4 * self.rp
        self.pairs = n * self.q
        self.ki = n * self.kp * 2
        self.rb = max(b for b in (4, 3, 2, 1) if rows % b == 0)
        self.chunks = rows // self.rb
        self.flat = self.rb * width
        self.flatp = max(-(-self.flat // 256) * 256, channels)
        self.splits = max(b for b in (3, 2, 1) if self.flat % (16 * b) == 0 or b == 1)
        j = np.arange(n)[:, None]
        t = np.arange(self.kp)[None, :]
        self.k_index = (j * self.kk + t).astype(np.int64)
        self.k_valid = (t < self.kk) & (self.k_index < self.kw)
        k = np.where(self.k_valid, self.k_index, 0).reshape(-1)
        ok = self.k_valid.reshape(-1).astype(np.float64)
        angle = 2.0 * np.pi * ((k[:, None] * np.arange(width)[None, :]) % width) / width
        scale = ok[:, None] / math.sqrt(width)
        fwd = np.stack([np.cos(angle) * scale, -np.sin(angle) * scale], 1).reshape(self.ki, width)
        factor = np.where((k == 0) | (2 * k == width), 1.0, 2.0)[:, None, None]
        both = (fwd.reshape(-1, 2, width) * factor).reshape(self.ki, width)
        self.lon = np.stack(two_parts(fwd))
        self.lon_both = np.stack(two_parts(both))
        self.lon_t = np.stack(two_parts(np.ascontiguousarray(fwd.T)))
        self.lon_both_t = np.stack(two_parts(np.ascontiguousarray(both.T)))
        perm = np.zeros((16, self.rp, rows, 16))
        for a in range(16):
            for r in range(rows):
                perm[a, r, r, a] = 1.0
        self.perm = perm.reshape(16 * self.rp, rows * 16).astype(BF)
        self.perm_t = np.ascontiguousarray(self.perm.T)


class Tables:
    def __init__(self, plan, blocks, size):
        self.plan, self.blocks, self.size = plan, blocks, size
        n, rp, mb = plan.n, plan.rp, plan.mb
        kh, h = np.arange(HP)[:, None], np.arange(HP)[None, :]
        angle = 2.0 * np.pi * (kh * h % H) / H
        weight = ((kh < H) & (h < H)) / math.sqrt(H)
        cosine, sine = np.cos(angle) * weight, np.sin(angle) * weight
        part = np.block([[cosine, sine], [-sine, cosine]])
        self.base = np.stack(two_parts(np.kron(np.eye(2), part)))
        col = np.arange(n * 4 * rp)
        group, step = col // rp % 4, col % rp
        self.columns = np.stack([col // (4 * rp), group * HP + step, step]).astype(np.int32)
        line = np.arange(n * 4 * mb)
        group, step = line // mb % 4, line % mb
        lines = np.stack([line // (4 * mb), group * HP + step, step]).astype(np.int32)
        self.lines = lines[:, :, None]
        half = blocks // 2
        spots = np.zeros((half, size, half * size))
        for i in range(half):
            spots[i, :, i * size : (i + 1) * size] = np.eye(size)
        self.spots = spots.astype(BF)
        wide = 4 * HP
        d = plan.d
        shapes = [(2, wide, n * 4 * rp), (2, n * 4 * rp, wide), (n * 4 * mb, wide)] + [(2, d, d)] * 4
        self.shapes = [jax.ShapeDtypeStruct(x, BF) for x in shapes]

    def operands(self, row_count, band_count, spec_w1, spec_w2):
        return [
            row_count,
            band_count,
            spec_w1,
            spec_w2,
            self.base,
            self.columns[:, None, :],
            self.lines,
            self.spots,
        ]

    def in_specs(self):
        weight = (2, self.blocks, self.size, self.size)
        shapes = [weight, weight, self.base.shape, (3, 1, self.columns.shape[1])]
        shapes += [self.lines.shape, self.spots.shape]
        return [SMEM, SMEM] + [whole(x) for x in shapes]

    def out_specs(self):
        return [whole(x.shape) for x in self.shapes]

    def build(self, ins, outs):
        rows_ref, bands_ref, w1_ref, w2_ref, base_ref, col_ref, line_ref, spot_ref = ins
        lat_ref, lat_t_ref, slot_ref, m1_ref, m2_ref, m1t_ref, m2t_ref = outs
        n = self.plan.n

        def spread(counts_ref, owner):
            first = jnp.zeros(owner.shape, jnp.int32)
            held = jnp.zeros(owner.shape, jnp.int32)
            start = jnp.int32(0)
            for j in range(n):
                count = counts_ref[j]
                first = jnp.where(owner == j, start, first)
                held = jnp.where(owner == j, count, held)
                start = start + count
            return first, held

        first, held = spread(rows_ref, col_ref[0])
        target = jnp.where(col_ref[2] < held, col_ref[1] + first, -1)
        pick = lax.broadcasted_iota(jnp.int32, (4 * HP, target.shape[1]), 0) == target
        pick = jnp.where(pick, 1.0, 0.0).astype(BF)
        for part in range(2):
            full = dot(base_ref[part], pick)
            lat_ref[part] = full.astype(BF)
            lat_t_ref[part] = full.T.astype(BF)
        first, held = spread(bands_ref, line_ref[0])
        target = jnp.where(line_ref[2] < held, line_ref[1] + first, -1)
        pick = lax.broadcasted_iota(jnp.int32, (target.shape[0], 4 * HP), 1) == target
        slot_ref[...] = jnp.where(pick, 1.0, 0.0).astype(BF)
        half, size = self.blocks // 2, self.size
        mid = half * size
        for w_ref, m_ref, mt_ref in ((w1_ref, m1_ref, m1t_ref), (w2_ref, m2_ref, m2t_ref)):
            for g in range(2):
                for i in range(half):
                    low = slice(i * size, (i + 1) * size)
                    high = slice(mid + i * size, mid + (i + 1) * size)
                    re, im = w_ref[0, g * half + i], w_ref[1, g * half + i]
                    for ref, place_in, sign in ((m_ref, dot, 1.0), (mt_ref, dot_tn, -1.0)):
                        real = place_in(re, spot_ref[i]).astype(BF)
                        imag = place_in(im, spot_ref[i]) * sign
                        ref[g, low, :mid] = real
                        ref[g, high, mid:] = real
                        ref[g, low, mid:] = imag.astype(BF)
                        ref[g, high, :mid] = (-imag).astype(BF)


def wide_bias(bias):
    return bias.reshape(2, 2, -1).transpose(1, 0, 2).reshape(2, 1, -1)


def narrow_bias(wide, blocks, size):
    return wide.reshape(2, 2, -1).transpose(1, 0, 2).reshape(2, blocks, size)


def whole(shape):
    zeros = (0,) * len(shape)
    return pl.BlockSpec(shape, lambda *_: zeros)


def whole_once(shape):
    zeros = (0,) * len(shape)
    return pl.BlockSpec(shape, lambda *_: zeros, pipeline_mode=pl.Buffered(1))


SMEM = pl.BlockSpec(memory_space=pltpu.SMEM)
ANY = pl.BlockSpec(memory_space=pl.ANY)


def params(collective_id=None):
    if collective_id is None:
        return pltpu.CompilerParams(
            dimension_semantics=("arbitrary",), vmem_limit_bytes=VMEM_BYTES
        )
    return pltpu.CompilerParams(
        dimension_semantics=("arbitrary",),
        vmem_limit_bytes=VMEM_BYTES,
        collective_id=collective_id,
        has_side_effects=True,
    )


def ride_copy(n, me, src, dst, send, recv, e, step):
    peer = lax.rem(me + step, n)
    return pltpu.make_async_remote_copy(
        src_ref=src.at[peer],
        dst_ref=dst.at[me],
        send_sem=send.at[e, step],
        recv_sem=recv.at[e, step],
        device_id={"lat": peer},
        device_id_type=pl.DeviceIdType.MESH,
    )


def ride_arrival(n, me, src, dst, send, recv, e, step):
    peer = lax.rem(me + n - step, n)
    return pltpu.make_async_remote_copy(
        src_ref=src.at[peer],
        dst_ref=dst.at[peer],
        send_sem=send.at[e, step],
        recv_sem=recv.at[e, step],
        device_id={"lat": peer},
        device_id_type=pl.DeviceIdType.MESH,
    )


def ride_start(n, srcs, dsts, send, recv, own):
    me = lax.axis_index("lat")
    barrier = pltpu.get_barrier_semaphore()
    for step in range(1, n):
        pl.semaphore_signal(
            barrier,
            inc=1,
            device_id={"lat": lax.rem(me + step, n)},
            device_id_type=pl.DeviceIdType.MESH,
        )
    pl.semaphore_wait(barrier, n - 1)
    for e, (src, dst) in enumerate(zip(srcs, dsts)):
        for step in range(1, n):
            ride_copy(n, me, src, dst, send, recv, e, step).start()
        pltpu.make_async_copy(src.at[me], dst.at[me], own.at[e]).start()


def ride_wait(n, srcs, dsts, send, recv, own):
    me = lax.axis_index("lat")
    for e, (src, dst) in enumerate(zip(srcs, dsts)):
        pltpu.make_async_copy(src.at[me], dst.at[me], own.at[e]).wait()
        for step in range(1, n):
            ride_copy(n, me, src, dst, send, recv, e, step).wait_send()
            ride_arrival(n, me, src, dst, send, recv, e, step).wait_recv()


def cost(flops, size):
    return pl.CostEstimate(flops=int(flops), bytes_accessed=int(size), transcendentals=0)


def interleave(plan, perm_ref, rows_ref, out_ref):
    def body(c, carry):
        at = pl.multiple_of(c * 16, 16)
        block = rows_ref[:, pl.ds(at, 16), :].reshape(plan.r * 16, plan.d)
        mixed = dot(perm_ref[...], block).astype(BF)
        out_ref[pl.ds(c * 4, 4)] = mixed.reshape(4, plan.t, plan.d)
        return carry

    lax.fori_loop(0, plan.ki // 16, body, 0)


def deinterleave(plan, perm_t_ref, in_ref, rows_ref):
    def body(c, carry):
        at = pl.multiple_of(c * 16, 16)
        block = in_ref[pl.ds(c * 4, 4)].reshape(4 * plan.t, plan.d)
        rows = dot(perm_t_ref[...], block).astype(BF)
        rows_ref[:, pl.ds(at, 16), :] = rows.reshape(plan.r, 16, plan.d)
        return carry

    lax.fori_loop(0, plan.ki // 16, body, 0)


def interleave_out(plan, perm_ref, rows_ref, ring, sem, out_ref):
    def copy(c):
        return pltpu.make_async_copy(
            ring.at[lax.rem(c, 2)], out_ref.at[pl.ds(c * 4, 4)], sem.at[lax.rem(c, 2)]
        )

    def body(c, carry):
        @pl.when(c >= 2)
        def _():
            copy(c - 2).wait()

        at = pl.multiple_of(c * 16, 16)
        block = rows_ref[:, pl.ds(at, 16), :].reshape(plan.r * 16, plan.d)
        mixed = dot(perm_ref[...], block).astype(BF)
        ring[lax.rem(c, 2)] = mixed.reshape(4, plan.t, plan.d)
        copy(c).start()
        return carry

    lax.fori_loop(0, plan.ki // 16, body, 0)
    return [copy(plan.ki // 16 - 2), copy(plan.ki // 16 - 1)]


def ring_load(plan, in_ref, ring, sem, c):
    return pltpu.make_async_copy(
        in_ref.at[pl.ds(c * 4, 4)], ring.at[lax.rem(c, 2)], sem.at[lax.rem(c, 2)]
    )


def deinterleave_in(plan, perm_t_ref, in_ref, ring, sem, rows_ref):
    steps = plan.ki // 16

    def body(c, carry):
        ring_load(plan, in_ref, ring, sem, c).wait()
        at = pl.multiple_of(c * 16, 16)
        block = ring[lax.rem(c, 2)].reshape(4 * plan.t, plan.d)
        rows = dot(perm_t_ref[...], block).astype(BF)
        rows_ref[:, pl.ds(at, 16), :] = rows.reshape(plan.r, 16, plan.d)

        @pl.when(c + 2 < steps)
        def _():
            ring_load(plan, in_ref, ring, sem, c + 2).start()

        return carry

    lax.fori_loop(0, steps, body, 0)


class Riders:
    def __init__(self, plan, passengers):
        self.n = plan.n
        self.arrays = [a for a, _ in passengers]
        self.leads = [lead for _, lead in passengers]
        self.count = len(passengers)

    def shapes(self):
        return [
            jax.ShapeDtypeStruct(a.shape if lead is None else a.shape[1:], a.dtype)
            for a, lead in zip(self.arrays, self.leads)
        ]

    def specs(self):
        return [ANY] * self.count

    def scratch(self):
        if not self.count:
            return []
        dma = pltpu.SemaphoreType.DMA
        return [dma((self.count, self.n)), dma((self.count, self.n)), dma((self.count,))]

    def bind(self, srcs, dsts, sems):
        srcs = [r if lead is None else r.at[lead] for r, lead in zip(srcs, self.leads)]
        return (self.n, srcs, dsts) + tuple(sems)


def first_kernel(plan, riders, tables, tok_ref, gain_ref, bias_ref, lon_ref, perm_ref, *rest):
    e = riders.count
    t_in = 0 if tables is None else 8
    t_out = 0 if tables is None else 7
    t_ins, rest = rest[:t_in], rest[t_in:]
    srcs, rest = rest[:e], rest[e:]
    out_ref, rest = rest[0], rest[1:]
    t_outs, rest = rest[:t_out], rest[t_out:]
    dsts, rows_ref, sems = rest[:e], rest[e], rest[e + 1 :]
    i = pl.program_id(0)
    c = lax.rem(i, plan.chunks)
    if e:
        ride = riders.bind(srcs, dsts, sems)

        @pl.when(i == 0)
        def _():
            ride_start(*ride)

    for u in range(plan.rb):
        unit, _ = norm_parts(tok_ref[0, u].astype(F32))
        normed = (unit * gain_ref[...] + bias_ref[...]).astype(BF)
        rows_ref[c * plan.rb + u] = dot_table(lon_ref, normed).astype(BF)

    @pl.when(c == plan.chunks - 1)
    def _():
        interleave(plan, perm_ref, rows_ref, out_ref.at[0])

    @pl.when(i == pl.num_programs(0) - 1)
    def _():
        if tables is not None:
            tables.build(t_ins, t_outs)
        if e:
            ride_wait(*ride)


def row_block(plan, s):
    return pl.BlockSpec((1, plan.rb, plan.w, plan.d), lambda i: (s, i, 0, 0))


def own_block(plan):
    return pl.BlockSpec((plan.rb, plan.w, plan.d), lambda i: (i, 0, 0))


def first_call(
    plan, start, count, tokens, gain, bias, passengers=(), collective_id=None, tables=None, extra=()
):
    shape = (plan.pairs, plan.t, plan.d)
    chunks = plan.chunks
    riders = Riders(plan, passengers)
    return pl.pallas_call(
        functools.partial(first_kernel, plan, riders, tables),
        grid=(count * chunks,),
        in_specs=[
            pl.BlockSpec(
                (1, plan.rb, plan.w, plan.d),
                lambda i: (start + i // chunks, lax.rem(i, chunks), 0, 0),
            ),
            whole((1, plan.d)),
            whole((1, plan.d)),
            whole((2, plan.ki, plan.w)),
            whole(plan.perm.shape),
        ]
        + (tables.in_specs() if tables else [])
        + riders.specs(),
        out_specs=[pl.BlockSpec((1,) + shape, lambda i: (i // chunks, 0, 0, 0))]
        + (tables.out_specs() if tables else [])
        + riders.specs(),
        out_shape=[jax.ShapeDtypeStruct((count,) + shape, BF)]
        + (tables.shapes if tables else [])
        + riders.shapes(),
        scratch_shapes=[pltpu.VMEM((plan.r, plan.ki, plan.d), BF)] + riders.scratch(),
        compiler_params=params(collective_id),
        cost_estimate=cost(9e9 * count, 8e6 * count),
        name="lon_forward",
    )(tokens, gain, bias, plan.lon, plan.perm, *extra, *riders.arrays)


def spectral_kernel(
    plan,
    riders,
    valid_ref,
    in_ref,
    lat_ref,
    lat_t_ref,
    slot_ref,
    m1_ref,
    b1_ref,
    m2_ref,
    b2_ref,
    *rest,
):
    e = riders.count
    srcs, rest = rest[:e], rest[e:]
    back_ref, band_ref, spec_ref, hid_ref, slope1_ref, slope2_ref, zero_ref = rest[:7]
    dsts, shr_ref, sems = rest[7 : 7 + e], rest[7 + e], rest[8 + e :]
    q = pl.program_id(0)
    half = plan.d // 2
    if e:
        ride = riders.bind(srcs, dsts, sems)

        @pl.when(q == 0)
        def _():
            ride_start(*ride)

    @pl.when(q == 0)
    def _():
        zero_ref[...] = jnp.zeros_like(zero_ref)

    x = in_ref[:, 0].reshape(plan.n * plan.t, plan.d)
    spec = dot_table(lat_ref, x).astype(BF)
    ok = (lax.broadcasted_iota(jnp.int32, (HP, 1), 0) < H).astype(F32)
    for g in range(2):
        lanes = slice(g * half, (g + 1) * half)
        for a in range(2):
            top = a * 2 * HP
            spec_ref[0, g, a * HP : (a + 1) * HP, :half] = spec[top : top + HP, lanes]
            spec_ref[0, g, a * HP : (a + 1) * HP, half:] = spec[top + HP : top + 2 * HP, lanes]
        u1 = dot(spec_ref[0, g], m1_ref[g]) + b1_ref[g]
        hidden, slope = gelu_both(u1)
        hid_ref[0, g] = hidden.astype(BF)
        slope1_ref[0, g] = slope.astype(BF)
        u2 = dot(hid_ref[0, g], m2_ref[g]) + b2_ref[g]
        small = (jnp.abs(u2) <= SHRINK_LAMBDA).astype(F32)
        for a in range(2):
            part = small[a * HP : (a + 1) * HP] * ok
            zero_ref[...] += jnp.sum(part, 0, keepdims=True) * valid_ref[q * 2 + a]
        value, slope = shrink_both(u2)
        slope2_ref[0, g] = slope.astype(BF)
        value = value.astype(BF)
        for a in range(2):
            top = a * 2 * HP
            shr_ref[top : top + HP, lanes] = value[a * HP : (a + 1) * HP, :half]
            shr_ref[top + HP : top + 2 * HP, lanes] = value[a * HP : (a + 1) * HP, half:]
    shrunk = shr_ref[...]
    back_ref[:, 0] = dot_table(lat_t_ref, shrunk).astype(BF).reshape(plan.n, plan.t, plan.d)
    band = dot(slot_ref[...], shrunk).astype(BF)
    rows = 4 * plan.mb
    for j in range(plan.n):
        band_ref[j, 0] = band[j * rows : (j + 1) * rows]
    if e:

        @pl.when(q == plan.q - 1)
        def _():
            ride_wait(*ride)


def pair_block(plan, rows):
    return pl.BlockSpec((plan.n, 1, rows, plan.d), lambda q: (0, q, 0, 0))


def spectral_call(
    plan, valid, received, lat, lat_t, slots, m1, b1, m2, b2, passengers=(), collective_id=None
):
    riders = Riders(plan, passengers)
    kept = (plan.q, 2, 2 * HP, plan.d)
    kept_spec = pl.BlockSpec((1, 2, 2 * HP, plan.d), lambda q: (q, 0, 0, 0))
    kept_shape = jax.ShapeDtypeStruct(kept, BF)
    rows = 4 * plan.mb
    return pl.pallas_call(
        functools.partial(spectral_kernel, plan, riders),
        grid=(plan.q,),
        in_specs=[
            SMEM,
            pair_block(plan, plan.t),
            whole(lat.shape),
            whole(lat_t.shape),
            whole(slots.shape),
            whole(m1.shape),
            whole(b1.shape),
            whole(m2.shape),
            whole(b2.shape),
        ]
        + riders.specs(),
        out_specs=[
            pair_block(plan, plan.t),
            pair_block(plan, rows),
            kept_spec,
            kept_spec,
            kept_spec,
            kept_spec,
            whole((1, plan.d)),
        ]
        + riders.specs(),
        out_shape=[
            jax.ShapeDtypeStruct((plan.n, plan.q, plan.t, plan.d), BF),
            jax.ShapeDtypeStruct((plan.n, plan.q, rows, plan.d), BF),
            kept_shape,
            kept_shape,
            kept_shape,
            kept_shape,
            jax.ShapeDtypeStruct((1, plan.d), F32),
        ]
        + riders.shapes(),
        scratch_shapes=[pltpu.VMEM((4 * HP, plan.d), BF)] + riders.scratch(),
        compiler_params=params(collective_id),
        cost_estimate=cost(20e9, 25e6),
        name="spectral_forward",
    )(valid, received, lat, lat_t, slots, m1, b1, m2, b2, *riders.arrays)


def feed_kernel(
    plan,
    first,
    final,
    riders,
    tiles,
    scale_ref,
    tok_ref,
    cot_ref,
    recv_ref,
    gain1_ref,
    bias1_ref,
    gain2_ref,
    bias2_ref,
    lon_t_ref,
    lon_ref,
    perm_ref,
    perm_t_ref,
    w1_ref,
    b1_ref,
    w2_ref,
    b2_ref,
    *rest,
):
    e = riders.count
    srcs, rest = rest[:e], rest[e:]
    if first:
        in1_ref = in2_ref = None
    else:
        in1_ref, in2_ref = rest[:2]
        rest = rest[2:]
    mixed_ref, send_ref, gx_ref, out1_ref, out2_ref, db1_ref, vec_ref = rest[:7]
    dsts, rest = rest[7 : 7 + e], rest[7 + e :]
    (
        dw1,
        dw2,
        ring,
        rows_ref,
        x1_ref,
        xn,
        xn_t,
        gm,
        gm_t,
        act_a,
        gz_a,
        act_b,
        gz_b,
        down,
        up,
        sem,
        ring_sem,
        *ride_sems,
    ) = rest
    i = pl.program_id(0)
    last = plan.chunks - 1
    tile = act_a.shape[1]
    flat = plan.flat
    ride = riders.bind(srcs, dsts, ride_sems)

    @pl.when(i == 0)
    def _():
        for c in range(2):
            ring_load(plan, recv_ref, ring, ring_sem, c).start()
        if not first:
            pltpu.make_async_copy(in1_ref, dw1, sem.at[1]).start()
            pltpu.make_async_copy(in2_ref, dw2, sem.at[2]).start()
        ride_start(*ride)
        if first:
            dw1[...] = jnp.zeros_like(dw1)
            dw2[...] = jnp.zeros_like(dw2)
        db1_ref[...] = jnp.zeros_like(db1_ref)
        vec_ref[...] = jnp.zeros_like(vec_ref)
        if plan.flatp > flat:
            pad = jnp.zeros((plan.flatp - flat, tile), BF)
            for ref in (act_a, gz_a, act_b, gz_b):
                ref[flat:, :] = pad
            pad = jnp.zeros((plan.flatp - flat, plan.d), F32)
            down[flat:, :] = pad
            up[flat:, :] = pad
        deinterleave_in(plan, perm_t_ref, recv_ref, ring, ring_sem, rows_ref)

    for u in range(plan.rb):
        span = slice(u * plan.w, (u + 1) * plan.w)
        x = tok_ref[0, u].astype(F32)
        unit, _ = norm_parts(x)
        filtered = dot_table(lon_t_ref, rows_ref[i * plan.rb + u])
        x1 = x + filtered + (unit * gain1_ref[...] + bias1_ref[...])
        x1_ref[u] = x1
        unit, _ = norm_parts(x1)
        down[span, :] = unit * gain2_ref[...] + bias2_ref[...]
        up[span, :] = cot_ref[0, u].astype(F32) * scale_ref[i * plan.rb + u]
    normed = down[...].astype(BF)
    xn[...] = normed[:flat]
    xn_t[...] = normed.T
    grads = up[...].astype(BF)
    gm[...] = grads[:flat]
    gm_t[...] = grads.T
    vec_ref[0:1] += jnp.sum(grads.astype(F32), 0, keepdims=True)
    down[...] = jnp.zeros_like(down)
    up[...] = jnp.zeros_like(up)

    if not first:

        @pl.when(i == 0)
        def _():
            pltpu.make_async_copy(in1_ref, dw1, sem.at[1]).wait()
            pltpu.make_async_copy(in2_ref, dw2, sem.at[2]).wait()

    def columns(t):
        return pl.ds(pl.multiple_of(t * tile, tile), tile)

    step = flat // plan.splits

    def body(t, carry):
        cols = columns(t)
        opened = {}

        def enter(b):
            span = slice(b * step, (b + 1) * step)
            z = dot(xn[span, :], w1_ref[:, cols]) + b1_ref[:, cols]
            opened[b] = (z, dot_nt(gm[span, :], w2_ref[cols, :]))

        def middle(b):
            span = slice(b * step, (b + 1) * step)
            z, ga = opened.pop(b)
            hidden, slope = gelu_both(z)
            grad = ga * slope
            act_a[span, :] = hidden.astype(BF)
            gz_a[span, :] = grad.astype(BF)
            db1_ref[:, cols] += jnp.sum(grad, 0, keepdims=True)

        def leave(b):
            span = slice(b * step, (b + 1) * step)
            down[span, :] += dot(act_a[span, :], w2_ref[cols, :])
            up[span, :] += dot_nt(gz_a[span, :], w1_ref[:, cols])

        for b in range(plan.splits + 2):
            if b < plan.splits:
                enter(b)
            if 1 <= b <= plan.splits:
                middle(b - 1)
            if b >= 2:
                leave(b - 2)
        dw1[:, cols] += dot(xn_t[...], gz_a[...])
        dw2[:, cols] += dot(gm_t[...], act_a[...])
        return carry

    lax.fori_loop(0, tiles, body, 0)

    if not final:

        @pl.when(i == last)
        def _():
            pltpu.make_async_copy(dw1, out1_ref, sem.at[1]).start()
            pltpu.make_async_copy(dw2, out2_ref, sem.at[2]).start()

    for u in range(plan.rb):
        span = slice(u * plan.w, (u + 1) * plan.w)
        x1 = x1_ref[u]
        scale = scale_ref[i * plan.rb + u]
        keep = jnp.where(scale > 0.0, 1.0, 0.0)
        mixed_ref[u] = ((x1 + down[span, :] + b2_ref[...]) * keep).astype(BF)
        unit, rstd = norm_parts(x1)
        grad = up[span, :]
        vec_ref[1:2] += jnp.sum(grad * unit, 0, keepdims=True)
        vec_ref[2:3] += jnp.sum(grad, 0, keepdims=True)
        gx = cot_ref[0, u].astype(F32) * scale + norm_back(grad, unit, rstd, gain2_ref[...])
        gx_ref[u] = gx.astype(gx_ref.dtype)
        rows_ref[i * plan.rb + u] = dot_table(lon_ref, gx.astype(BF)).astype(BF)

    if plan.flatp > flat:
        down[flat:, :] = jnp.zeros((plan.flatp - flat, plan.d), F32)
        up[flat:, :] = jnp.zeros((plan.flatp - flat, plan.d), F32)

    @pl.when(i == last)
    def _():
        stores = interleave_out(plan, perm_ref, rows_ref, ring, ring_sem, send_ref)
        if final:
            pending = {}
            for t in range(tiles):
                cols = slice(t * tile, (t + 1) * tile)
                side = t % 2
                for copy in pending.pop(side, ()):
                    copy.wait()
                one, two = ((act_a, gz_a), (act_b, gz_b))[side]
                one[: plan.d, :] = dw1[:, cols].astype(BF)
                xn_part = (xn_t, gm_t)[side]
                xn_part[:tile, : plan.d] = dw2[:, cols].astype(BF).T
                copies = (
                    pltpu.make_async_copy(one.at[: plan.d], out1_ref.at[:, cols], sem.at[1 + side]),
                    pltpu.make_async_copy(
                        xn_part.at[:tile, : plan.d], out2_ref.at[cols], sem.at[3 + side]
                    ),
                )
                for copy in copies:
                    copy.start()
                pending[side] = copies
            for copies in pending.values():
                for copy in copies:
                    copy.wait()
        else:
            pltpu.make_async_copy(dw1, out1_ref, sem.at[1]).wait()
            pltpu.make_async_copy(dw2, out2_ref, sem.at[2]).wait()
        for store in stores:
            store.wait()
        ride_wait(*ride)


def feed_call(
    plan, s, scales, tokens, cotangent, received, vectors, w1, b1, w2, b2, sums, final, passengers,
    collective_id
):
    gain1, bias1, gain2, bias2 = vectors
    first = sums is None
    ff = w1.shape[1]
    tile = 512
    d, flat = plan.d, plan.flat
    flatp = plan.flatp
    shape = (plan.pairs, plan.t, d)
    vec = whole((1, d))
    riders = Riders(plan, passengers)
    in_specs = [
        SMEM,
        row_block(plan, s),
        row_block(plan, s),
        ANY,
        vec,
        vec,
        vec,
        vec,
        whole((2, plan.w, plan.ki)),
        whole((2, plan.ki, plan.w)),
        whole(plan.perm.shape),
        whole(plan.perm_t.shape),
        whole_once((d, ff)),
        whole((1, ff)),
        whole_once((ff, d)),
        vec,
    ] + riders.specs()
    operands = [
        scales,
        tokens,
        cotangent,
        received,
        gain1,
        bias1,
        gain2,
        bias2,
        plan.lon_both_t,
        plan.lon_both,
        plan.perm,
        plan.perm_t,
        w1,
        b1,
        w2,
        b2,
        *riders.arrays,
    ]
    aliases = {}
    if not first:
        if not final:
            aliases = {len(operands): 3, len(operands) + 1: 4}
        in_specs += [ANY, ANY]
        operands += list(sums)
    if final:
        wides = [jax.ShapeDtypeStruct((d, ff), BF), jax.ShapeDtypeStruct((ff, d), BF)]
    else:
        wides = [jax.ShapeDtypeStruct((d, ff), F32)] * 2
    return pl.pallas_call(
        functools.partial(feed_kernel, plan, first, final, riders, ff // tile),
        grid=(plan.chunks,),
        in_specs=in_specs,
        out_specs=[
            own_block(plan),
            ANY,
            own_block(plan),
            ANY,
            ANY,
            whole((1, ff)),
            whole((8, d)),
        ]
        + riders.specs(),
        out_shape=[
            jax.ShapeDtypeStruct((plan.r, plan.w, d), BF),
            jax.ShapeDtypeStruct(shape, BF),
            jax.ShapeDtypeStruct((plan.r, plan.w, d), BF),
            *wides,
            jax.ShapeDtypeStruct((1, ff), F32),
            jax.ShapeDtypeStruct((8, d), F32),
        ]
        + riders.shapes(),
        scratch_shapes=[
            pltpu.VMEM((d, ff), F32),
            pltpu.VMEM((d, ff), F32),
            pltpu.VMEM((2, 4, plan.t, d), BF),
            pltpu.VMEM((plan.r, plan.ki, d), BF),
            pltpu.VMEM((plan.rb, plan.w, d), F32),
            pltpu.VMEM((flat, d), BF),
            pltpu.VMEM((d, flatp), BF),
            pltpu.VMEM((flat, d), BF),
            pltpu.VMEM((d, flatp), BF),
            pltpu.VMEM((flatp, tile), BF),
            pltpu.VMEM((flatp, tile), BF),
            pltpu.VMEM((flatp, tile), BF),
            pltpu.VMEM((flatp, tile), BF),
            pltpu.VMEM((flatp, d), F32),
            pltpu.VMEM((flatp, d), F32),
            pltpu.SemaphoreType.DMA((5,)),
            pltpu.SemaphoreType.DMA((2,)),
        ]
        + riders.scratch(),
        input_output_aliases=aliases,
        compiler_params=params(collective_id),
        cost_estimate=cost(70e9, 60e6),
        name="feed_forward",
    )(*operands)


def spectral_back_kernel(
    plan,
    riders,
    in_ref,
    spec_ref,
    hid_ref,
    slope1_ref,
    slope2_ref,
    lat_ref,
    lat_t_ref,
    m1t_ref,
    m2t_ref,
    *rest,
):
    e = riders.count
    srcs, rest = rest[:e], rest[e:]
    out_ref, dw1_ref, dw2_ref, db1_ref, db2_ref = rest[:5]
    dsts, rest = rest[5 : 5 + e], rest[5 + e :]
    dm1_ref, dm2_ref, gs_ref, gu_ref = rest[:4]
    q = pl.program_id(0)
    half = plan.d // 2
    if e:
        ride = riders.bind(srcs, dsts, rest[4:])

        @pl.when(q == 0)
        def _():
            ride_start(*ride)

    @pl.when(q == 0)
    def _():
        dm1_ref[...] = jnp.zeros_like(dm1_ref)
        dm2_ref[...] = jnp.zeros_like(dm2_ref)
        db1_ref[...] = jnp.zeros_like(db1_ref)
        db2_ref[...] = jnp.zeros_like(db2_ref)

    x = in_ref[:, 0].reshape(plan.n * plan.t, plan.d)
    grad = dot_table(lat_ref, x).astype(BF)
    for g in range(2):
        lanes = slice(g * half, (g + 1) * half)
        for a in range(2):
            top = a * 2 * HP
            gu_ref[a * HP : (a + 1) * HP, :half] = grad[top : top + HP, lanes]
            gu_ref[a * HP : (a + 1) * HP, half:] = grad[top + HP : top + 2 * HP, lanes]
        gu2 = gu_ref[...].astype(F32) * slope2_ref[0, g].astype(F32)
        db2_ref[g] += jnp.sum(gu2, 0, keepdims=True)
        gu2 = gu2.astype(BF)
        dm2_ref[g] += dot_tn(hid_ref[0, g], gu2)
        gu1 = (dot(gu2, m2t_ref[g]) * slope1_ref[0, g].astype(F32)).astype(BF)
        db1_ref[g] += jnp.sum(gu1.astype(F32), 0, keepdims=True)
        dm1_ref[g] += dot_tn(spec_ref[0, g], gu1)
        gs = dot(gu1, m1t_ref[g]).astype(BF)
        for a in range(2):
            top = a * 2 * HP
            gs_ref[top : top + HP, lanes] = gs[a * HP : (a + 1) * HP, :half]
            gs_ref[top + HP : top + 2 * HP, lanes] = gs[a * HP : (a + 1) * HP, half:]
    out_ref[:, 0] = dot_table(lat_t_ref, gs_ref[...]).astype(BF).reshape(plan.n, plan.t, plan.d)

    @pl.when(q == plan.q - 1)
    def _():
        blocks, size = dw1_ref.shape[2:4]
        for wide, narrow in ((dm1_ref, dw1_ref), (dm2_ref, dw2_ref)):
            for g in range(2):
                for b in range(blocks):
                    re = slice(b * size, (b + 1) * size)
                    im = slice(half + b * size, half + (b + 1) * size)
                    narrow[0, g, b] = wide[g, re, re] + wide[g, im, im]
                    narrow[1, g, b] = wide[g, re, im] - wide[g, im, re]
        if e:
            ride_wait(*ride)


def spectral_back_call(
    plan, blocks, size, received, kept, lat, lat_t, m1t, m2t, passengers=(), collective_id=None
):
    riders = Riders(plan, passengers)
    small = (2, 2, blocks // 2, size, size)
    kept_spec = pl.BlockSpec((1, 2, 2 * HP, plan.d), lambda q: (q, 0, 0, 0))
    wide = (2, plan.d, plan.d)
    thin = (2, 1, plan.d)
    return pl.pallas_call(
        functools.partial(spectral_back_kernel, plan, riders),
        grid=(plan.q,),
        in_specs=[pair_block(plan, plan.t)]
        + [kept_spec] * 4
        + [whole(lat.shape), whole(lat_t.shape), whole(wide), whole(wide)]
        + riders.specs(),
        out_specs=[
            pair_block(plan, plan.t),
            whole(small),
            whole(small),
            whole(thin),
            whole(thin),
        ]
        + riders.specs(),
        out_shape=[
            jax.ShapeDtypeStruct((plan.n, plan.q, plan.t, plan.d), BF),
            jax.ShapeDtypeStruct(small, F32),
            jax.ShapeDtypeStruct(small, F32),
            jax.ShapeDtypeStruct(thin, F32),
            jax.ShapeDtypeStruct(thin, F32),
        ]
        + riders.shapes(),
        scratch_shapes=[
            pltpu.VMEM(wide, F32),
            pltpu.VMEM(wide, F32),
            pltpu.VMEM((4 * HP, plan.d), BF),
            pltpu.VMEM((2 * HP, plan.d), BF),
        ]
        + riders.scratch(),
        compiler_params=params(collective_id),
        cost_estimate=cost(1e9, 1e6),
        name="spectral_backward",
    )(received, *kept, lat, lat_t, m1t, m2t, *riders.arrays)


def last_kernel(
    plan,
    scale_ref,
    tok_ref,
    gx_ref,
    in_ref,
    gain_ref,
    lon_t_ref,
    perm_t_ref,
    *rest,
):
    out_ref, vec_ref, rows_ref = rest[-3:]
    i = pl.program_id(0)

    @pl.when(i == 0)
    def _():
        vec_ref[...] = jnp.zeros_like(vec_ref)
        deinterleave(plan, perm_t_ref, in_ref, rows_ref)

    for u in range(plan.rb):
        keep = jnp.where(scale_ref[i * plan.rb + u] > 0.0, 1.0, 0.0)
        unit, rstd = norm_parts(tok_ref[0, u].astype(F32))
        gx = gx_ref[u].astype(F32)
        grad = gx + dot_table(lon_t_ref, rows_ref[i * plan.rb + u])
        vec_ref[0:1] += jnp.sum(grad * unit, 0, keepdims=True) * keep
        vec_ref[1:2] += jnp.sum(grad, 0, keepdims=True) * keep
        out_ref[0, u] = (gx + norm_back(grad, unit, rstd, gain_ref[...])) * keep


def last_call(plan, s, scales, tokens, gx, received, gain, earlier):
    operands = [scales, tokens, gx, received, gain, plan.lon_t, plan.perm_t]
    in_specs = [
        SMEM,
        row_block(plan, s),
        own_block(plan),
        whole((plan.pairs, plan.t, plan.d)),
        whole((1, plan.d)),
        whole((2, plan.w, plan.ki)),
        whole(plan.perm_t.shape),
    ]
    aliases = {}
    if earlier is not None:
        aliases = {len(operands): 0}
        operands.append(earlier)
        in_specs.append(ANY)
    return pl.pallas_call(
        functools.partial(last_kernel, plan),
        grid=(plan.chunks,),
        in_specs=in_specs,
        out_specs=[row_block(plan, s), whole((2, plan.d))],
        out_shape=[
            jax.ShapeDtypeStruct((plan.s, plan.r, plan.w, plan.d), F32),
            jax.ShapeDtypeStruct((2, plan.d), F32),
        ],
        scratch_shapes=[pltpu.VMEM((plan.r, plan.ki, plan.d), BF)],
        input_output_aliases=aliases,
        compiler_params=params(),
        cost_estimate=cost(1e9, 1e6),
        name="lon_backward",
    )(*operands)


def band_kernel(plan, in_ref, *rest):
    out_ref, tall = rest[-2:]
    mb = plan.mb
    height = 2 * plan.kw
    for src in range(plan.n):
        for t in range(plan.kk):
            k = src * plan.kk + t
            if k >= plan.kw:
                continue
            both = in_ref[src, t // 2].astype(F32)
            for p in range(2):
                at = ((t % 2) * 2 + p) * mb
                part = both[at : at + mb]
                for g in range(plan.d // 128):
                    tall[g, pl.ds(2 * k + p, mb, stride=height), :] = part[
                        :, g * 128 : (g + 1) * 128
                    ]
    for m in range(mb):
        for g in range(plan.d // 128):
            piece = tall[g, m * height : (m + 1) * height, :].astype(BF)
            out_ref[0, m, :, :, g * 128 : (g + 1) * 128] = piece.reshape(plan.kw, 2, 128)


def band_call(plan, s, received, earlier):
    shape = (plan.s, plan.mb, plan.kw, 2, plan.d)
    operands = [received]
    in_specs = [whole(received.shape)]
    aliases = {}
    if earlier is not None:
        aliases = {1: 0}
        operands.append(earlier)
        in_specs.append(ANY)
    return pl.pallas_call(
        functools.partial(band_kernel, plan),
        grid=(1,),
        in_specs=in_specs,
        out_specs=pl.BlockSpec((1,) + shape[1:], lambda i: (s, 0, 0, 0, 0)),
        out_shape=jax.ShapeDtypeStruct(shape, BF),
        scratch_shapes=[pltpu.VMEM((plan.d // 128, 2 * plan.mb * plan.kw, 128), F32)],
        input_output_aliases=aliases,
        compiler_params=params(),
        cost_estimate=cost(1e8, 1e6),
        name="band_output",
    )(*operands)


def every_peer(total, step_of):
    def body(step, carry):
        step_of(step)
        return carry

    lax.fori_loop(1, total, body, 0)


def place(lanes, index):
    return {"batch": index // lanes, "lat": lax.rem(index, lanes)}


def greet_all(total, lanes, me):
    barrier = pltpu.get_barrier_semaphore()

    def greet(step):
        pl.semaphore_signal(
            barrier,
            inc=1,
            device_id=place(lanes, lax.rem(me + step, total)),
            device_id_type=pl.DeviceIdType.MESH,
        )

    every_peer(total, greet)
    pl.semaphore_wait(barrier, total - 1)


def block_sum_kernel(total, lanes, xs, *rest):
    ins, outs, helds, sems = rest[:xs], rest[xs : 2 * xs], rest[2 * xs : 3 * xs], rest[3 * xs :]
    me = lax.axis_index("batch") * lanes + lax.axis_index("lat")
    greet_all(total, lanes, me)

    def part(a, step, peer):
        return pltpu.make_async_remote_copy(
            src_ref=ins[a].at[peer],
            dst_ref=helds[a].at[step],
            send_sem=sems[4 * a].at[step],
            recv_sem=sems[4 * a + 1].at[step],
            device_id=place(lanes, peer),
            device_id_type=pl.DeviceIdType.MESH,
        )

    def result(a, step, peer, slot):
        return pltpu.make_async_remote_copy(
            src_ref=outs[a].at[me],
            dst_ref=outs[a].at[slot],
            send_sem=sems[4 * a + 2].at[step],
            recv_sem=sems[4 * a + 3].at[step],
            device_id=place(lanes, peer),
            device_id_type=pl.DeviceIdType.MESH,
        )

    ahead = lambda step: lax.rem(me + step, total)
    behind = lambda step: lax.rem(me + total - step, total)
    for a in range(xs):
        every_peer(total, lambda step: part(a, step, ahead(step)).start())
    for a in range(xs):
        helds[a][0] = ins[a][me]
        every_peer(total, lambda step: part(a, step, behind(step)).wait_recv())
        outs[a][me] = jnp.sum(helds[a][...].astype(F32), 0).astype(outs[a].dtype)
        every_peer(total, lambda step: result(a, step, ahead(step), me).start())
    for a in range(xs):
        every_peer(total, lambda step: part(a, step, ahead(step)).wait_send())
        every_peer(total, lambda step: result(a, step, behind(step), behind(step)).wait_recv())
        every_peer(total, lambda step: result(a, step, ahead(step), me).wait_send())


def block_sum(total, lanes, xs, collective_id):
    vmem = pl.BlockSpec(memory_space=pltpu.VMEM)
    sems = [pltpu.SemaphoreType.DMA((total,))] * (4 * len(xs))
    return pl.pallas_call(
        functools.partial(block_sum_kernel, total, lanes, len(xs)),
        in_specs=[vmem] * len(xs),
        out_specs=[vmem] * len(xs),
        out_shape=[jax.ShapeDtypeStruct(x.shape, x.dtype) for x in xs],
        scratch_shapes=[pltpu.VMEM(x.shape, x.dtype) for x in xs] + sems,
        compiler_params=pltpu.CompilerParams(
            collective_id=collective_id, has_side_effects=True, vmem_limit_bytes=VMEM_BYTES
        ),
        cost_estimate=cost(1e8, 1e6),
        name="block_sum",
    )(*xs)


def pack(total, parts, dtype, rows):
    flat = jnp.concatenate([x.reshape(-1).astype(dtype) for x in parts])
    unit = total * rows * 128
    padded = -(-flat.shape[0] // unit) * unit
    return jnp.pad(flat, (0, padded - flat.shape[0])).reshape(total, -1, 128)


def unpack(packed, parts):
    flat = packed.reshape(-1).astype(F32)
    out, at = [], 0
    for x in parts:
        out.append(flat[at : at + x.size].reshape(x.shape))
        at += x.size
    return out


def whole_sum_kernel(total, lanes, x_ref, out_ref, held, send, recv):
    me = lax.axis_index("batch") * lanes + lax.axis_index("lat")
    greet_all(total, lanes, me)

    def part(step, peer):
        return pltpu.make_async_remote_copy(
            src_ref=x_ref,
            dst_ref=held.at[step],
            send_sem=send.at[step],
            recv_sem=recv.at[step],
            device_id=place(lanes, peer),
            device_id_type=pl.DeviceIdType.MESH,
        )

    ahead = lambda step: lax.rem(me + step, total)
    every_peer(total, lambda step: part(step, ahead(step)).start())
    held[0] = x_ref[...]
    every_peer(total, lambda step: part(step, ahead(step)).wait_recv())
    out_ref[...] = jnp.sum(held[...], 0)
    every_peer(total, lambda step: part(step, ahead(step)).wait_send())


def whole_sum(total, lanes, x, collective_id):
    sems = [pltpu.SemaphoreType.DMA((total,))] * 2
    return pl.pallas_call(
        functools.partial(whole_sum_kernel, total, lanes),
        in_specs=[pl.BlockSpec(memory_space=pltpu.VMEM)],
        out_specs=pl.BlockSpec(memory_space=pltpu.VMEM),
        out_shape=jax.ShapeDtypeStruct(x.shape, x.dtype),
        scratch_shapes=[pltpu.VMEM((total,) + x.shape, x.dtype)] + sems,
        compiler_params=pltpu.CompilerParams(
            collective_id=collective_id, has_side_effects=True, vmem_limit_bytes=VMEM_BYTES
        ),
        cost_estimate=cost(1e8, 1e6),
        name="whole_sum",
    )(x)


def exchange(x):
    return lax.all_to_all(x, "lat", split_axis=0, concat_axis=0, tiled=True)


def on_device(
    bands,
    tokens,
    cotangent,
    sample_weight,
    row_count,
    band_count,
    norm1_gain,
    norm1_bias,
    spec_w1,
    spec_b1,
    spec_w2,
    spec_b2,
    norm2_gain,
    norm2_bias,
    fc1_weight,
    fc1_bias,
    fc2_weight,
    fc2_bias,
):
    lane = lax.axis_index("lat")
    n = lax.axis_size("lat")
    samples, row_slots, width, channels = tokens.shape
    blocks, size = spec_w1.shape[1], spec_w1.shape[2]
    plan = Plan(n, samples, row_slots, width, channels, bands)
    wb1, wb2 = wide_bias(spec_b1), wide_bias(spec_b2)
    row = lambda v: v.reshape(1, -1)
    vectors = (row(norm1_gain), row(norm1_bias), row(norm2_gain), row(norm2_bias))
    own_rows = jnp.sum(jnp.where(jnp.arange(n) == lane, row_count, 0))
    held = jnp.arange(row_slots) < own_rows
    scales = sample_weight.astype(F32)[:, None] * 0.5 * held[None, :].astype(F32)
    slot_step = jnp.arange(plan.kp)
    valid = ((slot_step < plan.kk) & (lane * plan.kk + slot_step < plan.kw)).astype(F32)
    grouped = (n, plan.q, plan.t, channels)
    listed = (plan.pairs, plan.t, channels)

    ids = itertools.count()
    spread = (-1,) + grouped

    def spectral_forward(x, passengers=()):
        collective_id = next(ids) if passengers else None
        out = spectral_call(
            plan, valid, x, lat, lat_t, slots, m1, wb1, m2, wb2, passengers, collective_id
        )
        forward.append(out)
        return out[7:]

    def feed(s, back, sums, passengers):
        out = feed_call(
            plan,
            s,
            scales[s],
            tokens,
            cotangent,
            back.reshape(listed),
            vectors,
            fc1_weight,
            row(fc1_bias),
            fc2_weight,
            row(fc2_bias),
            sums,
            s == samples - 1,
            passengers,
            next(ids),
        )
        feeds.append(out)
        return out[7:]

    def backward(s, grads, passengers=()):
        out = spectral_back_call(
            plan,
            blocks,
            size,
            grads,
            forward[s][2:6],
            lat,
            lat_t,
            m1t,
            m2t,
            passengers,
            next(ids) if passengers else None,
        )
        spectral.append(out)
        return out[0], out[5:]

    forward, feeds, spectral, band_parts, grads, lon_grads = [], [], [], {}, {}, {}
    sent = first_call(plan, 0, 1, tokens, *vectors[:2])[0].reshape(spread)
    tables = Tables(plan, blocks, size)
    extra = tables.operands(row_count, band_count, spec_w1, spec_w2)
    others, lat, lat_t, slots, m1, m2, m1t, m2t, spectra = first_call(
        plan, 1, samples - 1, tokens, *vectors[:2], [(sent, 0)], next(ids), tables, extra
    )
    others = others.reshape(spread)
    (spectra,) = spectral_forward(spectra, [(others, 0)])
    (back,) = spectral_forward(spectra, [(forward[0][0], None)])
    for s in range(samples):
        sums = (feeds[-1][3], feeds[-1][4]) if s else None
        kinds, passengers = [], []
        if s + 1 < samples:
            kinds.append("back")
            passengers.append((forward[s + 1][0], None))
        if s + 2 < samples:
            kinds.append("spectra")
            passengers.append((others, s + 1))
        if s >= 1:
            kinds.append("grads")
            passengers.append((feeds[s - 1][1].reshape(grouped), None))
        if s >= 2:
            kinds.append("lon")
            lon, got = backward(s - 2, grads[s - 2], [(forward[s - 1][1], None)])
            band_parts[s - 1] = got[0]
            passengers.append((lon, None))
        arrived = dict(zip(kinds, feed(s, back, sums, passengers)))
        back = arrived.get("back")
        if s + 2 < samples:
            got = spectral_forward(arrived["spectra"], [(forward[s][1], None)])
            band_parts[s] = got[0]
        if s >= 1:
            grads[s - 1] = arrived["grads"]
        if s >= 2:
            lon_grads[s - 2] = arrived["lon"]
    grads[samples - 1] = exchange(feeds[-1][1].reshape(grouped))
    for s in range(samples - 2, samples):
        missing = [p for p in range(samples) if p not in band_parts][:1]
        lon, got = backward(s, grads[s], [(forward[p][1], None) for p in missing])
        for p, part in zip(missing, got):
            band_parts[p] = part
        lon_grads[s] = exchange(lon)

    tokens_grad, spectrum, finals = None, None, []
    for s in range(samples):
        tokens_grad, vec = last_call(
            plan,
            s,
            scales[s],
            tokens,
            feeds[s][2],
            lon_grads[s].reshape(listed),
            vectors[0],
            tokens_grad,
        )
        finals.append(vec)
        spectrum = band_call(plan, s, band_parts[s], spectrum)
    mixed = jnp.stack([f[0] for f in feeds])

    add = lambda parts: functools.reduce(jnp.add, parts)
    devices = lax.axis_size("batch") * n
    feed_vec = add([f[6] for f in feeds])
    block_grad = lambda i: add([b[i] for b in spectral]).reshape(2, blocks, size, size)
    large = lax.psum((feeds[-1][3], feeds[-1][4]), ("batch", "lat"))
    large = (large[0].astype(F32), large[1].astype(F32))
    zeros = jnp.sum(add([f[6] for f in forward]))
    small = [
        feed_vec[1],
        feed_vec[2],
        add([f[5] for f in feeds]),
        feed_vec[0],
        narrow_bias(add([b[3] for b in spectral]), blocks, size),
        narrow_bias(add([b[4] for b in spectral]), blocks, size),
        zeros.reshape(1),
    ]
    blocky = [block_grad(1), block_grad(2)]
    packed = [pack(devices, blocky, BF, 16), pack(devices, small, F32, 8)]
    packed = block_sum(devices, n, packed, next(ids))
    blocky = unpack(packed[0], blocky)
    small = unpack(packed[1], small)
    last_vec = whole_sum(devices, n, add(finals), next(ids))
    zero_fraction = small[6][0] / (lax.axis_size("batch") * samples * H * plan.kw * 2 * channels)
    return (
        mixed,
        spectrum.transpose(0, 1, 3, 2, 4),
        tokens_grad,
        last_vec[0],
        last_vec[1],
        blocky[0],
        small[4],
        blocky[1],
        small[5],
        small[0],
        small[1],
        large[0],
        small[2].reshape(-1),
        large[1],
        small[3],
        zero_fraction,
    )


def solution(mesh):
    rows = P("batch", "lat", None, None)
    in_specs = (rows, rows, P("batch")) + (P(),) * 14
    out_specs = (rows, P("batch", "lat", None, None, None), rows) + (P(),) * 13
    lanes = mesh.shape["lat"]

    def run(tokens, cotangent, *rest):
        row_slots = tokens.shape[1] // lanes
        return jax.shard_map(
            functools.partial(on_device, row_slots + 1),
            mesh=mesh,
            in_specs=in_specs,
            out_specs=out_specs,
            check_vma=False,
        )(tokens, cotangent, *rest)

    return run
```

```python
import functools
import itertools
import math

import jax
import jax.numpy as jnp
import numpy as np
from jax import lax
from jax.experimental import pallas as pl
from jax.experimental.pallas import tpu as pltpu
from jax.sharding import PartitionSpec as P

H = 90
HP = 96

NORM_EPS = 1e-06
SHRINK_LAMBDA = 0.01
SHRINK_SOFTNESS = 0.1
INV_ROOT_TAU = 1.0 / math.sqrt(2.0 * math.pi)
BF = jnp.bfloat16
F32 = jnp.float32
VMEM_BYTES = 64 * 1024 * 1024


def dot(a, b):
    return jnp.dot(a, b, preferred_element_type=F32)


def dot_nt(a, b):
    return lax.dot_general(a, b, (((1,), (1,)), ((), ())), preferred_element_type=F32)


def dot_tn(a, b):
    return lax.dot_general(a, b, (((0,), (0,)), ((), ())), preferred_element_type=F32)


def dot_table(table_ref, x):
    return dot(table_ref[0], x) + dot(table_ref[1], x)


def two_parts(table):
    high = table.astype(BF)
    return high, (table - high.astype(table.dtype)).astype(BF)


def norm_parts(x):
    mean = jnp.mean(x, -1, keepdims=True)
    centred = x - mean
    rstd = lax.rsqrt(jnp.mean(centred * centred, -1, keepdims=True) + NORM_EPS)
    return centred * rstd, rstd


def norm_back(grad, unit, rstd, gain):
    e = grad * gain
    return rstd * (
        e - jnp.mean(e, -1, keepdims=True) - unit * jnp.mean(e * unit, -1, keepdims=True)
    )


def gauss_parts(v):
    d = 1.0 + jnp.abs(v) * (0.3275911 / math.sqrt(2.0))
    t = pl.reciprocal(d, approx=True)
    e = jnp.exp2(v * v * (-0.5 * math.log2(math.e)))
    poly = 1.061405429 * 0.5
    for c in (-1.453152027, 1.421413741, -0.284496736, 0.254829592):
        poly = poly * t + 0.5 * c
    tail = poly * t * e
    cdf = jnp.where(v >= 0.0, 1.0 - tail, tail)
    return cdf, v * e * INV_ROOT_TAU


def gelu_both(v):
    cdf, slope_part = gauss_parts(v)
    return v * cdf, cdf + slope_part


def shrink_both(u):
    a = jnp.maximum(jnp.abs(u) - SHRINK_LAMBDA, 0.0)
    d = a + SHRINK_SOFTNESS
    t = pl.reciprocal(d, approx=True)
    t = t * (2.0 - d * t)
    size = a * a * t
    value = jnp.where(u >= 0.0, size, -size)
    slope = a * (a + 2.0 * SHRINK_SOFTNESS) * (t * t)
    return value, slope


class Plan:
    def __init__(self, n, samples, rows, width, channels, bands):
        self.n, self.s, self.r, self.w, self.d, self.mb = n, samples, rows, width, channels, bands
        self.kw = width // 2 + 1
        self.kk = -(-self.kw // n)
        self.kp = self.kk + self.kk % 2
        self.q = self.kp // 2
        self.rp = -(-rows // 4) * 4
        self.t = 4 * self.rp
        self.pairs = n * self.q
        self.ki = n * self.kp * 2
        self.rb = max(b for b in (4, 3, 2, 1) if rows % b == 0)
        self.chunks = rows // self.rb
        self.flat = self.rb * width
        self.flatp = max(-(-self.flat // 256) * 256, channels)
        self.bt = -(-4 * bands // 8) * 8
        j = np.arange(n)[:, None]
        t = np.arange(self.kp)[None, :]
        self.k_index = (j * self.kk + t).astype(np.int64)
        self.k_valid = (t < self.kk) & (self.k_index < self.kw)
        k = np.where(self.k_valid, self.k_index, 0).reshape(-1)
        ok = self.k_valid.reshape(-1).astype(np.float64)
        angle = 2.0 * np.pi * ((k[:, None] * np.arange(width)[None, :]) % width) / width
        scale = ok[:, None] / math.sqrt(width)
        fwd = np.stack([np.cos(angle) * scale, -np.sin(angle) * scale], 1).reshape(self.ki, width)
        factor = np.where((k == 0) | (2 * k == width), 1.0, 2.0)[:, None, None]
        both = (fwd.reshape(-1, 2, width) * factor).reshape(self.ki, width)
        self.lon = np.stack(two_parts(fwd))
        self.lon_both = np.stack(two_parts(both))
        self.lon_t = np.stack(two_parts(np.ascontiguousarray(fwd.T)))
        self.lon_both_t = np.stack(two_parts(np.ascontiguousarray(both.T)))
        perm = np.zeros((16, self.rp, rows, 16))
        for a in range(16):
            for r in range(rows):
                perm[a, r, r, a] = 1.0
        self.perm = perm.reshape(16 * self.rp, rows * 16).astype(BF)
        self.perm_t = np.ascontiguousarray(self.perm.T)


class Tables:
    def __init__(self, plan, blocks, size):
        self.plan, self.blocks, self.size = plan, blocks, size
        n, rp, mb = plan.n, plan.rp, plan.mb
        kh, h = np.arange(HP)[:, None], np.arange(HP)[None, :]
        angle = 2.0 * np.pi * (kh * h % H) / H
        weight = ((kh < H) & (h < H)) / math.sqrt(H)
        cosine, sine = np.cos(angle) * weight, np.sin(angle) * weight
        part = np.block([[cosine, sine], [-sine, cosine]])
        self.base = np.stack(two_parts(np.kron(np.eye(2), part)))
        col = np.arange(n * 4 * rp)
        group, step = col // rp % 4, col % rp
        self.columns = np.stack([col // (4 * rp), group * HP + step, step]).astype(np.int32)
        bt = plan.bt
        line = np.arange(n * bt)
        group, step = line % bt // mb, line % bt % mb
        step = np.where(group < 4, step, 1 << 20)
        lines = np.stack([line // bt, group * HP + step, step]).astype(np.int32)
        self.lines = lines[:, :, None]
        half = blocks // 2
        spots = np.zeros((half, size, half * size))
        for i in range(half):
            spots[i, :, i * size : (i + 1) * size] = np.eye(size)
        self.spots = spots.astype(BF)
        wide = 4 * HP
        d = plan.d
        shapes = [(2, wide, n * 4 * rp), (2, n * 4 * rp, wide), (n * bt, wide)] + [(2, d, d)] * 4
        self.shapes = [jax.ShapeDtypeStruct(x, BF) for x in shapes]

    def operands(self, row_count, band_count, spec_w1, spec_w2):
        return [
            row_count,
            band_count,
            spec_w1,
            spec_w2,
            self.base,
            self.columns[:, None, :],
            self.lines,
            self.spots,
        ]

    def in_specs(self):
        weight = (2, self.blocks, self.size, self.size)
        shapes = [weight, weight, self.base.shape, (3, 1, self.columns.shape[1])]
        shapes += [self.lines.shape, self.spots.shape]
        return [SMEM, SMEM] + [whole(x) for x in shapes]

    def out_specs(self):
        return [whole(x.shape) for x in self.shapes]

    def build(self, ins, outs):
        rows_ref, bands_ref, w1_ref, w2_ref, base_ref, col_ref, line_ref, spot_ref = ins
        lat_ref, lat_t_ref, slot_ref, m1_ref, m2_ref, m1t_ref, m2t_ref = outs
        n = self.plan.n

        def spread(counts_ref, owner):
            first = jnp.zeros(owner.shape, jnp.int32)
            held = jnp.zeros(owner.shape, jnp.int32)
            start = jnp.int32(0)
            for j in range(n):
                count = counts_ref[j]
                first = jnp.where(owner == j, start, first)
                held = jnp.where(owner == j, count, held)
                start = start + count
            return first, held

        first, held = spread(rows_ref, col_ref[0])
        target = jnp.where(col_ref[2] < held, col_ref[1] + first, -1)
        pick = lax.broadcasted_iota(jnp.int32, (4 * HP, target.shape[1]), 0) == target
        pick = jnp.where(pick, 1.0, 0.0).astype(BF)
        for part in range(2):
            full = dot(base_ref[part], pick)
            lat_ref[part] = full.astype(BF)
            lat_t_ref[part] = full.T.astype(BF)
        first, held = spread(bands_ref, line_ref[0])
        target = jnp.where(line_ref[2] < held, line_ref[1] + first, -1)
        pick = lax.broadcasted_iota(jnp.int32, (target.shape[0], 4 * HP), 1) == target
        slot_ref[...] = jnp.where(pick, 1.0, 0.0).astype(BF)
        half, size = self.blocks // 2, self.size
        mid = half * size
        for w_ref, m_ref, mt_ref in ((w1_ref, m1_ref, m1t_ref), (w2_ref, m2_ref, m2t_ref)):
            for g in range(2):
                for i in range(half):
                    low = slice(i * size, (i + 1) * size)
                    high = slice(mid + i * size, mid + (i + 1) * size)
                    re, im = w_ref[0, g * half + i], w_ref[1, g * half + i]
                    for ref, place_in, sign in ((m_ref, dot, 1.0), (mt_ref, dot_tn, -1.0)):
                        real = place_in(re, spot_ref[i]).astype(BF)
                        imag = place_in(im, spot_ref[i]) * sign
                        ref[g, low, :mid] = real
                        ref[g, high, mid:] = real
                        ref[g, low, mid:] = imag.astype(BF)
                        ref[g, high, :mid] = (-imag).astype(BF)


def wide_bias(bias):
    return bias.reshape(2, 2, -1).transpose(1, 0, 2).reshape(2, 1, -1)


def narrow_bias(wide, blocks, size):
    return wide.reshape(2, 2, -1).transpose(1, 0, 2).reshape(2, blocks, size)


def whole(shape):
    zeros = (0,) * len(shape)
    return pl.BlockSpec(shape, lambda *_: zeros)


def whole_once(shape):
    zeros = (0,) * len(shape)
    return pl.BlockSpec(shape, lambda *_: zeros, pipeline_mode=pl.Buffered(1))


SMEM = pl.BlockSpec(memory_space=pltpu.SMEM)
ANY = pl.BlockSpec(memory_space=pl.ANY)


def params(collective_id=None):
    if collective_id is None:
        return pltpu.CompilerParams(
            dimension_semantics=("arbitrary",), vmem_limit_bytes=VMEM_BYTES
        )
    return pltpu.CompilerParams(
        dimension_semantics=("arbitrary",),
        vmem_limit_bytes=VMEM_BYTES,
        collective_id=collective_id,
        has_side_effects=True,
    )


def ride_copy(n, me, src, dst, send, recv, e, step):
    peer = lax.rem(me + step, n)
    return pltpu.make_async_remote_copy(
        src_ref=src.at[peer],
        dst_ref=dst.at[me],
        send_sem=send.at[e, step],
        recv_sem=recv.at[e, step],
        device_id={"lat": peer},
        device_id_type=pl.DeviceIdType.MESH,
    )


def ride_arrival(n, me, src, dst, send, recv, e, step):
    peer = lax.rem(me + n - step, n)
    return pltpu.make_async_remote_copy(
        src_ref=src.at[peer],
        dst_ref=dst.at[peer],
        send_sem=send.at[e, step],
        recv_sem=recv.at[e, step],
        device_id={"lat": peer},
        device_id_type=pl.DeviceIdType.MESH,
    )


def ride_start(n, srcs, dsts, send, recv, own):
    me = lax.axis_index("lat")
    barrier = pltpu.get_barrier_semaphore()
    for step in range(1, n):
        pl.semaphore_signal(
            barrier,
            inc=1,
            device_id={"lat": lax.rem(me + step, n)},
            device_id_type=pl.DeviceIdType.MESH,
        )
    pl.semaphore_wait(barrier, n - 1)
    for e, (src, dst) in enumerate(zip(srcs, dsts)):
        for step in range(1, n):
            ride_copy(n, me, src, dst, send, recv, e, step).start()
        pltpu.make_async_copy(src.at[me], dst.at[me], own.at[e]).start()


def ride_wait(n, srcs, dsts, send, recv, own):
    me = lax.axis_index("lat")
    for e, (src, dst) in enumerate(zip(srcs, dsts)):
        pltpu.make_async_copy(src.at[me], dst.at[me], own.at[e]).wait()
        for step in range(1, n):
            ride_copy(n, me, src, dst, send, recv, e, step).wait_send()
            ride_arrival(n, me, src, dst, send, recv, e, step).wait_recv()


def cost(flops, size):
    return pl.CostEstimate(flops=int(flops), bytes_accessed=int(size), transcendentals=0)


def interleave(plan, perm_ref, rows_ref, out_ref):
    def body(c, carry):
        at = pl.multiple_of(c * 16, 16)
        block = rows_ref[:, pl.ds(at, 16), :].reshape(plan.r * 16, plan.d)
        mixed = dot(perm_ref[...], block).astype(BF)
        out_ref[pl.ds(c * 4, 4)] = mixed.reshape(4, plan.t, plan.d)
        return carry

    lax.fori_loop(0, plan.ki // 16, body, 0)


def deinterleave(plan, perm_t_ref, in_ref, rows_ref):
    def body(c, carry):
        at = pl.multiple_of(c * 16, 16)
        block = in_ref[pl.ds(c * 4, 4)].reshape(4 * plan.t, plan.d)
        rows = dot(perm_t_ref[...], block).astype(BF)
        rows_ref[:, pl.ds(at, 16), :] = rows.reshape(plan.r, 16, plan.d)
        return carry

    lax.fori_loop(0, plan.ki // 16, body, 0)


def interleave_out(plan, perm_ref, rows_ref, ring, sem, out_ref):
    def copy(c):
        return pltpu.make_async_copy(
            ring.at[lax.rem(c, 2)], out_ref.at[pl.ds(c * 4, 4)], sem.at[lax.rem(c, 2)]
        )

    def body(c, carry):
        @pl.when(c >= 2)
        def _():
            copy(c - 2).wait()

        at = pl.multiple_of(c * 16, 16)
        block = rows_ref[:, pl.ds(at, 16), :].reshape(plan.r * 16, plan.d)
        mixed = dot(perm_ref[...], block).astype(BF)
        ring[lax.rem(c, 2)] = mixed.reshape(4, plan.t, plan.d)
        copy(c).start()
        return carry

    lax.fori_loop(0, plan.ki // 16, body, 0)
    return [copy(plan.ki // 16 - 2), copy(plan.ki // 16 - 1)]


def ring_load(plan, in_ref, ring, sem, c):
    return pltpu.make_async_copy(
        in_ref.at[pl.ds(c * 4, 4)], ring.at[lax.rem(c, 2)], sem.at[lax.rem(c, 2)]
    )


def deinterleave_in(plan, perm_t_ref, in_ref, ring, sem, rows_ref):
    steps = plan.ki // 16

    def body(c, carry):
        ring_load(plan, in_ref, ring, sem, c).wait()
        at = pl.multiple_of(c * 16, 16)
        block = ring[lax.rem(c, 2)].reshape(4 * plan.t, plan.d)
        rows = dot(perm_t_ref[...], block).astype(BF)
        rows_ref[:, pl.ds(at, 16), :] = rows.reshape(plan.r, 16, plan.d)

        @pl.when(c + 2 < steps)
        def _():
            ring_load(plan, in_ref, ring, sem, c + 2).start()

        return carry

    lax.fori_loop(0, steps, body, 0)


class Riders:
    def __init__(self, plan, passengers):
        self.n = plan.n
        self.arrays = [a for a, _ in passengers]
        self.leads = [lead for _, lead in passengers]
        self.count = len(passengers)

    def shapes(self):
        return [
            jax.ShapeDtypeStruct(a.shape if lead is None else a.shape[1:], a.dtype)
            for a, lead in zip(self.arrays, self.leads)
        ]

    def specs(self):
        return [ANY] * self.count

    def scratch(self):
        if not self.count:
            return []
        dma = pltpu.SemaphoreType.DMA
        return [dma((self.count, self.n)), dma((self.count, self.n)), dma((self.count,))]

    def bind(self, srcs, dsts, sems):
        srcs = [r if lead is None else r.at[lead] for r, lead in zip(srcs, self.leads)]
        return (self.n, srcs, dsts) + tuple(sems)


def first_kernel(plan, riders, tables, tok_ref, gain_ref, bias_ref, lon_ref, perm_ref, *rest):
    e = riders.count
    t_in = 0 if tables is None else 8
    t_out = 0 if tables is None else 7
    t_ins, rest = rest[:t_in], rest[t_in:]
    srcs, rest = rest[:e], rest[e:]
    out_ref, rest = rest[0], rest[1:]
    t_outs, rest = rest[:t_out], rest[t_out:]
    dsts, rows_ref, sems = rest[:e], rest[e], rest[e + 1 :]
    i = pl.program_id(0)
    c = lax.rem(i, plan.chunks)
    if e:
        ride = riders.bind(srcs, dsts, sems)

        @pl.when(i == 0)
        def _():
            ride_start(*ride)

    for u in range(plan.rb):
        unit, _ = norm_parts(tok_ref[0, u].astype(F32))
        normed = (unit * gain_ref[...] + bias_ref[...]).astype(BF)
        rows_ref[c * plan.rb + u] = dot_table(lon_ref, normed).astype(BF)

    @pl.when(c == plan.chunks - 1)
    def _():
        interleave(plan, perm_ref, rows_ref, out_ref.at[0])

    @pl.when(i == pl.num_programs(0) - 1)
    def _():
        if tables is not None:
            tables.build(t_ins, t_outs)
        if e:
            ride_wait(*ride)


def row_block(plan, s):
    return pl.BlockSpec((1, plan.rb, plan.w, plan.d), lambda i: (s, i, 0, 0))


def own_block(plan):
    return pl.BlockSpec((plan.rb, plan.w, plan.d), lambda i: (i, 0, 0))


def first_call(
    plan, start, count, tokens, gain, bias, passengers=(), collective_id=None, tables=None, extra=()
):
    shape = (plan.pairs, plan.t, plan.d)
    chunks = plan.chunks
    riders = Riders(plan, passengers)
    return pl.pallas_call(
        functools.partial(first_kernel, plan, riders, tables),
        grid=(count * chunks,),
        in_specs=[
            pl.BlockSpec(
                (1, plan.rb, plan.w, plan.d),
                lambda i: (start + i // chunks, lax.rem(i, chunks), 0, 0),
            ),
            whole((1, plan.d)),
            whole((1, plan.d)),
            whole((2, plan.ki, plan.w)),
            whole(plan.perm.shape),
        ]
        + (tables.in_specs() if tables else [])
        + riders.specs(),
        out_specs=[pl.BlockSpec((1,) + shape, lambda i: (i // chunks, 0, 0, 0))]
        + (tables.out_specs() if tables else [])
        + riders.specs(),
        out_shape=[jax.ShapeDtypeStruct((count,) + shape, BF)]
        + (tables.shapes if tables else [])
        + riders.shapes(),
        scratch_shapes=[pltpu.VMEM((plan.r, plan.ki, plan.d), BF)] + riders.scratch(),
        compiler_params=params(collective_id),
        cost_estimate=cost(9e9 * count, 8e6 * count),
        name="lon_forward",
    )(tokens, gain, bias, plan.lon, plan.perm, *extra, *riders.arrays)


def spectral_kernel(
    plan,
    riders,
    valid_ref,
    in_ref,
    lat_ref,
    lat_t_ref,
    slot_ref,
    m1_ref,
    b1_ref,
    m2_ref,
    b2_ref,
    *rest,
):
    e = riders.count
    srcs, rest = rest[:e], rest[e:]
    back_ref, band_ref, spec_ref, hid_ref, slope1_ref, slope2_ref, zero_ref = rest[:7]
    dsts, shr_ref, sems = rest[7 : 7 + e], rest[7 + e], rest[8 + e :]
    q = pl.program_id(0)
    half = plan.d // 2
    if e:
        ride = riders.bind(srcs, dsts, sems)

        @pl.when(q == 0)
        def _():
            ride_start(*ride)

    @pl.when(q == 0)
    def _():
        zero_ref[...] = jnp.zeros_like(zero_ref)

    x = in_ref[:, 0].reshape(plan.n * plan.t, plan.d)
    spec = dot_table(lat_ref, x).astype(BF)
    ok = (lax.broadcasted_iota(jnp.int32, (HP, 1), 0) < H).astype(F32)
    for g in range(2):
        lanes = slice(g * half, (g + 1) * half)
        for a in range(2):
            top = a * 2 * HP
            spec_ref[0, g, a * HP : (a + 1) * HP, :half] = spec[top : top + HP, lanes]
            spec_ref[0, g, a * HP : (a + 1) * HP, half:] = spec[top + HP : top + 2 * HP, lanes]
        u1 = dot(spec_ref[0, g], m1_ref[g]) + b1_ref[g]
        hidden, slope = gelu_both(u1)
        hid_ref[0, g] = hidden.astype(BF)
        slope1_ref[0, g] = slope.astype(BF)
        u2 = dot(hid_ref[0, g], m2_ref[g]) + b2_ref[g]
        small = (jnp.abs(u2) <= SHRINK_LAMBDA).astype(F32)
        for a in range(2):
            part = small[a * HP : (a + 1) * HP] * ok
            zero_ref[...] += jnp.sum(part, 0, keepdims=True) * valid_ref[q * 2 + a]
        value, slope = shrink_both(u2)
        slope2_ref[0, g] = slope.astype(BF)
        value = value.astype(BF)
        for a in range(2):
            top = a * 2 * HP
            shr_ref[top : top + HP, lanes] = value[a * HP : (a + 1) * HP, :half]
            shr_ref[top + HP : top + 2 * HP, lanes] = value[a * HP : (a + 1) * HP, half:]
    shrunk = shr_ref[...]
    back_ref[:, 0] = dot_table(lat_t_ref, shrunk).astype(BF).reshape(plan.n, plan.t, plan.d)
    band = dot(slot_ref[...], shrunk).astype(BF)
    band_ref[:, 0] = band.reshape(plan.n, plan.bt, plan.d)
    if e:

        @pl.when(q == plan.q - 1)
        def _():
            ride_wait(*ride)


def pair_block(plan, rows):
    return pl.BlockSpec((plan.n, 1, rows, plan.d), lambda q: (0, q, 0, 0))


def spectral_call(
    plan, valid, received, lat, lat_t, slots, m1, b1, m2, b2, passengers=(), collective_id=None
):
    riders = Riders(plan, passengers)
    kept = (plan.q, 2, 2 * HP, plan.d)
    kept_spec = pl.BlockSpec((1, 2, 2 * HP, plan.d), lambda q: (q, 0, 0, 0))
    kept_shape = jax.ShapeDtypeStruct(kept, BF)
    rows = plan.bt
    return pl.pallas_call(
        functools.partial(spectral_kernel, plan, riders),
        grid=(plan.q,),
        in_specs=[
            SMEM,
            pair_block(plan, plan.t),
            whole(lat.shape),
            whole(lat_t.shape),
            whole(slots.shape),
            whole(m1.shape),
            whole(b1.shape),
            whole(m2.shape),
            whole(b2.shape),
        ]
        + riders.specs(),
        out_specs=[
            pair_block(plan, plan.t),
            pair_block(plan, rows),
            kept_spec,
            kept_spec,
            kept_spec,
            kept_spec,
            whole((1, plan.d)),
        ]
        + riders.specs(),
        out_shape=[
            jax.ShapeDtypeStruct((plan.n, plan.q, plan.t, plan.d), BF),
            jax.ShapeDtypeStruct((plan.n, plan.q, rows, plan.d), BF),
            kept_shape,
            kept_shape,
            kept_shape,
            kept_shape,
            jax.ShapeDtypeStruct((1, plan.d), F32),
        ]
        + riders.shapes(),
        scratch_shapes=[pltpu.VMEM((4 * HP, plan.d), BF)] + riders.scratch(),
        compiler_params=params(collective_id),
        cost_estimate=cost(20e9, 25e6),
        name="spectral_forward",
    )(valid, received, lat, lat_t, slots, m1, b1, m2, b2, *riders.arrays)


def feed_kernel(
    plan,
    first,
    final,
    riders,
    tiles,
    scale_ref,
    tok_ref,
    cot_ref,
    recv_ref,
    gain1_ref,
    bias1_ref,
    gain2_ref,
    bias2_ref,
    lon_t_ref,
    lon_ref,
    perm_ref,
    perm_t_ref,
    w1_ref,
    b1_ref,
    w2_ref,
    b2_ref,
    *rest,
):
    e = riders.count
    srcs, rest = rest[:e], rest[e:]
    if first:
        in1_ref = in2_ref = None
    else:
        in1_ref, in2_ref = rest[:2]
        rest = rest[2:]
    mixed_ref, send_ref, gx_ref, out1_ref, out2_ref, db1_ref, vec_ref = rest[:7]
    dsts, rest = rest[7 : 7 + e], rest[7 + e :]
    (
        dw1,
        dw2,
        ring,
        rows_ref,
        x1_ref,
        xn,
        xn_t,
        gm,
        gm_t,
        act_a,
        gz_a,
        down,
        up,
        sem,
        ring_sem,
        *ride_sems,
    ) = rest
    i = pl.program_id(0)
    last = plan.chunks - 1
    tile = act_a.shape[1]
    flat = plan.flat
    ride = riders.bind(srcs, dsts, ride_sems)

    @pl.when(i == 0)
    def _():
        for c in range(2):
            ring_load(plan, recv_ref, ring, ring_sem, c).start()
        if not first:
            pltpu.make_async_copy(in1_ref, dw1, sem.at[1]).start()
            pltpu.make_async_copy(in2_ref, dw2, sem.at[2]).start()
        ride_start(*ride)
        if first:
            dw1[...] = jnp.zeros_like(dw1)
            dw2[...] = jnp.zeros_like(dw2)
        db1_ref[...] = jnp.zeros_like(db1_ref)
        vec_ref[...] = jnp.zeros_like(vec_ref)
        if plan.flatp > flat:
            pad = jnp.zeros((plan.flatp - flat, tile), BF)
            for ref in (act_a, gz_a):
                ref[flat:, :] = pad
            pad = jnp.zeros((plan.flatp - flat, plan.d), F32)
            down[flat:, :] = pad
            up[flat:, :] = pad
        deinterleave_in(plan, perm_t_ref, recv_ref, ring, ring_sem, rows_ref)

    for u in range(plan.rb):
        span = slice(u * plan.w, (u + 1) * plan.w)
        x = tok_ref[0, u].astype(F32)
        unit, _ = norm_parts(x)
        filtered = dot_table(lon_t_ref, rows_ref[i * plan.rb + u])
        x1 = x + filtered + (unit * gain1_ref[...] + bias1_ref[...])
        x1_ref[u] = x1
        unit, _ = norm_parts(x1)
        down[span, :] = unit * gain2_ref[...] + bias2_ref[...]
        up[span, :] = cot_ref[0, u].astype(F32) * scale_ref[i * plan.rb + u]
    normed = down[...].astype(BF)
    xn[...] = normed[:flat]
    xn_t[...] = normed.T
    grads = up[...].astype(BF)
    gm[...] = grads[:flat]
    gm_t[...] = grads.T
    vec_ref[0:1] += jnp.sum(grads.astype(F32), 0, keepdims=True)
    down[...] = jnp.zeros_like(down)
    up[...] = jnp.zeros_like(up)

    if not first:

        @pl.when(i == 0)
        def _():
            pltpu.make_async_copy(in1_ref, dw1, sem.at[1]).wait()
            pltpu.make_async_copy(in2_ref, dw2, sem.at[2]).wait()

    def columns(t):
        return pl.ds(pl.multiple_of(t * tile, tile), tile)

    part = 256
    blocks = tile // part

    def body(t, carry):
        opened = {}

        def enter(c):
            cols = pl.ds(pl.multiple_of(t * tile + c * part, part), part)
            z = dot(xn[...], w1_ref[:, cols]) + b1_ref[:, cols]
            opened[c] = (z, dot_nt(gm[...], w2_ref[cols, :]))

        enter(0)
        for c in range(blocks):
            if c + 1 < blocks:
                enter(c + 1)
            z, ga = opened.pop(c)
            hidden, slope = gelu_both(z)
            grad = ga * slope
            here = slice(c * part, (c + 1) * part)
            act_a[:flat, here] = hidden.astype(BF)
            gz_a[:flat, here] = grad.astype(BF)
            cols = pl.ds(pl.multiple_of(t * tile + c * part, part), part)
            db1_ref[:, cols] += jnp.sum(grad, 0, keepdims=True)
            dw1[:, cols] += dot(xn_t[...], gz_a[:, here])
            dw2[:, cols] += dot(gm_t[...], act_a[:, here])
        cols = columns(t)
        down[:flat, :] += dot(act_a[:flat, :], w2_ref[cols, :])
        up[:flat, :] += dot_nt(gz_a[:flat, :], w1_ref[:, cols])
        return carry

    lax.fori_loop(0, tiles, body, 0)

    if not final:

        @pl.when(i == last)
        def _():
            pltpu.make_async_copy(dw1, out1_ref, sem.at[1]).start()
            pltpu.make_async_copy(dw2, out2_ref, sem.at[2]).start()

    for u in range(plan.rb):
        span = slice(u * plan.w, (u + 1) * plan.w)
        x1 = x1_ref[u]
        scale = scale_ref[i * plan.rb + u]
        keep = jnp.where(scale > 0.0, 1.0, 0.0)
        mixed_ref[u] = ((x1 + down[span, :] + b2_ref[...]) * keep).astype(BF)
        unit, rstd = norm_parts(x1)
        grad = up[span, :]
        vec_ref[1:2] += jnp.sum(grad * unit, 0, keepdims=True)
        vec_ref[2:3] += jnp.sum(grad, 0, keepdims=True)
        gx = cot_ref[0, u].astype(F32) * scale + norm_back(grad, unit, rstd, gain2_ref[...])
        gx_ref[u] = gx.astype(gx_ref.dtype)
        rows_ref[i * plan.rb + u] = dot_table(lon_ref, gx.astype(BF)).astype(BF)

    if plan.flatp > flat:
        down[flat:, :] = jnp.zeros((plan.flatp - flat, plan.d), F32)
        up[flat:, :] = jnp.zeros((plan.flatp - flat, plan.d), F32)

    @pl.when(i == last)
    def _():
        stores = interleave_out(plan, perm_ref, rows_ref, ring, ring_sem, send_ref)
        if final:
            stage = (xn_t, gm_t, act_a, gz_a)
            height = 512
            pending = {}
            for t in range(2 * (dw1.shape[1] // height)):
                side = t % 4
                if side in pending:
                    pending.pop(side).wait()
                cols = slice(t // 2 * height, (t // 2 + 1) * height)
                held = stage[side].at[:height, : plan.d]
                held[...] = (dw1, dw2)[t % 2][:, cols].astype(BF).T
                pending[side] = pltpu.make_async_copy(
                    held, out1_ref.at[t % 2, cols], sem.at[1 + side]
                )
                pending[side].start()
            for copy in pending.values():
                copy.wait()
        else:
            pltpu.make_async_copy(dw1, out1_ref, sem.at[1]).wait()
            pltpu.make_async_copy(dw2, out2_ref, sem.at[2]).wait()
        for store in stores:
            store.wait()
        ride_wait(*ride)


def feed_call(
    plan, s, scales, tokens, cotangent, received, vectors, w1, b1, w2, b2, sums, final, passengers,
    collective_id
):
    gain1, bias1, gain2, bias2 = vectors
    first = sums is None
    ff = w1.shape[1]
    tile = 1024
    d, flat = plan.d, plan.flat
    flatp = plan.flatp
    shape = (plan.pairs, plan.t, d)
    vec = whole((1, d))
    riders = Riders(plan, passengers)
    in_specs = [
        SMEM,
        row_block(plan, s),
        row_block(plan, s),
        ANY,
        vec,
        vec,
        vec,
        vec,
        whole((2, plan.w, plan.ki)),
        whole((2, plan.ki, plan.w)),
        whole(plan.perm.shape),
        whole(plan.perm_t.shape),
        whole_once((d, ff)),
        whole((1, ff)),
        whole_once((ff, d)),
        vec,
    ] + riders.specs()
    operands = [
        scales,
        tokens,
        cotangent,
        received,
        gain1,
        bias1,
        gain2,
        bias2,
        plan.lon_both_t,
        plan.lon_both,
        plan.perm,
        plan.perm_t,
        w1,
        b1,
        w2,
        b2,
        *riders.arrays,
    ]
    aliases = {}
    if not first:
        if not final:
            aliases = {len(operands): 3, len(operands) + 1: 4}
        in_specs += [ANY, ANY]
        operands += list(sums)
    if final:
        wides = [jax.ShapeDtypeStruct((2, ff, d), BF), jax.ShapeDtypeStruct((8, 128), F32)]
    else:
        wides = [jax.ShapeDtypeStruct((d, ff), F32)] * 2
    return pl.pallas_call(
        functools.partial(feed_kernel, plan, first, final, riders, ff // tile),
        grid=(plan.chunks,),
        in_specs=in_specs,
        out_specs=[
            own_block(plan),
            ANY,
            own_block(plan),
            ANY,
            ANY,
            whole((1, ff)),
            whole((8, d)),
        ]
        + riders.specs(),
        out_shape=[
            jax.ShapeDtypeStruct((plan.r, plan.w, d), BF),
            jax.ShapeDtypeStruct(shape, BF),
            jax.ShapeDtypeStruct((plan.r, plan.w, d), BF),
            *wides,
            jax.ShapeDtypeStruct((1, ff), F32),
            jax.ShapeDtypeStruct((8, d), F32),
        ]
        + riders.shapes(),
        scratch_shapes=[
            pltpu.VMEM((d, ff), F32),
            pltpu.VMEM((d, ff), F32),
            pltpu.VMEM((2, 4, plan.t, d), BF),
            pltpu.VMEM((plan.r, plan.ki, d), BF),
            pltpu.VMEM((plan.rb, plan.w, d), F32),
            pltpu.VMEM((flat, d), BF),
            pltpu.VMEM((d, flatp), BF),
            pltpu.VMEM((flat, d), BF),
            pltpu.VMEM((d, flatp), BF),
            pltpu.VMEM((flatp, tile), BF),
            pltpu.VMEM((flatp, tile), BF),
            pltpu.VMEM((flatp, d), F32),
            pltpu.VMEM((flatp, d), F32),
            pltpu.SemaphoreType.DMA((5,)),
            pltpu.SemaphoreType.DMA((2,)),
        ]
        + riders.scratch(),
        input_output_aliases=aliases,
        compiler_params=params(collective_id),
        cost_estimate=cost(70e9, 60e6),
        name="feed_forward",
    )(*operands)


def spectral_back_kernel(
    plan,
    riders,
    in_ref,
    spec_ref,
    hid_ref,
    slope1_ref,
    slope2_ref,
    lat_ref,
    lat_t_ref,
    m1t_ref,
    m2t_ref,
    *rest,
):
    e = riders.count
    srcs, rest = rest[:e], rest[e:]
    out_ref, dw1_ref, dw2_ref, db1_ref, db2_ref = rest[:5]
    dsts, rest = rest[5 : 5 + e], rest[5 + e :]
    dm1_ref, dm2_ref, gs_ref, gu_ref = rest[:4]
    q = pl.program_id(0)
    half = plan.d // 2
    if e:
        ride = riders.bind(srcs, dsts, rest[4:])

        @pl.when(q == 0)
        def _():
            ride_start(*ride)

    @pl.when(q == 0)
    def _():
        dm1_ref[...] = jnp.zeros_like(dm1_ref)
        dm2_ref[...] = jnp.zeros_like(dm2_ref)
        db1_ref[...] = jnp.zeros_like(db1_ref)
        db2_ref[...] = jnp.zeros_like(db2_ref)

    x = in_ref[:, 0].reshape(plan.n * plan.t, plan.d)
    grad = dot_table(lat_ref, x).astype(BF)
    for g in range(2):
        lanes = slice(g * half, (g + 1) * half)
        for a in range(2):
            top = a * 2 * HP
            gu_ref[a * HP : (a + 1) * HP, :half] = grad[top : top + HP, lanes]
            gu_ref[a * HP : (a + 1) * HP, half:] = grad[top + HP : top + 2 * HP, lanes]
        gu2 = gu_ref[...].astype(F32) * slope2_ref[0, g].astype(F32)
        db2_ref[g] += jnp.sum(gu2, 0, keepdims=True)
        gu2 = gu2.astype(BF)
        dm2_ref[g] += dot_tn(hid_ref[0, g], gu2)
        gu1 = (dot(gu2, m2t_ref[g]) * slope1_ref[0, g].astype(F32)).astype(BF)
        db1_ref[g] += jnp.sum(gu1.astype(F32), 0, keepdims=True)
        dm1_ref[g] += dot_tn(spec_ref[0, g], gu1)
        gs = dot(gu1, m1t_ref[g]).astype(BF)
        for a in range(2):
            top = a * 2 * HP
            gs_ref[top : top + HP, lanes] = gs[a * HP : (a + 1) * HP, :half]
            gs_ref[top + HP : top + 2 * HP, lanes] = gs[a * HP : (a + 1) * HP, half:]
    out_ref[:, 0] = dot_table(lat_t_ref, gs_ref[...]).astype(BF).reshape(plan.n, plan.t, plan.d)

    @pl.when(q == plan.q - 1)
    def _():
        blocks, size = dw1_ref.shape[2:4]
        for wide, narrow in ((dm1_ref, dw1_ref), (dm2_ref, dw2_ref)):
            for g in range(2):
                for b in range(blocks):
                    re = slice(b * size, (b + 1) * size)
                    im = slice(half + b * size, half + (b + 1) * size)
                    narrow[0, g, b] = wide[g, re, re] + wide[g, im, im]
                    narrow[1, g, b] = wide[g, re, im] - wide[g, im, re]
        if e:
            ride_wait(*ride)


def spectral_back_call(
    plan, blocks, size, received, kept, lat, lat_t, m1t, m2t, passengers=(), collective_id=None
):
    riders = Riders(plan, passengers)
    small = (2, 2, blocks // 2, size, size)
    kept_spec = pl.BlockSpec((1, 2, 2 * HP, plan.d), lambda q: (q, 0, 0, 0))
    wide = (2, plan.d, plan.d)
    thin = (2, 1, plan.d)
    return pl.pallas_call(
        functools.partial(spectral_back_kernel, plan, riders),
        grid=(plan.q,),
        in_specs=[pair_block(plan, plan.t)]
        + [kept_spec] * 4
        + [whole(lat.shape), whole(lat_t.shape), whole(wide), whole(wide)]
        + riders.specs(),
        out_specs=[
            pair_block(plan, plan.t),
            whole(small),
            whole(small),
            whole(thin),
            whole(thin),
        ]
        + riders.specs(),
        out_shape=[
            jax.ShapeDtypeStruct((plan.n, plan.q, plan.t, plan.d), BF),
            jax.ShapeDtypeStruct(small, F32),
            jax.ShapeDtypeStruct(small, F32),
            jax.ShapeDtypeStruct(thin, F32),
            jax.ShapeDtypeStruct(thin, F32),
        ]
        + riders.shapes(),
        scratch_shapes=[
            pltpu.VMEM(wide, F32),
            pltpu.VMEM(wide, F32),
            pltpu.VMEM((4 * HP, plan.d), BF),
            pltpu.VMEM((2 * HP, plan.d), BF),
        ]
        + riders.scratch(),
        compiler_params=params(collective_id),
        cost_estimate=cost(1e9, 1e6),
        name="spectral_backward",
    )(received, *kept, lat, lat_t, m1t, m2t, *riders.arrays)


def last_kernel(
    plan,
    scale_ref,
    tok_ref,
    gx_ref,
    in_ref,
    gain_ref,
    lon_t_ref,
    perm_t_ref,
    *rest,
):
    out_ref, vec_ref, rows_ref = rest[-3:]
    i = pl.program_id(0)

    @pl.when(i == 0)
    def _():
        vec_ref[...] = jnp.zeros_like(vec_ref)
        deinterleave(plan, perm_t_ref, in_ref, rows_ref)

    for u in range(plan.rb):
        keep = jnp.where(scale_ref[i * plan.rb + u] > 0.0, 1.0, 0.0)
        unit, rstd = norm_parts(tok_ref[0, u].astype(F32))
        gx = gx_ref[u].astype(F32)
        grad = gx + dot_table(lon_t_ref, rows_ref[i * plan.rb + u])
        vec_ref[0:1] += jnp.sum(grad * unit, 0, keepdims=True) * keep
        vec_ref[1:2] += jnp.sum(grad, 0, keepdims=True) * keep
        out_ref[0, u] = (gx + norm_back(grad, unit, rstd, gain_ref[...])) * keep


def last_call(plan, s, scales, tokens, gx, received, gain, earlier):
    operands = [scales, tokens, gx, received, gain, plan.lon_t, plan.perm_t]
    in_specs = [
        SMEM,
        row_block(plan, s),
        own_block(plan),
        whole((plan.pairs, plan.t, plan.d)),
        whole((1, plan.d)),
        whole((2, plan.w, plan.ki)),
        whole(plan.perm_t.shape),
    ]
    aliases = {}
    if earlier is not None:
        aliases = {len(operands): 0}
        operands.append(earlier)
        in_specs.append(ANY)
    return pl.pallas_call(
        functools.partial(last_kernel, plan),
        grid=(plan.chunks,),
        in_specs=in_specs,
        out_specs=[row_block(plan, s), whole((2, plan.d))],
        out_shape=[
            jax.ShapeDtypeStruct((plan.s, plan.r, plan.w, plan.d), F32),
            jax.ShapeDtypeStruct((2, plan.d), F32),
        ],
        scratch_shapes=[pltpu.VMEM((plan.r, plan.ki, plan.d), BF)],
        input_output_aliases=aliases,
        compiler_params=params(),
        cost_estimate=cost(1e9, 1e6),
        name="lon_backward",
    )(*operands)


def band_kernel(plan, in_ref, *rest):
    out_ref, tall = rest[-2:]
    mb = plan.mb
    height = 2 * plan.kw
    for src in range(plan.n):
        for t in range(plan.kk):
            k = src * plan.kk + t
            if k >= plan.kw:
                continue
            both = in_ref[src, t // 2].astype(F32)
            for p in range(2):
                at = ((t % 2) * 2 + p) * mb
                part = both[at : at + mb]
                for g in range(plan.d // 128):
                    tall[g, pl.ds(2 * k + p, mb, stride=height), :] = part[
                        :, g * 128 : (g + 1) * 128
                    ]
    for m in range(mb):
        for g in range(plan.d // 128):
            piece = tall[g, m * height : (m + 1) * height, :].astype(BF)
            out_ref[0, m, :, :, g * 128 : (g + 1) * 128] = piece.reshape(plan.kw, 2, 128)


def band_call(plan, s, received, earlier):
    shape = (plan.s, plan.mb, plan.kw, 2, plan.d)
    operands = [received]
    in_specs = [whole(received.shape)]
    aliases = {}
    if earlier is not None:
        aliases = {1: 0}
        operands.append(earlier)
        in_specs.append(ANY)
    return pl.pallas_call(
        functools.partial(band_kernel, plan),
        grid=(1,),
        in_specs=in_specs,
        out_specs=pl.BlockSpec((1,) + shape[1:], lambda i: (s, 0, 0, 0, 0)),
        out_shape=jax.ShapeDtypeStruct(shape, BF),
        scratch_shapes=[pltpu.VMEM((plan.d // 128, 2 * plan.mb * plan.kw, 128), F32)],
        input_output_aliases=aliases,
        compiler_params=params(),
        cost_estimate=cost(1e8, 1e6),
        name="band_output",
    )(*operands)


def every_peer(total, step_of):
    def body(step, carry):
        step_of(step)
        return carry

    lax.fori_loop(1, total, body, 0)


def place(lanes, index):
    return {"batch": index // lanes, "lat": lax.rem(index, lanes)}


def greet_all(total, lanes, me):
    barrier = pltpu.get_barrier_semaphore()

    def greet(step):
        pl.semaphore_signal(
            barrier,
            inc=1,
            device_id=place(lanes, lax.rem(me + step, total)),
            device_id_type=pl.DeviceIdType.MESH,
        )

    every_peer(total, greet)
    pl.semaphore_wait(barrier, total - 1)


def block_sum_kernel(total, lanes, xs, *rest):
    ins, outs, helds, sems = rest[:xs], rest[xs : 2 * xs], rest[2 * xs : 3 * xs], rest[3 * xs :]
    me = lax.axis_index("batch") * lanes + lax.axis_index("lat")
    greet_all(total, lanes, me)

    def part(a, step, peer):
        return pltpu.make_async_remote_copy(
            src_ref=ins[a].at[peer],
            dst_ref=helds[a].at[step],
            send_sem=sems[4 * a].at[step],
            recv_sem=sems[4 * a + 1].at[step],
            device_id=place(lanes, peer),
            device_id_type=pl.DeviceIdType.MESH,
        )

    def result(a, step, peer, slot):
        return pltpu.make_async_remote_copy(
            src_ref=outs[a].at[me],
            dst_ref=outs[a].at[slot],
            send_sem=sems[4 * a + 2].at[step],
            recv_sem=sems[4 * a + 3].at[step],
            device_id=place(lanes, peer),
            device_id_type=pl.DeviceIdType.MESH,
        )

    ahead = lambda step: lax.rem(me + step, total)
    behind = lambda step: lax.rem(me + total - step, total)
    for a in range(xs):
        every_peer(total, lambda step: part(a, step, ahead(step)).start())
    for a in range(xs):
        helds[a][0] = ins[a][me]
        every_peer(total, lambda step: part(a, step, behind(step)).wait_recv())
        outs[a][me] = jnp.sum(helds[a][...].astype(F32), 0).astype(outs[a].dtype)
        every_peer(total, lambda step: result(a, step, ahead(step), me).start())
    for a in range(xs):
        every_peer(total, lambda step: part(a, step, ahead(step)).wait_send())
        every_peer(total, lambda step: result(a, step, behind(step), behind(step)).wait_recv())
        every_peer(total, lambda step: result(a, step, ahead(step), me).wait_send())


def block_sum(total, lanes, xs, collective_id):
    vmem = pl.BlockSpec(memory_space=pltpu.VMEM)
    sems = [pltpu.SemaphoreType.DMA((total,))] * (4 * len(xs))
    return pl.pallas_call(
        functools.partial(block_sum_kernel, total, lanes, len(xs)),
        in_specs=[vmem] * len(xs),
        out_specs=[vmem] * len(xs),
        out_shape=[jax.ShapeDtypeStruct(x.shape, x.dtype) for x in xs],
        scratch_shapes=[pltpu.VMEM(x.shape, x.dtype) for x in xs] + sems,
        compiler_params=pltpu.CompilerParams(
            collective_id=collective_id, has_side_effects=True, vmem_limit_bytes=VMEM_BYTES
        ),
        cost_estimate=cost(1e8, 1e6),
        name="block_sum",
    )(*xs)


def pack(total, parts, dtype, rows):
    flat = jnp.concatenate([x.reshape(-1).astype(dtype) for x in parts])
    unit = total * rows * 128
    padded = -(-flat.shape[0] // unit) * unit
    return jnp.pad(flat, (0, padded - flat.shape[0])).reshape(total, -1, 128)


def unpack(packed, parts):
    flat = packed.reshape(-1).astype(F32)
    out, at = [], 0
    for x in parts:
        out.append(flat[at : at + x.size].reshape(x.shape))
        at += x.size
    return out


def whole_sum_kernel(total, lanes, x_ref, out_ref, held, send, recv):
    me = lax.axis_index("batch") * lanes + lax.axis_index("lat")
    greet_all(total, lanes, me)

    def part(step, peer):
        return pltpu.make_async_remote_copy(
            src_ref=x_ref,
            dst_ref=held.at[step],
            send_sem=send.at[step],
            recv_sem=recv.at[step],
            device_id=place(lanes, peer),
            device_id_type=pl.DeviceIdType.MESH,
        )

    ahead = lambda step: lax.rem(me + step, total)
    every_peer(total, lambda step: part(step, ahead(step)).start())
    held[0] = x_ref[...]
    every_peer(total, lambda step: part(step, ahead(step)).wait_recv())
    out_ref[...] = jnp.sum(held[...], 0)
    every_peer(total, lambda step: part(step, ahead(step)).wait_send())


def whole_sum(total, lanes, x, collective_id):
    sems = [pltpu.SemaphoreType.DMA((total,))] * 2
    return pl.pallas_call(
        functools.partial(whole_sum_kernel, total, lanes),
        in_specs=[pl.BlockSpec(memory_space=pltpu.VMEM)],
        out_specs=pl.BlockSpec(memory_space=pltpu.VMEM),
        out_shape=jax.ShapeDtypeStruct(x.shape, x.dtype),
        scratch_shapes=[pltpu.VMEM((total,) + x.shape, x.dtype)] + sems,
        compiler_params=pltpu.CompilerParams(
            collective_id=collective_id, has_side_effects=True, vmem_limit_bytes=VMEM_BYTES
        ),
        cost_estimate=cost(1e8, 1e6),
        name="whole_sum",
    )(x)


def exchange(x):
    return lax.all_to_all(x, "lat", split_axis=0, concat_axis=0, tiled=True)


def on_device(
    bands,
    tokens,
    cotangent,
    sample_weight,
    row_count,
    band_count,
    norm1_gain,
    norm1_bias,
    spec_w1,
    spec_b1,
    spec_w2,
    spec_b2,
    norm2_gain,
    norm2_bias,
    fc1_weight,
    fc1_bias,
    fc2_weight,
    fc2_bias,
):
    lane = lax.axis_index("lat")
    n = lax.axis_size("lat")
    samples, row_slots, width, channels = tokens.shape
    blocks, size = spec_w1.shape[1], spec_w1.shape[2]
    plan = Plan(n, samples, row_slots, width, channels, bands)
    wb1, wb2 = wide_bias(spec_b1), wide_bias(spec_b2)
    row = lambda v: v.reshape(1, -1)
    vectors = (row(norm1_gain), row(norm1_bias), row(norm2_gain), row(norm2_bias))
    own_rows = jnp.sum(jnp.where(jnp.arange(n) == lane, row_count, 0))
    held = jnp.arange(row_slots) < own_rows
    scales = sample_weight.astype(F32)[:, None] * 0.5 * held[None, :].astype(F32)
    slot_step = jnp.arange(plan.kp)
    valid = ((slot_step < plan.kk) & (lane * plan.kk + slot_step < plan.kw)).astype(F32)
    grouped = (n, plan.q, plan.t, channels)
    listed = (plan.pairs, plan.t, channels)

    ids = itertools.count()
    spread = (-1,) + grouped

    def spectral_forward(x, passengers=()):
        collective_id = next(ids) if passengers else None
        out = spectral_call(
            plan, valid, x, lat, lat_t, slots, m1, wb1, m2, wb2, passengers, collective_id
        )
        forward.append(out)
        return out[7:]

    def feed(s, back, sums, passengers):
        out = feed_call(
            plan,
            s,
            scales[s],
            tokens,
            cotangent,
            back.reshape(listed),
            vectors,
            fc1_weight,
            row(fc1_bias),
            fc2_weight,
            row(fc2_bias),
            sums,
            s == samples - 1,
            passengers,
            next(ids),
        )
        feeds.append(out)
        return out[7:]

    def backward(s, grads, passengers=()):
        out = spectral_back_call(
            plan,
            blocks,
            size,
            grads,
            forward[s][2:6],
            lat,
            lat_t,
            m1t,
            m2t,
            passengers,
            next(ids) if passengers else None,
        )
        spectral.append(out)
        return out[0], out[5:]

    forward, feeds, spectral, band_parts, grads, lon_grads = [], [], [], {}, {}, {}
    sent = first_call(plan, 0, 1, tokens, *vectors[:2])[0].reshape(spread)
    tables = Tables(plan, blocks, size)
    extra = tables.operands(row_count, band_count, spec_w1, spec_w2)
    others, lat, lat_t, slots, m1, m2, m1t, m2t, spectra = first_call(
        plan, 1, samples - 1, tokens, *vectors[:2], [(sent, 0)], next(ids), tables, extra
    )
    others = others.reshape(spread)
    (spectra,) = spectral_forward(spectra, [(others, 0)])
    (back,) = spectral_forward(spectra, [(forward[0][0], None)])
    for s in range(samples):
        sums = (feeds[-1][3], feeds[-1][4]) if s else None
        kinds, passengers = [], []
        if s + 1 < samples:
            kinds.append("back")
            passengers.append((forward[s + 1][0], None))
        if s + 2 < samples:
            kinds.append("spectra")
            passengers.append((others, s + 1))
        if s >= 1:
            kinds.append("grads")
            passengers.append((feeds[s - 1][1].reshape(grouped), None))
        if s >= 2:
            kinds.append("lon")
            lon, _ = backward(s - 2, grads[s - 2])
            passengers.append((lon, None))
        if s + 1 < samples:
            kinds.append("band")
            passengers.append((forward[s][1], None))
        arrived = dict(zip(kinds, feed(s, back, sums, passengers)))
        back = arrived.get("back")
        if s + 2 < samples:
            spectral_forward(arrived["spectra"])
        if s + 1 < samples:
            band_parts[s] = arrived["band"]
        if s >= 1:
            grads[s - 1] = arrived["grads"]
        if s >= 2:
            lon_grads[s - 2] = arrived["lon"]
    cores = [[j, j + 1] for j in range(0, n, 2)]
    chips = [list(range(c, n, 2)) for c in range(2)]
    after = lambda x, y: lax.optimization_barrier((x, y))[0]

    def last(s, earlier):
        return last_call(
            plan,
            s,
            scales[s],
            tokens,
            feeds[s][2],
            lon_grads[s].reshape(listed),
            vectors[0],
            earlier,
        )

    grads[samples - 1] = exchange(feeds[-1][1].reshape(grouped))
    large = lax.psum_scatter(
        feeds[-1][3], "lat", scatter_dimension=0, axis_index_groups=cores, tiled=True
    )
    tokens_grad, vec = last(0, None)
    finals = [vec]
    large = after(large, vec)
    grads[samples - 2] = after(grads[samples - 2], large)
    large = lax.psum_scatter(large, "batch", scatter_dimension=1, tiled=True)
    for s in range(samples - 2, samples):
        missing = [p for p in range(samples) if p not in band_parts][:1]
        lon, got = backward(s, grads[s], [(forward[p][1], None) for p in missing])
        for p, part in zip(missing, got):
            band_parts[p] = part
        lon_grads[s] = exchange(lon)
    large = after(large, spectral[-1][3])
    large = lax.psum(large, "lat", axis_index_groups=chips)

    spectrum = None
    for s in range(samples):
        if s:
            tokens_grad, vec = last(s, tokens_grad)
            finals.append(vec)
        spectrum = band_call(plan, s, band_parts[s], spectrum)
    mixed = jnp.stack([f[0] for f in feeds])

    add = lambda parts: functools.reduce(jnp.add, parts)
    devices = lax.axis_size("batch") * n
    feed_vec = add([f[6] for f in feeds])
    block_grad = lambda i: add([b[i] for b in spectral]).reshape(2, blocks, size, size)
    zeros = jnp.sum(add([f[6] for f in forward]))
    small = [
        feed_vec[1],
        feed_vec[2],
        add([f[5] for f in feeds]),
        feed_vec[0],
        narrow_bias(add([b[3] for b in spectral]), blocks, size),
        narrow_bias(add([b[4] for b in spectral]), blocks, size),
        zeros.reshape(1),
    ]
    blocky = [block_grad(1), block_grad(2)]
    packed = [pack(devices, blocky, BF, 16), pack(devices, small, F32, 8)]
    packed = block_sum(devices, n, packed, next(ids))
    large = after(large, packed[1])
    blocky = unpack(packed[0], blocky)
    small = unpack(packed[1], small)
    last_vec = whole_sum(devices, n, add(finals), next(ids))
    large = lax.all_gather(large, "batch", axis=1, tiled=True)
    large = after(large, last_vec)
    large = lax.all_gather(large, "lat", axis=0, axis_index_groups=cores, tiled=True)
    large = (large[0].astype(F32).T, large[1].astype(F32))
    zero_fraction = small[6][0] / (lax.axis_size("batch") * samples * H * plan.kw * 2 * channels)
    return (
        mixed,
        spectrum.transpose(0, 1, 3, 2, 4),
        tokens_grad,
        last_vec[0],
        last_vec[1],
        blocky[0],
        small[4],
        blocky[1],
        small[5],
        small[0],
        small[1],
        large[0],
        small[2].reshape(-1),
        large[1],
        small[3],
        zero_fraction,
    )


def solution(mesh):
    rows = P("batch", "lat", None, None)
    in_specs = (rows, rows, P("batch")) + (P(),) * 14
    out_specs = (rows, P("batch", "lat", None, None, None), rows) + (P(),) * 13
    lanes = mesh.shape["lat"]

    def run(tokens, cotangent, *rest):
        row_slots = tokens.shape[1] // lanes
        return jax.shard_map(
            functools.partial(on_device, row_slots + 1),
            mesh=mesh,
            in_specs=in_specs,
            out_specs=out_specs,
            check_vma=False,
        )(tokens, cotangent, *rest)

    return run
```

```python
import functools
import itertools
import math

import jax
import jax.numpy as jnp
import numpy as np
from jax import lax
from jax.experimental import pallas as pl
from jax.experimental.pallas import tpu as pltpu
from jax.sharding import PartitionSpec as P

H = 90
HP = 96

NORM_EPS = 1e-06
SHRINK_LAMBDA = 0.01
SHRINK_SOFTNESS = 0.1
INV_ROOT_TAU = 1.0 / math.sqrt(2.0 * math.pi)
BF = jnp.bfloat16
F32 = jnp.float32
VMEM_BYTES = 64 * 1024 * 1024


def dot(a, b):
    return jnp.dot(a, b, preferred_element_type=F32)


def dot_nt(a, b):
    return lax.dot_general(a, b, (((1,), (1,)), ((), ())), preferred_element_type=F32)


def dot_tn(a, b):
    return lax.dot_general(a, b, (((0,), (0,)), ((), ())), preferred_element_type=F32)


def dot_table(table_ref, x):
    return dot(table_ref[0], x) + dot(table_ref[1], x)


def two_parts(table):
    high = table.astype(BF)
    return high, (table - high.astype(table.dtype)).astype(BF)


def norm_parts(x):
    mean = jnp.mean(x, -1, keepdims=True)
    centred = x - mean
    rstd = lax.rsqrt(jnp.mean(centred * centred, -1, keepdims=True) + NORM_EPS)
    return centred * rstd, rstd


def norm_back(grad, unit, rstd, gain):
    e = grad * gain
    return rstd * (
        e - jnp.mean(e, -1, keepdims=True) - unit * jnp.mean(e * unit, -1, keepdims=True)
    )


def gauss_parts(v):
    d = 1.0 + jnp.abs(v) * (0.3275911 / math.sqrt(2.0))
    t = pl.reciprocal(d, approx=True)
    e = jnp.exp2(v * v * (-0.5 * math.log2(math.e)))
    poly = 1.061405429 * 0.5
    for c in (-1.453152027, 1.421413741, -0.284496736, 0.254829592):
        poly = poly * t + 0.5 * c
    tail = poly * t * e
    cdf = jnp.where(v >= 0.0, 1.0 - tail, tail)
    return cdf, v * e * INV_ROOT_TAU


def gelu_both(v):
    cdf, slope_part = gauss_parts(v)
    return v * cdf, cdf + slope_part


def shrink_both(u):
    a = jnp.maximum(jnp.abs(u) - SHRINK_LAMBDA, 0.0)
    d = a + SHRINK_SOFTNESS
    t = pl.reciprocal(d, approx=True)
    t = t * (2.0 - d * t)
    size = a * a * t
    value = jnp.where(u >= 0.0, size, -size)
    slope = a * (a + 2.0 * SHRINK_SOFTNESS) * (t * t)
    return value, slope


class Plan:
    def __init__(self, n, samples, rows, width, channels, bands):
        self.n, self.s, self.r, self.w, self.d, self.mb = n, samples, rows, width, channels, bands
        self.kw = width // 2 + 1
        self.kk = -(-self.kw // n)
        self.kp = self.kk + self.kk % 2
        self.q = self.kp // 2
        self.rp = -(-rows // 4) * 4
        self.t = 4 * self.rp
        self.pairs = n * self.q
        self.ki = n * self.kp * 2
        self.rb = max(b for b in (4, 3, 2, 1) if rows % b == 0)
        self.chunks = rows // self.rb
        self.flat = self.rb * width
        self.flatp = max(-(-self.flat // 256) * 256, channels)
        self.bt = -(-4 * bands // 8) * 8
        j = np.arange(n)[:, None]
        t = np.arange(self.kp)[None, :]
        self.k_index = (j * self.kk + t).astype(np.int64)
        self.k_valid = (t < self.kk) & (self.k_index < self.kw)
        k = np.where(self.k_valid, self.k_index, 0).reshape(-1)
        ok = self.k_valid.reshape(-1).astype(np.float64)
        angle = 2.0 * np.pi * ((k[:, None] * np.arange(width)[None, :]) % width) / width
        scale = ok[:, None] / math.sqrt(width)
        fwd = np.stack([np.cos(angle) * scale, -np.sin(angle) * scale], 1).reshape(self.ki, width)
        factor = np.where((k == 0) | (2 * k == width), 1.0, 2.0)[:, None, None]
        both = (fwd.reshape(-1, 2, width) * factor).reshape(self.ki, width)
        self.lon = np.stack(two_parts(fwd))
        self.lon_both = np.stack(two_parts(both))
        self.lon_t = np.stack(two_parts(np.ascontiguousarray(fwd.T)))
        self.lon_both_t = np.stack(two_parts(np.ascontiguousarray(both.T)))
        perm = np.zeros((16, self.rp, rows, 16))
        for a in range(16):
            for r in range(rows):
                perm[a, r, r, a] = 1.0
        self.perm = perm.reshape(16 * self.rp, rows * 16).astype(BF)
        self.perm_t = np.ascontiguousarray(self.perm.T)


class Tables:
    def __init__(self, plan, blocks, size):
        self.plan, self.blocks, self.size = plan, blocks, size
        n, rp, mb = plan.n, plan.rp, plan.mb
        kh, h = np.arange(HP)[:, None], np.arange(HP)[None, :]
        angle = 2.0 * np.pi * (kh * h % H) / H
        weight = ((kh < H) & (h < H)) / math.sqrt(H)
        cosine, sine = np.cos(angle) * weight, np.sin(angle) * weight
        part = np.block([[cosine, sine], [-sine, cosine]])
        self.base = np.stack(two_parts(np.kron(np.eye(2), part)))
        col = np.arange(n * 4 * rp)
        group, step = col // rp % 4, col % rp
        self.columns = np.stack([col // (4 * rp), group * HP + step, step]).astype(np.int32)
        bt = plan.bt
        line = np.arange(n * bt)
        group, step = line % bt // mb, line % bt % mb
        step = np.where(group < 4, step, 1 << 20)
        lines = np.stack([line // bt, group * HP + step, step]).astype(np.int32)
        self.lines = lines[:, :, None]
        half = blocks // 2
        spots = np.zeros((half, size, half * size))
        for i in range(half):
            spots[i, :, i * size : (i + 1) * size] = np.eye(size)
        self.spots = spots.astype(BF)
        wide = 4 * HP
        d = plan.d
        shapes = [(2, wide, n * 4 * rp), (2, n * 4 * rp, wide), (n * bt, wide)] + [(2, d, d)] * 4
        self.shapes = [jax.ShapeDtypeStruct(x, BF) for x in shapes]

    def operands(self, row_count, band_count, spec_w1, spec_w2):
        return [
            row_count,
            band_count,
            spec_w1,
            spec_w2,
            self.base,
            self.columns[:, None, :],
            self.lines,
            self.spots,
        ]

    def in_specs(self):
        weight = (2, self.blocks, self.size, self.size)
        shapes = [weight, weight, self.base.shape, (3, 1, self.columns.shape[1])]
        shapes += [self.lines.shape, self.spots.shape]
        return [SMEM, SMEM] + [whole(x) for x in shapes]

    def out_specs(self):
        return [whole(x.shape) for x in self.shapes]

    def build(self, ins, outs):
        rows_ref, bands_ref, w1_ref, w2_ref, base_ref, col_ref, line_ref, spot_ref = ins
        lat_ref, lat_t_ref, slot_ref, m1_ref, m2_ref, m1t_ref, m2t_ref = outs
        n = self.plan.n

        def spread(counts_ref, owner):
            first = jnp.zeros(owner.shape, jnp.int32)
            held = jnp.zeros(owner.shape, jnp.int32)
            start = jnp.int32(0)
            for j in range(n):
                count = counts_ref[j]
                first = jnp.where(owner == j, start, first)
                held = jnp.where(owner == j, count, held)
                start = start + count
            return first, held

        first, held = spread(rows_ref, col_ref[0])
        target = jnp.where(col_ref[2] < held, col_ref[1] + first, -1)
        pick = lax.broadcasted_iota(jnp.int32, (4 * HP, target.shape[1]), 0) == target
        pick = jnp.where(pick, 1.0, 0.0).astype(BF)
        for part in range(2):
            full = dot(base_ref[part], pick)
            lat_ref[part] = full.astype(BF)
            lat_t_ref[part] = full.T.astype(BF)
        first, held = spread(bands_ref, line_ref[0])
        target = jnp.where(line_ref[2] < held, line_ref[1] + first, -1)
        pick = lax.broadcasted_iota(jnp.int32, (target.shape[0], 4 * HP), 1) == target
        slot_ref[...] = jnp.where(pick, 1.0, 0.0).astype(BF)
        half, size = self.blocks // 2, self.size
        mid = half * size
        for w_ref, m_ref, mt_ref in ((w1_ref, m1_ref, m1t_ref), (w2_ref, m2_ref, m2t_ref)):
            for g in range(2):
                for i in range(half):
                    low = slice(i * size, (i + 1) * size)
                    high = slice(mid + i * size, mid + (i + 1) * size)
                    re, im = w_ref[0, g * half + i], w_ref[1, g * half + i]
                    for ref, place_in, sign in ((m_ref, dot, 1.0), (mt_ref, dot_tn, -1.0)):
                        real = place_in(re, spot_ref[i]).astype(BF)
                        imag = place_in(im, spot_ref[i]) * sign
                        ref[g, low, :mid] = real
                        ref[g, high, mid:] = real
                        ref[g, low, mid:] = imag.astype(BF)
                        ref[g, high, :mid] = (-imag).astype(BF)


def wide_bias(bias):
    return bias.reshape(2, 2, -1).transpose(1, 0, 2).reshape(2, 1, -1)


def narrow_bias(wide, blocks, size):
    return wide.reshape(2, 2, -1).transpose(1, 0, 2).reshape(2, blocks, size)


def whole(shape):
    zeros = (0,) * len(shape)
    return pl.BlockSpec(shape, lambda *_: zeros)


def whole_once(shape):
    zeros = (0,) * len(shape)
    return pl.BlockSpec(shape, lambda *_: zeros, pipeline_mode=pl.Buffered(1))


SMEM = pl.BlockSpec(memory_space=pltpu.SMEM)
ANY = pl.BlockSpec(memory_space=pl.ANY)


def params(collective_id=None):
    if collective_id is None:
        return pltpu.CompilerParams(
            dimension_semantics=("arbitrary",), vmem_limit_bytes=VMEM_BYTES
        )
    return pltpu.CompilerParams(
        dimension_semantics=("arbitrary",),
        vmem_limit_bytes=VMEM_BYTES,
        collective_id=collective_id,
        has_side_effects=True,
    )


def ride_copy(n, me, src, dst, send, recv, e, step):
    peer = lax.rem(me + step, n)
    return pltpu.make_async_remote_copy(
        src_ref=src.at[peer],
        dst_ref=dst.at[me],
        send_sem=send.at[e, step],
        recv_sem=recv.at[e, step],
        device_id={"lat": peer},
        device_id_type=pl.DeviceIdType.MESH,
    )


def ride_arrival(n, me, src, dst, send, recv, e, step):
    peer = lax.rem(me + n - step, n)
    return pltpu.make_async_remote_copy(
        src_ref=src.at[peer],
        dst_ref=dst.at[peer],
        send_sem=send.at[e, step],
        recv_sem=recv.at[e, step],
        device_id={"lat": peer},
        device_id_type=pl.DeviceIdType.MESH,
    )


def ride_start(n, srcs, dsts, send, recv, own):
    me = lax.axis_index("lat")
    barrier = pltpu.get_barrier_semaphore()
    for step in range(1, n):
        pl.semaphore_signal(
            barrier,
            inc=1,
            device_id={"lat": lax.rem(me + step, n)},
            device_id_type=pl.DeviceIdType.MESH,
        )
    pl.semaphore_wait(barrier, n - 1)
    for e, (src, dst) in enumerate(zip(srcs, dsts)):
        for step in range(1, n):
            ride_copy(n, me, src, dst, send, recv, e, step).start()
        pltpu.make_async_copy(src.at[me], dst.at[me], own.at[e]).start()


def ride_wait(n, srcs, dsts, send, recv, own):
    me = lax.axis_index("lat")
    for e, (src, dst) in enumerate(zip(srcs, dsts)):
        pltpu.make_async_copy(src.at[me], dst.at[me], own.at[e]).wait()
        for step in range(1, n):
            ride_copy(n, me, src, dst, send, recv, e, step).wait_send()
            ride_arrival(n, me, src, dst, send, recv, e, step).wait_recv()


def cost(flops, size):
    return pl.CostEstimate(flops=int(flops), bytes_accessed=int(size), transcendentals=0)


def interleave(plan, perm_ref, rows_ref, out_ref):
    def body(c, carry):
        at = pl.multiple_of(c * 16, 16)
        block = rows_ref[:, pl.ds(at, 16), :].reshape(plan.r * 16, plan.d)
        mixed = dot(perm_ref[...], block).astype(BF)
        out_ref[pl.ds(c * 4, 4)] = mixed.reshape(4, plan.t, plan.d)
        return carry

    lax.fori_loop(0, plan.ki // 16, body, 0)


def deinterleave(plan, perm_t_ref, in_ref, rows_ref):
    def body(c, carry):
        at = pl.multiple_of(c * 16, 16)
        block = in_ref[pl.ds(c * 4, 4)].reshape(4 * plan.t, plan.d)
        rows = dot(perm_t_ref[...], block).astype(BF)
        rows_ref[:, pl.ds(at, 16), :] = rows.reshape(plan.r, 16, plan.d)
        return carry

    lax.fori_loop(0, plan.ki // 16, body, 0)


def interleave_out(plan, perm_ref, rows_ref, ring, sem, out_ref):
    def copy(c):
        return pltpu.make_async_copy(
            ring.at[lax.rem(c, 2)], out_ref.at[pl.ds(c * 4, 4)], sem.at[lax.rem(c, 2)]
        )

    def body(c, carry):
        @pl.when(c >= 2)
        def _():
            copy(c - 2).wait()

        at = pl.multiple_of(c * 16, 16)
        block = rows_ref[:, pl.ds(at, 16), :].reshape(plan.r * 16, plan.d)
        mixed = dot(perm_ref[...], block).astype(BF)
        ring[lax.rem(c, 2)] = mixed.reshape(4, plan.t, plan.d)
        copy(c).start()
        return carry

    lax.fori_loop(0, plan.ki // 16, body, 0)
    return [copy(plan.ki // 16 - 2), copy(plan.ki // 16 - 1)]


def ring_load(plan, in_ref, ring, sem, c):
    return pltpu.make_async_copy(
        in_ref.at[pl.ds(c * 4, 4)], ring.at[lax.rem(c, 2)], sem.at[lax.rem(c, 2)]
    )


def deinterleave_in(plan, perm_t_ref, in_ref, ring, sem, rows_ref):
    steps = plan.ki // 16

    def body(c, carry):
        ring_load(plan, in_ref, ring, sem, c).wait()
        at = pl.multiple_of(c * 16, 16)
        block = ring[lax.rem(c, 2)].reshape(4 * plan.t, plan.d)
        rows = dot(perm_t_ref[...], block).astype(BF)
        rows_ref[:, pl.ds(at, 16), :] = rows.reshape(plan.r, 16, plan.d)

        @pl.when(c + 2 < steps)
        def _():
            ring_load(plan, in_ref, ring, sem, c + 2).start()

        return carry

    lax.fori_loop(0, steps, body, 0)


class Riders:
    def __init__(self, plan, passengers):
        self.n = plan.n
        self.arrays = [a for a, _ in passengers]
        self.leads = [lead for _, lead in passengers]
        self.count = len(passengers)

    def shapes(self):
        return [
            jax.ShapeDtypeStruct(a.shape if lead is None else a.shape[1:], a.dtype)
            for a, lead in zip(self.arrays, self.leads)
        ]

    def specs(self):
        return [ANY] * self.count

    def scratch(self):
        if not self.count:
            return []
        dma = pltpu.SemaphoreType.DMA
        return [dma((self.count, self.n)), dma((self.count, self.n)), dma((self.count,))]

    def bind(self, srcs, dsts, sems):
        srcs = [r if lead is None else r.at[lead] for r, lead in zip(srcs, self.leads)]
        return (self.n, srcs, dsts) + tuple(sems)


def first_kernel(plan, riders, tables, tok_ref, vec_ref, lon_ref, perm_ref, *rest):
    e = riders.count
    t_in = 0 if tables is None else 8
    t_out = 0 if tables is None else 7
    t_ins, rest = rest[:t_in], rest[t_in:]
    srcs, rest = rest[:e], rest[e:]
    out_ref, rest = rest[0], rest[1:]
    t_outs, rest = rest[:t_out], rest[t_out:]
    dsts, rows_ref, sems = rest[:e], rest[e], rest[e + 1 :]
    i = pl.program_id(0)
    c = lax.rem(i, plan.chunks)
    if e:
        ride = riders.bind(srcs, dsts, sems)

        @pl.when(i == 0)
        def _():
            ride_start(*ride)

    for u in range(plan.rb):
        unit, _ = norm_parts(tok_ref[0, u].astype(F32))
        normed = (unit * vec_ref[0:1] + vec_ref[1:2]).astype(BF)
        rows_ref[c * plan.rb + u] = dot_table(lon_ref, normed).astype(BF)

    @pl.when(c == plan.chunks - 1)
    def _():
        interleave(plan, perm_ref, rows_ref, out_ref.at[0])

    @pl.when(i == pl.num_programs(0) - 1)
    def _():
        if tables is not None:
            tables.build(t_ins, t_outs)
        if e:
            ride_wait(*ride)


def row_block(plan, s):
    return pl.BlockSpec((1, plan.rb, plan.w, plan.d), lambda i: (s, i, 0, 0))


def own_block(plan):
    return pl.BlockSpec((plan.rb, plan.w, plan.d), lambda i: (i, 0, 0))


def first_call(
    plan, start, count, tokens, vectors, passengers=(), collective_id=None, tables=None, extra=()
):
    shape = (plan.pairs, plan.t, plan.d)
    chunks = plan.chunks
    riders = Riders(plan, passengers)
    return pl.pallas_call(
        functools.partial(first_kernel, plan, riders, tables),
        grid=(count * chunks,),
        in_specs=[
            pl.BlockSpec(
                (1, plan.rb, plan.w, plan.d),
                lambda i: (start + i // chunks, lax.rem(i, chunks), 0, 0),
            ),
            whole((8, plan.d)),
            whole((2, plan.ki, plan.w)),
            whole(plan.perm.shape),
        ]
        + (tables.in_specs() if tables else [])
        + riders.specs(),
        out_specs=[pl.BlockSpec((1,) + shape, lambda i: (i // chunks, 0, 0, 0))]
        + (tables.out_specs() if tables else [])
        + riders.specs(),
        out_shape=[jax.ShapeDtypeStruct((count,) + shape, BF)]
        + (tables.shapes if tables else [])
        + riders.shapes(),
        scratch_shapes=[pltpu.VMEM((plan.r, plan.ki, plan.d), BF)] + riders.scratch(),
        compiler_params=params(collective_id),
        cost_estimate=cost(9e9 * count, 8e6 * count),
        name="lon_forward",
    )(tokens, vectors, plan.lon, plan.perm, *extra, *riders.arrays)


def spectral_kernel(
    plan,
    riders,
    valid_ref,
    in_ref,
    lat_ref,
    lat_t_ref,
    slot_ref,
    m1_ref,
    b1_ref,
    m2_ref,
    b2_ref,
    *rest,
):
    e = riders.count
    srcs, rest = rest[:e], rest[e:]
    back_ref, band_ref, spec_ref, hid_ref, slope1_ref, slope2_ref, zero_ref = rest[:7]
    dsts, shr_ref, sems = rest[7 : 7 + e], rest[7 + e], rest[8 + e :]
    q = pl.program_id(0)
    half = plan.d // 2
    if e:
        ride = riders.bind(srcs, dsts, sems)

        @pl.when(q == 0)
        def _():
            ride_start(*ride)

    @pl.when(q == 0)
    def _():
        zero_ref[...] = jnp.zeros_like(zero_ref)

    x = in_ref[:, 0].reshape(plan.n * plan.t, plan.d)
    spec = dot_table(lat_ref, x).astype(BF)
    ok = (lax.broadcasted_iota(jnp.int32, (HP, 1), 0) < H).astype(F32)
    for g in range(2):
        lanes = slice(g * half, (g + 1) * half)
        for a in range(2):
            top = a * 2 * HP
            spec_ref[0, g, a * HP : (a + 1) * HP, :half] = spec[top : top + HP, lanes]
            spec_ref[0, g, a * HP : (a + 1) * HP, half:] = spec[top + HP : top + 2 * HP, lanes]
        u1 = dot(spec_ref[0, g], m1_ref[g]) + b1_ref[g]
        hidden, slope = gelu_both(u1)
        hid_ref[0, g] = hidden.astype(BF)
        slope1_ref[0, g] = slope.astype(BF)
        u2 = dot(hid_ref[0, g], m2_ref[g]) + b2_ref[g]
        small = (jnp.abs(u2) <= SHRINK_LAMBDA).astype(F32)
        for a in range(2):
            part = small[a * HP : (a + 1) * HP] * ok
            zero_ref[...] += jnp.sum(part, 0, keepdims=True) * valid_ref[q * 2 + a]
        value, slope = shrink_both(u2)
        slope2_ref[0, g] = slope.astype(BF)
        value = value.astype(BF)
        for a in range(2):
            top = a * 2 * HP
            shr_ref[top : top + HP, lanes] = value[a * HP : (a + 1) * HP, :half]
            shr_ref[top + HP : top + 2 * HP, lanes] = value[a * HP : (a + 1) * HP, half:]
    shrunk = shr_ref[...]
    back_ref[:, 0] = dot_table(lat_t_ref, shrunk).astype(BF).reshape(plan.n, plan.t, plan.d)
    band = dot(slot_ref[...], shrunk).astype(BF)
    band_ref[:, 0] = band.reshape(plan.n, plan.bt, plan.d)
    if e:

        @pl.when(q == plan.q - 1)
        def _():
            ride_wait(*ride)


def pair_block(plan, rows):
    return pl.BlockSpec((plan.n, 1, rows, plan.d), lambda q: (0, q, 0, 0))


def spectral_call(
    plan, valid, received, lat, lat_t, slots, m1, b1, m2, b2, passengers=(), collective_id=None
):
    riders = Riders(plan, passengers)
    kept = (plan.q, 2, 2 * HP, plan.d)
    kept_spec = pl.BlockSpec((1, 2, 2 * HP, plan.d), lambda q: (q, 0, 0, 0))
    kept_shape = jax.ShapeDtypeStruct(kept, BF)
    rows = plan.bt
    return pl.pallas_call(
        functools.partial(spectral_kernel, plan, riders),
        grid=(plan.q,),
        in_specs=[
            SMEM,
            pair_block(plan, plan.t),
            whole(lat.shape),
            whole(lat_t.shape),
            whole(slots.shape),
            whole(m1.shape),
            whole(b1.shape),
            whole(m2.shape),
            whole(b2.shape),
        ]
        + riders.specs(),
        out_specs=[
            pair_block(plan, plan.t),
            pair_block(plan, rows),
            kept_spec,
            kept_spec,
            kept_spec,
            kept_spec,
            whole((1, plan.d)),
        ]
        + riders.specs(),
        out_shape=[
            jax.ShapeDtypeStruct((plan.n, plan.q, plan.t, plan.d), BF),
            jax.ShapeDtypeStruct((plan.n, plan.q, rows, plan.d), BF),
            kept_shape,
            kept_shape,
            kept_shape,
            kept_shape,
            jax.ShapeDtypeStruct((1, plan.d), F32),
        ]
        + riders.shapes(),
        scratch_shapes=[pltpu.VMEM((4 * HP, plan.d), BF)] + riders.scratch(),
        compiler_params=params(collective_id),
        cost_estimate=cost(20e9, 25e6),
        name="spectral_forward",
    )(valid, received, lat, lat_t, slots, m1, b1, m2, b2, *riders.arrays)


def feed_kernel(
    plan,
    first,
    final,
    riders,
    tiles,
    scale_ref,
    tok_ref,
    cot_ref,
    recv_ref,
    par_ref,
    lon_t_ref,
    lon_ref,
    perm_ref,
    perm_t_ref,
    w1_ref,
    b1_ref,
    w2_ref,
    *rest,
):
    e = riders.count
    srcs, rest = rest[:e], rest[e:]
    if first:
        in1_ref = in2_ref = None
    else:
        in1_ref, in2_ref = rest[:2]
        rest = rest[2:]
    mixed_ref, send_ref, gx_ref, out1_ref, out2_ref, db1_ref, vec_ref = rest[:7]
    dsts, rest = rest[7 : 7 + e], rest[7 + e :]
    (
        dw1,
        dw2,
        ring,
        rows_ref,
        x1_ref,
        xn,
        xn_t,
        gm,
        gm_t,
        act,
        gz,
        down,
        up,
        sem,
        ring_sem,
        *ride_sems,
    ) = rest
    i = pl.program_id(0)
    last = plan.chunks - 1
    tile = act.shape[1]
    flat = plan.flat
    ride = riders.bind(srcs, dsts, ride_sems)

    @pl.when(i == 0)
    def _():
        for c in range(2):
            ring_load(plan, recv_ref, ring, ring_sem, c).start()
        if not first:
            pltpu.make_async_copy(in1_ref, dw1, sem.at[1]).start()
            pltpu.make_async_copy(in2_ref, dw2, sem.at[2]).start()
        ride_start(*ride)
        if first:
            dw1[...] = jnp.zeros_like(dw1)
            dw2[...] = jnp.zeros_like(dw2)
        db1_ref[...] = jnp.zeros_like(db1_ref)
        vec_ref[...] = jnp.zeros_like(vec_ref)
        if plan.flatp > flat:
            pad = jnp.zeros((plan.flatp - flat, tile), BF)
            for ref in (act, gz):
                ref[flat:, :] = pad
            pad = jnp.zeros((plan.flatp - flat, plan.d), F32)
            down[flat:, :] = pad
            up[flat:, :] = pad
        deinterleave_in(plan, perm_t_ref, recv_ref, ring, ring_sem, rows_ref)

    for u in range(plan.rb):
        span = slice(u * plan.w, (u + 1) * plan.w)
        x = tok_ref[0, u].astype(F32)
        unit, _ = norm_parts(x)
        filtered = dot_table(lon_t_ref, rows_ref[i * plan.rb + u])
        x1 = x + filtered + (unit * par_ref[0:1] + par_ref[1:2])
        x1_ref[u] = x1
        unit, _ = norm_parts(x1)
        down[span, :] = unit * par_ref[2:3] + par_ref[3:4]
        up[span, :] = cot_ref[0, u].astype(F32) * scale_ref[i * plan.rb + u]
    normed = down[...].astype(BF)
    xn[...] = normed[:flat]
    xn_t[...] = normed.T
    grads = up[...].astype(BF)
    gm[...] = grads[:flat]
    gm_t[...] = grads.T
    vec_ref[0:1] += jnp.sum(grads.astype(F32), 0, keepdims=True)
    down[...] = jnp.zeros_like(down)
    up[...] = jnp.zeros_like(up)

    if not first:

        @pl.when(i == 0)
        def _():
            pltpu.make_async_copy(in1_ref, dw1, sem.at[1]).wait()
            pltpu.make_async_copy(in2_ref, dw2, sem.at[2]).wait()

    def columns(t):
        return pl.ds(pl.multiple_of(t * tile, tile), tile)

    def body(t, carry):
        cols = columns(t)
        z = dot(xn[...], w1_ref[:, cols]) + b1_ref[:, cols]
        ga = dot_nt(gm[...], w2_ref[cols, :])
        hidden, slope = gelu_both(z)
        grad = ga * slope
        act[:flat, :] = hidden.astype(BF)
        gz[:flat, :] = grad.astype(BF)
        db1_ref[:, cols] += jnp.sum(grad, 0, keepdims=True)
        down[:flat, :] += dot(act[:flat, :], w2_ref[cols, :])
        up[:flat, :] += dot_nt(gz[:flat, :], w1_ref[:, cols])
        dw1[:, cols] += dot(xn_t[...], gz[...])
        dw2[:, cols] += dot(gm_t[...], act[...])
        return carry

    lax.fori_loop(0, tiles, body, 0)

    if not final:

        @pl.when(i == last)
        def _():
            pltpu.make_async_copy(dw1, out1_ref, sem.at[1]).start()
            pltpu.make_async_copy(dw2, out2_ref, sem.at[2]).start()

    for u in range(plan.rb):
        span = slice(u * plan.w, (u + 1) * plan.w)
        x1 = x1_ref[u]
        scale = scale_ref[i * plan.rb + u]
        keep = jnp.where(scale > 0.0, 1.0, 0.0)
        mixed_ref[u] = ((x1 + down[span, :] + par_ref[4:5]) * keep).astype(BF)
        unit, rstd = norm_parts(x1)
        grad = up[span, :]
        vec_ref[1:2] += jnp.sum(grad * unit, 0, keepdims=True)
        vec_ref[2:3] += jnp.sum(grad, 0, keepdims=True)
        gx = cot_ref[0, u].astype(F32) * scale + norm_back(grad, unit, rstd, par_ref[2:3])
        gx_ref[u] = gx.astype(gx_ref.dtype)
        rows_ref[i * plan.rb + u] = dot_table(lon_ref, gx.astype(BF)).astype(BF)

    if plan.flatp > flat:
        down[flat:, :] = jnp.zeros((plan.flatp - flat, plan.d), F32)
        up[flat:, :] = jnp.zeros((plan.flatp - flat, plan.d), F32)

    @pl.when(i == last)
    def _():
        stores = interleave_out(plan, perm_ref, rows_ref, ring, ring_sem, send_ref)
        if final:
            stage = (act, xn_t, gz, gm_t)
            pending = {}
            for t in range(2 * tiles):
                side = t % 4
                if side in pending:
                    pending.pop(side).wait()
                cols = slice(t // 2 * tile, (t // 2 + 1) * tile)
                if t % 2 == 0:
                    held = stage[side].at[: plan.d, :]
                    held[...] = dw1[:, cols].astype(BF)
                    out = out1_ref.at[:, cols]
                else:
                    held = stage[side].at[:tile, : plan.d]
                    held[...] = dw2[:, cols].astype(BF).T
                    out = out2_ref.at[cols]
                pending[side] = pltpu.make_async_copy(held, out, sem.at[1 + side])
                pending[side].start()
            for copy in pending.values():
                copy.wait()
        else:
            pltpu.make_async_copy(dw1, out1_ref, sem.at[1]).wait()
            pltpu.make_async_copy(dw2, out2_ref, sem.at[2]).wait()
        for store in stores:
            store.wait()
        ride_wait(*ride)


def feed_call(
    plan, s, scales, tokens, cotangent, received, vectors, w1, b1, w2, sums, final, passengers,
    collective_id
):
    first = sums is None
    ff = w1.shape[1]
    tile = 512
    d, flat = plan.d, plan.flat
    flatp = plan.flatp
    shape = (plan.pairs, plan.t, d)
    riders = Riders(plan, passengers)
    in_specs = [
        SMEM,
        row_block(plan, s),
        row_block(plan, s),
        ANY,
        whole((8, d)),
        whole((2, plan.w, plan.ki)),
        whole((2, plan.ki, plan.w)),
        whole(plan.perm.shape),
        whole(plan.perm_t.shape),
        whole_once((d, ff)),
        whole((1, ff)),
        whole_once((ff, d)),
    ] + riders.specs()
    operands = [
        scales,
        tokens,
        cotangent,
        received,
        vectors,
        plan.lon_both_t,
        plan.lon_both,
        plan.perm,
        plan.perm_t,
        w1,
        b1,
        w2,
        *riders.arrays,
    ]
    aliases = {}
    if not first:
        if not final:
            aliases = {len(operands): 3, len(operands) + 1: 4}
        in_specs += [ANY, ANY]
        operands += list(sums)
    if final:
        wides = [jax.ShapeDtypeStruct((d, ff), BF), jax.ShapeDtypeStruct((ff, d), BF)]
    else:
        wides = [jax.ShapeDtypeStruct((d, ff), F32)] * 2
    return pl.pallas_call(
        functools.partial(feed_kernel, plan, first, final, riders, ff // tile),
        grid=(plan.chunks,),
        in_specs=in_specs,
        out_specs=[
            own_block(plan),
            ANY,
            own_block(plan),
            ANY,
            ANY,
            whole((1, ff)),
            whole((8, d)),
        ]
        + riders.specs(),
        out_shape=[
            jax.ShapeDtypeStruct((plan.r, plan.w, d), BF),
            jax.ShapeDtypeStruct(shape, BF),
            jax.ShapeDtypeStruct((plan.r, plan.w, d), BF),
            *wides,
            jax.ShapeDtypeStruct((1, ff), F32),
            jax.ShapeDtypeStruct((8, d), F32),
        ]
        + riders.shapes(),
        scratch_shapes=[
            pltpu.VMEM((d, ff), F32),
            pltpu.VMEM((d, ff), F32),
            pltpu.VMEM((2, 4, plan.t, d), BF),
            pltpu.VMEM((plan.r, plan.ki, d), BF),
            pltpu.VMEM((plan.rb, plan.w, d), F32),
            pltpu.VMEM((flat, d), BF),
            pltpu.VMEM((d, flatp), BF),
            pltpu.VMEM((flat, d), BF),
            pltpu.VMEM((d, flatp), BF),
            pltpu.VMEM((flatp, tile), BF),
            pltpu.VMEM((flatp, tile), BF),
            pltpu.VMEM((flatp, d), F32),
            pltpu.VMEM((flatp, d), F32),
            pltpu.SemaphoreType.DMA((5,)),
            pltpu.SemaphoreType.DMA((2,)),
        ]
        + riders.scratch(),
        input_output_aliases=aliases,
        compiler_params=params(collective_id),
        cost_estimate=cost(70e9, 60e6),
        name="feed_forward",
    )(*operands)


def spectral_back_kernel(
    plan,
    riders,
    in_ref,
    spec_ref,
    hid_ref,
    slope1_ref,
    slope2_ref,
    lat_ref,
    lat_t_ref,
    m1t_ref,
    m2t_ref,
    *rest,
):
    e = riders.count
    srcs, rest = rest[:e], rest[e:]
    out_ref, dw1_ref, dw2_ref, db1_ref, db2_ref = rest[:5]
    dsts, rest = rest[5 : 5 + e], rest[5 + e :]
    dm1_ref, dm2_ref, gs_ref, gu_ref = rest[:4]
    q = pl.program_id(0)
    half = plan.d // 2
    if e:
        ride = riders.bind(srcs, dsts, rest[4:])

        @pl.when(q == 0)
        def _():
            ride_start(*ride)

    @pl.when(q == 0)
    def _():
        dm1_ref[...] = jnp.zeros_like(dm1_ref)
        dm2_ref[...] = jnp.zeros_like(dm2_ref)
        db1_ref[...] = jnp.zeros_like(db1_ref)
        db2_ref[...] = jnp.zeros_like(db2_ref)

    x = in_ref[:, 0].reshape(plan.n * plan.t, plan.d)
    grad = dot_table(lat_ref, x).astype(BF)
    for g in range(2):
        lanes = slice(g * half, (g + 1) * half)
        for a in range(2):
            top = a * 2 * HP
            gu_ref[a * HP : (a + 1) * HP, :half] = grad[top : top + HP, lanes]
            gu_ref[a * HP : (a + 1) * HP, half:] = grad[top + HP : top + 2 * HP, lanes]
        gu2 = gu_ref[...].astype(F32) * slope2_ref[0, g].astype(F32)
        db2_ref[g] += jnp.sum(gu2, 0, keepdims=True)
        gu2 = gu2.astype(BF)
        dm2_ref[g] += dot_tn(hid_ref[0, g], gu2)
        gu1 = (dot(gu2, m2t_ref[g]) * slope1_ref[0, g].astype(F32)).astype(BF)
        db1_ref[g] += jnp.sum(gu1.astype(F32), 0, keepdims=True)
        dm1_ref[g] += dot_tn(spec_ref[0, g], gu1)
        gs = dot(gu1, m1t_ref[g]).astype(BF)
        for a in range(2):
            top = a * 2 * HP
            gs_ref[top : top + HP, lanes] = gs[a * HP : (a + 1) * HP, :half]
            gs_ref[top + HP : top + 2 * HP, lanes] = gs[a * HP : (a + 1) * HP, half:]
    out_ref[:, 0] = dot_table(lat_t_ref, gs_ref[...]).astype(BF).reshape(plan.n, plan.t, plan.d)

    @pl.when(q == plan.q - 1)
    def _():
        blocks, size = dw1_ref.shape[2:4]
        for wide, narrow in ((dm1_ref, dw1_ref), (dm2_ref, dw2_ref)):
            for g in range(2):
                for b in range(blocks):
                    re = slice(b * size, (b + 1) * size)
                    im = slice(half + b * size, half + (b + 1) * size)
                    narrow[0, g, b] = wide[g, re, re] + wide[g, im, im]
                    narrow[1, g, b] = wide[g, re, im] - wide[g, im, re]
        if e:
            ride_wait(*ride)


def spectral_back_call(
    plan, blocks, size, received, kept, lat, lat_t, m1t, m2t, passengers=(), collective_id=None
):
    riders = Riders(plan, passengers)
    small = (2, 2, blocks // 2, size, size)
    kept_spec = pl.BlockSpec((1, 2, 2 * HP, plan.d), lambda q: (q, 0, 0, 0))
    wide = (2, plan.d, plan.d)
    thin = (2, 1, plan.d)
    return pl.pallas_call(
        functools.partial(spectral_back_kernel, plan, riders),
        grid=(plan.q,),
        in_specs=[pair_block(plan, plan.t)]
        + [kept_spec] * 4
        + [whole(lat.shape), whole(lat_t.shape), whole(wide), whole(wide)]
        + riders.specs(),
        out_specs=[
            pair_block(plan, plan.t),
            whole(small),
            whole(small),
            whole(thin),
            whole(thin),
        ]
        + riders.specs(),
        out_shape=[
            jax.ShapeDtypeStruct((plan.n, plan.q, plan.t, plan.d), BF),
            jax.ShapeDtypeStruct(small, F32),
            jax.ShapeDtypeStruct(small, F32),
            jax.ShapeDtypeStruct(thin, F32),
            jax.ShapeDtypeStruct(thin, F32),
        ]
        + riders.shapes(),
        scratch_shapes=[
            pltpu.VMEM(wide, F32),
            pltpu.VMEM(wide, F32),
            pltpu.VMEM((4 * HP, plan.d), BF),
            pltpu.VMEM((2 * HP, plan.d), BF),
        ]
        + riders.scratch(),
        compiler_params=params(collective_id),
        cost_estimate=cost(1e9, 1e6),
        name="spectral_backward",
    )(received, *kept, lat, lat_t, m1t, m2t, *riders.arrays)


def last_kernel(
    plan,
    scale_ref,
    tok_ref,
    gx_ref,
    in_ref,
    gain_ref,
    lon_t_ref,
    perm_t_ref,
    *rest,
):
    out_ref, vec_ref, rows_ref = rest[-3:]
    i = pl.program_id(0)

    @pl.when(i == 0)
    def _():
        vec_ref[...] = jnp.zeros_like(vec_ref)
        deinterleave(plan, perm_t_ref, in_ref, rows_ref)

    for u in range(plan.rb):
        keep = jnp.where(scale_ref[i * plan.rb + u] > 0.0, 1.0, 0.0)
        unit, rstd = norm_parts(tok_ref[0, u].astype(F32))
        gx = gx_ref[u].astype(F32)
        grad = gx + dot_table(lon_t_ref, rows_ref[i * plan.rb + u])
        vec_ref[0:1] += jnp.sum(grad * unit, 0, keepdims=True) * keep
        vec_ref[1:2] += jnp.sum(grad, 0, keepdims=True) * keep
        out_ref[0, u] = (gx + norm_back(grad, unit, rstd, gain_ref[0:1])) * keep


def last_call(plan, s, scales, tokens, gx, received, gain, earlier):
    operands = [scales, tokens, gx, received, gain, plan.lon_t, plan.perm_t]
    in_specs = [
        SMEM,
        row_block(plan, s),
        own_block(plan),
        whole((plan.pairs, plan.t, plan.d)),
        whole((8, plan.d)),
        whole((2, plan.w, plan.ki)),
        whole(plan.perm_t.shape),
    ]
    aliases = {}
    if earlier is not None:
        aliases = {len(operands): 0}
        operands.append(earlier)
        in_specs.append(ANY)
    return pl.pallas_call(
        functools.partial(last_kernel, plan),
        grid=(plan.chunks,),
        in_specs=in_specs,
        out_specs=[row_block(plan, s), whole((2, plan.d))],
        out_shape=[
            jax.ShapeDtypeStruct((plan.s, plan.r, plan.w, plan.d), F32),
            jax.ShapeDtypeStruct((2, plan.d), F32),
        ],
        scratch_shapes=[pltpu.VMEM((plan.r, plan.ki, plan.d), BF)],
        input_output_aliases=aliases,
        compiler_params=params(),
        cost_estimate=cost(1e9, 1e6),
        name="lon_backward",
    )(*operands)


def band_kernel(plan, in_ref, *rest):
    out_ref, tall = rest[-2:]
    mb = plan.mb
    height = 2 * plan.kw
    for src in range(plan.n):
        for t in range(plan.kk):
            k = src * plan.kk + t
            if k >= plan.kw:
                continue
            both = in_ref[src, t // 2].astype(F32)
            for p in range(2):
                at = ((t % 2) * 2 + p) * mb
                part = both[at : at + mb]
                for g in range(plan.d // 128):
                    tall[g, pl.ds(2 * k + p, mb, stride=height), :] = part[
                        :, g * 128 : (g + 1) * 128
                    ]
    for m in range(mb):
        for g in range(plan.d // 128):
            piece = tall[g, m * height : (m + 1) * height, :].astype(BF)
            out_ref[0, m, :, :, g * 128 : (g + 1) * 128] = piece.reshape(plan.kw, 2, 128)


def band_call(plan, s, received, earlier):
    shape = (plan.s, plan.mb, plan.kw, 2, plan.d)
    operands = [received]
    in_specs = [whole(received.shape)]
    aliases = {}
    if earlier is not None:
        aliases = {1: 0}
        operands.append(earlier)
        in_specs.append(ANY)
    return pl.pallas_call(
        functools.partial(band_kernel, plan),
        grid=(1,),
        in_specs=in_specs,
        out_specs=pl.BlockSpec((1,) + shape[1:], lambda i: (s, 0, 0, 0, 0)),
        out_shape=jax.ShapeDtypeStruct(shape, BF),
        scratch_shapes=[pltpu.VMEM((plan.d // 128, 2 * plan.mb * plan.kw, 128), F32)],
        input_output_aliases=aliases,
        compiler_params=params(),
        cost_estimate=cost(1e8, 1e6),
        name="band_output",
    )(*operands)


def every_peer(total, step_of):
    def body(step, carry):
        step_of(step)
        return carry

    lax.fori_loop(1, total, body, 0)


def place(lanes, index):
    return {"batch": index // lanes, "lat": lax.rem(index, lanes)}


def greet_all(total, lanes, me):
    barrier = pltpu.get_barrier_semaphore()

    def greet(step):
        pl.semaphore_signal(
            barrier,
            inc=1,
            device_id=place(lanes, lax.rem(me + step, total)),
            device_id_type=pl.DeviceIdType.MESH,
        )

    every_peer(total, greet)
    pl.semaphore_wait(barrier, total - 1)


def block_sum_kernel(total, lanes, xs, *rest):
    ins, outs, helds, sems = rest[:xs], rest[xs : 2 * xs], rest[2 * xs : 3 * xs], rest[3 * xs :]
    me = lax.axis_index("batch") * lanes + lax.axis_index("lat")
    greet_all(total, lanes, me)

    def part(a, step, peer):
        return pltpu.make_async_remote_copy(
            src_ref=ins[a].at[peer],
            dst_ref=helds[a].at[step],
            send_sem=sems[4 * a].at[step],
            recv_sem=sems[4 * a + 1].at[step],
            device_id=place(lanes, peer),
            device_id_type=pl.DeviceIdType.MESH,
        )

    def result(a, step, peer, slot):
        return pltpu.make_async_remote_copy(
            src_ref=outs[a].at[me],
            dst_ref=outs[a].at[slot],
            send_sem=sems[4 * a + 2].at[step],
            recv_sem=sems[4 * a + 3].at[step],
            device_id=place(lanes, peer),
            device_id_type=pl.DeviceIdType.MESH,
        )

    ahead = lambda step: lax.rem(me + step, total)
    behind = lambda step: lax.rem(me + total - step, total)
    for a in range(xs):
        every_peer(total, lambda step: part(a, step, ahead(step)).start())
    for a in range(xs):
        helds[a][0] = ins[a][me]
        every_peer(total, lambda step: part(a, step, behind(step)).wait_recv())
        outs[a][me] = jnp.sum(helds[a][...].astype(F32), 0).astype(outs[a].dtype)
        every_peer(total, lambda step: result(a, step, ahead(step), me).start())
    for a in range(xs):
        every_peer(total, lambda step: part(a, step, ahead(step)).wait_send())
        every_peer(total, lambda step: result(a, step, behind(step), behind(step)).wait_recv())
        every_peer(total, lambda step: result(a, step, ahead(step), me).wait_send())


def block_sum(total, lanes, xs, collective_id):
    vmem = pl.BlockSpec(memory_space=pltpu.VMEM)
    sems = [pltpu.SemaphoreType.DMA((total,))] * (4 * len(xs))
    return pl.pallas_call(
        functools.partial(block_sum_kernel, total, lanes, len(xs)),
        in_specs=[vmem] * len(xs),
        out_specs=[vmem] * len(xs),
        out_shape=[jax.ShapeDtypeStruct(x.shape, x.dtype) for x in xs],
        scratch_shapes=[pltpu.VMEM(x.shape, x.dtype) for x in xs] + sems,
        compiler_params=pltpu.CompilerParams(
            collective_id=collective_id, has_side_effects=True, vmem_limit_bytes=VMEM_BYTES
        ),
        cost_estimate=cost(1e8, 1e6),
        name="block_sum",
    )(*xs)


def pack(total, parts, dtype, rows):
    flat = jnp.concatenate([x.reshape(-1).astype(dtype) for x in parts])
    unit = total * rows * 128
    padded = -(-flat.shape[0] // unit) * unit
    return jnp.pad(flat, (0, padded - flat.shape[0])).reshape(total, -1, 128)


def unpack(packed, parts):
    flat = packed.reshape(-1).astype(F32)
    out, at = [], 0
    for x in parts:
        out.append(flat[at : at + x.size].reshape(x.shape))
        at += x.size
    return out


def whole_sum_kernel(total, lanes, x_ref, out_ref, held, send, recv):
    me = lax.axis_index("batch") * lanes + lax.axis_index("lat")
    greet_all(total, lanes, me)

    def part(step, peer):
        return pltpu.make_async_remote_copy(
            src_ref=x_ref,
            dst_ref=held.at[step],
            send_sem=send.at[step],
            recv_sem=recv.at[step],
            device_id=place(lanes, peer),
            device_id_type=pl.DeviceIdType.MESH,
        )

    ahead = lambda step: lax.rem(me + step, total)
    every_peer(total, lambda step: part(step, ahead(step)).start())
    held[0] = x_ref[...]
    every_peer(total, lambda step: part(step, ahead(step)).wait_recv())
    out_ref[...] = jnp.sum(held[...], 0)
    every_peer(total, lambda step: part(step, ahead(step)).wait_send())


def whole_sum(total, lanes, x, collective_id):
    sems = [pltpu.SemaphoreType.DMA((total,))] * 2
    return pl.pallas_call(
        functools.partial(whole_sum_kernel, total, lanes),
        in_specs=[pl.BlockSpec(memory_space=pltpu.VMEM)],
        out_specs=pl.BlockSpec(memory_space=pltpu.VMEM),
        out_shape=jax.ShapeDtypeStruct(x.shape, x.dtype),
        scratch_shapes=[pltpu.VMEM((total,) + x.shape, x.dtype)] + sems,
        compiler_params=pltpu.CompilerParams(
            collective_id=collective_id, has_side_effects=True, vmem_limit_bytes=VMEM_BYTES
        ),
        cost_estimate=cost(1e8, 1e6),
        name="whole_sum",
    )(x)


def exchange(x):
    return lax.all_to_all(x, "lat", split_axis=0, concat_axis=0, tiled=True)


def on_device(
    bands,
    tokens,
    cotangent,
    sample_weight,
    row_count,
    band_count,
    norm1_gain,
    norm1_bias,
    spec_w1,
    spec_b1,
    spec_w2,
    spec_b2,
    norm2_gain,
    norm2_bias,
    fc1_weight,
    fc1_bias,
    fc2_weight,
    fc2_bias,
):
    lane = lax.axis_index("lat")
    n = lax.axis_size("lat")
    samples, row_slots, width, channels = tokens.shape
    blocks, size = spec_w1.shape[1], spec_w1.shape[2]
    plan = Plan(n, samples, row_slots, width, channels, bands)
    wb1, wb2 = wide_bias(spec_b1), wide_bias(spec_b2)
    row = lambda v: v.reshape(1, -1)
    blank = jnp.zeros_like(fc2_bias)
    vectors = jnp.stack([norm1_gain, norm1_bias, norm2_gain, norm2_bias, fc2_bias] + [blank] * 3)
    own_rows = jnp.sum(jnp.where(jnp.arange(n) == lane, row_count, 0))
    held = jnp.arange(row_slots) < own_rows
    scales = sample_weight.astype(F32)[:, None] * 0.5 * held[None, :].astype(F32)
    slot_step = jnp.arange(plan.kp)
    valid = ((slot_step < plan.kk) & (lane * plan.kk + slot_step < plan.kw)).astype(F32)
    grouped = (n, plan.q, plan.t, channels)
    listed = (plan.pairs, plan.t, channels)

    ids = itertools.count()
    spread = (-1,) + grouped

    def spectral_forward(x, passengers=()):
        collective_id = next(ids) if passengers else None
        out = spectral_call(
            plan, valid, x, lat, lat_t, slots, m1, wb1, m2, wb2, passengers, collective_id
        )
        forward.append(out)
        return out[7:]

    def feed(s, back, sums, passengers):
        out = feed_call(
            plan,
            s,
            scales[s],
            tokens,
            cotangent,
            back.reshape(listed),
            vectors,
            fc1_weight,
            row(fc1_bias),
            fc2_weight,
            sums,
            s == samples - 1,
            passengers,
            next(ids),
        )
        feeds.append(out)
        return out[7:]

    def backward(s, grads, passengers=()):
        out = spectral_back_call(
            plan,
            blocks,
            size,
            grads,
            forward[s][2:6],
            lat,
            lat_t,
            m1t,
            m2t,
            passengers,
            next(ids) if passengers else None,
        )
        spectral.append(out)
        return out[0], out[5:]

    forward, feeds, spectral, band_parts, grads, lon_grads = [], [], [], {}, {}, {}
    sent = first_call(plan, 0, 1, tokens, vectors)[0].reshape(spread)
    tables = Tables(plan, blocks, size)
    extra = tables.operands(row_count, band_count, spec_w1, spec_w2)
    others, lat, lat_t, slots, m1, m2, m1t, m2t, spectra = first_call(
        plan, 1, samples - 1, tokens, vectors, [(sent, 0)], next(ids), tables, extra
    )
    others = others.reshape(spread)
    (spectra,) = spectral_forward(spectra, [(others, 0)])
    (back,) = spectral_forward(spectra, [(forward[0][0], None)])
    for s in range(samples):
        sums = (feeds[-1][3], feeds[-1][4]) if s else None
        kinds, passengers = [], []
        if s + 1 < samples:
            kinds.append("back")
            passengers.append((forward[s + 1][0], None))
        if s + 2 < samples:
            kinds.append("spectra")
            passengers.append((others, s + 1))
        if s >= 1:
            kinds.append("grads")
            passengers.append((feeds[s - 1][1].reshape(grouped), None))
        kinds.append("band")
        passengers.append((forward[s][1], None))
        arrived = dict(zip(kinds, feed(s, back, sums, passengers)))
        back = arrived.get("back")
        if s + 2 < samples:
            spectral_forward(arrived["spectra"])
        band_parts[s] = arrived["band"]
        if s >= 1:
            grads[s - 1] = arrived["grads"]
    after = lambda x, y: lax.optimization_barrier((x, y))[0]

    def last(s, earlier):
        return last_call(
            plan,
            s,
            scales[s],
            tokens,
            feeds[s][2],
            lon_grads[s].reshape(listed),
            vectors,
            earlier,
        )

    large = lax.psum((feeds[-1][3], feeds[-1][4]), ("batch", "lat"))
    grads[samples - 1] = exchange(feeds[-1][1].reshape(grouped))
    grads[0] = after(grads[0], feeds[-1][6])
    lon = None
    for s in range(samples):
        lon, got = backward(s, grads[s], [(lon, None)] if s else ())
        if s:
            lon_grads[s - 1] = got[0]
    lon_grads[samples - 1] = exchange(lon)
    tokens_grad, spectrum, finals = None, None, []
    for s in range(samples):
        tokens_grad, vec = last(s, tokens_grad)
        finals.append(vec)
        spectrum = band_call(plan, s, band_parts[s], spectrum)
    mixed = jnp.stack([f[0] for f in feeds])

    add = lambda parts: functools.reduce(jnp.add, parts)
    devices = lax.axis_size("batch") * n
    feed_vec = add([f[6] for f in feeds])
    block_grad = lambda i: add([b[i] for b in spectral]).reshape(2, blocks, size, size)
    zeros = jnp.sum(add([f[6] for f in forward]))
    small = [
        feed_vec[1],
        feed_vec[2],
        add([f[5] for f in feeds]),
        feed_vec[0],
        narrow_bias(add([b[3] for b in spectral]), blocks, size),
        narrow_bias(add([b[4] for b in spectral]), blocks, size),
        zeros.reshape(1),
    ]
    blocky = [block_grad(1), block_grad(2)]
    packed = [pack(devices, blocky, BF, 16), pack(devices, small, F32, 8)]
    packed = after(packed, finals[samples - 2])
    packed = block_sum(devices, n, packed, next(ids))
    blocky = unpack(packed[0], blocky)
    small = unpack(packed[1], small)
    last_vec = whole_sum(devices, n, add(finals), next(ids))
    large = after(large, last_vec)
    large = (large[0].astype(F32), large[1].astype(F32))
    zero_fraction = small[6][0] / (lax.axis_size("batch") * samples * H * plan.kw * 2 * channels)
    return (
        mixed,
        spectrum.transpose(0, 1, 3, 2, 4),
        tokens_grad,
        last_vec[0],
        last_vec[1],
        blocky[0],
        small[4],
        blocky[1],
        small[5],
        small[0],
        small[1],
        large[0],
        small[2].reshape(-1),
        large[1],
        small[3],
        zero_fraction,
    )


def solution(mesh):
    rows = P("batch", "lat", None, None)
    in_specs = (rows, rows, P("batch")) + (P(),) * 14
    out_specs = (rows, P("batch", "lat", None, None, None), rows) + (P(),) * 13
    lanes = mesh.shape["lat"]

    def run(tokens, cotangent, *rest):
        row_slots = tokens.shape[1] // lanes
        return jax.shard_map(
            functools.partial(on_device, row_slots + 1),
            mesh=mesh,
            in_specs=in_specs,
            out_specs=out_specs,
            check_vma=False,
        )(tokens, cotangent, *rest)

    return run
```

```python
import functools
import itertools
import math

import jax
import jax.numpy as jnp
import numpy as np
from jax import lax
from jax.experimental import pallas as pl
from jax.experimental.pallas import tpu as pltpu
from jax.sharding import PartitionSpec as P

H = 90
HP = 96

NORM_EPS = 1e-06
SHRINK_LAMBDA = 0.01
SHRINK_SOFTNESS = 0.1
INV_ROOT_TAU = 1.0 / math.sqrt(2.0 * math.pi)
BF = jnp.bfloat16
F32 = jnp.float32
VMEM_BYTES = 64 * 1024 * 1024


def dot(a, b):
    return jnp.dot(a, b, preferred_element_type=F32)


def dot_nt(a, b):
    return lax.dot_general(a, b, (((1,), (1,)), ((), ())), preferred_element_type=F32)


def dot_tn(a, b):
    return lax.dot_general(a, b, (((0,), (0,)), ((), ())), preferred_element_type=F32)


def dot_table(table_ref, x):
    return dot(table_ref[0], x) + dot(table_ref[1], x)


def two_parts(table):
    high = table.astype(BF)
    return high, (table - high.astype(table.dtype)).astype(BF)


def norm_parts(x):
    mean = jnp.mean(x, -1, keepdims=True)
    centred = x - mean
    rstd = lax.rsqrt(jnp.mean(centred * centred, -1, keepdims=True) + NORM_EPS)
    return centred * rstd, rstd


def norm_back(grad, unit, rstd, gain):
    e = grad * gain
    return rstd * (
        e - jnp.mean(e, -1, keepdims=True) - unit * jnp.mean(e * unit, -1, keepdims=True)
    )


def gauss_parts(v):
    d = 1.0 + jnp.abs(v) * (0.3275911 / math.sqrt(2.0))
    t = pl.reciprocal(d, approx=True)
    e = jnp.exp2(v * v * (-0.5 * math.log2(math.e)))
    poly = 1.061405429 * 0.5
    for c in (-1.453152027, 1.421413741, -0.284496736, 0.254829592):
        poly = poly * t + 0.5 * c
    tail = poly * t * e
    cdf = jnp.where(v >= 0.0, 1.0 - tail, tail)
    return cdf, v * e * INV_ROOT_TAU


def gelu_both(v):
    cdf, slope_part = gauss_parts(v)
    return v * cdf, cdf + slope_part


def shrink_both(u):
    a = jnp.maximum(jnp.abs(u) - SHRINK_LAMBDA, 0.0)
    d = a + SHRINK_SOFTNESS
    t = pl.reciprocal(d, approx=True)
    t = t * (2.0 - d * t)
    size = a * a * t
    value = jnp.where(u >= 0.0, size, -size)
    slope = a * (a + 2.0 * SHRINK_SOFTNESS) * (t * t)
    return value, slope


class Plan:
    def __init__(self, n, samples, rows, width, channels, bands):
        self.n, self.s, self.r, self.w, self.d, self.mb = n, samples, rows, width, channels, bands
        self.kw = width // 2 + 1
        self.kk = -(-self.kw // n)
        self.kp = self.kk + self.kk % 2
        self.q = self.kp // 2
        self.rp = -(-rows // 4) * 4
        self.t = 4 * self.rp
        self.pairs = n * self.q
        self.ki = n * self.kp * 2
        self.rb = max(b for b in (4, 3, 2, 1) if rows % b == 0)
        self.chunks = rows // self.rb
        self.flat = self.rb * width
        self.flatp = max(-(-self.flat // 256) * 256, channels)
        self.bt = -(-4 * bands // 8) * 8
        j = np.arange(n)[:, None]
        t = np.arange(self.kp)[None, :]
        self.k_index = (j * self.kk + t).astype(np.int64)
        self.k_valid = (t < self.kk) & (self.k_index < self.kw)
        k = np.where(self.k_valid, self.k_index, 0).reshape(-1)
        ok = self.k_valid.reshape(-1).astype(np.float64)
        angle = 2.0 * np.pi * ((k[:, None] * np.arange(width)[None, :]) % width) / width
        scale = ok[:, None] / math.sqrt(width)
        fwd = np.stack([np.cos(angle) * scale, -np.sin(angle) * scale], 1).reshape(self.ki, width)
        factor = np.where((k == 0) | (2 * k == width), 1.0, 2.0)[:, None, None]
        both = (fwd.reshape(-1, 2, width) * factor).reshape(self.ki, width)
        self.lon = np.stack(two_parts(fwd))
        self.lon_both = np.stack(two_parts(both))
        self.lon_t = np.stack(two_parts(np.ascontiguousarray(fwd.T)))
        self.lon_both_t = np.stack(two_parts(np.ascontiguousarray(both.T)))
        perm = np.zeros((16, self.rp, rows, 16))
        for a in range(16):
            for r in range(rows):
                perm[a, r, r, a] = 1.0
        self.perm = perm.reshape(16 * self.rp, rows * 16).astype(BF)
        self.perm_t = np.ascontiguousarray(self.perm.T)


class Tables:
    def __init__(self, plan, blocks, size):
        self.plan, self.blocks, self.size = plan, blocks, size
        n, rp, mb = plan.n, plan.rp, plan.mb
        kh, h = np.arange(HP)[:, None], np.arange(HP)[None, :]
        angle = 2.0 * np.pi * (kh * h % H) / H
        weight = ((kh < H) & (h < H)) / math.sqrt(H)
        cosine, sine = np.cos(angle) * weight, np.sin(angle) * weight
        part = np.block([[cosine, sine], [-sine, cosine]])
        self.base = np.stack(two_parts(np.kron(np.eye(2), part)))
        col = np.arange(n * 4 * rp)
        group, step = col // rp % 4, col % rp
        self.columns = np.stack([col // (4 * rp), group * HP + step, step]).astype(np.int32)
        bt = plan.bt
        line = np.arange(n * bt)
        group, step = line % bt // mb, line % bt % mb
        step = np.where(group < 4, step, 1 << 20)
        lines = np.stack([line // bt, group * HP + step, step]).astype(np.int32)
        self.lines = lines[:, :, None]
        half = blocks // 2
        spots = np.zeros((half, size, half * size))
        for i in range(half):
            spots[i, :, i * size : (i + 1) * size] = np.eye(size)
        self.spots = spots.astype(BF)
        wide = 4 * HP
        d = plan.d
        shapes = [(2, wide, n * 4 * rp), (2, n * 4 * rp, wide), (n * bt, wide)] + [(2, d, d)] * 4
        self.shapes = [jax.ShapeDtypeStruct(x, BF) for x in shapes]

    def operands(self, row_count, band_count, spec_w1, spec_w2):
        return [
            row_count,
            band_count,
            spec_w1,
            spec_w2,
            self.base,
            self.columns[:, None, :],
            self.lines,
            self.spots,
        ]

    def in_specs(self):
        weight = (2, self.blocks, self.size, self.size)
        shapes = [weight, weight, self.base.shape, (3, 1, self.columns.shape[1])]
        shapes += [self.lines.shape, self.spots.shape]
        return [SMEM, SMEM] + [whole(x) for x in shapes]

    def out_specs(self):
        return [whole(x.shape) for x in self.shapes]

    def build(self, ins, outs):
        rows_ref, bands_ref, w1_ref, w2_ref, base_ref, col_ref, line_ref, spot_ref = ins
        lat_ref, lat_t_ref, slot_ref, m1_ref, m2_ref, m1t_ref, m2t_ref = outs
        n = self.plan.n

        def spread(counts_ref, owner):
            first = jnp.zeros(owner.shape, jnp.int32)
            held = jnp.zeros(owner.shape, jnp.int32)
            start = jnp.int32(0)
            for j in range(n):
                count = counts_ref[j]
                first = jnp.where(owner == j, start, first)
                held = jnp.where(owner == j, count, held)
                start = start + count
            return first, held

        first, held = spread(rows_ref, col_ref[0])
        target = jnp.where(col_ref[2] < held, col_ref[1] + first, -1)
        pick = lax.broadcasted_iota(jnp.int32, (4 * HP, target.shape[1]), 0) == target
        pick = jnp.where(pick, 1.0, 0.0).astype(BF)
        for part in range(2):
            full = dot(base_ref[part], pick)
            lat_ref[part] = full.astype(BF)
            lat_t_ref[part] = full.T.astype(BF)
        first, held = spread(bands_ref, line_ref[0])
        target = jnp.where(line_ref[2] < held, line_ref[1] + first, -1)
        pick = lax.broadcasted_iota(jnp.int32, (target.shape[0], 4 * HP), 1) == target
        slot_ref[...] = jnp.where(pick, 1.0, 0.0).astype(BF)
        half, size = self.blocks // 2, self.size
        mid = half * size
        for w_ref, m_ref, mt_ref in ((w1_ref, m1_ref, m1t_ref), (w2_ref, m2_ref, m2t_ref)):
            for g in range(2):
                for i in range(half):
                    low = slice(i * size, (i + 1) * size)
                    high = slice(mid + i * size, mid + (i + 1) * size)
                    re, im = w_ref[0, g * half + i], w_ref[1, g * half + i]
                    for ref, place_in, sign in ((m_ref, dot, 1.0), (mt_ref, dot_tn, -1.0)):
                        real = place_in(re, spot_ref[i]).astype(BF)
                        imag = place_in(im, spot_ref[i]) * sign
                        ref[g, low, :mid] = real
                        ref[g, high, mid:] = real
                        ref[g, low, mid:] = imag.astype(BF)
                        ref[g, high, :mid] = (-imag).astype(BF)


def wide_bias(bias):
    return bias.reshape(2, 2, -1).transpose(1, 0, 2).reshape(2, 1, -1)


def narrow_bias(wide, blocks, size):
    return wide.reshape(2, 2, -1).transpose(1, 0, 2).reshape(2, blocks, size)


def whole(shape):
    zeros = (0,) * len(shape)
    return pl.BlockSpec(shape, lambda *_: zeros)


def whole_once(shape):
    zeros = (0,) * len(shape)
    return pl.BlockSpec(shape, lambda *_: zeros, pipeline_mode=pl.Buffered(1))


SMEM = pl.BlockSpec(memory_space=pltpu.SMEM)
ANY = pl.BlockSpec(memory_space=pl.ANY)


def params(collective_id=None):
    if collective_id is None:
        return pltpu.CompilerParams(
            dimension_semantics=("arbitrary",), vmem_limit_bytes=VMEM_BYTES
        )
    return pltpu.CompilerParams(
        dimension_semantics=("arbitrary",),
        vmem_limit_bytes=VMEM_BYTES,
        collective_id=collective_id,
        has_side_effects=True,
    )


def ride_copy(n, me, src, dst, send, recv, e, step):
    peer = lax.rem(me + step, n)
    return pltpu.make_async_remote_copy(
        src_ref=src.at[peer],
        dst_ref=dst.at[me],
        send_sem=send.at[e, step],
        recv_sem=recv.at[e, step],
        device_id={"lat": peer},
        device_id_type=pl.DeviceIdType.MESH,
    )


def ride_arrival(n, me, src, dst, send, recv, e, step):
    peer = lax.rem(me + n - step, n)
    return pltpu.make_async_remote_copy(
        src_ref=src.at[peer],
        dst_ref=dst.at[peer],
        send_sem=send.at[e, step],
        recv_sem=recv.at[e, step],
        device_id={"lat": peer},
        device_id_type=pl.DeviceIdType.MESH,
    )


def ride_start(n, srcs, dsts, send, recv, own):
    me = lax.axis_index("lat")
    barrier = pltpu.get_barrier_semaphore()
    for step in range(1, n):
        pl.semaphore_signal(
            barrier,
            inc=1,
            device_id={"lat": lax.rem(me + step, n)},
            device_id_type=pl.DeviceIdType.MESH,
        )
    pl.semaphore_wait(barrier, n - 1)
    for e, (src, dst) in enumerate(zip(srcs, dsts)):
        for step in range(1, n):
            ride_copy(n, me, src, dst, send, recv, e, step).start()
        pltpu.make_async_copy(src.at[me], dst.at[me], own.at[e]).start()


def ride_wait(n, srcs, dsts, send, recv, own):
    me = lax.axis_index("lat")
    for e, (src, dst) in enumerate(zip(srcs, dsts)):
        pltpu.make_async_copy(src.at[me], dst.at[me], own.at[e]).wait()
        for step in range(1, n):
            ride_copy(n, me, src, dst, send, recv, e, step).wait_send()
            ride_arrival(n, me, src, dst, send, recv, e, step).wait_recv()


def cost(flops, size):
    return pl.CostEstimate(flops=int(flops), bytes_accessed=int(size), transcendentals=0)


def interleave(plan, perm_ref, rows_ref, out_ref):
    def body(c, carry):
        at = pl.multiple_of(c * 16, 16)
        block = rows_ref[:, pl.ds(at, 16), :].reshape(plan.r * 16, plan.d)
        mixed = dot(perm_ref[...], block).astype(BF)
        out_ref[pl.ds(c * 4, 4)] = mixed.reshape(4, plan.t, plan.d)
        return carry

    lax.fori_loop(0, plan.ki // 16, body, 0)


def deinterleave(plan, perm_t_ref, in_ref, rows_ref):
    def body(c, carry):
        at = pl.multiple_of(c * 16, 16)
        block = in_ref[pl.ds(c * 4, 4)].reshape(4 * plan.t, plan.d)
        rows = dot(perm_t_ref[...], block).astype(BF)
        rows_ref[:, pl.ds(at, 16), :] = rows.reshape(plan.r, 16, plan.d)
        return carry

    lax.fori_loop(0, plan.ki // 16, body, 0)


def interleave_out(plan, perm_ref, rows_ref, ring, sem, out_ref):
    def copy(c):
        return pltpu.make_async_copy(
            ring.at[lax.rem(c, 2)], out_ref.at[pl.ds(c * 4, 4)], sem.at[lax.rem(c, 2)]
        )

    def body(c, carry):
        @pl.when(c >= 2)
        def _():
            copy(c - 2).wait()

        at = pl.multiple_of(c * 16, 16)
        block = rows_ref[:, pl.ds(at, 16), :].reshape(plan.r * 16, plan.d)
        mixed = dot(perm_ref[...], block).astype(BF)
        ring[lax.rem(c, 2)] = mixed.reshape(4, plan.t, plan.d)
        copy(c).start()
        return carry

    lax.fori_loop(0, plan.ki // 16, body, 0)
    return [copy(plan.ki // 16 - 2), copy(plan.ki // 16 - 1)]


def ring_load(plan, in_ref, ring, sem, c):
    return pltpu.make_async_copy(
        in_ref.at[pl.ds(c * 4, 4)], ring.at[lax.rem(c, 2)], sem.at[lax.rem(c, 2)]
    )


def deinterleave_in(plan, perm_t_ref, in_ref, ring, sem, rows_ref):
    steps = plan.ki // 16

    def body(c, carry):
        ring_load(plan, in_ref, ring, sem, c).wait()
        at = pl.multiple_of(c * 16, 16)
        block = ring[lax.rem(c, 2)].reshape(4 * plan.t, plan.d)
        rows = dot(perm_t_ref[...], block).astype(BF)
        rows_ref[:, pl.ds(at, 16), :] = rows.reshape(plan.r, 16, plan.d)

        @pl.when(c + 2 < steps)
        def _():
            ring_load(plan, in_ref, ring, sem, c + 2).start()

        return carry

    lax.fori_loop(0, steps, body, 0)


class Riders:
    def __init__(self, plan, passengers):
        self.n = plan.n
        self.arrays = [a for a, _ in passengers]
        self.leads = [lead for _, lead in passengers]
        self.count = len(passengers)

    def shapes(self):
        return [
            jax.ShapeDtypeStruct(a.shape if lead is None else a.shape[1:], a.dtype)
            for a, lead in zip(self.arrays, self.leads)
        ]

    def specs(self):
        return [ANY] * self.count

    def scratch(self):
        if not self.count:
            return []
        dma = pltpu.SemaphoreType.DMA
        return [dma((self.count, self.n)), dma((self.count, self.n)), dma((self.count,))]

    def bind(self, srcs, dsts, sems):
        srcs = [r if lead is None else r.at[lead] for r, lead in zip(srcs, self.leads)]
        return (self.n, srcs, dsts) + tuple(sems)


def first_kernel(plan, riders, tables, tok_ref, vec_ref, lon_ref, perm_ref, *rest):
    e = riders.count
    t_in = 0 if tables is None else 8
    t_out = 0 if tables is None else 7
    t_ins, rest = rest[:t_in], rest[t_in:]
    srcs, rest = rest[:e], rest[e:]
    out_ref, rest = rest[0], rest[1:]
    t_outs, rest = rest[:t_out], rest[t_out:]
    dsts, rows_ref, sems = rest[:e], rest[e], rest[e + 1 :]
    i = pl.program_id(0)
    c = lax.rem(i, plan.chunks)
    if e:
        ride = riders.bind(srcs, dsts, sems)

        @pl.when(i == 0)
        def _():
            ride_start(*ride)

    for u in range(plan.rb):
        unit, _ = norm_parts(tok_ref[0, u].astype(F32))
        normed = (unit * vec_ref[0:1] + vec_ref[1:2]).astype(BF)
        rows_ref[c * plan.rb + u] = dot_table(lon_ref, normed).astype(BF)

    @pl.when(c == plan.chunks - 1)
    def _():
        interleave(plan, perm_ref, rows_ref, out_ref.at[0])

    @pl.when(i == pl.num_programs(0) - 1)
    def _():
        if tables is not None:
            tables.build(t_ins, t_outs)
        if e:
            ride_wait(*ride)


def row_block(plan, s):
    return pl.BlockSpec((1, plan.rb, plan.w, plan.d), lambda i: (s, i, 0, 0))


def own_block(plan):
    return pl.BlockSpec((plan.rb, plan.w, plan.d), lambda i: (i, 0, 0))


def first_call(
    plan, start, count, tokens, vectors, passengers=(), collective_id=None, tables=None, extra=()
):
    shape = (plan.pairs, plan.t, plan.d)
    chunks = plan.chunks
    riders = Riders(plan, passengers)
    return pl.pallas_call(
        functools.partial(first_kernel, plan, riders, tables),
        grid=(count * chunks,),
        in_specs=[
            pl.BlockSpec(
                (1, plan.rb, plan.w, plan.d),
                lambda i: (start + i // chunks, lax.rem(i, chunks), 0, 0),
            ),
            whole((8, plan.d)),
            whole((2, plan.ki, plan.w)),
            whole(plan.perm.shape),
        ]
        + (tables.in_specs() if tables else [])
        + riders.specs(),
        out_specs=[pl.BlockSpec((1,) + shape, lambda i: (i // chunks, 0, 0, 0))]
        + (tables.out_specs() if tables else [])
        + riders.specs(),
        out_shape=[jax.ShapeDtypeStruct((count,) + shape, BF)]
        + (tables.shapes if tables else [])
        + riders.shapes(),
        scratch_shapes=[pltpu.VMEM((plan.r, plan.ki, plan.d), BF)] + riders.scratch(),
        compiler_params=params(collective_id),
        cost_estimate=cost(9e9 * count, 8e6 * count),
        name="lon_forward",
    )(tokens, vectors, plan.lon, plan.perm, *extra, *riders.arrays)


def spectral_kernel(
    plan,
    riders,
    valid_ref,
    in_ref,
    lat_ref,
    lat_t_ref,
    slot_ref,
    m1_ref,
    b1_ref,
    m2_ref,
    b2_ref,
    *rest,
):
    e = riders.count
    srcs, rest = rest[:e], rest[e:]
    back_ref, band_ref, spec_ref, hid_ref, slope1_ref, slope2_ref, zero_ref = rest[:7]
    dsts, shr_ref, sems = rest[7 : 7 + e], rest[7 + e], rest[8 + e :]
    q = pl.program_id(0)
    half = plan.d // 2
    if e:
        ride = riders.bind(srcs, dsts, sems)

        @pl.when(q == 0)
        def _():
            ride_start(*ride)

    @pl.when(q == 0)
    def _():
        zero_ref[...] = jnp.zeros_like(zero_ref)

    x = in_ref[:, 0].reshape(plan.n * plan.t, plan.d)
    spec = dot_table(lat_ref, x).astype(BF)
    ok = (lax.broadcasted_iota(jnp.int32, (HP, 1), 0) < H).astype(F32)
    for g in range(2):
        lanes = slice(g * half, (g + 1) * half)
        for a in range(2):
            top = a * 2 * HP
            spec_ref[0, g, a * HP : (a + 1) * HP, :half] = spec[top : top + HP, lanes]
            spec_ref[0, g, a * HP : (a + 1) * HP, half:] = spec[top + HP : top + 2 * HP, lanes]
        u1 = dot(spec_ref[0, g], m1_ref[g]) + b1_ref[g]
        hidden, slope = gelu_both(u1)
        hid_ref[0, g] = hidden.astype(BF)
        slope1_ref[0, g] = slope.astype(BF)
        u2 = dot(hid_ref[0, g], m2_ref[g]) + b2_ref[g]
        small = (jnp.abs(u2) <= SHRINK_LAMBDA).astype(F32)
        for a in range(2):
            part = small[a * HP : (a + 1) * HP] * ok
            zero_ref[...] += jnp.sum(part, 0, keepdims=True) * valid_ref[q * 2 + a]
        value, slope = shrink_both(u2)
        slope2_ref[0, g] = slope.astype(BF)
        value = value.astype(BF)
        for a in range(2):
            top = a * 2 * HP
            shr_ref[top : top + HP, lanes] = value[a * HP : (a + 1) * HP, :half]
            shr_ref[top + HP : top + 2 * HP, lanes] = value[a * HP : (a + 1) * HP, half:]
    shrunk = shr_ref[...]
    back_ref[:, 0] = dot_table(lat_t_ref, shrunk).astype(BF).reshape(plan.n, plan.t, plan.d)
    band = dot(slot_ref[...], shrunk).astype(BF)
    band_ref[:, 0] = band.reshape(plan.n, plan.bt, plan.d)
    if e:

        @pl.when(q == plan.q - 1)
        def _():
            ride_wait(*ride)


def pair_block(plan, rows):
    return pl.BlockSpec((plan.n, 1, rows, plan.d), lambda q: (0, q, 0, 0))


def spectral_call(
    plan, valid, received, lat, lat_t, slots, m1, b1, m2, b2, passengers=(), collective_id=None
):
    riders = Riders(plan, passengers)
    kept = (plan.q, 2, 2 * HP, plan.d)
    kept_spec = pl.BlockSpec((1, 2, 2 * HP, plan.d), lambda q: (q, 0, 0, 0))
    kept_shape = jax.ShapeDtypeStruct(kept, BF)
    rows = plan.bt
    return pl.pallas_call(
        functools.partial(spectral_kernel, plan, riders),
        grid=(plan.q,),
        in_specs=[
            SMEM,
            pair_block(plan, plan.t),
            whole(lat.shape),
            whole(lat_t.shape),
            whole(slots.shape),
            whole(m1.shape),
            whole(b1.shape),
            whole(m2.shape),
            whole(b2.shape),
        ]
        + riders.specs(),
        out_specs=[
            pair_block(plan, plan.t),
            pair_block(plan, rows),
            kept_spec,
            kept_spec,
            kept_spec,
            kept_spec,
            whole((1, plan.d)),
        ]
        + riders.specs(),
        out_shape=[
            jax.ShapeDtypeStruct((plan.n, plan.q, plan.t, plan.d), BF),
            jax.ShapeDtypeStruct((plan.n, plan.q, rows, plan.d), BF),
            kept_shape,
            kept_shape,
            kept_shape,
            kept_shape,
            jax.ShapeDtypeStruct((1, plan.d), F32),
        ]
        + riders.shapes(),
        scratch_shapes=[pltpu.VMEM((4 * HP, plan.d), BF)] + riders.scratch(),
        compiler_params=params(collective_id),
        cost_estimate=cost(20e9, 25e6),
        name="spectral_forward",
    )(valid, received, lat, lat_t, slots, m1, b1, m2, b2, *riders.arrays)


def feed_kernel(
    plan,
    first,
    final,
    riders,
    tiles,
    scale_ref,
    tok_ref,
    cot_ref,
    recv_ref,
    par_ref,
    lon_t_ref,
    lon_ref,
    perm_ref,
    perm_t_ref,
    w1_ref,
    b1_ref,
    w2_ref,
    *rest,
):
    e = riders.count
    srcs, rest = rest[:e], rest[e:]
    if first:
        in1_ref = in2_ref = None
    else:
        in1_ref, in2_ref = rest[:2]
        rest = rest[2:]
    mixed_ref, send_ref, gx_ref, out1_ref, out2_ref, db1_ref, vec_ref = rest[:7]
    dsts, rest = rest[7 : 7 + e], rest[7 + e :]
    (
        dw1,
        dw2,
        ring,
        rows_ref,
        x1_ref,
        xn,
        xn_t,
        gm,
        gm_t,
        act,
        gz,
        down,
        up,
        sem,
        ring_sem,
        *ride_sems,
    ) = rest
    i = pl.program_id(0)
    last = plan.chunks - 1
    tile = act.shape[1]
    flat = plan.flat
    ride = riders.bind(srcs, dsts, ride_sems)

    @pl.when(i == 0)
    def _():
        for c in range(2):
            ring_load(plan, recv_ref, ring, ring_sem, c).start()
        if not first:
            pltpu.make_async_copy(in1_ref, dw1, sem.at[1]).start()
            pltpu.make_async_copy(in2_ref, dw2, sem.at[2]).start()
        ride_start(*ride)
        if first:
            dw1[...] = jnp.zeros_like(dw1)
            dw2[...] = jnp.zeros_like(dw2)
        db1_ref[...] = jnp.zeros_like(db1_ref)
        vec_ref[...] = jnp.zeros_like(vec_ref)
        if plan.flatp > flat:
            pad = jnp.zeros((plan.flatp - flat, tile), BF)
            for ref in (act, gz):
                ref[flat:, :] = pad
            pad = jnp.zeros((plan.flatp - flat, plan.d), F32)
            down[flat:, :] = pad
            up[flat:, :] = pad
        deinterleave_in(plan, perm_t_ref, recv_ref, ring, ring_sem, rows_ref)

    for u in range(plan.rb):
        span = slice(u * plan.w, (u + 1) * plan.w)
        x = tok_ref[0, u].astype(F32)
        unit, _ = norm_parts(x)
        filtered = dot_table(lon_t_ref, rows_ref[i * plan.rb + u])
        x1 = x + filtered + (unit * par_ref[0:1] + par_ref[1:2])
        x1_ref[u] = x1
        unit, _ = norm_parts(x1)
        down[span, :] = unit * par_ref[2:3] + par_ref[3:4]
        up[span, :] = cot_ref[0, u].astype(F32) * scale_ref[i * plan.rb + u]
    normed = down[...].astype(BF)
    xn[...] = normed[:flat]
    xn_t[...] = normed.T
    grads = up[...].astype(BF)
    gm[...] = grads[:flat]
    gm_t[...] = grads.T
    vec_ref[0:1] += jnp.sum(grads.astype(F32), 0, keepdims=True)
    down[...] = jnp.zeros_like(down)
    up[...] = jnp.zeros_like(up)

    if not first:

        @pl.when(i == 0)
        def _():
            pltpu.make_async_copy(in1_ref, dw1, sem.at[1]).wait()
            pltpu.make_async_copy(in2_ref, dw2, sem.at[2]).wait()

    def columns(t):
        return pl.ds(pl.multiple_of(t * tile, tile), tile)

    def body(t, carry):
        cols = columns(t)
        z = dot(xn[...], w1_ref[:, cols]) + b1_ref[:, cols]
        ga = dot_nt(gm[...], w2_ref[cols, :])
        hidden, slope = gelu_both(z)
        grad = ga * slope
        act[:flat, :] = hidden.astype(BF)
        gz[:flat, :] = grad.astype(BF)
        db1_ref[:, cols] += jnp.sum(grad, 0, keepdims=True)
        down[:flat, :] += dot(act[:flat, :], w2_ref[cols, :])
        up[:flat, :] += dot_nt(gz[:flat, :], w1_ref[:, cols])
        dw1[:, cols] += dot(xn_t[...], gz[...])
        dw2[:, cols] += dot(gm_t[...], act[...])
        return carry

    lax.fori_loop(0, tiles, body, 0)

    if not final:

        @pl.when(i == last)
        def _():
            pltpu.make_async_copy(dw1, out1_ref, sem.at[1]).start()
            pltpu.make_async_copy(dw2, out2_ref, sem.at[2]).start()

    for u in range(plan.rb):
        span = slice(u * plan.w, (u + 1) * plan.w)
        x1 = x1_ref[u]
        scale = scale_ref[i * plan.rb + u]
        keep = jnp.where(scale > 0.0, 1.0, 0.0)
        mixed_ref[u] = ((x1 + down[span, :] + par_ref[4:5]) * keep).astype(BF)
        unit, rstd = norm_parts(x1)
        grad = up[span, :]
        vec_ref[1:2] += jnp.sum(grad * unit, 0, keepdims=True)
        vec_ref[2:3] += jnp.sum(grad, 0, keepdims=True)
        gx = cot_ref[0, u].astype(F32) * scale + norm_back(grad, unit, rstd, par_ref[2:3])
        gx_ref[u] = gx.astype(gx_ref.dtype)
        rows_ref[i * plan.rb + u] = dot_table(lon_ref, gx.astype(BF)).astype(BF)

    if plan.flatp > flat:
        down[flat:, :] = jnp.zeros((plan.flatp - flat, plan.d), F32)
        up[flat:, :] = jnp.zeros((plan.flatp - flat, plan.d), F32)

    @pl.when(i == last)
    def _():
        stores = interleave_out(plan, perm_ref, rows_ref, ring, ring_sem, send_ref)
        if final:
            stage = (act, xn_t, gz, gm_t)
            pending = {}
            for t in range(2 * tiles):
                side = t % 4
                if side in pending:
                    pending.pop(side).wait()
                cols = slice(t // 2 * tile, (t // 2 + 1) * tile)
                if t % 2 == 0:
                    held = stage[side].at[: plan.d, :]
                    held[...] = dw1[:, cols].astype(BF)
                    out = out1_ref.at[:, cols]
                else:
                    held = stage[side].at[:tile, : plan.d]
                    held[...] = dw2[:, cols].astype(BF).T
                    out = out2_ref.at[cols]
                pending[side] = pltpu.make_async_copy(held, out, sem.at[1 + side])
                pending[side].start()
            for copy in pending.values():
                copy.wait()
        else:
            pltpu.make_async_copy(dw1, out1_ref, sem.at[1]).wait()
            pltpu.make_async_copy(dw2, out2_ref, sem.at[2]).wait()
        for store in stores:
            store.wait()
        ride_wait(*ride)


def feed_call(
    plan, s, scales, tokens, cotangent, received, vectors, w1, b1, w2, sums, final, passengers,
    collective_id
):
    first = sums is None
    ff = w1.shape[1]
    tile = 512
    d, flat = plan.d, plan.flat
    flatp = plan.flatp
    shape = (plan.pairs, plan.t, d)
    riders = Riders(plan, passengers)
    in_specs = [
        SMEM,
        row_block(plan, s),
        row_block(plan, s),
        ANY,
        whole((8, d)),
        whole((2, plan.w, plan.ki)),
        whole((2, plan.ki, plan.w)),
        whole(plan.perm.shape),
        whole(plan.perm_t.shape),
        whole_once((d, ff)),
        whole((1, ff)),
        whole_once((ff, d)),
    ] + riders.specs()
    operands = [
        scales,
        tokens,
        cotangent,
        received,
        vectors,
        plan.lon_both_t,
        plan.lon_both,
        plan.perm,
        plan.perm_t,
        w1,
        b1,
        w2,
        *riders.arrays,
    ]
    aliases = {}
    if not first:
        if not final:
            aliases = {len(operands): 3, len(operands) + 1: 4}
        in_specs += [ANY, ANY]
        operands += list(sums)
    if final:
        wides = [jax.ShapeDtypeStruct((d, ff), BF), jax.ShapeDtypeStruct((ff, d), BF)]
    else:
        wides = [jax.ShapeDtypeStruct((d, ff), F32)] * 2
    return pl.pallas_call(
        functools.partial(feed_kernel, plan, first, final, riders, ff // tile),
        grid=(plan.chunks,),
        in_specs=in_specs,
        out_specs=[
            own_block(plan),
            ANY,
            own_block(plan),
            ANY,
            ANY,
            whole((1, ff)),
            whole((8, d)),
        ]
        + riders.specs(),
        out_shape=[
            jax.ShapeDtypeStruct((plan.r, plan.w, d), BF),
            jax.ShapeDtypeStruct(shape, BF),
            jax.ShapeDtypeStruct((plan.r, plan.w, d), BF),
            *wides,
            jax.ShapeDtypeStruct((1, ff), F32),
            jax.ShapeDtypeStruct((8, d), F32),
        ]
        + riders.shapes(),
        scratch_shapes=[
            pltpu.VMEM((d, ff), F32),
            pltpu.VMEM((d, ff), F32),
            pltpu.VMEM((2, 4, plan.t, d), BF),
            pltpu.VMEM((plan.r, plan.ki, d), BF),
            pltpu.VMEM((plan.rb, plan.w, d), F32),
            pltpu.VMEM((flat, d), BF),
            pltpu.VMEM((d, flatp), BF),
            pltpu.VMEM((flat, d), BF),
            pltpu.VMEM((d, flatp), BF),
            pltpu.VMEM((flatp, tile), BF),
            pltpu.VMEM((flatp, tile), BF),
            pltpu.VMEM((flatp, d), F32),
            pltpu.VMEM((flatp, d), F32),
            pltpu.SemaphoreType.DMA((5,)),
            pltpu.SemaphoreType.DMA((2,)),
        ]
        + riders.scratch(),
        input_output_aliases=aliases,
        compiler_params=params(collective_id),
        cost_estimate=cost(70e9, 60e6),
        name="feed_forward",
    )(*operands)


def spectral_back_kernel(
    plan,
    riders,
    in_ref,
    spec_ref,
    hid_ref,
    slope1_ref,
    slope2_ref,
    lat_ref,
    lat_t_ref,
    m1t_ref,
    m2t_ref,
    *rest,
):
    e = riders.count
    srcs, rest = rest[:e], rest[e:]
    out_ref, dw1_ref, dw2_ref, db1_ref, db2_ref = rest[:5]
    dsts, rest = rest[5 : 5 + e], rest[5 + e :]
    dm1_ref, dm2_ref, gs_ref, gu_ref = rest[:4]
    q = pl.program_id(0)
    half = plan.d // 2
    if e:
        ride = riders.bind(srcs, dsts, rest[4:])

        @pl.when(q == 0)
        def _():
            ride_start(*ride)

    @pl.when(q == 0)
    def _():
        dm1_ref[...] = jnp.zeros_like(dm1_ref)
        dm2_ref[...] = jnp.zeros_like(dm2_ref)
        db1_ref[...] = jnp.zeros_like(db1_ref)
        db2_ref[...] = jnp.zeros_like(db2_ref)

    x = in_ref[:, 0].reshape(plan.n * plan.t, plan.d)
    grad = dot_table(lat_ref, x).astype(BF)
    for g in range(2):
        lanes = slice(g * half, (g + 1) * half)
        for a in range(2):
            top = a * 2 * HP
            gu_ref[a * HP : (a + 1) * HP, :half] = grad[top : top + HP, lanes]
            gu_ref[a * HP : (a + 1) * HP, half:] = grad[top + HP : top + 2 * HP, lanes]
        gu2 = gu_ref[...].astype(F32) * slope2_ref[0, g].astype(F32)
        db2_ref[g] += jnp.sum(gu2, 0, keepdims=True)
        gu2 = gu2.astype(BF)
        dm2_ref[g] += dot_tn(hid_ref[0, g], gu2)
        gu1 = (dot(gu2, m2t_ref[g]) * slope1_ref[0, g].astype(F32)).astype(BF)
        db1_ref[g] += jnp.sum(gu1.astype(F32), 0, keepdims=True)
        dm1_ref[g] += dot_tn(spec_ref[0, g], gu1)
        gs = dot(gu1, m1t_ref[g]).astype(BF)
        for a in range(2):
            top = a * 2 * HP
            gs_ref[top : top + HP, lanes] = gs[a * HP : (a + 1) * HP, :half]
            gs_ref[top + HP : top + 2 * HP, lanes] = gs[a * HP : (a + 1) * HP, half:]
    out_ref[:, 0] = dot_table(lat_t_ref, gs_ref[...]).astype(BF).reshape(plan.n, plan.t, plan.d)

    @pl.when(q == plan.q - 1)
    def _():
        blocks, size = dw1_ref.shape[2:4]
        for wide, narrow in ((dm1_ref, dw1_ref), (dm2_ref, dw2_ref)):
            for g in range(2):
                for b in range(blocks):
                    re = slice(b * size, (b + 1) * size)
                    im = slice(half + b * size, half + (b + 1) * size)
                    narrow[0, g, b] = wide[g, re, re] + wide[g, im, im]
                    narrow[1, g, b] = wide[g, re, im] - wide[g, im, re]
        if e:
            ride_wait(*ride)


def spectral_back_call(
    plan, blocks, size, received, kept, lat, lat_t, m1t, m2t, passengers=(), collective_id=None
):
    riders = Riders(plan, passengers)
    small = (2, 2, blocks // 2, size, size)
    kept_spec = pl.BlockSpec((1, 2, 2 * HP, plan.d), lambda q: (q, 0, 0, 0))
    wide = (2, plan.d, plan.d)
    thin = (2, 1, plan.d)
    return pl.pallas_call(
        functools.partial(spectral_back_kernel, plan, riders),
        grid=(plan.q,),
        in_specs=[pair_block(plan, plan.t)]
        + [kept_spec] * 4
        + [whole(lat.shape), whole(lat_t.shape), whole(wide), whole(wide)]
        + riders.specs(),
        out_specs=[
            pair_block(plan, plan.t),
            whole(small),
            whole(small),
            whole(thin),
            whole(thin),
        ]
        + riders.specs(),
        out_shape=[
            jax.ShapeDtypeStruct((plan.n, plan.q, plan.t, plan.d), BF),
            jax.ShapeDtypeStruct(small, F32),
            jax.ShapeDtypeStruct(small, F32),
            jax.ShapeDtypeStruct(thin, F32),
            jax.ShapeDtypeStruct(thin, F32),
        ]
        + riders.shapes(),
        scratch_shapes=[
            pltpu.VMEM(wide, F32),
            pltpu.VMEM(wide, F32),
            pltpu.VMEM((4 * HP, plan.d), BF),
            pltpu.VMEM((2 * HP, plan.d), BF),
        ]
        + riders.scratch(),
        compiler_params=params(collective_id),
        cost_estimate=cost(1e9, 1e6),
        name="spectral_backward",
    )(received, *kept, lat, lat_t, m1t, m2t, *riders.arrays)


def last_kernel(
    plan,
    scale_ref,
    tok_ref,
    gx_ref,
    in_ref,
    gain_ref,
    lon_t_ref,
    perm_t_ref,
    *rest,
):
    out_ref, vec_ref, rows_ref = rest[-3:]
    i = pl.program_id(0)

    @pl.when(i == 0)
    def _():
        vec_ref[...] = jnp.zeros_like(vec_ref)
        deinterleave(plan, perm_t_ref, in_ref, rows_ref)

    for u in range(plan.rb):
        keep = jnp.where(scale_ref[i * plan.rb + u] > 0.0, 1.0, 0.0)
        unit, rstd = norm_parts(tok_ref[0, u].astype(F32))
        gx = gx_ref[u].astype(F32)
        grad = gx + dot_table(lon_t_ref, rows_ref[i * plan.rb + u])
        vec_ref[0:1] += jnp.sum(grad * unit, 0, keepdims=True) * keep
        vec_ref[1:2] += jnp.sum(grad, 0, keepdims=True) * keep
        out_ref[0, u] = (gx + norm_back(grad, unit, rstd, gain_ref[0:1])) * keep


def last_call(plan, s, scales, tokens, gx, received, gain, earlier):
    operands = [scales, tokens, gx, received, gain, plan.lon_t, plan.perm_t]
    in_specs = [
        SMEM,
        row_block(plan, s),
        own_block(plan),
        whole((plan.pairs, plan.t, plan.d)),
        whole((8, plan.d)),
        whole((2, plan.w, plan.ki)),
        whole(plan.perm_t.shape),
    ]
    aliases = {}
    if earlier is not None:
        aliases = {len(operands): 0}
        operands.append(earlier)
        in_specs.append(ANY)
    return pl.pallas_call(
        functools.partial(last_kernel, plan),
        grid=(plan.chunks,),
        in_specs=in_specs,
        out_specs=[row_block(plan, s), whole((2, plan.d))],
        out_shape=[
            jax.ShapeDtypeStruct((plan.s, plan.r, plan.w, plan.d), F32),
            jax.ShapeDtypeStruct((2, plan.d), F32),
        ],
        scratch_shapes=[pltpu.VMEM((plan.r, plan.ki, plan.d), BF)],
        input_output_aliases=aliases,
        compiler_params=params(),
        cost_estimate=cost(1e9, 1e6),
        name="lon_backward",
    )(*operands)


def band_kernel(plan, in_ref, *rest):
    out_ref, tall = rest[-2:]
    mb = plan.mb
    height = 2 * plan.kw
    for src in range(plan.n):
        for t in range(plan.kk):
            k = src * plan.kk + t
            if k >= plan.kw:
                continue
            both = in_ref[src, t // 2].astype(F32)
            for p in range(2):
                at = ((t % 2) * 2 + p) * mb
                part = both[at : at + mb]
                for g in range(plan.d // 128):
                    tall[g, pl.ds(2 * k + p, mb, stride=height), :] = part[
                        :, g * 128 : (g + 1) * 128
                    ]
    for m in range(mb):
        for g in range(plan.d // 128):
            piece = tall[g, m * height : (m + 1) * height, :].astype(BF)
            out_ref[0, m, :, :, g * 128 : (g + 1) * 128] = piece.reshape(plan.kw, 2, 128)


def band_call(plan, s, received, earlier):
    shape = (plan.s, plan.mb, plan.kw, 2, plan.d)
    operands = [received]
    in_specs = [whole(received.shape)]
    aliases = {}
    if earlier is not None:
        aliases = {1: 0}
        operands.append(earlier)
        in_specs.append(ANY)
    return pl.pallas_call(
        functools.partial(band_kernel, plan),
        grid=(1,),
        in_specs=in_specs,
        out_specs=pl.BlockSpec((1,) + shape[1:], lambda i: (s, 0, 0, 0, 0)),
        out_shape=jax.ShapeDtypeStruct(shape, BF),
        scratch_shapes=[pltpu.VMEM((plan.d // 128, 2 * plan.mb * plan.kw, 128), F32)],
        input_output_aliases=aliases,
        compiler_params=params(),
        cost_estimate=cost(1e8, 1e6),
        name="band_output",
    )(*operands)


def every_peer(total, step_of):
    def body(step, carry):
        step_of(step)
        return carry

    lax.fori_loop(1, total, body, 0)


def place(lanes, index):
    return {"batch": index // lanes, "lat": lax.rem(index, lanes)}


def greet_all(total, lanes, me):
    barrier = pltpu.get_barrier_semaphore()

    def greet(step):
        pl.semaphore_signal(
            barrier,
            inc=1,
            device_id=place(lanes, lax.rem(me + step, total)),
            device_id_type=pl.DeviceIdType.MESH,
        )

    every_peer(total, greet)
    pl.semaphore_wait(barrier, total - 1)


def block_sum_kernel(total, lanes, xs, *rest):
    ins, outs, helds, sems = rest[:xs], rest[xs : 2 * xs], rest[2 * xs : 3 * xs], rest[3 * xs :]
    me = lax.axis_index("batch") * lanes + lax.axis_index("lat")
    greet_all(total, lanes, me)

    def part(a, step, peer):
        return pltpu.make_async_remote_copy(
            src_ref=ins[a].at[peer],
            dst_ref=helds[a].at[step],
            send_sem=sems[4 * a].at[step],
            recv_sem=sems[4 * a + 1].at[step],
            device_id=place(lanes, peer),
            device_id_type=pl.DeviceIdType.MESH,
        )

    def result(a, step, peer, slot):
        return pltpu.make_async_remote_copy(
            src_ref=outs[a].at[me],
            dst_ref=outs[a].at[slot],
            send_sem=sems[4 * a + 2].at[step],
            recv_sem=sems[4 * a + 3].at[step],
            device_id=place(lanes, peer),
            device_id_type=pl.DeviceIdType.MESH,
        )

    ahead = lambda step: lax.rem(me + step, total)
    behind = lambda step: lax.rem(me + total - step, total)
    for a in range(xs):
        every_peer(total, lambda step: part(a, step, ahead(step)).start())
    for a in range(xs):
        helds[a][0] = ins[a][me]
        every_peer(total, lambda step: part(a, step, behind(step)).wait_recv())
        outs[a][me] = jnp.sum(helds[a][...].astype(F32), 0).astype(outs[a].dtype)
        every_peer(total, lambda step: result(a, step, ahead(step), me).start())
    for a in range(xs):
        every_peer(total, lambda step: part(a, step, ahead(step)).wait_send())
        every_peer(total, lambda step: result(a, step, behind(step), behind(step)).wait_recv())
        every_peer(total, lambda step: result(a, step, ahead(step), me).wait_send())


def block_sum(total, lanes, xs, collective_id):
    vmem = pl.BlockSpec(memory_space=pltpu.VMEM)
    sems = [pltpu.SemaphoreType.DMA((total,))] * (4 * len(xs))
    return pl.pallas_call(
        functools.partial(block_sum_kernel, total, lanes, len(xs)),
        in_specs=[vmem] * len(xs),
        out_specs=[vmem] * len(xs),
        out_shape=[jax.ShapeDtypeStruct(x.shape, x.dtype) for x in xs],
        scratch_shapes=[pltpu.VMEM(x.shape, x.dtype) for x in xs] + sems,
        compiler_params=pltpu.CompilerParams(
            collective_id=collective_id, has_side_effects=True, vmem_limit_bytes=VMEM_BYTES
        ),
        cost_estimate=cost(1e8, 1e6),
        name="block_sum",
    )(*xs)


def pack(total, parts, dtype, rows):
    flat = jnp.concatenate([x.reshape(-1).astype(dtype) for x in parts])
    unit = total * rows * 128
    padded = -(-flat.shape[0] // unit) * unit
    return jnp.pad(flat, (0, padded - flat.shape[0])).reshape(total, -1, 128)


def unpack(packed, parts):
    flat = packed.reshape(-1).astype(F32)
    out, at = [], 0
    for x in parts:
        out.append(flat[at : at + x.size].reshape(x.shape))
        at += x.size
    return out


def exchange(x):
    return lax.all_to_all(x, "lat", split_axis=0, concat_axis=0, tiled=True)


def on_device(
    bands,
    tokens,
    cotangent,
    sample_weight,
    row_count,
    band_count,
    norm1_gain,
    norm1_bias,
    spec_w1,
    spec_b1,
    spec_w2,
    spec_b2,
    norm2_gain,
    norm2_bias,
    fc1_weight,
    fc1_bias,
    fc2_weight,
    fc2_bias,
):
    lane = lax.axis_index("lat")
    n = lax.axis_size("lat")
    samples, row_slots, width, channels = tokens.shape
    blocks, size = spec_w1.shape[1], spec_w1.shape[2]
    plan = Plan(n, samples, row_slots, width, channels, bands)
    wb1, wb2 = wide_bias(spec_b1), wide_bias(spec_b2)
    row = lambda v: v.reshape(1, -1)
    blank = jnp.zeros_like(fc2_bias)
    vectors = jnp.stack([norm1_gain, norm1_bias, norm2_gain, norm2_bias, fc2_bias] + [blank] * 3)
    own_rows = jnp.sum(jnp.where(jnp.arange(n) == lane, row_count, 0))
    held = jnp.arange(row_slots) < own_rows
    scales = sample_weight.astype(F32)[:, None] * 0.5 * held[None, :].astype(F32)
    slot_step = jnp.arange(plan.kp)
    valid = ((slot_step < plan.kk) & (lane * plan.kk + slot_step < plan.kw)).astype(F32)
    grouped = (n, plan.q, plan.t, channels)
    listed = (plan.pairs, plan.t, channels)

    ids = itertools.count()
    spread = (-1,) + grouped

    def spectral_forward(x, passengers=()):
        collective_id = next(ids) if passengers else None
        out = spectral_call(
            plan, valid, x, lat, lat_t, slots, m1, wb1, m2, wb2, passengers, collective_id
        )
        forward.append(out)
        return out[7:]

    def feed(s, back, sums, passengers):
        out = feed_call(
            plan,
            s,
            scales[s],
            tokens,
            cotangent,
            back.reshape(listed),
            vectors,
            fc1_weight,
            row(fc1_bias),
            fc2_weight,
            sums,
            s == samples - 1,
            passengers,
            next(ids),
        )
        feeds.append(out)
        return out[7:]

    def backward(s, grads, passengers=()):
        out = spectral_back_call(
            plan,
            blocks,
            size,
            grads,
            forward[s][2:6],
            lat,
            lat_t,
            m1t,
            m2t,
            passengers,
            next(ids) if passengers else None,
        )
        spectral.append(out)
        return out[0], out[5:]

    forward, feeds, spectral, band_parts, grads, lon_grads = [], [], [], {}, {}, {}
    sent = first_call(plan, 0, 1, tokens, vectors)[0].reshape(spread)
    tables = Tables(plan, blocks, size)
    extra = tables.operands(row_count, band_count, spec_w1, spec_w2)
    others, lat, lat_t, slots, m1, m2, m1t, m2t, spectra = first_call(
        plan, 1, samples - 1, tokens, vectors, [(sent, 0)], next(ids), tables, extra
    )
    others = others.reshape(spread)
    (spectra,) = spectral_forward(spectra, [(others, 0)])
    (back,) = spectral_forward(spectra, [(forward[0][0], None)])
    for s in range(samples):
        sums = (feeds[-1][3], feeds[-1][4]) if s else None
        kinds, passengers = [], []
        if s + 1 < samples:
            kinds.append("back")
            passengers.append((forward[s + 1][0], None))
        if s + 2 < samples:
            kinds.append("spectra")
            passengers.append((others, s + 1))
        if s >= 1:
            kinds.append("grads")
            passengers.append((feeds[s - 1][1].reshape(grouped), None))
        kinds.append("band")
        passengers.append((forward[s][1], None))
        arrived = dict(zip(kinds, feed(s, back, sums, passengers)))
        back = arrived.get("back")
        if s + 2 < samples:
            spectral_forward(arrived["spectra"])
        band_parts[s] = arrived["band"]
        if s >= 1:
            grads[s - 1] = arrived["grads"]
    after = lambda x, y: lax.optimization_barrier((x, y))[0]

    def last(s, earlier):
        return last_call(
            plan,
            s,
            scales[s],
            tokens,
            feeds[s][2],
            lon_grads[s].reshape(listed),
            vectors,
            earlier,
        )

    large = lax.psum((feeds[-1][3], feeds[-1][4]), ("batch", "lat"))
    grads[0] = after(grads[0], feeds[-1][6])
    lon, got = backward(0, grads[0], [(feeds[-1][1].reshape(grouped), None)])
    grads[samples - 1] = got[0]
    for s in range(1, samples):
        lon, got = backward(s, grads[s], [(lon, None)])
        lon_grads[s - 1] = got[0]
    lon_grads[samples - 1] = exchange(lon)
    ended = spectral[-1][3]
    band_parts = {s: after(part, ended) for s, part in band_parts.items()}
    for s in range(samples - 1):
        lon_grads[s] = after(lon_grads[s], ended)
    tokens_grad, spectrum, finals = None, None, []
    for s in range(samples):
        tokens_grad, vec = last(s, tokens_grad)
        finals.append(vec)
        spectrum = band_call(plan, s, band_parts[s], spectrum)
    mixed = jnp.stack([f[0] for f in feeds])

    add = lambda parts: functools.reduce(jnp.add, parts)
    devices = lax.axis_size("batch") * n
    feed_vec = add([f[6] for f in feeds])
    block_grad = lambda i: add([b[i] for b in spectral]).reshape(2, blocks, size, size)
    zeros = jnp.sum(add([f[6] for f in forward]))
    small = [
        feed_vec[1],
        feed_vec[2],
        add([f[5] for f in feeds]),
        feed_vec[0],
        narrow_bias(add([b[3] for b in spectral]), blocks, size),
        narrow_bias(add([b[4] for b in spectral]), blocks, size),
        zeros.reshape(1),
        add(finals),
    ]
    blocky = [block_grad(1), block_grad(2)]
    packed = [pack(devices, blocky, BF, 16), pack(devices, small, F32, 8)]
    packed = block_sum(devices, n, packed, next(ids))
    blocky = unpack(packed[0], blocky)
    small = unpack(packed[1], small)
    large = after(large, small[7])
    large = (large[0].astype(F32), large[1].astype(F32))
    zero_fraction = small[6][0] / (lax.axis_size("batch") * samples * H * plan.kw * 2 * channels)
    return (
        mixed,
        spectrum.transpose(0, 1, 3, 2, 4),
        tokens_grad,
        small[7][0],
        small[7][1],
        blocky[0],
        small[4],
        blocky[1],
        small[5],
        small[0],
        small[1],
        large[0],
        small[2].reshape(-1),
        large[1],
        small[3],
        zero_fraction,
    )


def solution(mesh):
    rows = P("batch", "lat", None, None)
    in_specs = (rows, rows, P("batch")) + (P(),) * 14
    out_specs = (rows, P("batch", "lat", None, None, None), rows) + (P(),) * 13
    lanes = mesh.shape["lat"]

    def run(tokens, cotangent, *rest):
        row_slots = tokens.shape[1] // lanes
        return jax.shard_map(
            functools.partial(on_device, row_slots + 1),
            mesh=mesh,
            in_specs=in_specs,
            out_specs=out_specs,
            check_vma=False,
        )(tokens, cotangent, *rest)

    return run
```

```python
import functools
import itertools
import math

import jax
import jax.numpy as jnp
import numpy as np
from jax import lax
from jax.experimental import pallas as pl
from jax.experimental.pallas import tpu as pltpu
from jax.sharding import PartitionSpec as P

H = 90
HP = 96

NORM_EPS = 1e-06
SHRINK_LAMBDA = 0.01
SHRINK_SOFTNESS = 0.1
INV_ROOT_TAU = 1.0 / math.sqrt(2.0 * math.pi)
BF = jnp.bfloat16
F32 = jnp.float32
VMEM_BYTES = 64 * 1024 * 1024


def dot(a, b):
    return jnp.dot(a, b, preferred_element_type=F32)


def dot_nt(a, b):
    return lax.dot_general(a, b, (((1,), (1,)), ((), ())), preferred_element_type=F32)


def dot_tn(a, b):
    return lax.dot_general(a, b, (((0,), (0,)), ((), ())), preferred_element_type=F32)


def dot_table(table_ref, x):
    return dot(table_ref[0], x) + dot(table_ref[1], x)


def two_parts(table):
    high = table.astype(BF)
    return high, (table - high.astype(table.dtype)).astype(BF)


def norm_parts(x):
    mean = jnp.mean(x, -1, keepdims=True)
    centred = x - mean
    rstd = lax.rsqrt(jnp.mean(centred * centred, -1, keepdims=True) + NORM_EPS)
    return centred * rstd, rstd


def norm_back(grad, unit, rstd, gain):
    e = grad * gain
    return rstd * (
        e - jnp.mean(e, -1, keepdims=True) - unit * jnp.mean(e * unit, -1, keepdims=True)
    )


def gauss_parts(v):
    d = 1.0 + jnp.abs(v) * (0.3275911 / math.sqrt(2.0))
    t = pl.reciprocal(d, approx=True)
    e = jnp.exp2(v * v * (-0.5 * math.log2(math.e)))
    poly = 1.061405429 * 0.5
    for c in (-1.453152027, 1.421413741, -0.284496736, 0.254829592):
        poly = poly * t + 0.5 * c
    tail = poly * t * e
    cdf = jnp.where(v >= 0.0, 1.0 - tail, tail)
    return cdf, v * e * INV_ROOT_TAU


def gelu_both(v):
    cdf, slope_part = gauss_parts(v)
    return v * cdf, cdf + slope_part


def shrink_both(u):
    a = jnp.maximum(jnp.abs(u) - SHRINK_LAMBDA, 0.0)
    d = a + SHRINK_SOFTNESS
    t = pl.reciprocal(d, approx=True)
    t = t * (2.0 - d * t)
    size = a * a * t
    value = jnp.where(u >= 0.0, size, -size)
    slope = a * (a + 2.0 * SHRINK_SOFTNESS) * (t * t)
    return value, slope


class Plan:
    def __init__(self, n, samples, rows, width, channels, bands):
        self.n, self.s, self.r, self.w, self.d, self.mb = n, samples, rows, width, channels, bands
        self.kw = width // 2 + 1
        self.kk = -(-self.kw // n)
        self.kp = self.kk + self.kk % 2
        self.q = self.kp // 2
        self.rp = -(-rows // 4) * 4
        self.t = 4 * self.rp
        self.pairs = n * self.q
        self.ki = n * self.kp * 2
        self.rb = max(b for b in (4, 3, 2, 1) if rows % b == 0)
        self.chunks = rows // self.rb
        self.flat = self.rb * width
        self.flatp = max(-(-self.flat // 256) * 256, channels)
        self.bt = -(-4 * bands // 8) * 8
        j = np.arange(n)[:, None]
        t = np.arange(self.kp)[None, :]
        self.k_index = (j * self.kk + t).astype(np.int64)
        self.k_valid = (t < self.kk) & (self.k_index < self.kw)
        k = np.where(self.k_valid, self.k_index, 0).reshape(-1)
        ok = self.k_valid.reshape(-1).astype(np.float64)
        angle = 2.0 * np.pi * ((k[:, None] * np.arange(width)[None, :]) % width) / width
        scale = ok[:, None] / math.sqrt(width)
        fwd = np.stack([np.cos(angle) * scale, -np.sin(angle) * scale], 1).reshape(self.ki, width)
        factor = np.where((k == 0) | (2 * k == width), 1.0, 2.0)[:, None, None]
        both = (fwd.reshape(-1, 2, width) * factor).reshape(self.ki, width)
        self.lon = np.stack(two_parts(fwd))
        self.lon_both = np.stack(two_parts(both))
        self.lon_t = np.stack(two_parts(np.ascontiguousarray(fwd.T)))
        self.lon_both_t = np.stack(two_parts(np.ascontiguousarray(both.T)))
        perm = np.zeros((16, self.rp, rows, 16))
        for a in range(16):
            for r in range(rows):
                perm[a, r, r, a] = 1.0
        self.perm = perm.reshape(16 * self.rp, rows * 16).astype(BF)
        self.perm_t = np.ascontiguousarray(self.perm.T)


class Tables:
    def __init__(self, plan, blocks, size):
        self.plan, self.blocks, self.size = plan, blocks, size
        n, rp, mb = plan.n, plan.rp, plan.mb
        kh, h = np.arange(HP)[:, None], np.arange(HP)[None, :]
        angle = 2.0 * np.pi * (kh * h % H) / H
        weight = ((kh < H) & (h < H)) / math.sqrt(H)
        cosine, sine = np.cos(angle) * weight, np.sin(angle) * weight
        part = np.block([[cosine, sine], [-sine, cosine]])
        self.base = np.stack(two_parts(np.kron(np.eye(2), part)))
        col = np.arange(n * 4 * rp)
        group, step = col // rp % 4, col % rp
        self.columns = np.stack([col // (4 * rp), group * HP + step, step]).astype(np.int32)
        bt = plan.bt
        line = np.arange(n * bt)
        group, step = line % bt // mb, line % bt % mb
        step = np.where(group < 4, step, 1 << 20)
        lines = np.stack([line // bt, group * HP + step, step]).astype(np.int32)
        self.lines = lines[:, :, None]
        half = blocks // 2
        spots = np.zeros((half, size, half * size))
        for i in range(half):
            spots[i, :, i * size : (i + 1) * size] = np.eye(size)
        self.spots = spots.astype(BF)
        wide = 4 * HP
        d = plan.d
        shapes = [(2, wide, n * 4 * rp), (2, n * 4 * rp, wide), (n * bt, wide)] + [(2, d, d)] * 4
        self.shapes = [jax.ShapeDtypeStruct(x, BF) for x in shapes]

    def operands(self, row_count, band_count, spec_w1, spec_w2):
        return [
            row_count,
            band_count,
            spec_w1,
            spec_w2,
            self.base,
            self.columns[:, None, :],
            self.lines,
            self.spots,
        ]

    def in_specs(self):
        weight = (2, self.blocks, self.size, self.size)
        shapes = [weight, weight, self.base.shape, (3, 1, self.columns.shape[1])]
        shapes += [self.lines.shape, self.spots.shape]
        return [SMEM, SMEM] + [whole(x) for x in shapes]

    def out_specs(self):
        return [whole(x.shape) for x in self.shapes]

    def build(self, ins, outs):
        rows_ref, bands_ref, w1_ref, w2_ref, base_ref, col_ref, line_ref, spot_ref = ins
        lat_ref, lat_t_ref, slot_ref, m1_ref, m2_ref, m1t_ref, m2t_ref = outs
        n = self.plan.n

        def spread(counts_ref, owner):
            first = jnp.zeros(owner.shape, jnp.int32)
            held = jnp.zeros(owner.shape, jnp.int32)
            start = jnp.int32(0)
            for j in range(n):
                count = counts_ref[j]
                first = jnp.where(owner == j, start, first)
                held = jnp.where(owner == j, count, held)
                start = start + count
            return first, held

        first, held = spread(rows_ref, col_ref[0])
        target = jnp.where(col_ref[2] < held, col_ref[1] + first, -1)
        pick = lax.broadcasted_iota(jnp.int32, (4 * HP, target.shape[1]), 0) == target
        pick = jnp.where(pick, 1.0, 0.0).astype(BF)
        for part in range(2):
            full = dot(base_ref[part], pick)
            lat_ref[part] = full.astype(BF)
            lat_t_ref[part] = full.T.astype(BF)
        first, held = spread(bands_ref, line_ref[0])
        target = jnp.where(line_ref[2] < held, line_ref[1] + first, -1)
        pick = lax.broadcasted_iota(jnp.int32, (target.shape[0], 4 * HP), 1) == target
        slot_ref[...] = jnp.where(pick, 1.0, 0.0).astype(BF)
        half, size = self.blocks // 2, self.size
        mid = half * size
        for w_ref, m_ref, mt_ref in ((w1_ref, m1_ref, m1t_ref), (w2_ref, m2_ref, m2t_ref)):
            for g in range(2):
                for i in range(half):
                    low = slice(i * size, (i + 1) * size)
                    high = slice(mid + i * size, mid + (i + 1) * size)
                    re, im = w_ref[0, g * half + i], w_ref[1, g * half + i]
                    for ref, place_in, sign in ((m_ref, dot, 1.0), (mt_ref, dot_tn, -1.0)):
                        real = place_in(re, spot_ref[i]).astype(BF)
                        imag = place_in(im, spot_ref[i]) * sign
                        ref[g, low, :mid] = real
                        ref[g, high, mid:] = real
                        ref[g, low, mid:] = imag.astype(BF)
                        ref[g, high, :mid] = (-imag).astype(BF)


def wide_bias(bias):
    return bias.reshape(2, 2, -1).transpose(1, 0, 2).reshape(2, 1, -1)


def narrow_bias(wide, blocks, size):
    return wide.reshape(2, 2, -1).transpose(1, 0, 2).reshape(2, blocks, size)


def whole(shape):
    zeros = (0,) * len(shape)
    return pl.BlockSpec(shape, lambda *_: zeros)


def whole_once(shape):
    zeros = (0,) * len(shape)
    return pl.BlockSpec(shape, lambda *_: zeros, pipeline_mode=pl.Buffered(1))


SMEM = pl.BlockSpec(memory_space=pltpu.SMEM)
ANY = pl.BlockSpec(memory_space=pl.ANY)


def params(collective_id=None):
    if collective_id is None:
        return pltpu.CompilerParams(
            dimension_semantics=("arbitrary",), vmem_limit_bytes=VMEM_BYTES
        )
    return pltpu.CompilerParams(
        dimension_semantics=("arbitrary",),
        vmem_limit_bytes=VMEM_BYTES,
        collective_id=collective_id,
        has_side_effects=True,
    )


def ride_copy(n, me, src, dst, send, recv, e, step):
    peer = lax.rem(me + step, n)
    return pltpu.make_async_remote_copy(
        src_ref=src.at[peer],
        dst_ref=dst.at[me],
        send_sem=send.at[e, step],
        recv_sem=recv.at[e, step],
        device_id={"lat": peer},
        device_id_type=pl.DeviceIdType.MESH,
    )


def ride_arrival(n, me, src, dst, send, recv, e, step):
    peer = lax.rem(me + n - step, n)
    return pltpu.make_async_remote_copy(
        src_ref=src.at[peer],
        dst_ref=dst.at[peer],
        send_sem=send.at[e, step],
        recv_sem=recv.at[e, step],
        device_id={"lat": peer},
        device_id_type=pl.DeviceIdType.MESH,
    )


def ride_greet(n):
    me = lax.axis_index("lat")
    barrier = pltpu.get_barrier_semaphore()
    for step in range(1, n):
        pl.semaphore_signal(
            barrier,
            inc=1,
            device_id={"lat": lax.rem(me + step, n)},
            device_id_type=pl.DeviceIdType.MESH,
        )
    pl.semaphore_wait(barrier, n - 1)


def ride_start(n, srcs, dsts, send, recv, own, greet=True):
    me = lax.axis_index("lat")
    if greet:
        ride_greet(n)
    for e, (src, dst) in enumerate(zip(srcs, dsts)):
        for step in range(1, n):
            ride_copy(n, me, src, dst, send, recv, e, step).start()
        pltpu.make_async_copy(src.at[me], dst.at[me], own.at[e]).start()


def ride_wait(n, srcs, dsts, send, recv, own):
    me = lax.axis_index("lat")
    for e, (src, dst) in enumerate(zip(srcs, dsts)):
        pltpu.make_async_copy(src.at[me], dst.at[me], own.at[e]).wait()
        for step in range(1, n):
            ride_copy(n, me, src, dst, send, recv, e, step).wait_send()
            ride_arrival(n, me, src, dst, send, recv, e, step).wait_recv()


def cost(flops, size):
    return pl.CostEstimate(flops=int(flops), bytes_accessed=int(size), transcendentals=0)


def interleave(plan, perm_ref, rows_ref, out_ref):
    def body(c, carry):
        at = pl.multiple_of(c * 16, 16)
        block = rows_ref[:, pl.ds(at, 16), :].reshape(plan.r * 16, plan.d)
        mixed = dot(perm_ref[...], block).astype(BF)
        out_ref[pl.ds(c * 4, 4)] = mixed.reshape(4, plan.t, plan.d)
        return carry

    lax.fori_loop(0, plan.ki // 16, body, 0)


def deinterleave(plan, perm_t_ref, in_ref, rows_ref):
    def body(c, carry):
        at = pl.multiple_of(c * 16, 16)
        block = in_ref[pl.ds(c * 4, 4)].reshape(4 * plan.t, plan.d)
        rows = dot(perm_t_ref[...], block).astype(BF)
        rows_ref[:, pl.ds(at, 16), :] = rows.reshape(plan.r, 16, plan.d)
        return carry

    lax.fori_loop(0, plan.ki // 16, body, 0)


def interleave_out(plan, perm_ref, rows_ref, ring, sem, out_ref):
    def copy(c):
        return pltpu.make_async_copy(
            ring.at[lax.rem(c, 2)], out_ref.at[pl.ds(c * 4, 4)], sem.at[lax.rem(c, 2)]
        )

    def body(c, carry):
        @pl.when(c >= 2)
        def _():
            copy(c - 2).wait()

        at = pl.multiple_of(c * 16, 16)
        block = rows_ref[:, pl.ds(at, 16), :].reshape(plan.r * 16, plan.d)
        mixed = dot(perm_ref[...], block).astype(BF)
        ring[lax.rem(c, 2)] = mixed.reshape(4, plan.t, plan.d)
        copy(c).start()
        return carry

    lax.fori_loop(0, plan.ki // 16, body, 0)
    return [copy(plan.ki // 16 - 2), copy(plan.ki // 16 - 1)]


def ring_load(plan, in_ref, ring, sem, c):
    return pltpu.make_async_copy(
        in_ref.at[pl.ds(c * 4, 4)], ring.at[lax.rem(c, 2)], sem.at[lax.rem(c, 2)]
    )


def deinterleave_in(plan, perm_t_ref, in_ref, ring, sem, rows_ref):
    steps = plan.ki // 16

    def body(c, carry):
        ring_load(plan, in_ref, ring, sem, c).wait()
        at = pl.multiple_of(c * 16, 16)
        block = ring[lax.rem(c, 2)].reshape(4 * plan.t, plan.d)
        rows = dot(perm_t_ref[...], block).astype(BF)
        rows_ref[:, pl.ds(at, 16), :] = rows.reshape(plan.r, 16, plan.d)

        @pl.when(c + 2 < steps)
        def _():
            ring_load(plan, in_ref, ring, sem, c + 2).start()

        return carry

    lax.fori_loop(0, steps, body, 0)


class Riders:
    def __init__(self, plan, passengers):
        self.n = plan.n
        self.arrays = [a for a, _ in passengers]
        self.leads = [lead for _, lead in passengers]
        self.count = len(passengers)

    def shapes(self):
        return [
            jax.ShapeDtypeStruct(a.shape if lead is None else a.shape[1:], a.dtype)
            for a, lead in zip(self.arrays, self.leads)
        ]

    def specs(self):
        return [ANY] * self.count

    def scratch(self):
        if not self.count:
            return []
        dma = pltpu.SemaphoreType.DMA
        return [dma((self.count, self.n)), dma((self.count, self.n)), dma((self.count,))]

    def bind(self, srcs, dsts, sems):
        srcs = [r if lead is None else r.at[lead] for r, lead in zip(srcs, self.leads)]
        return (self.n, srcs, dsts) + tuple(sems)


def first_kernel(plan, riders, tables, tok_ref, vec_ref, lon_ref, perm_ref, *rest):
    e = riders.count
    t_in = 0 if tables is None else 8
    t_out = 0 if tables is None else 7
    t_ins, rest = rest[:t_in], rest[t_in:]
    srcs, rest = rest[:e], rest[e:]
    out_ref, rest = rest[0], rest[1:]
    t_outs, rest = rest[:t_out], rest[t_out:]
    dsts, rows_ref, sems = rest[:e], rest[e], rest[e + 1 :]
    i = pl.program_id(0)
    c = lax.rem(i, plan.chunks)
    if e:
        ride = riders.bind(srcs, dsts, sems)

        @pl.when(i == 0)
        def _():
            ride_start(*ride)

    for u in range(plan.rb):
        unit, _ = norm_parts(tok_ref[0, u].astype(F32))
        normed = (unit * vec_ref[0:1] + vec_ref[1:2]).astype(BF)
        rows_ref[c * plan.rb + u] = dot_table(lon_ref, normed).astype(BF)

    @pl.when(c == plan.chunks - 1)
    def _():
        interleave(plan, perm_ref, rows_ref, out_ref.at[0])

    @pl.when(i == pl.num_programs(0) - 1)
    def _():
        if tables is not None:
            tables.build(t_ins, t_outs)
        if e:
            ride_wait(*ride)


def row_block(plan, s):
    return pl.BlockSpec((1, plan.rb, plan.w, plan.d), lambda i: (s, i, 0, 0))


def own_block(plan):
    return pl.BlockSpec((plan.rb, plan.w, plan.d), lambda i: (i, 0, 0))


def first_call(
    plan, start, count, tokens, vectors, passengers=(), collective_id=None, tables=None, extra=()
):
    shape = (plan.pairs, plan.t, plan.d)
    chunks = plan.chunks
    riders = Riders(plan, passengers)
    return pl.pallas_call(
        functools.partial(first_kernel, plan, riders, tables),
        grid=(count * chunks,),
        in_specs=[
            pl.BlockSpec(
                (1, plan.rb, plan.w, plan.d),
                lambda i: (start + i // chunks, lax.rem(i, chunks), 0, 0),
            ),
            whole((8, plan.d)),
            whole((2, plan.ki, plan.w)),
            whole(plan.perm.shape),
        ]
        + (tables.in_specs() if tables else [])
        + riders.specs(),
        out_specs=[pl.BlockSpec((1,) + shape, lambda i: (i // chunks, 0, 0, 0))]
        + (tables.out_specs() if tables else [])
        + riders.specs(),
        out_shape=[jax.ShapeDtypeStruct((count,) + shape, BF)]
        + (tables.shapes if tables else [])
        + riders.shapes(),
        scratch_shapes=[pltpu.VMEM((plan.r, plan.ki, plan.d), BF)] + riders.scratch(),
        compiler_params=params(collective_id),
        cost_estimate=cost(9e9 * count, 8e6 * count),
        name="lon_forward",
    )(tokens, vectors, plan.lon, plan.perm, *extra, *riders.arrays)


def spectral_kernel(
    plan,
    riders,
    carried,
    valid_ref,
    in_ref,
    lat_ref,
    lat_t_ref,
    slot_ref,
    m1_ref,
    b1_ref,
    m2_ref,
    b2_ref,
    *rest,
):
    e = riders.count
    earlier, srcs, rest = rest[:carried], rest[carried : carried + e], rest[carried + e :]
    back_ref, band_ref, spec_ref, hid_ref, slope1_ref, slope2_ref, zero_ref = rest[:7]
    dsts, shr_ref, sems = rest[7 : 7 + e], rest[7 + e], rest[8 + e :]
    q = pl.program_id(0)
    half = plan.d // 2
    if e:
        ride = riders.bind(srcs, dsts, sems)

        @pl.when(q == 0)
        def _():
            ride_start(*ride)

    @pl.when(q == 0)
    def _():
        zero_ref[...] = earlier[0][...] if carried else jnp.zeros_like(zero_ref)

    x = in_ref[:, 0].reshape(plan.n * plan.t, plan.d)
    spec = dot_table(lat_ref, x).astype(BF)
    ok = (lax.broadcasted_iota(jnp.int32, (HP, 1), 0) < H).astype(F32)
    for g in range(2):
        lanes = slice(g * half, (g + 1) * half)
        for a in range(2):
            top = a * 2 * HP
            spec_ref[0, g, a * HP : (a + 1) * HP, :half] = spec[top : top + HP, lanes]
            spec_ref[0, g, a * HP : (a + 1) * HP, half:] = spec[top + HP : top + 2 * HP, lanes]
        u1 = dot(spec_ref[0, g], m1_ref[g]) + b1_ref[g]
        hidden, slope = gelu_both(u1)
        hid_ref[0, g] = hidden.astype(BF)
        slope1_ref[0, g] = slope.astype(BF)
        u2 = dot(hid_ref[0, g], m2_ref[g]) + b2_ref[g]
        small = (jnp.abs(u2) <= SHRINK_LAMBDA).astype(F32)
        for a in range(2):
            part = small[a * HP : (a + 1) * HP] * ok
            zero_ref[...] += jnp.sum(part, 0, keepdims=True) * valid_ref[q * 2 + a]
        value, slope = shrink_both(u2)
        slope2_ref[0, g] = slope.astype(BF)
        value = value.astype(BF)
        for a in range(2):
            top = a * 2 * HP
            shr_ref[top : top + HP, lanes] = value[a * HP : (a + 1) * HP, :half]
            shr_ref[top + HP : top + 2 * HP, lanes] = value[a * HP : (a + 1) * HP, half:]
    shrunk = shr_ref[...]
    back_ref[:, 0] = dot_table(lat_t_ref, shrunk).astype(BF).reshape(plan.n, plan.t, plan.d)
    band = dot(slot_ref[...], shrunk).astype(BF)
    band_ref[:, 0] = band.reshape(plan.n, plan.bt, plan.d)
    if e:

        @pl.when(q == plan.q - 1)
        def _():
            ride_wait(*ride)


def pair_block(plan, rows):
    return pl.BlockSpec((plan.n, 1, rows, plan.d), lambda q: (0, q, 0, 0))


def spectral_call(
    plan, valid, received, lat, lat_t, slots, m1, b1, m2, b2, earlier, passengers, collective_id
):
    riders = Riders(plan, passengers)
    kept = (plan.q, 2, 2 * HP, plan.d)
    kept_spec = pl.BlockSpec((1, 2, 2 * HP, plan.d), lambda q: (q, 0, 0, 0))
    kept_shape = jax.ShapeDtypeStruct(kept, BF)
    rows = plan.bt
    return pl.pallas_call(
        functools.partial(spectral_kernel, plan, riders, len(earlier)),
        grid=(plan.q,),
        in_specs=[
            SMEM,
            pair_block(plan, plan.t),
            whole(lat.shape),
            whole(lat_t.shape),
            whole(slots.shape),
            whole(m1.shape),
            whole(b1.shape),
            whole(m2.shape),
            whole(b2.shape),
        ]
        + [whole((1, plan.d))] * len(earlier)
        + riders.specs(),
        out_specs=[
            pair_block(plan, plan.t),
            pair_block(plan, rows),
            kept_spec,
            kept_spec,
            kept_spec,
            kept_spec,
            whole((1, plan.d)),
        ]
        + riders.specs(),
        out_shape=[
            jax.ShapeDtypeStruct((plan.n, plan.q, plan.t, plan.d), BF),
            jax.ShapeDtypeStruct((plan.n, plan.q, rows, plan.d), BF),
            kept_shape,
            kept_shape,
            kept_shape,
            kept_shape,
            jax.ShapeDtypeStruct((1, plan.d), F32),
        ]
        + riders.shapes(),
        scratch_shapes=[pltpu.VMEM((4 * HP, plan.d), BF)] + riders.scratch(),
        compiler_params=params(collective_id),
        cost_estimate=cost(20e9, 25e6),
        name="spectral_forward",
    )(valid, received, lat, lat_t, slots, m1, b1, m2, b2, *earlier, *riders.arrays)


def feed_kernel(
    plan,
    first,
    final,
    riders,
    tiles,
    scale_ref,
    tok_ref,
    cot_ref,
    recv_ref,
    par_ref,
    lon_t_ref,
    lon_ref,
    perm_ref,
    perm_t_ref,
    w1_ref,
    b1_ref,
    w2_ref,
    *rest,
):
    e = riders.count
    srcs, rest = rest[:e], rest[e:]
    if first:
        in1_ref = in2_ref = None
    else:
        in1_ref, in2_ref, _, db1_in, vec_in = rest[:5]
        rest = rest[5:]
    mixed_ref, send_ref, gx_ref, out1_ref, out2_ref, db1_ref, vec_ref = rest[:7]
    dsts, rest = rest[7 : 7 + e], rest[7 + e :]
    (
        dw1,
        dw2,
        ring,
        rows_ref,
        x1_ref,
        xn,
        xn_t,
        gm,
        gm_t,
        act,
        gz,
        down,
        up,
        sem,
        ring_sem,
        *ride_sems,
    ) = rest
    i = pl.program_id(0)
    last = plan.chunks - 1
    tile = act.shape[1]
    flat = plan.flat
    ride = riders.bind(srcs, dsts, ride_sems)

    @pl.when(i == 0)
    def _():
        for c in range(2):
            ring_load(plan, recv_ref, ring, ring_sem, c).start()
        if not first:
            pltpu.make_async_copy(in1_ref, dw1, sem.at[1]).start()
            pltpu.make_async_copy(in2_ref, dw2, sem.at[2]).start()
        ride_start(*ride)
        if first:
            dw1[...] = jnp.zeros_like(dw1)
            dw2[...] = jnp.zeros_like(dw2)
        db1_ref[...] = jnp.zeros_like(db1_ref) if first else db1_in[...]
        vec_ref[...] = jnp.zeros_like(vec_ref) if first else vec_in[...]
        if plan.flatp > flat:
            pad = jnp.zeros((plan.flatp - flat, tile), BF)
            for ref in (act, gz):
                ref[flat:, :] = pad
            pad = jnp.zeros((plan.flatp - flat, plan.d), F32)
            down[flat:, :] = pad
            up[flat:, :] = pad
        deinterleave_in(plan, perm_t_ref, recv_ref, ring, ring_sem, rows_ref)

    for u in range(plan.rb):
        span = slice(u * plan.w, (u + 1) * plan.w)
        x = tok_ref[0, u].astype(F32)
        unit, _ = norm_parts(x)
        filtered = dot_table(lon_t_ref, rows_ref[i * plan.rb + u])
        x1 = x + filtered + (unit * par_ref[0:1] + par_ref[1:2])
        x1_ref[u] = x1
        unit, _ = norm_parts(x1)
        down[span, :] = unit * par_ref[2:3] + par_ref[3:4]
        up[span, :] = cot_ref[0, u].astype(F32) * scale_ref[i * plan.rb + u]
    normed = down[...].astype(BF)
    xn[...] = normed[:flat]
    xn_t[...] = normed.T
    grads = up[...].astype(BF)
    gm[...] = grads[:flat]
    gm_t[...] = grads.T
    vec_ref[0:1] += jnp.sum(grads.astype(F32), 0, keepdims=True)
    down[...] = jnp.zeros_like(down)
    up[...] = jnp.zeros_like(up)

    if not first:

        @pl.when(i == 0)
        def _():
            pltpu.make_async_copy(in1_ref, dw1, sem.at[1]).wait()
            pltpu.make_async_copy(in2_ref, dw2, sem.at[2]).wait()

    def columns(t):
        return pl.ds(pl.multiple_of(t * tile, tile), tile)

    def body(t, carry):
        cols = columns(t)
        z = dot(xn[...], w1_ref[:, cols]) + b1_ref[:, cols]
        ga = dot_nt(gm[...], w2_ref[cols, :])
        hidden, slope = gelu_both(z)
        grad = ga * slope
        act[:flat, :] = hidden.astype(BF)
        gz[:flat, :] = grad.astype(BF)
        db1_ref[:, cols] += jnp.sum(grad, 0, keepdims=True)
        down[:flat, :] += dot(act[:flat, :], w2_ref[cols, :])
        up[:flat, :] += dot_nt(gz[:flat, :], w1_ref[:, cols])
        dw1[:, cols] += dot(xn_t[...], gz[...])
        dw2[:, cols] += dot(gm_t[...], act[...])
        return carry

    lax.fori_loop(0, tiles, body, 0)

    if not final:

        @pl.when(i == last)
        def _():
            pltpu.make_async_copy(dw1, out1_ref, sem.at[1]).start()
            pltpu.make_async_copy(dw2, out2_ref, sem.at[2]).start()

    for u in range(plan.rb):
        span = slice(u * plan.w, (u + 1) * plan.w)
        x1 = x1_ref[u]
        scale = scale_ref[i * plan.rb + u]
        keep = jnp.where(scale > 0.0, 1.0, 0.0)
        mixed_ref[0, u] = ((x1 + down[span, :] + par_ref[4:5]) * keep).astype(BF)
        unit, rstd = norm_parts(x1)
        grad = up[span, :]
        vec_ref[1:2] += jnp.sum(grad * unit, 0, keepdims=True)
        vec_ref[2:3] += jnp.sum(grad, 0, keepdims=True)
        gx = cot_ref[0, u].astype(F32) * scale + norm_back(grad, unit, rstd, par_ref[2:3])
        gx_ref[u] = gx.astype(gx_ref.dtype)
        rows_ref[i * plan.rb + u] = dot_table(lon_ref, gx.astype(BF)).astype(BF)

    if plan.flatp > flat:
        down[flat:, :] = jnp.zeros((plan.flatp - flat, plan.d), F32)
        up[flat:, :] = jnp.zeros((plan.flatp - flat, plan.d), F32)

    @pl.when(i == last)
    def _():
        stores = interleave_out(plan, perm_ref, rows_ref, ring, ring_sem, send_ref)
        if final:
            stage = (act, xn_t, gz, gm_t)
            pending = {}
            for t in range(2 * tiles):
                side = t % 4
                if side in pending:
                    pending.pop(side).wait()
                cols = slice(t // 2 * tile, (t // 2 + 1) * tile)
                if t % 2 == 0:
                    held = stage[side].at[: plan.d, :]
                    held[...] = dw1[:, cols].astype(BF)
                    out = out1_ref.at[:, cols]
                else:
                    held = stage[side].at[:tile, : plan.d]
                    held[...] = dw2[:, cols].astype(BF).T
                    out = out2_ref.at[cols]
                pending[side] = pltpu.make_async_copy(held, out, sem.at[1 + side])
                pending[side].start()
            for copy in pending.values():
                copy.wait()
        else:
            pltpu.make_async_copy(dw1, out1_ref, sem.at[1]).wait()
            pltpu.make_async_copy(dw2, out2_ref, sem.at[2]).wait()
        for store in stores:
            store.wait()
        ride_wait(*ride)


def feed_call(
    plan, s, scales, tokens, cotangent, received, vectors, w1, b1, w2, sums, final, passengers,
    collective_id
):
    first = sums is None
    ff = w1.shape[1]
    tile = 512
    d, flat = plan.d, plan.flat
    flatp = plan.flatp
    shape = (plan.pairs, plan.t, d)
    riders = Riders(plan, passengers)
    in_specs = [
        SMEM,
        row_block(plan, s),
        row_block(plan, s),
        ANY,
        whole((8, d)),
        whole((2, plan.w, plan.ki)),
        whole((2, plan.ki, plan.w)),
        whole(plan.perm.shape),
        whole(plan.perm_t.shape),
        whole_once((d, ff)),
        whole((1, ff)),
        whole_once((ff, d)),
    ] + riders.specs()
    operands = [
        scales,
        tokens,
        cotangent,
        received,
        vectors,
        plan.lon_both_t,
        plan.lon_both,
        plan.perm,
        plan.perm_t,
        w1,
        b1,
        w2,
        *riders.arrays,
    ]
    aliases = {}
    if not first:
        aliases = {len(operands) + 2: 0}
        if not final:
            aliases.update({len(operands): 3, len(operands) + 1: 4})
        in_specs += [ANY, ANY, ANY, whole((1, ff)), whole((8, d))]
        operands += list(sums)
    if final:
        wides = [jax.ShapeDtypeStruct((d, ff), BF), jax.ShapeDtypeStruct((ff, d), BF)]
    else:
        wides = [jax.ShapeDtypeStruct((d, ff), F32)] * 2
    return pl.pallas_call(
        functools.partial(feed_kernel, plan, first, final, riders, ff // tile),
        grid=(plan.chunks,),
        in_specs=in_specs,
        out_specs=[
            row_block(plan, s),
            ANY,
            own_block(plan),
            ANY,
            ANY,
            whole((1, ff)),
            whole((8, d)),
        ]
        + riders.specs(),
        out_shape=[
            jax.ShapeDtypeStruct((plan.s, plan.r, plan.w, d), BF),
            jax.ShapeDtypeStruct(shape, BF),
            jax.ShapeDtypeStruct((plan.r, plan.w, d), BF),
            *wides,
            jax.ShapeDtypeStruct((1, ff), F32),
            jax.ShapeDtypeStruct((8, d), F32),
        ]
        + riders.shapes(),
        scratch_shapes=[
            pltpu.VMEM((d, ff), F32),
            pltpu.VMEM((d, ff), F32),
            pltpu.VMEM((2, 4, plan.t, d), BF),
            pltpu.VMEM((plan.r, plan.ki, d), BF),
            pltpu.VMEM((plan.rb, plan.w, d), F32),
            pltpu.VMEM((flat, d), BF),
            pltpu.VMEM((d, flatp), BF),
            pltpu.VMEM((flat, d), BF),
            pltpu.VMEM((d, flatp), BF),
            pltpu.VMEM((flatp, tile), BF),
            pltpu.VMEM((flatp, tile), BF),
            pltpu.VMEM((flatp, d), F32),
            pltpu.VMEM((flatp, d), F32),
            pltpu.SemaphoreType.DMA((5,)),
            pltpu.SemaphoreType.DMA((2,)),
        ]
        + riders.scratch(),
        input_output_aliases=aliases,
        compiler_params=params(collective_id),
        cost_estimate=cost(70e9, 60e6),
        name="feed_forward",
    )(*operands)


def spectral_back_kernel(
    plan,
    riders,
    carried,
    in_ref,
    spec_ref,
    hid_ref,
    slope1_ref,
    slope2_ref,
    lat_ref,
    lat_t_ref,
    m1t_ref,
    m2t_ref,
    *rest,
):
    e = riders.count
    earlier, srcs, rest = rest[:carried], rest[carried : carried + e], rest[carried + e :]
    out_ref, dw1_ref, dw2_ref, db1_ref, db2_ref = rest[:5]
    dsts, rest = rest[5 : 5 + e], rest[5 + e :]
    dm1_ref, dm2_ref, gs_ref, gu_ref = rest[:4]
    q = pl.program_id(0)
    half = plan.d // 2
    if e:
        ride = riders.bind(srcs, dsts, rest[4:])

        @pl.when(q == 0)
        def _():
            ride_start(*ride)

    @pl.when(q == 0)
    def _():
        dm1_ref[...] = jnp.zeros_like(dm1_ref)
        dm2_ref[...] = jnp.zeros_like(dm2_ref)
        db1_ref[...] = earlier[2][...] if carried else jnp.zeros_like(db1_ref)
        db2_ref[...] = earlier[3][...] if carried else jnp.zeros_like(db2_ref)

    x = in_ref[:, 0].reshape(plan.n * plan.t, plan.d)
    grad = dot_table(lat_ref, x).astype(BF)
    for g in range(2):
        lanes = slice(g * half, (g + 1) * half)
        for a in range(2):
            top = a * 2 * HP
            gu_ref[a * HP : (a + 1) * HP, :half] = grad[top : top + HP, lanes]
            gu_ref[a * HP : (a + 1) * HP, half:] = grad[top + HP : top + 2 * HP, lanes]
        gu2 = gu_ref[...].astype(F32) * slope2_ref[0, g].astype(F32)
        db2_ref[g] += jnp.sum(gu2, 0, keepdims=True)
        gu2 = gu2.astype(BF)
        dm2_ref[g] += dot_tn(hid_ref[0, g], gu2)
        gu1 = (dot(gu2, m2t_ref[g]) * slope1_ref[0, g].astype(F32)).astype(BF)
        db1_ref[g] += jnp.sum(gu1.astype(F32), 0, keepdims=True)
        dm1_ref[g] += dot_tn(spec_ref[0, g], gu1)
        gs = dot(gu1, m1t_ref[g]).astype(BF)
        for a in range(2):
            top = a * 2 * HP
            gs_ref[top : top + HP, lanes] = gs[a * HP : (a + 1) * HP, :half]
            gs_ref[top + HP : top + 2 * HP, lanes] = gs[a * HP : (a + 1) * HP, half:]
    out_ref[:, 0] = dot_table(lat_t_ref, gs_ref[...]).astype(BF).reshape(plan.n, plan.t, plan.d)

    @pl.when(q == plan.q - 1)
    def _():
        blocks, size = dw1_ref.shape[2:4]
        for i, (wide, narrow) in enumerate(((dm1_ref, dw1_ref), (dm2_ref, dw2_ref))):
            for g in range(2):
                for b in range(blocks):
                    re = slice(b * size, (b + 1) * size)
                    im = slice(half + b * size, half + (b + 1) * size)
                    real = wide[g, re, re] + wide[g, im, im]
                    imag = wide[g, re, im] - wide[g, im, re]
                    if carried:
                        real += earlier[i][0, g, b]
                        imag += earlier[i][1, g, b]
                    narrow[0, g, b] = real
                    narrow[1, g, b] = imag
        if e:
            ride_wait(*ride)


def spectral_back_call(
    plan, blocks, size, received, kept, lat, lat_t, m1t, m2t, earlier, passengers, collective_id
):
    riders = Riders(plan, passengers)
    small = (2, 2, blocks // 2, size, size)
    kept_spec = pl.BlockSpec((1, 2, 2 * HP, plan.d), lambda q: (q, 0, 0, 0))
    wide = (2, plan.d, plan.d)
    thin = (2, 1, plan.d)
    return pl.pallas_call(
        functools.partial(spectral_back_kernel, plan, riders, len(earlier)),
        grid=(plan.q,),
        in_specs=[pair_block(plan, plan.t)]
        + [kept_spec] * 4
        + [whole(lat.shape), whole(lat_t.shape), whole(wide), whole(wide)]
        + [whole(x.shape) for x in earlier]
        + riders.specs(),
        out_specs=[
            pair_block(plan, plan.t),
            whole(small),
            whole(small),
            whole(thin),
            whole(thin),
        ]
        + riders.specs(),
        out_shape=[
            jax.ShapeDtypeStruct((plan.n, plan.q, plan.t, plan.d), BF),
            jax.ShapeDtypeStruct(small, F32),
            jax.ShapeDtypeStruct(small, F32),
            jax.ShapeDtypeStruct(thin, F32),
            jax.ShapeDtypeStruct(thin, F32),
        ]
        + riders.shapes(),
        scratch_shapes=[
            pltpu.VMEM(wide, F32),
            pltpu.VMEM(wide, F32),
            pltpu.VMEM((4 * HP, plan.d), BF),
            pltpu.VMEM((2 * HP, plan.d), BF),
        ]
        + riders.scratch(),
        compiler_params=params(collective_id),
        cost_estimate=cost(1e9, 1e6),
        name="spectral_backward",
    )(received, *kept, lat, lat_t, m1t, m2t, *earlier, *riders.arrays)


def last_kernel(
    plan,
    scale_ref,
    tok_ref,
    gx_ref,
    in_ref,
    gain_ref,
    lon_t_ref,
    perm_t_ref,
    *rest,
):
    out_ref, vec_ref, rows_ref = rest[-3:]
    i = pl.program_id(0)

    @pl.when(i == 0)
    def _():
        vec_ref[...] = jnp.zeros_like(vec_ref)
        deinterleave(plan, perm_t_ref, in_ref, rows_ref)

    for u in range(plan.rb):
        keep = jnp.where(scale_ref[i * plan.rb + u] > 0.0, 1.0, 0.0)
        unit, rstd = norm_parts(tok_ref[0, u].astype(F32))
        gx = gx_ref[u].astype(F32)
        grad = gx + dot_table(lon_t_ref, rows_ref[i * plan.rb + u])
        vec_ref[0:1] += jnp.sum(grad * unit, 0, keepdims=True) * keep
        vec_ref[1:2] += jnp.sum(grad, 0, keepdims=True) * keep
        out_ref[0, u] = (gx + norm_back(grad, unit, rstd, gain_ref[0:1])) * keep


def last_call(plan, s, scales, tokens, gx, received, gain, earlier):
    operands = [scales, tokens, gx, received, gain, plan.lon_t, plan.perm_t]
    in_specs = [
        SMEM,
        row_block(plan, s),
        own_block(plan),
        whole((plan.pairs, plan.t, plan.d)),
        whole((8, plan.d)),
        whole((2, plan.w, plan.ki)),
        whole(plan.perm_t.shape),
    ]
    aliases = {}
    if earlier is not None:
        aliases = {len(operands): 0}
        operands.append(earlier)
        in_specs.append(ANY)
    return pl.pallas_call(
        functools.partial(last_kernel, plan),
        grid=(plan.chunks,),
        in_specs=in_specs,
        out_specs=[row_block(plan, s), whole((2, plan.d))],
        out_shape=[
            jax.ShapeDtypeStruct((plan.s, plan.r, plan.w, plan.d), F32),
            jax.ShapeDtypeStruct((2, plan.d), F32),
        ],
        scratch_shapes=[pltpu.VMEM((plan.r, plan.ki, plan.d), BF)],
        input_output_aliases=aliases,
        compiler_params=params(),
        cost_estimate=cost(1e9, 1e6),
        name="lon_backward",
    )(*operands)


def band_kernel(plan, in_ref, *rest):
    out_ref, tall = rest[-2:]
    mb = plan.mb
    height = 2 * plan.kw
    for src in range(plan.n):
        for t in range(plan.kk):
            k = src * plan.kk + t
            if k >= plan.kw:
                continue
            both = in_ref[src, t // 2].astype(F32)
            for p in range(2):
                at = ((t % 2) * 2 + p) * mb
                part = both[at : at + mb]
                for g in range(plan.d // 128):
                    tall[g, pl.ds(2 * k + p, mb, stride=height), :] = part[
                        :, g * 128 : (g + 1) * 128
                    ]
    for m in range(mb):
        for g in range(plan.d // 128):
            piece = tall[g, m * height : (m + 1) * height, :].astype(BF)
            out_ref[0, m, :, :, g * 128 : (g + 1) * 128] = piece.reshape(plan.kw, 2, 128)


def band_call(plan, s, received, earlier):
    shape = (plan.s, plan.mb, plan.kw, 2, plan.d)
    operands = [received]
    in_specs = [whole(received.shape)]
    aliases = {}
    if earlier is not None:
        aliases = {1: 0}
        operands.append(earlier)
        in_specs.append(ANY)
    return pl.pallas_call(
        functools.partial(band_kernel, plan),
        grid=(1,),
        in_specs=in_specs,
        out_specs=pl.BlockSpec((1,) + shape[1:], lambda i: (s, 0, 0, 0, 0)),
        out_shape=jax.ShapeDtypeStruct(shape, BF),
        scratch_shapes=[pltpu.VMEM((plan.d // 128, 2 * plan.mb * plan.kw, 128), F32)],
        input_output_aliases=aliases,
        compiler_params=params(),
        cost_estimate=cost(1e8, 1e6),
        name="band_output",
    )(*operands)


def every_peer(total, step_of):
    def body(step, carry):
        step_of(step)
        return carry

    lax.fori_loop(1, total, body, 0)


def place(lanes, index):
    return {"batch": index // lanes, "lat": lax.rem(index, lanes)}


def greet_all(total, lanes, me):
    barrier = pltpu.get_barrier_semaphore()

    def greet(step):
        pl.semaphore_signal(
            barrier,
            inc=1,
            device_id=place(lanes, lax.rem(me + step, total)),
            device_id_type=pl.DeviceIdType.MESH,
        )

    every_peer(total, greet)
    pl.semaphore_wait(barrier, total - 1)


def block_sum_kernel(total, lanes, xs, riders, *rest):
    e = riders.count
    ins, srcs, rest = rest[:xs], rest[xs : xs + e], rest[xs + e :]
    outs, dsts, rest = rest[:xs], rest[xs : xs + e], rest[xs + e :]
    helds, sems = rest[:xs], rest[xs:]
    ride = riders.bind(srcs, dsts, sems[4 * xs :])
    me = lax.axis_index("batch") * lanes + lax.axis_index("lat")
    greet_all(total, lanes, me)

    def part(a, step, peer):
        return pltpu.make_async_remote_copy(
            src_ref=ins[a].at[peer],
            dst_ref=helds[a].at[step],
            send_sem=sems[4 * a].at[step],
            recv_sem=sems[4 * a + 1].at[step],
            device_id=place(lanes, peer),
            device_id_type=pl.DeviceIdType.MESH,
        )

    def result(a, step, peer, slot):
        return pltpu.make_async_remote_copy(
            src_ref=outs[a].at[me],
            dst_ref=outs[a].at[slot],
            send_sem=sems[4 * a + 2].at[step],
            recv_sem=sems[4 * a + 3].at[step],
            device_id=place(lanes, peer),
            device_id_type=pl.DeviceIdType.MESH,
        )

    ahead = lambda step: lax.rem(me + step, total)
    behind = lambda step: lax.rem(me + total - step, total)
    for a in range(xs):
        every_peer(total, lambda step: part(a, step, ahead(step)).start())
    ride_start(*ride, greet=False)
    for a in range(xs):
        helds[a][0] = ins[a][me]
        every_peer(total, lambda step: part(a, step, behind(step)).wait_recv())
        outs[a][me] = jnp.sum(helds[a][...].astype(F32), 0).astype(outs[a].dtype)
        every_peer(total, lambda step: result(a, step, ahead(step), me).start())
    for a in range(xs):
        every_peer(total, lambda step: part(a, step, ahead(step)).wait_send())
        every_peer(total, lambda step: result(a, step, behind(step), behind(step)).wait_recv())
        every_peer(total, lambda step: result(a, step, ahead(step), me).wait_send())
    ride_wait(*ride)


def block_sum(total, plan, xs, passengers, collective_id):
    riders = Riders(plan, passengers)
    vmem = pl.BlockSpec(memory_space=pltpu.VMEM)
    sems = [pltpu.SemaphoreType.DMA((total,))] * (4 * len(xs))
    return pl.pallas_call(
        functools.partial(block_sum_kernel, total, plan.n, len(xs), riders),
        in_specs=[vmem] * len(xs) + riders.specs(),
        out_specs=[vmem] * len(xs) + riders.specs(),
        out_shape=[jax.ShapeDtypeStruct(x.shape, x.dtype) for x in xs] + riders.shapes(),
        scratch_shapes=[pltpu.VMEM(x.shape, x.dtype) for x in xs] + sems + riders.scratch(),
        compiler_params=pltpu.CompilerParams(
            collective_id=collective_id, has_side_effects=True, vmem_limit_bytes=VMEM_BYTES
        ),
        cost_estimate=cost(1e8, 1e6),
        name="block_sum",
    )(*xs, *riders.arrays)


def pack(total, parts, dtype, rows):
    flat = jnp.concatenate([x.reshape(-1).astype(dtype) for x in parts])
    unit = total * rows * 128
    padded = -(-flat.shape[0] // unit) * unit
    return jnp.pad(flat, (0, padded - flat.shape[0])).reshape(total, -1, 128)


def unpack(packed, parts):
    flat = packed.reshape(-1).astype(F32)
    out, at = [], 0
    for x in parts:
        out.append(flat[at : at + x.size].reshape(x.shape))
        at += x.size
    return out


def whole_sum_kernel(total, lanes, x_ref, out_ref, held, send, recv):
    me = lax.axis_index("batch") * lanes + lax.axis_index("lat")
    greet_all(total, lanes, me)

    def part(step, peer):
        return pltpu.make_async_remote_copy(
            src_ref=x_ref,
            dst_ref=held.at[step],
            send_sem=send.at[step],
            recv_sem=recv.at[step],
            device_id=place(lanes, peer),
            device_id_type=pl.DeviceIdType.MESH,
        )

    ahead = lambda step: lax.rem(me + step, total)
    every_peer(total, lambda step: part(step, ahead(step)).start())
    held[0] = x_ref[...]
    every_peer(total, lambda step: part(step, ahead(step)).wait_recv())
    out_ref[...] = jnp.sum(held[...], 0)
    every_peer(total, lambda step: part(step, ahead(step)).wait_send())


def whole_sum(total, lanes, x, collective_id):
    sems = [pltpu.SemaphoreType.DMA((total,))] * 2
    return pl.pallas_call(
        functools.partial(whole_sum_kernel, total, lanes),
        in_specs=[pl.BlockSpec(memory_space=pltpu.VMEM)],
        out_specs=pl.BlockSpec(memory_space=pltpu.VMEM),
        out_shape=jax.ShapeDtypeStruct(x.shape, x.dtype),
        scratch_shapes=[pltpu.VMEM((total,) + x.shape, x.dtype)] + sems,
        compiler_params=pltpu.CompilerParams(
            collective_id=collective_id, has_side_effects=True, vmem_limit_bytes=VMEM_BYTES
        ),
        cost_estimate=cost(1e8, 1e6),
        name="whole_sum",
    )(x)


def on_device(
    bands,
    tokens,
    cotangent,
    sample_weight,
    row_count,
    band_count,
    norm1_gain,
    norm1_bias,
    spec_w1,
    spec_b1,
    spec_w2,
    spec_b2,
    norm2_gain,
    norm2_bias,
    fc1_weight,
    fc1_bias,
    fc2_weight,
    fc2_bias,
):
    lane = lax.axis_index("lat")
    n = lax.axis_size("lat")
    samples, row_slots, width, channels = tokens.shape
    blocks, size = spec_w1.shape[1], spec_w1.shape[2]
    plan = Plan(n, samples, row_slots, width, channels, bands)
    wb1, wb2 = wide_bias(spec_b1), wide_bias(spec_b2)
    row = lambda v: v.reshape(1, -1)
    blank = jnp.zeros_like(fc2_bias)
    vectors = jnp.stack([norm1_gain, norm1_bias, norm2_gain, norm2_bias, fc2_bias] + [blank] * 3)
    own_rows = jnp.sum(jnp.where(jnp.arange(n) == lane, row_count, 0))
    held = jnp.arange(row_slots) < own_rows
    scales = sample_weight.astype(F32)[:, None] * 0.5 * held[None, :].astype(F32)
    slot_step = jnp.arange(plan.kp)
    valid = ((slot_step < plan.kk) & (lane * plan.kk + slot_step < plan.kw)).astype(F32)
    grouped = (n, plan.q, plan.t, channels)
    listed = (plan.pairs, plan.t, channels)

    ids = itertools.count()
    spread = (-1,) + grouped

    def spectral_forward(x, passengers=()):
        collective_id = next(ids) if passengers else None
        out = spectral_call(
            plan,
            valid,
            x,
            lat,
            lat_t,
            slots,
            m1,
            wb1,
            m2,
            wb2,
            [forward[-1][6]] if forward else [],
            passengers,
            collective_id,
        )
        forward.append(out)
        return out[7:]

    def feed(s, back, sums, passengers):
        out = feed_call(
            plan,
            s,
            scales[s],
            tokens,
            cotangent,
            back.reshape(listed),
            vectors,
            fc1_weight,
            row(fc1_bias),
            fc2_weight,
            sums,
            s == samples - 1,
            passengers,
            next(ids),
        )
        feeds.append(out)
        return out[7:]

    def backward(s, grads, passengers=()):
        out = spectral_back_call(
            plan,
            blocks,
            size,
            grads,
            forward[s][2:6],
            lat,
            lat_t,
            m1t,
            m2t,
            list(spectral[-1][1:5]) if spectral else [],
            passengers,
            next(ids) if passengers else None,
        )
        spectral.append(out)
        return out[0], out[5:]

    forward, feeds, spectral, band_parts, grads, lon_grads = [], [], [], {}, {}, {}
    sent = first_call(plan, 0, 1, tokens, vectors)[0].reshape(spread)
    tables = Tables(plan, blocks, size)
    extra = tables.operands(row_count, band_count, spec_w1, spec_w2)
    others, lat, lat_t, slots, m1, m2, m1t, m2t, spectra = first_call(
        plan, 1, samples - 1, tokens, vectors, [(sent, 0)], next(ids), tables, extra
    )
    others = others.reshape(spread)
    (spectra,) = spectral_forward(spectra, [(others, 0)])
    (back,) = spectral_forward(spectra, [(forward[0][0], None)])
    for s in range(samples):
        sums = [feeds[-1][i] for i in (3, 4, 0, 5, 6)] if s else None
        kinds, passengers = [], []
        if s + 1 < samples:
            kinds.append("back")
            passengers.append((forward[s + 1][0], None))
        if s + 2 < samples:
            kinds.append("spectra")
            passengers.append((others, s + 1))
        if s >= 1:
            kinds.append("grads")
            passengers.append((feeds[s - 1][1].reshape(grouped), None))
        kinds.append("band")
        passengers.append((forward[s][1], None))
        arrived = dict(zip(kinds, feed(s, back, sums, passengers)))
        back = arrived.get("back")
        if s + 2 < samples:
            spectral_forward(arrived["spectra"])
        band_parts[s] = arrived["band"]
        if s >= 1:
            grads[s - 1] = arrived["grads"]
    after = lambda x, y: lax.optimization_barrier((x, y))[0]

    def last(s, earlier):
        return last_call(
            plan,
            s,
            scales[s],
            tokens,
            feeds[s][2],
            lon_grads[s].reshape(listed),
            vectors,
            earlier,
        )

    large = lax.psum((feeds[-1][3], feeds[-1][4]), ("batch", "lat"))
    grads[0] = after(grads[0], feeds[-1][6])
    lon, got = backward(0, grads[0], [(feeds[-1][1].reshape(grouped), None)])
    grads[samples - 1] = got[0]
    for s in range(1, samples):
        lon, got = backward(s, grads[s], [(lon, None)])
        lon_grads[s - 1] = got[0]
    ended = spectral[-1][3]
    add = lambda parts: functools.reduce(jnp.add, parts)
    devices = lax.axis_size("batch") * n
    feed_vec = feeds[-1][6]
    block_grad = lambda i: spectral[-1][i].reshape(2, blocks, size, size)
    small = [
        feed_vec[1],
        feed_vec[2],
        feeds[-1][5],
        feed_vec[0],
        narrow_bias(spectral[-1][3], blocks, size),
        narrow_bias(spectral[-1][4], blocks, size),
        jnp.sum(forward[-1][6]).reshape(1),
    ]
    blocky = [block_grad(1), block_grad(2)]
    packed = [pack(devices, blocky, BF, 16), pack(devices, small, F32, 8)]
    packed = block_sum(devices, plan, packed, [(lon, None)], next(ids))
    lon_grads[samples - 1] = packed[2]
    blocky = unpack(packed[0], blocky)
    small = unpack(packed[1], small)
    band_parts = {s: after(part, ended) for s, part in band_parts.items()}
    for s in range(samples - 1):
        lon_grads[s] = after(lon_grads[s], ended)
    tokens_grad, spectrum, finals = None, None, []
    for s in range(samples):
        tokens_grad, vec = last(s, tokens_grad)
        finals.append(vec)
        spectrum = band_call(plan, s, band_parts[s], spectrum)
    mixed = feeds[-1][0]

    last_vec = whole_sum(devices, n, add(finals), next(ids))
    large = after(large, last_vec)
    large = (large[0].astype(F32), large[1].astype(F32))
    zero_fraction = small[6][0] / (lax.axis_size("batch") * samples * H * plan.kw * 2 * channels)
    return (
        mixed,
        spectrum.transpose(0, 1, 3, 2, 4),
        tokens_grad,
        last_vec[0],
        last_vec[1],
        blocky[0],
        small[4],
        blocky[1],
        small[5],
        small[0],
        small[1],
        large[0],
        small[2].reshape(-1),
        large[1],
        small[3],
        zero_fraction,
    )


def solution(mesh):
    rows = P("batch", "lat", None, None)
    in_specs = (rows, rows, P("batch")) + (P(),) * 14
    out_specs = (rows, P("batch", "lat", None, None, None), rows) + (P(),) * 13
    lanes = mesh.shape["lat"]

    def run(tokens, cotangent, *rest):
        row_slots = tokens.shape[1] // lanes
        return jax.shard_map(
            functools.partial(on_device, row_slots + 1),
            mesh=mesh,
            in_specs=in_specs,
            out_specs=out_specs,
            check_vma=False,
        )(tokens, cotangent, *rest)

    return run
```

```python
import functools
import itertools
import math

import jax
import jax.numpy as jnp
import numpy as np
from jax import lax
from jax.experimental import pallas as pl
from jax.experimental.pallas import tpu as pltpu
from jax.sharding import PartitionSpec as P

H = 90
HP = 96

NORM_EPS = 1e-06
SHRINK_LAMBDA = 0.01
SHRINK_SOFTNESS = 0.1
INV_ROOT_TAU = 1.0 / math.sqrt(2.0 * math.pi)
BF = jnp.bfloat16
F32 = jnp.float32
VMEM_BYTES = 64 * 1024 * 1024


def dot(a, b):
    return jnp.dot(a, b, preferred_element_type=F32)


def dot_nt(a, b):
    return lax.dot_general(a, b, (((1,), (1,)), ((), ())), preferred_element_type=F32)


def dot_tn(a, b):
    return lax.dot_general(a, b, (((0,), (0,)), ((), ())), preferred_element_type=F32)


def dot_table(table_ref, x):
    return dot(table_ref[0], x) + dot(table_ref[1], x)


def two_parts(table):
    high = table.astype(BF)
    return high, (table - high.astype(table.dtype)).astype(BF)


def norm_parts(x):
    mean = jnp.mean(x, -1, keepdims=True)
    centred = x - mean
    rstd = lax.rsqrt(jnp.mean(centred * centred, -1, keepdims=True) + NORM_EPS)
    return centred * rstd, rstd


def norm_back(grad, unit, rstd, gain):
    e = grad * gain
    return rstd * (
        e - jnp.mean(e, -1, keepdims=True) - unit * jnp.mean(e * unit, -1, keepdims=True)
    )


def gauss_parts(v):
    d = 1.0 + jnp.abs(v) * (0.3275911 / math.sqrt(2.0))
    t = pl.reciprocal(d, approx=True)
    e = jnp.exp2(v * v * (-0.5 * math.log2(math.e)))
    poly = 1.061405429 * 0.5
    for c in (-1.453152027, 1.421413741, -0.284496736, 0.254829592):
        poly = poly * t + 0.5 * c
    tail = poly * t * e
    cdf = jnp.where(v >= 0.0, 1.0 - tail, tail)
    return cdf, v * e * INV_ROOT_TAU


def gelu_both(v):
    cdf, slope_part = gauss_parts(v)
    return v * cdf, cdf + slope_part


def shrink_both(u):
    a = jnp.maximum(jnp.abs(u) - SHRINK_LAMBDA, 0.0)
    d = a + SHRINK_SOFTNESS
    t = pl.reciprocal(d, approx=True)
    t = t * (2.0 - d * t)
    size = a * a * t
    value = jnp.where(u >= 0.0, size, -size)
    slope = a * (a + 2.0 * SHRINK_SOFTNESS) * (t * t)
    return value, slope


class Plan:
    def __init__(self, n, samples, rows, width, channels, bands):
        self.n, self.s, self.r, self.w, self.d, self.mb = n, samples, rows, width, channels, bands
        self.kw = width // 2 + 1
        self.kk = -(-self.kw // n)
        self.kp = self.kk + self.kk % 2
        self.q = self.kp // 2
        self.rp = -(-rows // 4) * 4
        self.t = 4 * self.rp
        self.pairs = n * self.q
        self.ki = n * self.kp * 2
        self.rb = max(b for b in (4, 3, 2, 1) if rows % b == 0)
        self.chunks = rows // self.rb
        self.flat = self.rb * width
        self.flatp = max(-(-self.flat // 256) * 256, channels)
        self.bt = -(-4 * bands // 8) * 8
        j = np.arange(n)[:, None]
        t = np.arange(self.kp)[None, :]
        self.k_index = (j * self.kk + t).astype(np.int64)
        self.k_valid = (t < self.kk) & (self.k_index < self.kw)
        k = np.where(self.k_valid, self.k_index, 0).reshape(-1)
        ok = self.k_valid.reshape(-1).astype(np.float64)
        angle = 2.0 * np.pi * ((k[:, None] * np.arange(width)[None, :]) % width) / width
        scale = ok[:, None] / math.sqrt(width)
        fwd = np.stack([np.cos(angle) * scale, -np.sin(angle) * scale], 1).reshape(self.ki, width)
        factor = np.where((k == 0) | (2 * k == width), 1.0, 2.0)[:, None, None]
        both = (fwd.reshape(-1, 2, width) * factor).reshape(self.ki, width)
        self.lon = np.stack(two_parts(fwd))
        self.lon_both = np.stack(two_parts(both))
        self.lon_t = np.stack(two_parts(np.ascontiguousarray(fwd.T)))
        self.lon_both_t = np.stack(two_parts(np.ascontiguousarray(both.T)))
        perm = np.zeros((16, self.rp, rows, 16))
        for a in range(16):
            for r in range(rows):
                perm[a, r, r, a] = 1.0
        self.perm = perm.reshape(16 * self.rp, rows * 16).astype(BF)
        self.perm_t = np.ascontiguousarray(self.perm.T)


class Tables:
    def __init__(self, plan, blocks, size):
        self.plan, self.blocks, self.size = plan, blocks, size
        n, rp, mb = plan.n, plan.rp, plan.mb
        kh, h = np.arange(HP)[:, None], np.arange(HP)[None, :]
        angle = 2.0 * np.pi * (kh * h % H) / H
        weight = ((kh < H) & (h < H)) / math.sqrt(H)
        cosine, sine = np.cos(angle) * weight, np.sin(angle) * weight
        part = np.block([[cosine, sine], [-sine, cosine]])
        self.base = np.stack(two_parts(np.kron(np.eye(2), part)))
        col = np.arange(n * 4 * rp)
        group, step = col // rp % 4, col % rp
        self.columns = np.stack([col // (4 * rp), group * HP + step, step]).astype(np.int32)
        bt = plan.bt
        line = np.arange(n * bt)
        group, step = line % bt // mb, line % bt % mb
        step = np.where(group < 4, step, 1 << 20)
        lines = np.stack([line // bt, group * HP + step, step]).astype(np.int32)
        self.lines = lines[:, :, None]
        half = blocks // 2
        spots = np.zeros((half, size, half * size))
        for i in range(half):
            spots[i, :, i * size : (i + 1) * size] = np.eye(size)
        self.spots = spots.astype(BF)
        wide = 4 * HP
        d = plan.d
        shapes = [(2, wide, n * 4 * rp), (2, n * 4 * rp, wide), (n * bt, wide)] + [(2, d, d)] * 4
        self.shapes = [jax.ShapeDtypeStruct(x, BF) for x in shapes]

    def operands(self, row_count, band_count, spec_w1, spec_w2):
        return [
            row_count,
            band_count,
            spec_w1,
            spec_w2,
            self.base,
            self.columns[:, None, :],
            self.lines,
            self.spots,
        ]

    def in_specs(self):
        weight = (2, self.blocks, self.size, self.size)
        shapes = [weight, weight, self.base.shape, (3, 1, self.columns.shape[1])]
        shapes += [self.lines.shape, self.spots.shape]
        return [SMEM, SMEM] + [whole(x) for x in shapes]

    def out_specs(self):
        return [whole(x.shape) for x in self.shapes]

    def build(self, ins, outs):
        rows_ref, bands_ref, w1_ref, w2_ref, base_ref, col_ref, line_ref, spot_ref = ins
        lat_ref, lat_t_ref, slot_ref, m1_ref, m2_ref, m1t_ref, m2t_ref = outs
        n = self.plan.n

        def spread(counts_ref, owner):
            first = jnp.zeros(owner.shape, jnp.int32)
            held = jnp.zeros(owner.shape, jnp.int32)
            start = jnp.int32(0)
            for j in range(n):
                count = counts_ref[j]
                first = jnp.where(owner == j, start, first)
                held = jnp.where(owner == j, count, held)
                start = start + count
            return first, held

        first, held = spread(rows_ref, col_ref[0])
        target = jnp.where(col_ref[2] < held, col_ref[1] + first, -1)
        pick = lax.broadcasted_iota(jnp.int32, (4 * HP, target.shape[1]), 0) == target
        pick = jnp.where(pick, 1.0, 0.0).astype(BF)
        for part in range(2):
            full = dot(base_ref[part], pick)
            lat_ref[part] = full.astype(BF)
            lat_t_ref[part] = full.T.astype(BF)
        first, held = spread(bands_ref, line_ref[0])
        target = jnp.where(line_ref[2] < held, line_ref[1] + first, -1)
        pick = lax.broadcasted_iota(jnp.int32, (target.shape[0], 4 * HP), 1) == target
        slot_ref[...] = jnp.where(pick, 1.0, 0.0).astype(BF)
        half, size = self.blocks // 2, self.size
        mid = half * size
        for w_ref, m_ref, mt_ref in ((w1_ref, m1_ref, m1t_ref), (w2_ref, m2_ref, m2t_ref)):
            for g in range(2):
                for i in range(half):
                    low = slice(i * size, (i + 1) * size)
                    high = slice(mid + i * size, mid + (i + 1) * size)
                    re, im = w_ref[0, g * half + i], w_ref[1, g * half + i]
                    for ref, place_in, sign in ((m_ref, dot, 1.0), (mt_ref, dot_tn, -1.0)):
                        real = place_in(re, spot_ref[i]).astype(BF)
                        imag = place_in(im, spot_ref[i]) * sign
                        ref[g, low, :mid] = real
                        ref[g, high, mid:] = real
                        ref[g, low, mid:] = imag.astype(BF)
                        ref[g, high, :mid] = (-imag).astype(BF)


def wide_bias(bias):
    return bias.reshape(2, 2, -1).transpose(1, 0, 2).reshape(2, 1, -1)


def narrow_bias(wide, blocks, size):
    return wide.reshape(2, 2, -1).transpose(1, 0, 2).reshape(2, blocks, size)


def whole(shape):
    zeros = (0,) * len(shape)
    return pl.BlockSpec(shape, lambda *_: zeros)


def whole_once(shape):
    zeros = (0,) * len(shape)
    return pl.BlockSpec(shape, lambda *_: zeros, pipeline_mode=pl.Buffered(1))


SMEM = pl.BlockSpec(memory_space=pltpu.SMEM)
ANY = pl.BlockSpec(memory_space=pl.ANY)


def params(collective_id=None):
    if collective_id is None:
        return pltpu.CompilerParams(
            dimension_semantics=("arbitrary",), vmem_limit_bytes=VMEM_BYTES
        )
    return pltpu.CompilerParams(
        dimension_semantics=("arbitrary",),
        vmem_limit_bytes=VMEM_BYTES,
        collective_id=collective_id,
        has_side_effects=True,
    )


def ride_copy(n, me, src, dst, send, recv, e, step):
    peer = lax.rem(me + step, n)
    return pltpu.make_async_remote_copy(
        src_ref=src.at[peer],
        dst_ref=dst.at[me],
        send_sem=send.at[e, step],
        recv_sem=recv.at[e, step],
        device_id={"lat": peer},
        device_id_type=pl.DeviceIdType.MESH,
    )


def ride_arrival(n, me, src, dst, send, recv, e, step):
    peer = lax.rem(me + n - step, n)
    return pltpu.make_async_remote_copy(
        src_ref=src.at[peer],
        dst_ref=dst.at[peer],
        send_sem=send.at[e, step],
        recv_sem=recv.at[e, step],
        device_id={"lat": peer},
        device_id_type=pl.DeviceIdType.MESH,
    )


def ride_greet(n):
    me = lax.axis_index("lat")
    barrier = pltpu.get_barrier_semaphore()
    for step in range(1, n):
        pl.semaphore_signal(
            barrier,
            inc=1,
            device_id={"lat": lax.rem(me + step, n)},
            device_id_type=pl.DeviceIdType.MESH,
        )
    pl.semaphore_wait(barrier, n - 1)


def ride_start(n, srcs, dsts, send, recv, own, greet=True):
    me = lax.axis_index("lat")
    if greet:
        ride_greet(n)
    for e, (src, dst) in enumerate(zip(srcs, dsts)):
        for step in range(1, n):
            ride_copy(n, me, src, dst, send, recv, e, step).start()
        pltpu.make_async_copy(src.at[me], dst.at[me], own.at[e]).start()


def ride_wait(n, srcs, dsts, send, recv, own):
    me = lax.axis_index("lat")
    for e, (src, dst) in enumerate(zip(srcs, dsts)):
        pltpu.make_async_copy(src.at[me], dst.at[me], own.at[e]).wait()
        for step in range(1, n):
            ride_copy(n, me, src, dst, send, recv, e, step).wait_send()
            ride_arrival(n, me, src, dst, send, recv, e, step).wait_recv()


def cost(flops, size):
    return pl.CostEstimate(flops=int(flops), bytes_accessed=int(size), transcendentals=0)


def interleave(plan, perm_ref, rows_ref, out_ref):
    def body(c, carry):
        at = pl.multiple_of(c * 16, 16)
        block = rows_ref[:, pl.ds(at, 16), :].reshape(plan.r * 16, plan.d)
        mixed = dot(perm_ref[...], block).astype(BF)
        out_ref[pl.ds(c * 4, 4)] = mixed.reshape(4, plan.t, plan.d)
        return carry

    lax.fori_loop(0, plan.ki // 16, body, 0)


def deinterleave(plan, perm_t_ref, in_ref, rows_ref):
    def body(c, carry):
        at = pl.multiple_of(c * 16, 16)
        block = in_ref[pl.ds(c * 4, 4)].reshape(4 * plan.t, plan.d)
        rows = dot(perm_t_ref[...], block).astype(BF)
        rows_ref[:, pl.ds(at, 16), :] = rows.reshape(plan.r, 16, plan.d)
        return carry

    lax.fori_loop(0, plan.ki // 16, body, 0)


def interleave_out(plan, perm_ref, rows_ref, ring, sem, out_ref):
    def copy(c):
        return pltpu.make_async_copy(
            ring.at[lax.rem(c, 2)], out_ref.at[pl.ds(c * 4, 4)], sem.at[lax.rem(c, 2)]
        )

    def body(c, carry):
        @pl.when(c >= 2)
        def _():
            copy(c - 2).wait()

        at = pl.multiple_of(c * 16, 16)
        block = rows_ref[:, pl.ds(at, 16), :].reshape(plan.r * 16, plan.d)
        mixed = dot(perm_ref[...], block).astype(BF)
        ring[lax.rem(c, 2)] = mixed.reshape(4, plan.t, plan.d)
        copy(c).start()
        return carry

    lax.fori_loop(0, plan.ki // 16, body, 0)
    return [copy(plan.ki // 16 - 2), copy(plan.ki // 16 - 1)]


def ring_load(plan, in_ref, ring, sem, c):
    return pltpu.make_async_copy(
        in_ref.at[pl.ds(c * 4, 4)], ring.at[lax.rem(c, 2)], sem.at[lax.rem(c, 2)]
    )


def deinterleave_in(plan, perm_t_ref, in_ref, ring, sem, rows_ref):
    steps = plan.ki // 16

    def body(c, carry):
        ring_load(plan, in_ref, ring, sem, c).wait()
        at = pl.multiple_of(c * 16, 16)
        block = ring[lax.rem(c, 2)].reshape(4 * plan.t, plan.d)
        rows = dot(perm_t_ref[...], block).astype(BF)
        rows_ref[:, pl.ds(at, 16), :] = rows.reshape(plan.r, 16, plan.d)

        @pl.when(c + 2 < steps)
        def _():
            ring_load(plan, in_ref, ring, sem, c + 2).start()

        return carry

    lax.fori_loop(0, steps, body, 0)


class Riders:
    def __init__(self, plan, passengers):
        self.n = plan.n
        self.arrays = [a for a, _ in passengers]
        self.leads = [lead for _, lead in passengers]
        self.count = len(passengers)

    def shapes(self):
        return [
            jax.ShapeDtypeStruct(a.shape if lead is None else a.shape[1:], a.dtype)
            for a, lead in zip(self.arrays, self.leads)
        ]

    def specs(self):
        return [ANY] * self.count

    def scratch(self):
        if not self.count:
            return []
        dma = pltpu.SemaphoreType.DMA
        return [dma((self.count, self.n)), dma((self.count, self.n)), dma((self.count,))]

    def bind(self, srcs, dsts, sems):
        srcs = [r if lead is None else r.at[lead] for r, lead in zip(srcs, self.leads)]
        return (self.n, srcs, dsts) + tuple(sems)


def first_kernel(plan, riders, tables, tok_ref, vec_ref, lon_ref, perm_ref, *rest):
    e = riders.count
    t_in = 0 if tables is None else 8
    t_out = 0 if tables is None else 7
    t_ins, rest = rest[:t_in], rest[t_in:]
    srcs, rest = rest[:e], rest[e:]
    out_ref, rest = rest[0], rest[1:]
    t_outs, rest = rest[:t_out], rest[t_out:]
    dsts, rows_ref, sems = rest[:e], rest[e], rest[e + 1 :]
    i = pl.program_id(0)
    c = lax.rem(i, plan.chunks)
    if e:
        ride = riders.bind(srcs, dsts, sems)

        @pl.when(i == 0)
        def _():
            ride_start(*ride)

    for u in range(plan.rb):
        unit, _ = norm_parts(tok_ref[0, u].astype(F32))
        normed = (unit * vec_ref[0:1] + vec_ref[1:2]).astype(BF)
        rows_ref[c * plan.rb + u] = dot_table(lon_ref, normed).astype(BF)

    @pl.when(c == plan.chunks - 1)
    def _():
        interleave(plan, perm_ref, rows_ref, out_ref.at[0])

    @pl.when(i == pl.num_programs(0) - 1)
    def _():
        if tables is not None:
            tables.build(t_ins, t_outs)
        if e:
            ride_wait(*ride)


def row_block(plan, s):
    return pl.BlockSpec((1, plan.rb, plan.w, plan.d), lambda i: (s, i, 0, 0))


def own_block(plan):
    return pl.BlockSpec((plan.rb, plan.w, plan.d), lambda i: (i, 0, 0))


def first_call(
    plan, start, count, tokens, vectors, passengers=(), collective_id=None, tables=None, extra=()
):
    shape = (plan.pairs, plan.t, plan.d)
    chunks = plan.chunks
    riders = Riders(plan, passengers)
    return pl.pallas_call(
        functools.partial(first_kernel, plan, riders, tables),
        grid=(count * chunks,),
        in_specs=[
            pl.BlockSpec(
                (1, plan.rb, plan.w, plan.d),
                lambda i: (start + i // chunks, lax.rem(i, chunks), 0, 0),
            ),
            whole((8, plan.d)),
            whole((2, plan.ki, plan.w)),
            whole(plan.perm.shape),
        ]
        + (tables.in_specs() if tables else [])
        + riders.specs(),
        out_specs=[pl.BlockSpec((1,) + shape, lambda i: (i // chunks, 0, 0, 0))]
        + (tables.out_specs() if tables else [])
        + riders.specs(),
        out_shape=[jax.ShapeDtypeStruct((count,) + shape, BF)]
        + (tables.shapes if tables else [])
        + riders.shapes(),
        scratch_shapes=[pltpu.VMEM((plan.r, plan.ki, plan.d), BF)] + riders.scratch(),
        compiler_params=params(collective_id),
        cost_estimate=cost(9e9 * count, 8e6 * count),
        name="lon_forward",
    )(tokens, vectors, plan.lon, plan.perm, *extra, *riders.arrays)


def spectral_kernel(
    plan,
    riders,
    carried,
    valid_ref,
    in_ref,
    lat_ref,
    lat_t_ref,
    slot_ref,
    m1_ref,
    b1_ref,
    m2_ref,
    b2_ref,
    *rest,
):
    e = riders.count
    earlier, srcs, rest = rest[:carried], rest[carried : carried + e], rest[carried + e :]
    back_ref, band_ref, spec_ref, hid_ref, slope1_ref, slope2_ref, zero_ref = rest[:7]
    dsts, shr_ref, sems = rest[7 : 7 + e], rest[7 + e], rest[8 + e :]
    q = pl.program_id(0)
    half = plan.d // 2
    if e:
        ride = riders.bind(srcs, dsts, sems)

        @pl.when(q == 0)
        def _():
            ride_start(*ride)

    @pl.when(q == 0)
    def _():
        zero_ref[...] = earlier[0][...] if carried else jnp.zeros_like(zero_ref)

    x = in_ref[:, 0].reshape(plan.n * plan.t, plan.d)
    spec = dot_table(lat_ref, x).astype(BF)
    ok = (lax.broadcasted_iota(jnp.int32, (HP, 1), 0) < H).astype(F32)
    for g in range(2):
        lanes = slice(g * half, (g + 1) * half)
        for a in range(2):
            top = a * 2 * HP
            spec_ref[0, g, a * HP : (a + 1) * HP, :half] = spec[top : top + HP, lanes]
            spec_ref[0, g, a * HP : (a + 1) * HP, half:] = spec[top + HP : top + 2 * HP, lanes]
        u1 = dot(spec_ref[0, g], m1_ref[g]) + b1_ref[g]
        hidden, slope = gelu_both(u1)
        hid_ref[0, g] = hidden.astype(BF)
        slope1_ref[0, g] = slope.astype(BF)
        u2 = dot(hid_ref[0, g], m2_ref[g]) + b2_ref[g]
        small = (jnp.abs(u2) <= SHRINK_LAMBDA).astype(F32)
        for a in range(2):
            part = small[a * HP : (a + 1) * HP] * ok
            zero_ref[...] += jnp.sum(part, 0, keepdims=True) * valid_ref[q * 2 + a]
        value, slope = shrink_both(u2)
        slope2_ref[0, g] = slope.astype(BF)
        value = value.astype(BF)
        for a in range(2):
            top = a * 2 * HP
            shr_ref[top : top + HP, lanes] = value[a * HP : (a + 1) * HP, :half]
            shr_ref[top + HP : top + 2 * HP, lanes] = value[a * HP : (a + 1) * HP, half:]
    shrunk = shr_ref[...]
    back_ref[:, 0] = dot_table(lat_t_ref, shrunk).astype(BF).reshape(plan.n, plan.t, plan.d)
    band = dot(slot_ref[...], shrunk).astype(BF)
    band_ref[:, 0] = band.reshape(plan.n, plan.bt, plan.d)
    if e:

        @pl.when(q == plan.q - 1)
        def _():
            ride_wait(*ride)


def pair_block(plan, rows):
    return pl.BlockSpec((plan.n, 1, rows, plan.d), lambda q: (0, q, 0, 0))


def spectral_call(
    plan, valid, received, lat, lat_t, slots, m1, b1, m2, b2, earlier, passengers, collective_id
):
    riders = Riders(plan, passengers)
    kept = (plan.q, 2, 2 * HP, plan.d)
    kept_spec = pl.BlockSpec((1, 2, 2 * HP, plan.d), lambda q: (q, 0, 0, 0))
    kept_shape = jax.ShapeDtypeStruct(kept, BF)
    rows = plan.bt
    return pl.pallas_call(
        functools.partial(spectral_kernel, plan, riders, len(earlier)),
        grid=(plan.q,),
        in_specs=[
            SMEM,
            pair_block(plan, plan.t),
            whole(lat.shape),
            whole(lat_t.shape),
            whole(slots.shape),
            whole(m1.shape),
            whole(b1.shape),
            whole(m2.shape),
            whole(b2.shape),
        ]
        + [whole((1, plan.d))] * len(earlier)
        + riders.specs(),
        out_specs=[
            pair_block(plan, plan.t),
            pair_block(plan, rows),
            kept_spec,
            kept_spec,
            kept_spec,
            kept_spec,
            whole((1, plan.d)),
        ]
        + riders.specs(),
        out_shape=[
            jax.ShapeDtypeStruct((plan.n, plan.q, plan.t, plan.d), BF),
            jax.ShapeDtypeStruct((plan.n, plan.q, rows, plan.d), BF),
            kept_shape,
            kept_shape,
            kept_shape,
            kept_shape,
            jax.ShapeDtypeStruct((1, plan.d), F32),
        ]
        + riders.shapes(),
        scratch_shapes=[pltpu.VMEM((4 * HP, plan.d), BF)] + riders.scratch(),
        compiler_params=params(collective_id),
        cost_estimate=cost(20e9, 25e6),
        name="spectral_forward",
    )(valid, received, lat, lat_t, slots, m1, b1, m2, b2, *earlier, *riders.arrays)


def feed_kernel(
    plan,
    first,
    final,
    riders,
    tiles,
    scale_ref,
    tok_ref,
    cot_ref,
    recv_ref,
    par_ref,
    lon_t_ref,
    lon_ref,
    perm_ref,
    perm_t_ref,
    w1_ref,
    b1_ref,
    w2_ref,
    *rest,
):
    e = riders.count
    srcs, rest = rest[:e], rest[e:]
    if first:
        in1_ref = in2_ref = None
    else:
        in1_ref, in2_ref, _, db1_in, vec_in = rest[:5]
        rest = rest[5:]
    mixed_ref, send_ref, gx_ref, out1_ref, out2_ref, db1_ref, vec_ref = rest[:7]
    dsts, rest = rest[7 : 7 + e], rest[7 + e :]
    (
        dw1,
        dw2,
        ring,
        rows_ref,
        x1_ref,
        xn,
        xn_t,
        gm,
        gm_t,
        act,
        gz,
        down,
        up,
        sem,
        ring_sem,
        *ride_sems,
    ) = rest
    i = pl.program_id(0)
    last = plan.chunks - 1
    tile = act.shape[1]
    flat = plan.flat
    ride = riders.bind(srcs, dsts, ride_sems)

    @pl.when(i == 0)
    def _():
        for c in range(2):
            ring_load(plan, recv_ref, ring, ring_sem, c).start()
        if not first:
            pltpu.make_async_copy(in1_ref, dw1, sem.at[1]).start()
            pltpu.make_async_copy(in2_ref, dw2, sem.at[2]).start()
        ride_start(*ride)
        if first:
            dw1[...] = jnp.zeros_like(dw1)
            dw2[...] = jnp.zeros_like(dw2)
        db1_ref[...] = jnp.zeros_like(db1_ref) if first else db1_in[...]
        vec_ref[...] = jnp.zeros_like(vec_ref) if first else vec_in[...]
        if plan.flatp > flat:
            pad = jnp.zeros((plan.flatp - flat, tile), BF)
            for ref in (act, gz):
                ref[flat:, :] = pad
            pad = jnp.zeros((plan.flatp - flat, plan.d), F32)
            down[flat:, :] = pad
            up[flat:, :] = pad
        deinterleave_in(plan, perm_t_ref, recv_ref, ring, ring_sem, rows_ref)

    for u in range(plan.rb):
        span = slice(u * plan.w, (u + 1) * plan.w)
        x = tok_ref[0, u].astype(F32)
        unit, _ = norm_parts(x)
        filtered = dot_table(lon_t_ref, rows_ref[i * plan.rb + u])
        x1 = x + filtered + (unit * par_ref[0:1] + par_ref[1:2])
        x1_ref[u] = x1
        unit, _ = norm_parts(x1)
        down[span, :] = unit * par_ref[2:3] + par_ref[3:4]
        up[span, :] = cot_ref[0, u].astype(F32) * scale_ref[i * plan.rb + u]
    normed = down[...].astype(BF)
    xn[...] = normed[:flat]
    xn_t[...] = normed.T
    grads = up[...].astype(BF)
    gm[...] = grads[:flat]
    gm_t[...] = grads.T
    vec_ref[0:1] += jnp.sum(grads.astype(F32), 0, keepdims=True)
    down[...] = jnp.zeros_like(down)
    up[...] = jnp.zeros_like(up)

    if not first:

        @pl.when(i == 0)
        def _():
            pltpu.make_async_copy(in1_ref, dw1, sem.at[1]).wait()
            pltpu.make_async_copy(in2_ref, dw2, sem.at[2]).wait()

    def columns(t):
        return pl.ds(pl.multiple_of(t * tile, tile), tile)

    def body(t, carry):
        cols = columns(t)
        z = dot(xn[...], w1_ref[:, cols]) + b1_ref[:, cols]
        ga = dot_nt(gm[...], w2_ref[cols, :])
        hidden, slope = gelu_both(z)
        grad = ga * slope
        act[:flat, :] = hidden.astype(BF)
        gz[:flat, :] = grad.astype(BF)
        db1_ref[:, cols] += jnp.sum(grad, 0, keepdims=True)
        down[:flat, :] += dot(act[:flat, :], w2_ref[cols, :])
        up[:flat, :] += dot_nt(gz[:flat, :], w1_ref[:, cols])
        dw1[:, cols] += dot(xn_t[...], gz[...])
        dw2[:, cols] += dot(gm_t[...], act[...])
        return carry

    lax.fori_loop(0, tiles, body, 0)

    if not final:

        @pl.when(i == last)
        def _():
            pltpu.make_async_copy(dw1, out1_ref, sem.at[1]).start()
            pltpu.make_async_copy(dw2, out2_ref, sem.at[2]).start()

    for u in range(plan.rb):
        span = slice(u * plan.w, (u + 1) * plan.w)
        x1 = x1_ref[u]
        scale = scale_ref[i * plan.rb + u]
        keep = jnp.where(scale > 0.0, 1.0, 0.0)
        mixed_ref[0, u] = ((x1 + down[span, :] + par_ref[4:5]) * keep).astype(BF)
        unit, rstd = norm_parts(x1)
        grad = up[span, :]
        vec_ref[1:2] += jnp.sum(grad * unit, 0, keepdims=True)
        vec_ref[2:3] += jnp.sum(grad, 0, keepdims=True)
        gx = cot_ref[0, u].astype(F32) * scale + norm_back(grad, unit, rstd, par_ref[2:3])
        gx_ref[u] = gx.astype(gx_ref.dtype)
        rows_ref[i * plan.rb + u] = dot_table(lon_ref, gx.astype(BF)).astype(BF)

    if plan.flatp > flat:
        down[flat:, :] = jnp.zeros((plan.flatp - flat, plan.d), F32)
        up[flat:, :] = jnp.zeros((plan.flatp - flat, plan.d), F32)

    @pl.when(i == last)
    def _():
        stores = interleave_out(plan, perm_ref, rows_ref, ring, ring_sem, send_ref)
        if final:
            stage = (xn_t, gm_t)
            pending = {}
            for t in range(2 * tiles):
                side = t % 2
                if side in pending:
                    pending.pop(side).wait()
                cols = slice(t // 2 * tile, (t // 2 + 1) * tile)
                held = stage[side].at[:tile, : plan.d]
                held[...] = (dw1, dw2)[side][:, cols].astype(BF).T
                pending[side] = pltpu.make_async_copy(
                    held, out1_ref.at[side, cols], sem.at[1 + side]
                )
                pending[side].start()
            for copy in pending.values():
                copy.wait()
        else:
            pltpu.make_async_copy(dw1, out1_ref, sem.at[1]).wait()
            pltpu.make_async_copy(dw2, out2_ref, sem.at[2]).wait()
        for store in stores:
            store.wait()
        ride_wait(*ride)


def feed_call(
    plan, s, scales, tokens, cotangent, received, vectors, w1, b1, w2, sums, final, passengers,
    collective_id
):
    first = sums is None
    ff = w1.shape[1]
    tile = 512
    d, flat = plan.d, plan.flat
    flatp = plan.flatp
    shape = (plan.pairs, plan.t, d)
    riders = Riders(plan, passengers)
    in_specs = [
        SMEM,
        row_block(plan, s),
        row_block(plan, s),
        ANY,
        whole((8, d)),
        whole((2, plan.w, plan.ki)),
        whole((2, plan.ki, plan.w)),
        whole(plan.perm.shape),
        whole(plan.perm_t.shape),
        whole_once((d, ff)),
        whole((1, ff)),
        whole_once((ff, d)),
    ] + riders.specs()
    operands = [
        scales,
        tokens,
        cotangent,
        received,
        vectors,
        plan.lon_both_t,
        plan.lon_both,
        plan.perm,
        plan.perm_t,
        w1,
        b1,
        w2,
        *riders.arrays,
    ]
    aliases = {}
    if not first:
        aliases = {len(operands) + 2: 0}
        if not final:
            aliases.update({len(operands): 3, len(operands) + 1: 4})
        in_specs += [ANY, ANY, ANY, whole((1, ff)), whole((8, d))]
        operands += list(sums)
    if final:
        wides = [jax.ShapeDtypeStruct((2, ff, d), BF), jax.ShapeDtypeStruct((8, 128), F32)]
    else:
        wides = [jax.ShapeDtypeStruct((d, ff), F32)] * 2
    return pl.pallas_call(
        functools.partial(feed_kernel, plan, first, final, riders, ff // tile),
        grid=(plan.chunks,),
        in_specs=in_specs,
        out_specs=[
            row_block(plan, s),
            ANY,
            own_block(plan),
            ANY,
            ANY,
            whole((1, ff)),
            whole((8, d)),
        ]
        + riders.specs(),
        out_shape=[
            jax.ShapeDtypeStruct((plan.s, plan.r, plan.w, d), BF),
            jax.ShapeDtypeStruct(shape, BF),
            jax.ShapeDtypeStruct((plan.r, plan.w, d), BF),
            *wides,
            jax.ShapeDtypeStruct((1, ff), F32),
            jax.ShapeDtypeStruct((8, d), F32),
        ]
        + riders.shapes(),
        scratch_shapes=[
            pltpu.VMEM((d, ff), F32),
            pltpu.VMEM((d, ff), F32),
            pltpu.VMEM((2, 4, plan.t, d), BF),
            pltpu.VMEM((plan.r, plan.ki, d), BF),
            pltpu.VMEM((plan.rb, plan.w, d), F32),
            pltpu.VMEM((flat, d), BF),
            pltpu.VMEM((d, flatp), BF),
            pltpu.VMEM((flat, d), BF),
            pltpu.VMEM((d, flatp), BF),
            pltpu.VMEM((flatp, tile), BF),
            pltpu.VMEM((flatp, tile), BF),
            pltpu.VMEM((flatp, d), F32),
            pltpu.VMEM((flatp, d), F32),
            pltpu.SemaphoreType.DMA((5,)),
            pltpu.SemaphoreType.DMA((2,)),
        ]
        + riders.scratch(),
        input_output_aliases=aliases,
        compiler_params=params(collective_id),
        cost_estimate=cost(70e9, 60e6),
        name="feed_forward",
    )(*operands)


def spectral_back_kernel(
    plan,
    riders,
    carried,
    in_ref,
    spec_ref,
    hid_ref,
    slope1_ref,
    slope2_ref,
    lat_ref,
    lat_t_ref,
    m1t_ref,
    m2t_ref,
    *rest,
):
    e = riders.count
    earlier, srcs, rest = rest[:carried], rest[carried : carried + e], rest[carried + e :]
    out_ref, dw1_ref, dw2_ref, db1_ref, db2_ref = rest[:5]
    dsts, rest = rest[5 : 5 + e], rest[5 + e :]
    dm1_ref, dm2_ref, gs_ref, gu_ref = rest[:4]
    q = pl.program_id(0)
    half = plan.d // 2
    if e:
        ride = riders.bind(srcs, dsts, rest[4:])

        @pl.when(q == 0)
        def _():
            ride_start(*ride)

    @pl.when(q == 0)
    def _():
        dm1_ref[...] = jnp.zeros_like(dm1_ref)
        dm2_ref[...] = jnp.zeros_like(dm2_ref)
        db1_ref[...] = earlier[2][...] if carried else jnp.zeros_like(db1_ref)
        db2_ref[...] = earlier[3][...] if carried else jnp.zeros_like(db2_ref)

    x = in_ref[:, 0].reshape(plan.n * plan.t, plan.d)
    grad = dot_table(lat_ref, x).astype(BF)
    for g in range(2):
        lanes = slice(g * half, (g + 1) * half)
        for a in range(2):
            top = a * 2 * HP
            gu_ref[a * HP : (a + 1) * HP, :half] = grad[top : top + HP, lanes]
            gu_ref[a * HP : (a + 1) * HP, half:] = grad[top + HP : top + 2 * HP, lanes]
        gu2 = gu_ref[...].astype(F32) * slope2_ref[0, g].astype(F32)
        db2_ref[g] += jnp.sum(gu2, 0, keepdims=True)
        gu2 = gu2.astype(BF)
        dm2_ref[g] += dot_tn(hid_ref[0, g], gu2)
        gu1 = (dot(gu2, m2t_ref[g]) * slope1_ref[0, g].astype(F32)).astype(BF)
        db1_ref[g] += jnp.sum(gu1.astype(F32), 0, keepdims=True)
        dm1_ref[g] += dot_tn(spec_ref[0, g], gu1)
        gs = dot(gu1, m1t_ref[g]).astype(BF)
        for a in range(2):
            top = a * 2 * HP
            gs_ref[top : top + HP, lanes] = gs[a * HP : (a + 1) * HP, :half]
            gs_ref[top + HP : top + 2 * HP, lanes] = gs[a * HP : (a + 1) * HP, half:]
    out_ref[:, 0] = dot_table(lat_t_ref, gs_ref[...]).astype(BF).reshape(plan.n, plan.t, plan.d)

    @pl.when(q == plan.q - 1)
    def _():
        blocks, size = dw1_ref.shape[2:4]
        for i, (wide, narrow) in enumerate(((dm1_ref, dw1_ref), (dm2_ref, dw2_ref))):
            for g in range(2):
                for b in range(blocks):
                    re = slice(b * size, (b + 1) * size)
                    im = slice(half + b * size, half + (b + 1) * size)
                    real = wide[g, re, re] + wide[g, im, im]
                    imag = wide[g, re, im] - wide[g, im, re]
                    if carried:
                        real += earlier[i][0, g, b]
                        imag += earlier[i][1, g, b]
                    narrow[0, g, b] = real
                    narrow[1, g, b] = imag
        if e:
            ride_wait(*ride)


def spectral_back_call(
    plan, blocks, size, received, kept, lat, lat_t, m1t, m2t, earlier, passengers, collective_id
):
    riders = Riders(plan, passengers)
    small = (2, 2, blocks // 2, size, size)
    kept_spec = pl.BlockSpec((1, 2, 2 * HP, plan.d), lambda q: (q, 0, 0, 0))
    wide = (2, plan.d, plan.d)
    thin = (2, 1, plan.d)
    return pl.pallas_call(
        functools.partial(spectral_back_kernel, plan, riders, len(earlier)),
        grid=(plan.q,),
        in_specs=[pair_block(plan, plan.t)]
        + [kept_spec] * 4
        + [whole(lat.shape), whole(lat_t.shape), whole(wide), whole(wide)]
        + [whole(x.shape) for x in earlier]
        + riders.specs(),
        out_specs=[
            pair_block(plan, plan.t),
            whole(small),
            whole(small),
            whole(thin),
            whole(thin),
        ]
        + riders.specs(),
        out_shape=[
            jax.ShapeDtypeStruct((plan.n, plan.q, plan.t, plan.d), BF),
            jax.ShapeDtypeStruct(small, F32),
            jax.ShapeDtypeStruct(small, F32),
            jax.ShapeDtypeStruct(thin, F32),
            jax.ShapeDtypeStruct(thin, F32),
        ]
        + riders.shapes(),
        scratch_shapes=[
            pltpu.VMEM(wide, F32),
            pltpu.VMEM(wide, F32),
            pltpu.VMEM((4 * HP, plan.d), BF),
            pltpu.VMEM((2 * HP, plan.d), BF),
        ]
        + riders.scratch(),
        compiler_params=params(collective_id),
        cost_estimate=cost(1e9, 1e6),
        name="spectral_backward",
    )(received, *kept, lat, lat_t, m1t, m2t, *earlier, *riders.arrays)


def last_kernel(
    plan,
    scale_ref,
    tok_ref,
    gx_ref,
    in_ref,
    gain_ref,
    lon_t_ref,
    perm_t_ref,
    *rest,
):
    out_ref, vec_ref, rows_ref = rest[-3:]
    i = pl.program_id(0)

    @pl.when(i == 0)
    def _():
        vec_ref[...] = jnp.zeros_like(vec_ref)
        deinterleave(plan, perm_t_ref, in_ref, rows_ref)

    for u in range(plan.rb):
        keep = jnp.where(scale_ref[i * plan.rb + u] > 0.0, 1.0, 0.0)
        unit, rstd = norm_parts(tok_ref[0, u].astype(F32))
        gx = gx_ref[u].astype(F32)
        grad = gx + dot_table(lon_t_ref, rows_ref[i * plan.rb + u])
        vec_ref[0:1] += jnp.sum(grad * unit, 0, keepdims=True) * keep
        vec_ref[1:2] += jnp.sum(grad, 0, keepdims=True) * keep
        out_ref[0, u] = (gx + norm_back(grad, unit, rstd, gain_ref[0:1])) * keep


def last_call(plan, s, scales, tokens, gx, received, gain, earlier):
    operands = [scales, tokens, gx, received, gain, plan.lon_t, plan.perm_t]
    in_specs = [
        SMEM,
        row_block(plan, s),
        own_block(plan),
        whole((plan.pairs, plan.t, plan.d)),
        whole((8, plan.d)),
        whole((2, plan.w, plan.ki)),
        whole(plan.perm_t.shape),
    ]
    aliases = {}
    if earlier is not None:
        aliases = {len(operands): 0}
        operands.append(earlier)
        in_specs.append(ANY)
    return pl.pallas_call(
        functools.partial(last_kernel, plan),
        grid=(plan.chunks,),
        in_specs=in_specs,
        out_specs=[row_block(plan, s), whole((2, plan.d))],
        out_shape=[
            jax.ShapeDtypeStruct((plan.s, plan.r, plan.w, plan.d), F32),
            jax.ShapeDtypeStruct((2, plan.d), F32),
        ],
        scratch_shapes=[pltpu.VMEM((plan.r, plan.ki, plan.d), BF)],
        input_output_aliases=aliases,
        compiler_params=params(),
        cost_estimate=cost(1e9, 1e6),
        name="lon_backward",
    )(*operands)


def band_kernel(plan, in_ref, *rest):
    out_ref, tall = rest[-2:]
    mb = plan.mb
    height = 2 * plan.kw
    for src in range(plan.n):
        for t in range(plan.kk):
            k = src * plan.kk + t
            if k >= plan.kw:
                continue
            both = in_ref[src, t // 2].astype(F32)
            for p in range(2):
                at = ((t % 2) * 2 + p) * mb
                part = both[at : at + mb]
                for g in range(plan.d // 128):
                    tall[g, pl.ds(2 * k + p, mb, stride=height), :] = part[
                        :, g * 128 : (g + 1) * 128
                    ]
    for m in range(mb):
        for g in range(plan.d // 128):
            piece = tall[g, m * height : (m + 1) * height, :].astype(BF)
            out_ref[0, m, :, :, g * 128 : (g + 1) * 128] = piece.reshape(plan.kw, 2, 128)


def band_call(plan, s, received, earlier):
    shape = (plan.s, plan.mb, plan.kw, 2, plan.d)
    operands = [received]
    in_specs = [whole(received.shape)]
    aliases = {}
    if earlier is not None:
        aliases = {1: 0}
        operands.append(earlier)
        in_specs.append(ANY)
    return pl.pallas_call(
        functools.partial(band_kernel, plan),
        grid=(1,),
        in_specs=in_specs,
        out_specs=pl.BlockSpec((1,) + shape[1:], lambda i: (s, 0, 0, 0, 0)),
        out_shape=jax.ShapeDtypeStruct(shape, BF),
        scratch_shapes=[pltpu.VMEM((plan.d // 128, 2 * plan.mb * plan.kw, 128), F32)],
        input_output_aliases=aliases,
        compiler_params=params(),
        cost_estimate=cost(1e8, 1e6),
        name="band_output",
    )(*operands)


def every_peer(total, step_of):
    def body(step, carry):
        step_of(step)
        return carry

    lax.fori_loop(1, total, body, 0)


def place(lanes, index):
    return {"batch": index // lanes, "lat": lax.rem(index, lanes)}


def greet_all(total, lanes, me):
    barrier = pltpu.get_barrier_semaphore()

    def greet(step):
        pl.semaphore_signal(
            barrier,
            inc=1,
            device_id=place(lanes, lax.rem(me + step, total)),
            device_id_type=pl.DeviceIdType.MESH,
        )

    every_peer(total, greet)
    pl.semaphore_wait(barrier, total - 1)


def block_sum_kernel(total, lanes, xs, riders, *rest):
    e = riders.count
    ins, srcs, rest = rest[:xs], rest[xs : xs + e], rest[xs + e :]
    outs, dsts, rest = rest[:xs], rest[xs : xs + e], rest[xs + e :]
    helds, sems = rest[:xs], rest[xs:]
    ride = riders.bind(srcs, dsts, sems[4 * xs :])
    me = lax.axis_index("batch") * lanes + lax.axis_index("lat")
    greet_all(total, lanes, me)

    def part(a, step, peer):
        return pltpu.make_async_remote_copy(
            src_ref=ins[a].at[peer],
            dst_ref=helds[a].at[step],
            send_sem=sems[4 * a].at[step],
            recv_sem=sems[4 * a + 1].at[step],
            device_id=place(lanes, peer),
            device_id_type=pl.DeviceIdType.MESH,
        )

    def result(a, step, peer, slot):
        return pltpu.make_async_remote_copy(
            src_ref=outs[a].at[me],
            dst_ref=outs[a].at[slot],
            send_sem=sems[4 * a + 2].at[step],
            recv_sem=sems[4 * a + 3].at[step],
            device_id=place(lanes, peer),
            device_id_type=pl.DeviceIdType.MESH,
        )

    ahead = lambda step: lax.rem(me + step, total)
    behind = lambda step: lax.rem(me + total - step, total)
    for a in range(xs):
        every_peer(total, lambda step: part(a, step, ahead(step)).start())
    ride_start(*ride, greet=False)
    for a in range(xs):
        helds[a][0] = ins[a][me]
        every_peer(total, lambda step: part(a, step, behind(step)).wait_recv())
        outs[a][me] = jnp.sum(helds[a][...].astype(F32), 0).astype(outs[a].dtype)
        every_peer(total, lambda step: result(a, step, ahead(step), me).start())
    for a in range(xs):
        every_peer(total, lambda step: part(a, step, ahead(step)).wait_send())
        every_peer(total, lambda step: result(a, step, behind(step), behind(step)).wait_recv())
        every_peer(total, lambda step: result(a, step, ahead(step), me).wait_send())
    ride_wait(*ride)


def block_sum(total, plan, xs, passengers, collective_id):
    riders = Riders(plan, passengers)
    vmem = pl.BlockSpec(memory_space=pltpu.VMEM)
    sems = [pltpu.SemaphoreType.DMA((total,))] * (4 * len(xs))
    return pl.pallas_call(
        functools.partial(block_sum_kernel, total, plan.n, len(xs), riders),
        in_specs=[vmem] * len(xs) + riders.specs(),
        out_specs=[vmem] * len(xs) + riders.specs(),
        out_shape=[jax.ShapeDtypeStruct(x.shape, x.dtype) for x in xs] + riders.shapes(),
        scratch_shapes=[pltpu.VMEM(x.shape, x.dtype) for x in xs] + sems + riders.scratch(),
        compiler_params=pltpu.CompilerParams(
            collective_id=collective_id, has_side_effects=True, vmem_limit_bytes=VMEM_BYTES
        ),
        cost_estimate=cost(1e8, 1e6),
        name="block_sum",
    )(*xs, *riders.arrays)


def pack(total, parts, dtype, rows):
    flat = jnp.concatenate([x.reshape(-1).astype(dtype) for x in parts])
    unit = total * rows * 128
    padded = -(-flat.shape[0] // unit) * unit
    return jnp.pad(flat, (0, padded - flat.shape[0])).reshape(total, -1, 128)


def unpack(packed, parts):
    flat = packed.reshape(-1).astype(F32)
    out, at = [], 0
    for x in parts:
        out.append(flat[at : at + x.size].reshape(x.shape))
        at += x.size
    return out


def whole_sum_kernel(total, lanes, x_ref, out_ref, held, send, recv):
    me = lax.axis_index("batch") * lanes + lax.axis_index("lat")
    greet_all(total, lanes, me)

    def part(step, peer):
        return pltpu.make_async_remote_copy(
            src_ref=x_ref,
            dst_ref=held.at[step],
            send_sem=send.at[step],
            recv_sem=recv.at[step],
            device_id=place(lanes, peer),
            device_id_type=pl.DeviceIdType.MESH,
        )

    ahead = lambda step: lax.rem(me + step, total)
    every_peer(total, lambda step: part(step, ahead(step)).start())
    held[0] = x_ref[...]
    every_peer(total, lambda step: part(step, ahead(step)).wait_recv())
    out_ref[...] = jnp.sum(held[...], 0)
    every_peer(total, lambda step: part(step, ahead(step)).wait_send())


def whole_sum(total, lanes, x, collective_id):
    sems = [pltpu.SemaphoreType.DMA((total,))] * 2
    return pl.pallas_call(
        functools.partial(whole_sum_kernel, total, lanes),
        in_specs=[pl.BlockSpec(memory_space=pltpu.VMEM)],
        out_specs=pl.BlockSpec(memory_space=pltpu.VMEM),
        out_shape=jax.ShapeDtypeStruct(x.shape, x.dtype),
        scratch_shapes=[pltpu.VMEM((total,) + x.shape, x.dtype)] + sems,
        compiler_params=pltpu.CompilerParams(
            collective_id=collective_id, has_side_effects=True, vmem_limit_bytes=VMEM_BYTES
        ),
        cost_estimate=cost(1e8, 1e6),
        name="whole_sum",
    )(x)


def convert_kernel(in_ref, first_ref, second_ref):
    first_ref[...] = in_ref[0].astype(F32).T
    second_ref[...] = in_ref[1].astype(F32)


def convert_call(x):
    _, ff, d = x.shape
    tile = 512
    return pl.pallas_call(
        convert_kernel,
        grid=(ff // tile,),
        in_specs=[pl.BlockSpec((2, tile, d), lambda i: (0, i, 0))],
        out_specs=[
            pl.BlockSpec((d, tile), lambda i: (0, i)),
            pl.BlockSpec((tile, d), lambda i: (i, 0)),
        ],
        out_shape=[jax.ShapeDtypeStruct((d, ff), F32), jax.ShapeDtypeStruct((ff, d), F32)],
        compiler_params=params(),
        cost_estimate=cost(1e6, 1e6),
        name="weight_output",
    )(x)


def on_device(
    bands,
    tokens,
    cotangent,
    sample_weight,
    row_count,
    band_count,
    norm1_gain,
    norm1_bias,
    spec_w1,
    spec_b1,
    spec_w2,
    spec_b2,
    norm2_gain,
    norm2_bias,
    fc1_weight,
    fc1_bias,
    fc2_weight,
    fc2_bias,
):
    lane = lax.axis_index("lat")
    n = lax.axis_size("lat")
    samples, row_slots, width, channels = tokens.shape
    blocks, size = spec_w1.shape[1], spec_w1.shape[2]
    plan = Plan(n, samples, row_slots, width, channels, bands)
    wb1, wb2 = wide_bias(spec_b1), wide_bias(spec_b2)
    row = lambda v: v.reshape(1, -1)
    blank = jnp.zeros_like(fc2_bias)
    vectors = jnp.stack([norm1_gain, norm1_bias, norm2_gain, norm2_bias, fc2_bias] + [blank] * 3)
    own_rows = jnp.sum(jnp.where(jnp.arange(n) == lane, row_count, 0))
    held = jnp.arange(row_slots) < own_rows
    scales = sample_weight.astype(F32)[:, None] * 0.5 * held[None, :].astype(F32)
    slot_step = jnp.arange(plan.kp)
    valid = ((slot_step < plan.kk) & (lane * plan.kk + slot_step < plan.kw)).astype(F32)
    grouped = (n, plan.q, plan.t, channels)
    listed = (plan.pairs, plan.t, channels)

    ids = itertools.count()
    spread = (-1,) + grouped

    def spectral_forward(x, passengers=()):
        collective_id = next(ids) if passengers else None
        out = spectral_call(
            plan,
            valid,
            x,
            lat,
            lat_t,
            slots,
            m1,
            wb1,
            m2,
            wb2,
            [forward[-1][6]] if forward else [],
            passengers,
            collective_id,
        )
        forward.append(out)
        return out[7:]

    def feed(s, back, sums, passengers):
        out = feed_call(
            plan,
            s,
            scales[s],
            tokens,
            cotangent,
            back.reshape(listed),
            vectors,
            fc1_weight,
            row(fc1_bias),
            fc2_weight,
            sums,
            s == samples - 1,
            passengers,
            next(ids),
        )
        feeds.append(out)
        return out[7:]

    def backward(s, grads, passengers=()):
        out = spectral_back_call(
            plan,
            blocks,
            size,
            grads,
            forward[s][2:6],
            lat,
            lat_t,
            m1t,
            m2t,
            list(spectral[-1][1:5]) if spectral else [],
            passengers,
            next(ids) if passengers else None,
        )
        spectral.append(out)
        return out[0], out[5:]

    forward, feeds, spectral, band_parts, grads, lon_grads = [], [], [], {}, {}, {}
    sent = first_call(plan, 0, 1, tokens, vectors)[0].reshape(spread)
    tables = Tables(plan, blocks, size)
    extra = tables.operands(row_count, band_count, spec_w1, spec_w2)
    others, lat, lat_t, slots, m1, m2, m1t, m2t, spectra = first_call(
        plan, 1, samples - 1, tokens, vectors, [(sent, 0)], next(ids), tables, extra
    )
    others = others.reshape(spread)
    (spectra,) = spectral_forward(spectra, [(others, 0)])
    (back,) = spectral_forward(spectra, [(forward[0][0], None)])
    for s in range(samples):
        sums = [feeds[-1][i] for i in (3, 4, 0, 5, 6)] if s else None
        kinds, passengers = [], []
        if s + 1 < samples:
            kinds.append("back")
            passengers.append((forward[s + 1][0], None))
        if s + 2 < samples:
            kinds.append("spectra")
            passengers.append((others, s + 1))
        if s >= 1:
            kinds.append("grads")
            passengers.append((feeds[s - 1][1].reshape(grouped), None))
        kinds.append("band")
        passengers.append((forward[s][1], None))
        arrived = dict(zip(kinds, feed(s, back, sums, passengers)))
        back = arrived.get("back")
        if s + 2 < samples:
            spectral_forward(arrived["spectra"])
        band_parts[s] = arrived["band"]
        if s >= 1:
            grads[s - 1] = arrived["grads"]
    after = lambda x, y: lax.optimization_barrier((x, y))[0]

    def last(s, earlier):
        return last_call(
            plan,
            s,
            scales[s],
            tokens,
            feeds[s][2],
            lon_grads[s].reshape(listed),
            vectors,
            earlier,
        )

    cores = [[j, j + 1] for j in range(0, n, 2)]
    chips = [list(range(c, n, 2)) for c in range(2)]
    large = lax.psum_scatter(
        feeds[-1][3], "lat", scatter_dimension=0, axis_index_groups=cores, tiled=True
    )
    spectrum = None
    for s in range(samples):
        spectrum = band_call(plan, s, band_parts[s], spectrum)
    large = after(large, spectrum)
    grads[0] = after(grads[0], (large, feeds[-1][6]))
    large = lax.psum_scatter(large, "batch", scatter_dimension=1, tiled=True)
    lon, got = backward(0, grads[0], [(feeds[-1][1].reshape(grouped), None)])
    grads[samples - 1] = got[0]
    for s in range(1, samples):
        if s == samples - 1:
            large = after(large, spectral[-1][3])
            grads[s] = after(grads[s], large)
            large = lax.psum(large, "lat", axis_index_groups=chips)
        lon, got = backward(s, grads[s], [(lon, None)])
        lon_grads[s - 1] = got[0]
    lon_grads[0] = after(lon_grads[0], spectral[-1][3])
    large = after(large, spectral[-1][3])
    lon = after(lon, large)
    large = lax.all_gather(large, "batch", axis=1, tiled=True)
    add = lambda parts: functools.reduce(jnp.add, parts)
    devices = lax.axis_size("batch") * n
    feed_vec = feeds[-1][6]
    block_grad = lambda i: spectral[-1][i].reshape(2, blocks, size, size)
    small = [
        feed_vec[1],
        feed_vec[2],
        feeds[-1][5],
        feed_vec[0],
        narrow_bias(spectral[-1][3], blocks, size),
        narrow_bias(spectral[-1][4], blocks, size),
        jnp.sum(forward[-1][6]).reshape(1),
    ]
    blocky = [block_grad(1), block_grad(2)]
    packed = [pack(devices, blocky, BF, 16), pack(devices, small, F32, 8)]
    packed = block_sum(devices, plan, packed, [(lon, None)], next(ids))
    lon_grads[samples - 1] = packed[2]
    blocky = unpack(packed[0], blocky)
    small = unpack(packed[1], small)
    for s in range(1, samples - 1):
        lon_grads[s] = after(lon_grads[s], packed[1])
    tokens_grad, finals = None, []
    for s in range(samples):
        tokens_grad, vec = last(s, tokens_grad)
        finals.append(vec)
    large = after(large, finals[-1])
    last_vec = after(add(finals), large)
    large = lax.all_gather(large, "lat", axis=0, axis_index_groups=cores, tiled=True)
    mixed = feeds[-1][0]

    last_vec = whole_sum(devices, n, last_vec, next(ids))
    large = after(large, last_vec)
    large = convert_call(large)
    zero_fraction = small[6][0] / (lax.axis_size("batch") * samples * H * plan.kw * 2 * channels)
    return (
        mixed,
        spectrum.transpose(0, 1, 3, 2, 4),
        tokens_grad,
        last_vec[0],
        last_vec[1],
        blocky[0],
        small[4],
        blocky[1],
        small[5],
        small[0],
        small[1],
        large[0],
        small[2].reshape(-1),
        large[1],
        small[3],
        zero_fraction,
    )


def solution(mesh):
    rows = P("batch", "lat", None, None)
    in_specs = (rows, rows, P("batch")) + (P(),) * 14
    out_specs = (rows, P("batch", "lat", None, None, None), rows) + (P(),) * 13
    lanes = mesh.shape["lat"]

    def run(tokens, cotangent, *rest):
        row_slots = tokens.shape[1] // lanes
        return jax.shard_map(
            functools.partial(on_device, row_slots + 1),
            mesh=mesh,
            in_specs=in_specs,
            out_specs=out_specs,
            check_vma=False,
        )(tokens, cotangent, *rest)

    return run
```
